32 devices in a mesh: dp: 4 (over z), seq: 8 (over y, x, core).
Axes of the slice: x: 2, y: 2, z: 4, core: 2. Of those that a mesh axis runs over, the one named last changes fastest.
Arguments:
- inputs: bfloat16 [12, 1024, 512], P('dp', 'seq'), may hold values from -6 to 6
- random_blocks: int32 [12, 8, 16, 3], P('dp', None, 'seq'), may hold values from 1 to 14, as said below
- entry_weight: bfloat16 [512, 1536], replicated, may hold values from -0.375 to 0.375
- query_bias: bfloat16 [512], replicated, may hold values from -1.5 to 1.5
- value_bias: bfloat16 [512], replicated, may hold values from -1.5 to 1.5
- out_weight: bfloat16 [512, 512], replicated, may hold values from -1 to 1
- out_bias: bfloat16 [512], replicated, may hold values from -1.5 to 1.5
- norm_gain: bfloat16 [512], replicated, may hold values from 0.5 to 1.5
- norm_shift: bfloat16 [512], replicated, may hold values from -1.5 to 1.5
- inner_weight: bfloat16 [512, 2048], replicated, may hold values from -0.25 to 0.25
- inner_bias: bfloat16 [2048], replicated, may hold values from -2.5 to 2.5
- outer_weight: bfloat16 [2048, 512], replicated, may hold values from -0.25 to 0.25
- outer_bias: bfloat16 [512], replicated, may hold values from -1.5 to 1.5
- final_gain: bfloat16 [512], replicated, may hold values from 0.5 to 1.5
- final_shift: bfloat16 [512], replicated, may hold values from -1.5 to 1.5
- cotangent: bfloat16 [12, 1024, 512], P('dp', 'seq'), may hold values from -6 to 6
Outputs:
- layer_out: bfloat16 [12, 1024, 512], P('dp', 'seq')
- input_grad: bfloat16 [12, 1024, 512], P('dp', 'seq')
- entry_weight_grad: float32 [512, 1536], replicated
- query_bias_grad: float32 [512], replicated
- value_bias_grad: float32 [512], replicated
- out_weight_grad: float32 [512, 512], replicated
- out_bias_grad: float32 [512], replicated
- norm_gain_grad: float32 [512], replicated
- norm_shift_grad: float32 [512], replicated
- inner_weight_grad: float32 [512, 2048], replicated
- inner_bias_grad: float32 [2048], replicated
- outer_weight_grad: float32 [2048, 512], replicated
- outer_bias_grad: float32 [512], replicated
- final_gain_grad: float32 [512], replicated
- final_shift_grad: float32 [512], replicated
The draws below stay inside these ranges and needn't reach their ends.
Inputs may be any that keep to these rules, and one draw needn't show every extreme that they name: `random_blocks`: every entry names an interior block (neither 0 nor 16 - 1) of the same sequence that does not lie on the index of seq holding the query block; the three entries of one query block lie on three different indices of seq. Over all entries held by one index of seq (its sequences, heads and query blocks), at most 21 lie on any one index of seq, and every index of seq reaches 21 for some index.
All inputs are finite; a program needn't handle non-finite values.
Results may differ from the reference program's by a relative error of at most 0.015.
The reference program's roundings to bfloat16 on the way count: a program that leaves them out, or rounds other values in their place, can miss the bound.
Values may be sent and summed in bfloat16 or wider, within the bound.
A program may use at most 192 MiB of HBM per device.

```python
import jax
import jax.numpy as jnp
from jax import lax

D = 512
HEADS = 8
HEAD = 64
FF = 2048
BLOCK = 64
SEQ_DEV = 3
TOK_DEV = 128
LENGTH = 1024
BLOCKS = 16
SEQS = 12
N_SEQ = 8


def draw_random_blocks(key, part):
    key = jax.random.fold_in(key, 7)
    order_key, inner_key = jax.random.split(key)
    per_dev = TOK_DEV // BLOCK
    choice_count = N_SEQ - 1
    group_count = SEQS // SEQ_DEV
    ranking = jax.random.randint(order_key, (group_count, N_SEQ, choice_count), 0, 1 << 20) * choice_count + jnp.arange(choice_count, dtype=jnp.int32)
    order = jnp.argsort(ranking, axis=-1, stable=True).astype(jnp.int32)
    shape_all = (SEQS, HEADS, BLOCKS, 3)
    seq_index = lax.broadcasted_iota(jnp.int32, shape_all, 0)
    head_index = lax.broadcasted_iota(jnp.int32, shape_all, 1)
    block_index = lax.broadcasted_iota(jnp.int32, shape_all, 2)
    pick_index = lax.broadcasted_iota(jnp.int32, shape_all, 3)
    group = seq_index // SEQ_DEV
    local_seq = seq_index % SEQ_DEV
    device = block_index // per_dev
    inner_block = block_index % per_dev
    position = ((local_seq * HEADS + head_index) * per_dev + inner_block) * 3 + pick_index
    offset = 1 + order[group, device, position % choice_count]
    owner = (device + offset) % N_SEQ
    within = jax.random.randint(inner_key, shape_all, 0, per_dev)
    within = jnp.where((owner == 0) & (within == 0), 1, within)
    within = jnp.where((owner == N_SEQ - 1) & (within == per_dev - 1), per_dev - 2, within)
    return (owner * per_dev + within).astype(jnp.int32)


def level_of(stream_key, dims, pieces, low, top_value):
    factor_of, own = 1.0, jax.random.fold_in(stream_key, 6)
    for dim, blocks in pieces:
        heights = jnp.exp(jax.random.uniform(jax.random.fold_in(own, dim), (blocks,), jnp.float32, low / len(pieces), top_value / len(pieces)))
        factor_of = factor_of * jnp.repeat(heights, dims[dim] // blocks).reshape([-1 if axis == dim else 1 for axis in range(len(dims))])
    return factor_of


def scatter_about(stream_key, dims, width, limit, shards=(), kind=jnp.bfloat16):
    loudness = level_of(stream_key, dims, shards, -0.22, 0.18) if shards else 1.0
    values = jax.random.normal(stream_key, dims, jnp.float32) * width * loudness
    return jnp.minimum(jnp.maximum(values, -limit), limit).astype(kind)


def setup_inputs(seed: int = 0) -> dict:
    key_list = jax.random.split(jax.random.key(seed), 17)
    return {
        "inputs": scatter_about(key_list[0], (SEQS, LENGTH, D), 1.0, 6.0, ((0, 4), (1, 8))),
        "random_blocks": draw_random_blocks(jax.random.fold_in(key_list[16], 71), 0),
        "entry_weight": scatter_about(key_list[2], (D, 3 * D), (D // 2) ** -0.5, 0.375),
        "query_bias": scatter_about(key_list[3], (D,), 0.3, 1.5),
        "value_bias": scatter_about(key_list[4], (D,), 0.3, 1.5),
        "out_weight": scatter_about(key_list[5], (D, D), (D // 16) ** -0.5, 1.0),
        "out_bias": scatter_about(key_list[6], (D,), 0.3, 1.5),
        "norm_gain": jnp.clip(1.0 + 0.1 * jax.random.normal(key_list[7], (D,), jnp.float32), 0.5, 1.5).astype(jnp.bfloat16),
        "norm_shift": scatter_about(key_list[8], (D,), 0.3, 1.5),
        "inner_weight": scatter_about(key_list[9], (D, FF), D ** -0.5, 0.25),
        "inner_bias": scatter_about(key_list[10], (FF,), 0.5, 2.5),
        "outer_weight": scatter_about(key_list[11], (FF, D), (FF // 4) ** -0.5, 0.25),
        "outer_bias": scatter_about(key_list[12], (D,), 0.3, 1.5),
        "final_gain": jnp.clip(1.0 + 0.1 * jax.random.normal(key_list[13], (D,), jnp.float32), 0.5, 1.5).astype(jnp.bfloat16),
        "final_shift": scatter_about(key_list[14], (D,), 0.3, 1.5),
        "cotangent": scatter_about(key_list[15], (SEQS, LENGTH, D), 1.0, 6.0, ((0, 4), (1, 8))),
    }


HIGHEST = lax.Precision.HIGHEST
EPSILON = 1e-05
NEGATIVE = -1e+30

@jax.custom_vjp
def low(v):
    return lax.optimization_barrier(v.astype(jnp.bfloat16)).astype(jnp.float32)

@jax.custom_vjp
def low_back(v):
    return v

def low_keep(v):
    return (low(v), None)

def low_pass(kept, grad):
    return (grad,)

def back_keep(v):
    return (v, None)

def back_low(kept, grad):
    return (low(grad),)
low.defvjp(low_keep, low_pass)
low_back.defvjp(back_keep, back_low)

def norm_apply(values, gain_vec, shift_vec):
    center = values - lax.optimization_barrier(jnp.mean(values, axis=-1, keepdims=True))
    spread = lax.optimization_barrier(jnp.mean(center * center, axis=-1, keepdims=True))
    return center * lax.rsqrt(spread + EPSILON) * gain_vec + shift_vec

def head_view(matrix):
    return matrix.reshape(BLOCKS, BLOCK, HEADS, HEAD).transpose(2, 0, 1, 3)

def mixing(queries, keys, values, random_rows):
    query_view = head_view(queries)

    def key_set(blocked):
        padded = jnp.pad(blocked, ((0, 0), (1, 1), (0, 0), (0, 0)))
        window = jnp.stack([padded[:, :BLOCKS], padded[:, 1:BLOCKS + 1], padded[:, 2:]], axis=2)
        global_kv = jnp.stack([blocked[:, 0], blocked[:, BLOCKS - 1]], axis=1)
        global_kv = jnp.broadcast_to(global_kv[:, None], (HEADS, BLOCKS, 2, BLOCK, HEAD))
        chosen = jax.vmap(lambda lookup, picked: lookup[picked])(blocked, random_rows)
        joined = jnp.concatenate([window, global_kv, chosen], axis=2)
        return joined.reshape(HEADS, BLOCKS, 8 * BLOCK, HEAD)
    key_all = key_set(head_view(keys))
    value_all = key_set(head_view(values))
    scores = low_back(jnp.einsum('hbqd,hbkd->hbqk', query_view, key_all, precision=HIGHEST))
    block_ids = jnp.arange(BLOCKS)[:, None]
    column = jnp.arange(8 * BLOCK)[None, :]
    neighbor = block_ids + column // BLOCK - 1
    key_keep = (column >= 3 * BLOCK) | (neighbor >= 1) & (neighbor <= BLOCKS - 2)
    scores = jnp.where(key_keep[None, :, None, :], scores, NEGATIVE)
    probability = jax.nn.softmax(scores, axis=-1)
    window_out = jnp.einsum('hbqk,hbkd->hbqd', low(probability), value_all, precision=HIGHEST)
    global_query = jnp.concatenate([query_view[:, 0], query_view[:, BLOCKS - 1]], axis=1)
    key_rows = keys.reshape(LENGTH, HEADS, HEAD).transpose(1, 0, 2)
    value_rows = values.reshape(LENGTH, HEADS, HEAD).transpose(1, 0, 2)
    global_scores = low_back(jnp.einsum('hqd,hkd->hqk', global_query, key_rows, precision=HIGHEST))
    global_prob = jax.nn.softmax(global_scores, axis=-1)
    global_out = jnp.einsum('hqk,hkd->hqd', global_prob, value_rows, precision=HIGHEST)
    global_out = global_out.reshape(HEADS, 2, BLOCK, HEAD)
    mixed = jnp.concatenate([global_out[:, :1], window_out[:, 1:BLOCKS - 1], global_out[:, 1:]], axis=1)
    return mixed.transpose(1, 2, 0, 3).reshape(LENGTH, HEADS * HEAD)

def layer(tokens_in, params, random_rows):
    entry_weight, query_bias, value_bias, out_weight, out_bias, norm_gain, norm_shift, inner_weight, inner_bias, outer_weight, outer_bias, final_gain, final_shift = params
    entry_out = jnp.dot(tokens_in, entry_weight, precision=HIGHEST)
    query_scale = HEAD ** (-0.5)
    packed = jnp.concatenate([(entry_out[:, :D] + query_bias) * query_scale, entry_out[:, D:2 * D], entry_out[:, 2 * D:] + value_bias], axis=1)
    packed = low_back(low(packed))
    attended = mixing(packed[:, :D], packed[:, D:2 * D], packed[:, 2 * D:], random_rows)
    attended = low_back(low(attended))
    branch = low_back(jnp.dot(attended, out_weight, precision=HIGHEST) + out_bias)
    first_norm = norm_apply(tokens_in + branch, norm_gain, norm_shift)
    inner_pre = low_back(jnp.dot(low(first_norm), inner_weight, precision=HIGHEST) + inner_bias)
    hidden = low(jax.nn.gelu(inner_pre, approximate=False))
    second = first_norm + low_back(jnp.dot(hidden, outer_weight, precision=HIGHEST) + outer_bias)
    return norm_apply(second, final_gain, final_shift)

def reference(inputs, random_blocks, entry_weight, query_bias, value_bias, out_weight, out_bias, norm_gain, norm_shift, inner_weight, inner_bias, outer_weight, outer_bias, final_gain, final_shift, cotangent):
    params = tuple((weight_in.astype(jnp.float32) for weight_in in (entry_weight, query_bias, value_bias, out_weight, out_bias, norm_gain, norm_shift, inner_weight, inner_bias, outer_weight, outer_bias, final_gain, final_shift)))

    def one_sequence(totals, item):
        tokens_seq, random_rows, incoming = item
        result, pull = jax.vjp(lambda tokens_in, *weights: layer(tokens_in, weights, random_rows), tokens_seq.astype(jnp.float32), *params)
        grads = pull(incoming.astype(jnp.float32))
        totals = tuple((summed + added for summed, added in zip(totals, grads[1:])))
        return (totals, (result.astype(jnp.bfloat16), grads[0].astype(jnp.bfloat16)))
    zeros = tuple((jnp.zeros_like(weight_in) for weight_in in params))
    totals, outputs = lax.scan(one_sequence, zeros, (inputs, random_blocks, cotangent))
    layer_out, input_grad = outputs
    return (layer_out, input_grad, totals[0], totals[1], totals[2], totals[3], totals[4], totals[5], totals[6], totals[7], totals[8], totals[9], totals[10], totals[11], totals[12])
```

```python
from functools import partial

import jax
import jax.numpy as jnp
from jax import lax
from jax.experimental import pallas as pl
from jax.experimental.pallas import tpu as pltpu
from jax.sharding import PartitionSpec as P

HEADS = 8
HEAD = 64
BLOCK = 64


HIGHEST = lax.Precision.HIGHEST
EPSILON = 1e-05
NEGATIVE = -1e30


def spread_2(value, axis, root):
    mine = lax.axis_index(axis) == root
    return lax.psum(jnp.where(mine, value, jnp.zeros_like(value)), axis)


def for_sending(value):

    def short(part):
        return part.astype(jnp.bfloat16) if part.dtype == jnp.float32 else part

    return jax.tree.map(short, value)


def extended(block, sides, width):
    for axis, dim in sides:
        count = lax.axis_size(axis)
        forward = [(i, i + 1) for i in range(count - 1)]
        backward = [(target, source) for source, target in forward]
        low = lax.ppermute(
            lax.slice_in_dim(block, block.shape[dim] - width, None, axis=dim), axis, forward
        )
        high = lax.ppermute(lax.slice_in_dim(block, 0, width, axis=dim), axis, backward)
        block = jnp.concatenate([low, block, high], axis=dim)
    return block


def combined_all(part, axis, combine):
    gathered = jax.tree.map(lambda a: lax.all_gather(a, axis), part)

    def take(source):
        return jax.tree.map(lambda a: lax.dynamic_index_in_dim(a, source, 0, False), gathered)

    return lax.fori_loop(
        1, lax.axis_size(axis), lambda source, state: combine(state, take(source)), take(0)
    )


def norm_apply(values, gain_vec, shift_vec):
    center = values - jnp.mean(values, axis=-1, keepdims=True)
    spread = jnp.mean(center * center, axis=-1, keepdims=True)
    return center * lax.rsqrt(spread + EPSILON) * gain_vec + shift_vec


def pair_blocks(row_data, head_count, block_rows):
    seq_count, length_here, full_width = row_data.shape
    head_width = full_width // (2 * head_count)
    shaped = row_data.reshape(
        seq_count, length_here // block_rows, block_rows, 2, head_count, head_width
    )
    return shaped.transpose(0, 4, 1, 2, 3, 5).reshape(
        seq_count, head_count, length_here // block_rows, block_rows, 2 * head_width
    )


def pair_tokens(blocked):
    seq_count, head_count, block_count, block_rows, double_width = blocked.shape
    head_width = double_width // 2
    shaped = blocked.reshape(seq_count, head_count, block_count, block_rows, 2, head_width)
    return shaped.transpose(0, 2, 3, 4, 1, 5).reshape(
        seq_count, block_count * block_rows, 2 * head_count * head_width
    )


def head_rows(row_data, head_count):
    seq_count, length_here, full_width = row_data.shape
    return row_data.reshape(seq_count, length_here, head_count, full_width // head_count).transpose(
        0, 2, 1, 3
    )


def row_heads(split_rows):
    seq_count, head_count, length_here, head_width = split_rows.shape
    return split_rows.transpose(0, 2, 1, 3).reshape(seq_count, length_here, head_count * head_width)


def merge_parts(earlier, later):
    peak_one, total_one, out_one = earlier
    peak_two, total_two, out_two = later
    row_peak = jnp.maximum(peak_one, peak_two)
    factor_one = jnp.exp(peak_one - row_peak)
    factor_two = jnp.exp(peak_two - row_peak)
    return (
        row_peak,
        total_one * factor_one + total_two * factor_two,
        out_one * factor_one[..., None] + out_two * factor_two[..., None],
    )


def share_rows(row_data, root_device):
    return spread_2(row_data, "seq", root_device)


def share_grads(grad_rows, grad_delta, root_device):
    return (
        spread_2(grad_rows.astype(jnp.bfloat16), "seq", root_device).astype(grad_rows.dtype),
        spread_2(for_sending(grad_delta), "seq", root_device).astype(grad_delta.dtype),
    )


def on_device(
    inputs,
    random_blocks,
    entry_weight,
    query_bias,
    value_bias,
    out_weight,
    out_bias,
    norm_gain,
    norm_shift,
    inner_weight,
    inner_bias,
    outer_weight,
    outer_bias,
    final_gain,
    final_shift,
    cotangent,
):
    seq_count, token_count, model_width = inputs.shape
    head_count = HEADS
    head_width = HEAD
    block_rows = BLOCK
    per_dev = token_count // block_rows
    devices = lax.axis_size("seq")
    device = lax.axis_index("seq")
    block_total = devices * per_dev
    request_total = seq_count * head_count * per_dev * 3
    capacity = (request_total + devices - 2) // (devices - 1)
    table_rows = seq_count * head_count * per_dev
    query_scale = head_width ** (-0.5)
    is_first = device == 0
    is_last = device == devices - 1
    bfloat = jnp.bfloat16
    single = jnp.float32
    flat_in = inputs.reshape(-1, model_width)
    entry_out = jnp.dot(flat_in, entry_weight, preferred_element_type=single)
    packed = jnp.concatenate(
        [
            (entry_out[:, :model_width] + query_bias) * query_scale,
            entry_out[:, model_width : 2 * model_width],
            entry_out[:, 2 * model_width :] + value_bias,
        ],
        axis=1,
    )
    packed = packed.astype(bfloat).reshape(seq_count, token_count, 3 * model_width)
    key_value = packed[:, :, model_width:]
    padded = extended(key_value, (("seq", 1),), block_rows)
    global_rows = jnp.concatenate(
        [
            share_rows(packed[:, :block_rows], 0),
            share_rows(packed[:, token_count - block_rows :], devices - 1),
        ],
        axis=1,
    )
    owners = (random_blocks // per_dev).reshape(-1)
    within = random_blocks % per_dev
    seq_index = lax.broadcasted_iota(jnp.int32, random_blocks.shape, 0)
    head_index = lax.broadcasted_iota(jnp.int32, random_blocks.shape, 1)
    request_codes = ((seq_index * head_count + head_index) * per_dev + within).reshape(-1)
    onehot = (owners[:, None] == jnp.arange(devices, dtype=jnp.int32)[None, :]).astype(jnp.int32)
    slot_index = jnp.sum((jnp.cumsum(onehot, axis=0) - onehot) * onehot, axis=1)
    slot_place = owners * capacity + slot_index
    requests = (
        jnp.full((devices * capacity,), -1, jnp.int32)
        .at[slot_place]
        .set(request_codes)
        .reshape(devices, capacity)
    )
    incoming = lax.all_to_all(requests, "seq", split_axis=0, concat_axis=0, tiled=True)
    head_table = pair_blocks(key_value, head_count, block_rows).reshape(
        table_rows, block_rows, 2 * head_width
    )
    served = head_table[jnp.maximum(incoming, 0)]
    served = jnp.where((incoming >= 0)[:, :, None, None], served, jnp.zeros((), bfloat))
    fetched = lax.all_to_all(served, "seq", split_axis=0, concat_axis=0, tiled=True)
    random_kv = fetched.reshape(devices * capacity, block_rows, 2 * head_width)[slot_place]
    random_kv = random_kv.reshape(seq_count, head_count, per_dev, 3, block_rows, 2 * head_width)
    window_view = pair_blocks(padded, head_count, block_rows)
    window_kv = jnp.stack(
        [window_view[:, :, :per_dev], window_view[:, :, 1 : per_dev + 1], window_view[:, :, 2:]],
        axis=3,
    )
    global_kv = pair_blocks(global_rows[:, :, model_width:], head_count, block_rows)
    global_kv = jnp.broadcast_to(
        global_kv[:, :, None], (seq_count, head_count, per_dev, 2, block_rows, 2 * head_width)
    )
    all_kv = jnp.concatenate([window_kv, global_kv, random_kv], axis=3).reshape(
        seq_count, head_count, per_dev, 8 * block_rows, 2 * head_width
    )
    key_part = all_kv[..., :head_width]
    value_part = all_kv[..., head_width:]
    query_view = head_rows(packed[:, :, :model_width], head_count).reshape(
        seq_count, head_count, per_dev, block_rows, head_width
    )
    block_ids = device * per_dev + jnp.arange(per_dev)[:, None]
    column = jnp.arange(8 * block_rows)[None, :]
    neighbor = block_ids + column // block_rows - 1
    key_keep = (column >= 3 * block_rows) | (neighbor >= 1) & (neighbor <= block_total - 2)
    key_keep = key_keep[None, None, :, None, :]

    def block_scores():
        raw_scores = jnp.einsum(
            "shiqd,shikd->shiqk", query_view, key_part, preferred_element_type=single
        )
        return jnp.where(key_keep, raw_scores, NEGATIVE)

    scores = block_scores()
    row_peak = jnp.max(scores, axis=-1, keepdims=True)
    exponent = jnp.exp(scores - row_peak)
    row_total = jnp.sum(exponent, axis=-1, keepdims=True)
    probability = exponent / row_total
    log_total = row_peak + jnp.log(row_total)
    prob_low = probability.astype(bfloat)
    window_out = jnp.einsum(
        "shiqk,shikd->shiqd", prob_low, value_part, preferred_element_type=single
    )
    global_query = head_rows(global_rows[:, :, :model_width], head_count)
    local_keys = head_rows(packed[:, :, model_width : 2 * model_width], head_count)
    local_values = head_rows(packed[:, :, 2 * model_width :], head_count)
    global_scores = jnp.einsum(
        "shqd,shkd->shqk", global_query, local_keys, preferred_element_type=single
    )
    global_peak = jnp.max(global_scores, axis=-1)
    global_exp = jnp.exp(global_scores - global_peak[..., None])
    global_total = jnp.sum(global_exp, axis=-1)
    global_sum = jnp.einsum(
        "shqk,shkd->shqd", global_exp, local_values.astype(single), precision=HIGHEST
    )
    global_peak, global_total, global_sum = combined_all(
        (global_peak, global_total, global_sum), "seq", merge_parts
    )
    global_out = global_sum / global_total[..., None]
    global_log = global_peak + jnp.log(global_total)
    block_pos = jnp.arange(per_dev)
    take_first = ((block_pos == 0) & is_first)[None, None, :, None, None]
    take_last = ((block_pos == per_dev - 1) & is_last)[None, None, :, None, None]
    combined = jnp.where(take_first, global_out[:, :, None, :block_rows], window_out)
    combined = jnp.where(take_last, global_out[:, :, None, block_rows:], combined)
    attended = (
        row_heads(combined.reshape(seq_count, head_count, token_count, head_width))
        .reshape(-1, model_width)
        .astype(bfloat)
    )
    branch = jnp.dot(attended, out_weight, preferred_element_type=single) + out_bias
    residual_in = flat_in.astype(single) + branch
    first_norm, first_pull = jax.vjp(
        norm_apply, residual_in, norm_gain.astype(single), norm_shift.astype(single)
    )
    first_low = first_norm.astype(bfloat)
    inner_pre = jnp.dot(first_low, inner_weight, preferred_element_type=single) + inner_bias
    activated, gelu_pull = jax.vjp(partial(jax.nn.gelu, approximate=False), inner_pre)
    hidden = activated.astype(bfloat)
    second = first_norm + (
        jnp.dot(hidden, outer_weight, preferred_element_type=single) + outer_bias
    )
    final_norm, final_pull = jax.vjp(
        norm_apply, second, final_gain.astype(single), final_shift.astype(single)
    )
    layer_out = final_norm.astype(bfloat).reshape(inputs.shape)
    grad_second, final_gain_grad, final_shift_grad = final_pull(
        cotangent.reshape(-1, model_width).astype(single)
    )
    grad_outer = grad_second.astype(bfloat)
    outer_weight_grad = jnp.dot(hidden.T, grad_outer, preferred_element_type=single)
    outer_bias_grad = jnp.sum(grad_outer.astype(single), axis=0)
    (grad_active,) = gelu_pull(jnp.dot(grad_outer, outer_weight.T, preferred_element_type=single))
    grad_inner = grad_active.astype(bfloat)
    inner_weight_grad = jnp.dot(first_low.T, grad_inner, preferred_element_type=single)
    inner_bias_grad = jnp.sum(grad_inner.astype(single), axis=0)
    grad_first = grad_second + jnp.dot(grad_inner, inner_weight.T, preferred_element_type=single)
    grad_resid, norm_gain_grad, norm_shift_grad = first_pull(grad_first)
    grad_branch = grad_resid.astype(bfloat)
    out_weight_grad = jnp.dot(attended.T, grad_branch, preferred_element_type=single)
    out_bias_grad = jnp.sum(grad_branch.astype(single), axis=0)
    grad_attended = jnp.dot(grad_branch, out_weight.T, preferred_element_type=single).astype(bfloat)
    grad_heads = head_rows(
        grad_attended.reshape(seq_count, token_count, model_width), head_count
    ).reshape(seq_count, head_count, per_dev, block_rows, head_width)
    grad_window = jnp.where(take_first | take_last, jnp.zeros((), bfloat), grad_heads)
    probability = jnp.exp(block_scores() - log_total)
    prob_low = probability.astype(bfloat)
    grad_prob = jnp.einsum(
        "shiqd,shikd->shiqk", grad_window, value_part, preferred_element_type=single
    )
    row_delta = jnp.sum(probability * grad_prob, axis=-1, keepdims=True)
    grad_scores = (probability * (grad_prob - row_delta)).astype(bfloat)
    grad_query_block = jnp.einsum(
        "shiqk,shikd->shiqd", grad_scores, key_part, preferred_element_type=single
    )
    grad_key_block = jnp.einsum(
        "shiqk,shiqd->shikd", grad_scores, query_view, preferred_element_type=single
    )
    grad_value_block = jnp.einsum(
        "shiqk,shiqd->shikd", prob_low, grad_window, preferred_element_type=single
    )
    grad_kv = jnp.concatenate([grad_key_block, grad_value_block], axis=-1).reshape(
        seq_count, head_count, per_dev, 8, block_rows, 2 * head_width
    )
    pad_none = ((0, 0), (0, 0))
    grad_pad = (
        jnp.pad(grad_kv[:, :, :, 0], pad_none + ((0, 2), (0, 0), (0, 0)))
        + jnp.pad(grad_kv[:, :, :, 1], pad_none + ((1, 1), (0, 0), (0, 0)))
        + jnp.pad(grad_kv[:, :, :, 2], pad_none + ((2, 0), (0, 0), (0, 0)))
    )
    grad_tokens = pair_tokens(grad_pad)
    edge_grads = jnp.concatenate(
        [grad_tokens[:, :block_rows], grad_tokens[:, token_count + block_rows :]], axis=1
    )
    returned = extended(edge_grads.astype(jnp.bfloat16), (("seq", 1),), block_rows).astype(
        edge_grads.dtype
    )
    gap = token_count - block_rows
    grad_kv_local = (
        grad_tokens[:, block_rows : block_rows + token_count]
        + jnp.pad(returned[:, :block_rows], ((0, 0), (0, gap), (0, 0)))
        + jnp.pad(returned[:, 3 * block_rows :], ((0, 0), (gap, 0), (0, 0)))
    )
    grad_global_kv = pair_tokens(jnp.sum(grad_kv[:, :, :, 3:5], axis=2))
    grad_random = grad_kv[:, :, :, 5:8].reshape(request_total, block_rows, 2 * head_width)
    outgoing = (
        jnp.zeros((devices * capacity, block_rows, 2 * head_width), single)
        .at[slot_place]
        .set(grad_random)
    )
    outgoing = outgoing.reshape(devices, capacity, block_rows, 2 * head_width)
    returned_random = lax.all_to_all(
        outgoing.astype(jnp.bfloat16), "seq", split_axis=0, concat_axis=0, tiled=True
    ).astype(outgoing.dtype)
    segment_ids = jnp.where(incoming >= 0, incoming, table_rows).reshape(-1)
    grad_table = jax.ops.segment_sum(
        returned_random.reshape(devices * capacity, block_rows, 2 * head_width),
        segment_ids,
        num_segments=table_rows + 1,
    )[:table_rows]
    grad_owned = pair_tokens(
        grad_table.reshape(seq_count, head_count, per_dev, block_rows, 2 * head_width)
    )
    first_cot = grad_heads[:, :, 0].astype(single)
    last_cot = grad_heads[:, :, per_dev - 1].astype(single)
    first_cot, first_delta = share_grads(
        first_cot, jnp.sum(first_cot * global_out[:, :, :block_rows], axis=-1), 0
    )
    last_cot, last_delta = share_grads(
        last_cot, jnp.sum(last_cot * global_out[:, :, block_rows:], axis=-1), devices - 1
    )
    global_cot = jnp.concatenate([first_cot, last_cot], axis=2)
    global_delta = jnp.concatenate([first_delta, last_delta], axis=2)
    global_prob = jnp.exp(
        jnp.einsum("shqd,shkd->shqk", global_query, local_keys, preferred_element_type=single)
        - global_log[..., None]
    )
    global_dprob = jnp.einsum(
        "shqd,shkd->shqk", global_cot.astype(bfloat), local_values, preferred_element_type=single
    )
    global_grads = (global_prob * (global_dprob - global_delta[..., None])).astype(bfloat)
    grad_global_query = jnp.einsum(
        "shqk,shkd->shqd", global_grads, local_keys, preferred_element_type=single
    )
    grad_local_key = jnp.einsum(
        "shqk,shqd->shkd", global_grads, global_query, preferred_element_type=single
    )
    grad_local_value = jnp.einsum("shqk,shqd->shkd", global_prob, global_cot, precision=HIGHEST)
    partials = jnp.concatenate([row_heads(grad_global_query), grad_global_kv], axis=-1)
    partials = lax.psum(partials.astype(jnp.bfloat16), "seq").astype(jnp.float32)
    owner_part = jnp.where(
        is_first, jnp.pad(partials[:, :block_rows], ((0, 0), (0, gap), (0, 0))), 0.0
    ) + jnp.where(is_last, jnp.pad(partials[:, block_rows:], ((0, 0), (gap, 0), (0, 0))), 0.0)
    grad_query_tokens = row_heads(
        grad_query_block.reshape(seq_count, head_count, token_count, head_width)
    )
    grad_kv_tokens = (
        grad_kv_local
        + grad_owned
        + jnp.concatenate([row_heads(grad_local_key), row_heads(grad_local_value)], axis=-1)
    )
    grad_packed = (
        jnp.concatenate([grad_query_tokens, grad_kv_tokens], axis=-1) + owner_part
    ).astype(bfloat)
    column_scale = jnp.concatenate(
        [jnp.full((model_width,), query_scale, single), jnp.ones((2 * model_width,), single)]
    )
    grad_entry = (
        (grad_packed.astype(single) * column_scale).astype(bfloat).reshape(-1, 3 * model_width)
    )
    entry_weight_grad = jnp.dot(flat_in.T, grad_entry, preferred_element_type=single)
    query_bias_grad = jnp.sum(grad_entry[:, :model_width].astype(single), axis=0)
    value_bias_grad = jnp.sum(grad_entry[:, 2 * model_width :].astype(single), axis=0)
    input_grad = (
        (grad_resid + jnp.dot(grad_entry, entry_weight.T, preferred_element_type=single))
        .astype(bfloat)
        .reshape(inputs.shape)
    )
    (
        total_entry,
        total_query,
        total_value,
        total_out,
        total_out_bias,
        total_norm_gain,
        total_norm_shift,
        total_inner,
        total_inner_bias,
        total_outer,
        total_outer_bias,
        total_final_gain,
        total_final_shift,
    ) = lax.psum(
        (
            entry_weight_grad,
            query_bias_grad,
            value_bias_grad,
            out_weight_grad,
            out_bias_grad,
            norm_gain_grad,
            norm_shift_grad,
            inner_weight_grad,
            inner_bias_grad,
            outer_weight_grad,
            outer_bias_grad,
            final_gain_grad,
            final_shift_grad,
        ),
        ("dp", "seq"),
    )
    return (
        layer_out,
        input_grad,
        total_entry,
        total_query,
        total_value,
        total_out,
        total_out_bias,
        total_norm_gain,
        total_norm_shift,
        total_inner,
        total_inner_bias,
        total_outer,
        total_outer_bias,
        total_final_gain,
        total_final_shift,
    )


MESH = pl.DeviceIdType.MESH
bfloat = jnp.bfloat16
single = jnp.float32
WIDE = 512
PIECE = 256
QUERIES = 256
INV_SQRT2 = 0.7071067811865476
INV_SQRT_2PI = 0.3989422804014327


def dot(a, b, a_dim, b_dim):
    return lax.dot_general(
        a, b, (((a_dim,), (b_dim,)), ((), ())), preferred_element_type=single
    )


def aligned(index, step):
    return pl.multiple_of(index, step)


class Place:
    def __init__(self, groups):
        self.groups = groups
        self.z = lax.axis_index("dp")
        self.me = lax.axis_index("seq")
        self.y = self.me // 4
        self.x = (self.me // 2) % 2
        self.core = self.me % 2

    def peer(self, offset):
        off_y, off_x, off_core = offset // 4, (offset // 2) % 2, offset % 2
        return (
            ((self.y + off_y) % 2) * 4
            + ((self.x + off_x) % 2) * 2
            + (self.core + off_core) % 2
        )

    def in_plane(self, offset):
        return (self.z, self.peer(offset))

    def in_column(self, offset):
        return ((self.z + offset) % self.groups, self.me)


def remote(src, dst, send, recv, device):
    return pltpu.make_async_remote_copy(
        src_ref=src,
        dst_ref=dst,
        send_sem=send,
        recv_sem=recv,
        device_id=device,
        device_id_type=MESH,
    )


def layer_kernel(
    groups,
    cut,
    x_ref,
    blocks_ref,
    we_hbm,
    qb_ref,
    vb_ref,
    wo_hbm,
    bo_ref,
    g1_ref,
    s1_ref,
    w1_hbm,
    b1_ref,
    w2_hbm,
    b2_ref,
    g2_ref,
    s2_ref,
    cot_hbm,
    out_ref,
    dx_ref,
    sums_hbm,
    small_ref,
    we,
    wo,
    w1,
    w2,
    cot,
    load_sem,
    send_qkv,
    qkv,
    krow,
    vrow,
    probs,
    inv_total,
    out_wide,
    out_low,
    att_t,
    hat1,
    rstd1,
    low1,
    hidden,
    slope,
    grad_inner,
    grad_outer,
    grad_resid,
    grad_branch,
    gatt_t,
    dout_t,
    dqkv,
    dk_acc,
    dv_acc,
    gpacked_t,
    x_t,
    part,
    r0,
    r1,
    r2,
    r3,
    total,
    small_in,
    a_send,
    a_recv,
    o_send,
    o_recv,
    d_send,
    d_recv,
    p_send,
    p_recv,
    rs_send,
    rs_recv,
    z_send,
    z_recv,
    v_send,
    v_recv,
    done_sem,
):
    seqs, tokens, width = x_ref.shape
    rows = seqs * tokens
    place = Place(groups)
    me = place.me
    barrier = pltpu.get_barrier_semaphore()
    for k in range(1, 8):
        pl.semaphore_signal(
            barrier, inc=1, device_id=place.in_plane(k), device_id_type=MESH
        )
    for k in range(1, groups):
        pl.semaphore_signal(
            barrier, inc=1, device_id=place.in_column(k), device_id_type=MESH
        )
    loads = [
        pltpu.make_async_copy(src, dst, load_sem.at[i])
        for i, (src, dst) in enumerate(
            ((we_hbm, we), (wo_hbm, wo), (w1_hbm, w1), (w2_hbm, w2), (cot_hbm, cot))
        )
    ]
    for load in loads:
        load.start()

    lane = lax.broadcasted_iota(jnp.int32, (16, tokens), 1)
    key_block = lax.broadcasted_iota(jnp.int32, (16, tokens), 0)
    query_block = me * 2 + lane // BLOCK
    inside = (key_block >= 1) & (key_block <= 14)
    near = (key_block >= query_block - 1) & (key_block <= query_block + 1) & inside
    fixed = jnp.where(near, 1.0, 0.0) + jnp.where(inside, 0.0, 1.0)
    outer_query = (query_block == 0) | (query_block == 15)
    for s in range(seqs):
        for h in range(HEADS):
            times = fixed
            for j in range(3):
                picked = jnp.where(
                    lane < BLOCK, blocks_ref[s, h, 0, j], blocks_ref[s, h, 1, j]
                )
                times = times + jnp.where(picked == key_block, 1.0, 0.0)
            send_qkv[s, h, 3 * HEAD :, :] = jnp.where(outer_query, 1.0, times).astype(bfloat)
    for s in range(seqs):
        x_t[:, s * tokens : (s + 1) * tokens] = x_ref[s].T
    small_ref[...] = jnp.zeros(small_ref.shape, single)

    def vec(ref):
        return ref[...].astype(single).reshape(1, ref.shape[0])

    pl.semaphore_wait(barrier, 7 + groups - 1)
    loads[0].wait()

    def qkv_copy(s, k):
        other = place.peer(k)
        return other, remote(
            send_qkv.at[s, other],
            qkv.at[s, :, pl.ds(aligned(me * tokens, 128), tokens)],
            a_send.at[s, k],
            a_recv.at[s, k],
            place.in_plane(k),
        )

    def pack(s, _):
        packed = jnp.dot(x_ref[s], we[...], preferred_element_type=single)
        for j, bias in enumerate((qb_ref, None, vb_ref)):
            piece = packed[:, j * width : (j + 1) * width]
            if bias is not None:
                piece = piece + vec(bias)
            if j == 0:
                piece = piece * HEAD**-0.5
            piece = piece.astype(bfloat).T
            for h in range(HEADS):
                send_qkv[s, h, j * HEAD : (j + 1) * HEAD, :] = piece[
                    h * HEAD : (h + 1) * HEAD
                ]
        for k in (6, 7, 2, 3, 4, 5, 1):
            qkv_copy(s, k)[1].start()
        own = pl.ds(aligned(me * tokens, 128), tokens)
        qkv[s, :, own] = send_qkv[s, me]
        return 0

    lax.fori_loop(0, seqs, pack, 0)

    def arrived_at(ref_of, send, recv, s):
        for k in range(1, 8):
            other = place.peer(k)
            slot = ref_of(other)
            remote(slot, slot, send.at[s, k], recv.at[s, k], place.in_plane(k)).wait_recv()

    def sent(ref_of, send, recv, s):
        for k in range(1, 8):
            slot = ref_of(place.peer(k))
            remote(slot, slot, send.at[s, k], recv.at[s, k], place.in_plane(k)).wait_send()

    def lanes_of(device):
        return pl.ds(aligned(device * tokens, 128), tokens)

    length = qkv.shape[2]
    chunks = length // QUERIES

    def attend(s, _):
        arrived_at(lambda other: qkv.at[s, :, lanes_of(other)], a_send, a_recv, s)
        krow[s] = qkv[s, HEAD : 2 * HEAD, :].T
        vrow[s] = qkv[s, 2 * HEAD : 3 * HEAD, :].T

        def chunk(i, _):
            at = pl.ds(aligned(i * QUERIES, QUERIES), QUERIES)
            score = jnp.dot(krow[s], qkv[s, 0:HEAD, at], preferred_element_type=single)
            times = qkv[s, 3 * HEAD :, at].astype(single)
            bias = jnp.where(times > 1.5, 0.6931471805599453, 0.0)
            bias = jnp.where(times > 0.5, bias, NEGATIVE)
            score = score.reshape(16, BLOCK, QUERIES) + bias[:, None, :]
            score = score.reshape(length, QUERIES)
            peak = jnp.max(score, axis=0, keepdims=True)
            grown = jnp.exp(score - peak)
            inverse = 1.0 / jnp.sum(grown, axis=0, keepdims=True)
            grown = grown.astype(bfloat)
            probs[s, :, at] = grown
            inv_total[s, :, at] = inverse
            result = inverse * jnp.dot(
                qkv[s, 2 * HEAD : 3 * HEAD, :], grown, preferred_element_type=single
            )
            out_wide[s, :, at] = result
            out_low[s, :, at] = result.astype(bfloat)
            return 0

        lax.fori_loop(0, chunks, chunk, 0)
        for k in (6, 7, 2, 3, 4, 5, 1):
            out_copy(s, k).start()
        att_t[head_rows_of(me), seq_lanes(s)] = out_low[s, :, lanes_of(me)]
        return 0

    def head_rows_of(device):
        return pl.ds(aligned(device * HEAD, HEAD), HEAD)

    def seq_lanes(s):
        return pl.ds(aligned(s * tokens, 128), tokens)

    def out_copy(s, k):
        return remote(
            out_low.at[s, :, lanes_of(place.peer(k))],
            att_t.at[head_rows_of(me), seq_lanes(s)],
            o_send.at[s, k],
            o_recv.at[s, k],
            place.in_plane(k),
        )

    lax.fori_loop(0, seqs, attend, 0)
    for load in loads[1:]:
        load.wait()

    def dout_copy(s, k):
        return remote(
            gatt_t.at[head_rows_of(place.peer(k)), seq_lanes(s)],
            dout_t.at[s, :, lanes_of(me)],
            d_send.at[s, k],
            d_recv.at[s, k],
            place.in_plane(k),
        )

    def mean_of(value):
        return jnp.mean(value, axis=-1, keepdims=True)

    def add_small(row, value):
        small_ref[row : row + 1, :] += jnp.sum(value, axis=0, keepdims=True)

    def tokens_part(s, _):
        arrived_at(lambda other: att_t.at[head_rows_of(other), seq_lanes(s)], o_send, o_recv, s)
        here = pl.ds(aligned(s * tokens, 128), tokens)
        branch = dot(att_t[:, here], wo[...], 0, 0) + vec(bo_ref)
        resid = x_ref[s].astype(single) + branch
        center = resid - mean_of(resid)
        scale1 = lax.rsqrt(mean_of(center * center) + EPSILON)
        normed1 = center * scale1
        hat1[here, :] = normed1
        rstd1[here, :] = scale1
        first = normed1 * vec(g1_ref) + vec(s1_ref)
        first_low = first.astype(bfloat)
        low1[here, :] = first_low
        second = first + vec(b2_ref)
        bias1 = vec(b1_ref)
        for j in range(w1.shape[1] // WIDE):
            span = slice(j * WIDE, (j + 1) * WIDE)
            pre = jnp.dot(first_low, w1[:, span], preferred_element_type=single) + bias1[:, span]
            share = 0.5 * (1.0 + lax.erf(pre * INV_SQRT2))
            active = (pre * share).astype(bfloat)
            hidden[here, span] = active
            slope[:, span] = share + pre * jnp.exp(-0.5 * pre * pre) * INV_SQRT_2PI
            second = second + jnp.dot(active, w2[span, :], preferred_element_type=single)
        center = second - mean_of(second)
        scale2 = lax.rsqrt(mean_of(center * center) + EPSILON)
        normed2 = center * scale2
        out_ref[s] = (normed2 * vec(g2_ref) + vec(s2_ref)).astype(bfloat)
        incoming = cot[s].astype(single)
        add_small(10, incoming * normed2)
        add_small(11, incoming)
        scaled = incoming * vec(g2_ref)
        grad_second = scale2 * (
            scaled - mean_of(scaled) - normed2 * mean_of(scaled * normed2)
        )
        grad_low = grad_second.astype(bfloat)
        grad_outer[here, :] = grad_low
        add_small(9, grad_low.astype(single))
        back = grad_second
        for j in range(w1.shape[1] // WIDE):
            span = slice(j * WIDE, (j + 1) * WIDE)
            grad_hidden = dot(grad_low, w2[span, :], 1, 1)
            inner = (grad_hidden * slope[:, span]).astype(bfloat)
            grad_inner[here, span] = inner
            add_small(5 + j, inner.astype(single))
            back = back + dot(inner, w1[:, span], 1, 1)
        normed1 = hat1[here, :]
        add_small(3, back * normed1)
        add_small(4, back)
        scaled = back * vec(g1_ref)
        grad = rstd1[here, :] * (scaled - mean_of(scaled) - normed1 * mean_of(scaled * normed1))
        grad_resid[here, :] = grad
        grad = grad.astype(bfloat)
        grad_branch[here, :] = grad
        add_small(2, grad.astype(single))
        gatt_t[:, here] = dot(wo[...], grad, 1, 1).astype(bfloat)
        for k in (6, 7, 2, 3, 4, 5, 1):
            dout_copy(s, k).start()
        dout_t[s, :, lanes_of(me)] = gatt_t[head_rows_of(me), seq_lanes(s)]
        return 0

    lax.fori_loop(0, seqs, tokens_part, 0)

    def steps_of(half):
        along_x, along_y = (place.x, 2), (place.y, 4)
        return (along_x, along_y) if half == 0 else (along_y, along_x)

    def spans_of(base, count, half):
        (first, first_off), (last, last_off) = steps_of(half)
        core_at = base + place.core * (count // 2)
        core_not = base + (1 - place.core) * (count // 2)
        first_at = core_at + first * (count // 4)
        first_not = core_at + (1 - first) * (count // 4)
        last_at = first_at + last * (count // 8)
        last_not = first_at + (1 - last) * (count // 8)
        return (
            (core_at, core_not, count // 2, 1),
            (first_at, first_not, count // 4, first_off),
            (last_at, last_not, count // 8, last_off),
        )

    def rows_at(start, count):
        return pl.ds(aligned(start, 16), count)

    def landing(stage, base, count, half):
        buffer = (r0, r1, r2)[stage]
        return buffer.at[half, pl.ds(base >> (stage + 1), count), :]

    def reduce_copy(unit, stage, half):
        index, base, count = unit
        _, away, size, offset = spans_of(base, count, half)[stage]
        return remote(
            part.at[half, rows_at(away, size), :],
            landing(stage, base, size, half),
            rs_send.at[index, stage, half],
            rs_recv.at[index, stage, half],
            place.in_plane(offset),
        )

    def add_rows(half, start, buffer, at, size):
        step = 128 if size % 128 == 0 else 64

        def add(i, _):
            mine = rows_at(start + i * step, step)
            other = buffer[half, pl.ds(aligned(at + i * step, 16), step), :]
            value = part[half, mine, :].astype(single) + other.astype(single)
            part[half, mine, :] = value.astype(bfloat)
            return 0

        lax.fori_loop(0, size // step, add, 0)

    def reduce_start(unit, stage):
        for half in range(2):
            reduce_copy(unit, stage, half).start()

    def reduce_finish(unit, stage):
        _, base, count = unit
        for half in range(2):
            reduce_copy(unit, stage, half).wait()
            keep, _, size, _ = spans_of(base, count, half)[stage]
            add_rows(half, keep, (r0, r1, r2)[stage], base >> (stage + 1), size)

    def column_copy(unit, half, offset):
        index, base, count = unit
        keep, _, size, _ = spans_of(base, count, half)[2]
        size = size // groups
        target = (place.z + offset) % groups
        return remote(
            part.at[half, rows_at(keep + target * size, size), :],
            r3.at[offset - 1, half, pl.ds(base // (8 * groups), size), :],
            z_send.at[index, 0, offset - 1, half],
            z_recv.at[index, 0, offset - 1, half],
            place.in_column(offset),
        )

    def column_start(unit):
        for half in range(2):
            for offset in range(1, groups):
                column_copy(unit, half, offset).start()

    def column_back(unit, half, offset):
        index, base, count = unit
        keep, _, size, _ = spans_of(base, count, half)[2]
        size = size // groups
        at = rows_at(keep + place.z * size, size)
        return remote(
            total.at[half, at, :],
            total.at[half, at, :],
            z_send.at[index, 1, offset - 1, half],
            z_recv.at[index, 1, offset - 1, half],
            place.in_column(offset),
        )

    def column_back_from(unit, half, offset):
        index, base, count = unit
        keep, _, size, _ = spans_of(base, count, half)[2]
        size = size // groups
        source = (place.z + groups - offset) % groups
        at = rows_at(keep + source * size, size)
        return remote(
            total.at[half, at, :],
            total.at[half, at, :],
            z_send.at[index, 1, offset - 1, half],
            z_recv.at[index, 1, offset - 1, half],
            place.in_column(offset),
        )

    def column_finish(unit):
        _, base, count = unit
        for half in range(2):
            keep, _, size, _ = spans_of(base, count, half)[2]
            size = size // groups
            for offset in range(1, groups):
                column_copy(unit, half, offset).wait()
            mine = rows_at(keep + place.z * size, size)
            value = part[half, mine, :].astype(single)
            for offset in range(1, groups):
                value = value + r3[
                    offset - 1, half, pl.ds(base // (8 * groups), size), :
                ].astype(single)
            total[half, mine, :] = value.astype(bfloat)
            for offset in range(1, groups):
                column_back(unit, half, offset).start()

    def column_end(unit):
        for half in range(2):
            for offset in range(1, groups):
                column_back(unit, half, offset).wait_send()
                column_back_from(unit, half, offset).wait_recv()

    def gather_copy(unit, stage, half, arriving):
        index, base, count = unit
        keep, away, size, offset = spans_of(base, count, half)[stage]
        at = rows_at(away if arriving else keep, size)
        return remote(
            total.at[half, at, :],
            total.at[half, at, :],
            rs_send.at[index, 3 + stage, half],
            rs_recv.at[index, 3 + stage, half],
            place.in_plane(offset),
        )

    def gather_start(unit, stage):
        for half in range(2):
            gather_copy(unit, stage, half, False).start()

    def gather_finish(unit, stage):
        for half in range(2):
            gather_copy(unit, stage, half, False).wait_send()
            gather_copy(unit, stage, half, True).wait_recv()

    def result_copy(unit):
        index, base, count = unit
        return pltpu.make_async_copy(
            total.at[:, pl.ds(base, count), :],
            sums_hbm.at[:, pl.ds(base, count), :],
            done_sem.at[index],
        )

    ff = hidden.shape[1]
    outer_unit = (0, 0, ff)
    inner_unit = (1, ff, ff)
    out_unit = (2, 2 * ff, width)
    entry_unit = (3, 2 * ff + width, 3 * width)

    def keep_part(base, value):
        low = value.astype(bfloat)
        for half in range(2):
            part[half, pl.ds(aligned(base, 128), value.shape[0]), :] = low[
                :, half * PIECE : (half + 1) * PIECE
            ]

    def outer_tile(j, _):
        at = pl.ds(aligned(j * WIDE, WIDE), WIDE)
        keep_part(j * WIDE, dot(hidden[:, at], grad_outer[...], 0, 0))
        return 0

    def inner_tile(j, _):
        at = pl.ds(aligned(j * WIDE, WIDE), WIDE)
        keep_part(ff + j * WIDE, dot(low1[...], grad_inner[:, at], 0, 0))
        return 0

    lax.fori_loop(0, ff // WIDE, outer_tile, 0)
    reduce_start(outer_unit, 0)
    lax.fori_loop(0, ff // WIDE, inner_tile, 0)
    reduce_start(inner_unit, 0)
    keep_part(2 * ff, jnp.dot(att_t[...], grad_branch[...], preferred_element_type=single))
    reduce_start(out_unit, 0)

    def pack_copies(s, k):
        other = place.peer(k)
        return [
            remote(
                dqkv.at[s, j * HEAD : (j + 1) * HEAD, lanes_of(other)],
                gpacked_t.at[j, head_rows_of(me), seq_lanes(s)],
                p_send.at[s, k, j],
                p_recv.at[s, k, j],
                place.in_plane(k),
            )
            for j in range(3)
        ]

    def back_chunk(s):
        def chunk(i, _):
            at = pl.ds(aligned(i * QUERIES, QUERIES), QUERIES)
            cot_t = dout_t[s, :, at].astype(single)
            inverse = inv_total[s, :, at]
            delta = inverse * jnp.sum(cot_t * out_wide[s, :, at], axis=0, keepdims=True)
            cot_low = (cot_t * inverse).astype(bfloat)
            grown = probs[s, :, at]
            grad = jnp.dot(vrow[s], cot_low, preferred_element_type=single) - delta
            grad = (grown.astype(single) * grad).astype(bfloat)
            query_grad = jnp.dot(
                qkv[s, HEAD : 2 * HEAD, :], grad, preferred_element_type=single
            )
            dqkv[s, 0:HEAD, at] = (query_grad.astype(bfloat) * HEAD**-0.5).astype(bfloat)
            dv_acc[...] += dot(cot_low, grown, 1, 1)
            dk_acc[...] += dot(qkv[s, 0:HEAD, at], grad, 1, 1)
            return 0

        return chunk

    def back_begin(s):
        arrived_at(lambda other: dout_t.at[s, :, lanes_of(other)], d_send, d_recv, s)
        dk_acc[...] = jnp.zeros(dk_acc.shape, single)
        dv_acc[...] = jnp.zeros(dv_acc.shape, single)

    def back_end(s):
        dqkv[s, HEAD : 2 * HEAD, :] = dk_acc[...].astype(bfloat)
        dqkv[s, 2 * HEAD :, :] = dv_acc[...].astype(bfloat)
        for k in (6, 7, 2, 3, 4, 5, 1):
            for copy in pack_copies(s, k):
                copy.start()
        for j in range(3):
            gpacked_t[j, head_rows_of(me), seq_lanes(s)] = dqkv[
                s, j * HEAD : (j + 1) * HEAD, lanes_of(me)
            ]

    def ahead(*units_and_stages):
        for unit, stage in units_and_stages:
            if stage < 2:
                reduce_finish(unit, stage)
                reduce_start(unit, stage + 1)
            elif stage == 2:
                reduce_finish(unit, stage)
                column_start(unit)
            elif stage == 3:
                column_finish(unit)
            elif stage == 4:
                column_end(unit)
                gather_start(unit, 2)
            elif stage == 5:
                gather_finish(unit, 2)
                gather_start(unit, 1)
            elif stage == 6:
                gather_finish(unit, 1)
                gather_start(unit, 0)
            else:
                gather_finish(unit, 0)
                result_copy(unit).start()

    ahead((outer_unit, 0), (inner_unit, 0), (out_unit, 0))
    plan = (
        ((outer_unit, 1),),
        ((inner_unit, 1), (out_unit, 1), (outer_unit, 2)),
        ((inner_unit, 2), (out_unit, 2), (outer_unit, 3)),
        ((inner_unit, 3), (out_unit, 3), (outer_unit, 4)),
        ((inner_unit, 4), (out_unit, 4), (outer_unit, 5)),
        ((inner_unit, 5), (out_unit, 5), (outer_unit, 6)),
    )
    for s in range(seqs):
        back_begin(s)
        for turn in range(2):
            half_chunks = chunks // 2
            lax.fori_loop(turn * half_chunks, (turn + 1) * half_chunks, back_chunk(s), 0)
            if turn == 1:
                back_end(s)
            ahead(*plan[2 * s + turn])

    for s in range(seqs):
        for k in range(1, 8):
            other = place.peer(k)
            for j in range(3):
                slot = gpacked_t.at[j, head_rows_of(other), seq_lanes(s)]
                remote(
                    slot, slot, p_send.at[s, k, j], p_recv.at[s, k, j], place.in_plane(k)
                ).wait_recv()
    entry_base = entry_unit[1]
    for j in range(3):
        keep_part(entry_base + j * width, dot(x_t[...], gpacked_t[j], 1, 1))
    reduce_start(entry_unit, 0)
    ones = jnp.ones((8, rows), bfloat)
    small_ref[0:1, :] = dot(ones, gpacked_t[0], 1, 1)[0:1]
    small_ref[1:2, :] = dot(ones, gpacked_t[2], 1, 1)[0:1]

    def small_copy(turn, device):
        return remote(
            small_ref, small_in.at[turn], v_send.at[turn], v_recv.at[turn], device
        )

    def small_add(turn):
        small_ref[...] += small_in[turn]

    small_copy(0, place.in_plane(1)).start()
    grad_in = grad_resid[...]
    for j in range(3):
        grad_in = grad_in + dot(gpacked_t[j], we[:, j * width : (j + 1) * width], 0, 1)
    for s in range(seqs):
        dx_ref[s] = grad_in[s * tokens : (s + 1) * tokens].astype(bfloat)
    small_copy(0, place.in_plane(1)).wait()
    small_add(0)
    small_copy(1, place.in_plane(2)).start()
    ahead((entry_unit, 0), (inner_unit, 6), (out_unit, 6), (outer_unit, 7))
    small_copy(1, place.in_plane(2)).wait()
    small_add(1)
    small_copy(2, place.in_plane(4)).start()
    ahead((entry_unit, 1), (inner_unit, 7), (out_unit, 7))
    small_copy(2, place.in_plane(4)).wait()
    small_add(2)

    def small_column(offset):
        return small_copy(2 + offset, place.in_column(offset))

    for offset in range(1, groups):
        small_column(offset).start()
    ahead((entry_unit, 2), (entry_unit, 3))
    for offset in range(1, groups):
        small_column(offset).wait()
    sum_small = jnp.zeros(small_ref.shape, single)
    mine = small_ref[...]
    for source in range(groups):
        value = jnp.zeros(small_ref.shape, single)
        for offset in range(groups):
            term = mine if offset == 0 else small_in[2 + offset]
            value = value + jnp.where((place.z + groups - offset) % groups == source, term, 0.0)
        sum_small = sum_small + value
    small_ref[...] = sum_small
    ahead((entry_unit, 4), (entry_unit, 5), (entry_unit, 6), (entry_unit, 7))
    for unit in (outer_unit, inner_unit, out_unit, entry_unit):
        result_copy(unit).wait()
    for s in range(seqs):
        sent(lambda other: send_qkv.at[s, other], a_send, a_recv, s)
        sent(lambda other: out_low.at[s, :, lanes_of(other)], o_send, o_recv, s)
        sent(lambda other: gatt_t.at[head_rows_of(other), seq_lanes(s)], d_send, d_recv, s)
        for k in range(1, 8):
            for copy in pack_copies(s, k):
                copy.wait_send()


def widen_kernel(sums_ref, small_ref, *outs):
    entry, query_b, value_b, out_w, out_b, gain1, shift1, inner_w, inner_b, outer_w, outer_b, gain2, shift2 = outs
    step = pl.program_id(0)
    tiles = outer_w.shape[0], inner_w.shape[1]
    del tiles
    value = jnp.concatenate([sums_ref[0], sums_ref[1]], axis=1).astype(single)

    @pl.when(step < 4)
    def _():
        outer_w[...] = value

    @pl.when((step >= 4) & (step < 8))
    def _():
        inner_w[...] = value

    @pl.when(step == 8)
    def _():
        out_w[...] = value

    @pl.when(step > 8)
    def _():
        entry[...] = value

    @pl.when(step == 0)
    def _():
        def row(at):
            return small_ref[at : at + 1, :].reshape(WIDE)

        for ref, at in (
            (query_b, 0),
            (value_b, 1),
            (out_b, 2),
            (gain1, 3),
            (shift1, 4),
            (outer_b, 9),
            (gain2, 10),
            (shift2, 11),
        ):
            ref[...] = row(at)
        for j in range(inner_b.shape[0] // WIDE):
            inner_b[j * WIDE : (j + 1) * WIDE] = row(5 + j)


def by_heads(groups, cut=None):
    def run(inputs, blocks, we, qb, vb, wo, bo, g1, s1, w1, b1, w2, b2, g2, s2, cot):
        seqs, tokens, width = inputs.shape
        ff = w1.shape[1]
        rows = seqs * tokens
        length = tokens * HEADS
        grad_rows = 2 * ff + 4 * width
        vmem = pl.BlockSpec(memory_space=pltpu.VMEM)
        smem = pl.BlockSpec(memory_space=pltpu.SMEM)
        hbm = pl.BlockSpec(memory_space=pl.ANY)
        dma = pltpu.SemaphoreType.DMA
        out, dx, sums, small = pl.pallas_call(
            partial(layer_kernel, groups, cut),
            out_shape=[
                jax.ShapeDtypeStruct(inputs.shape, bfloat),
                jax.ShapeDtypeStruct(inputs.shape, bfloat),
                jax.ShapeDtypeStruct((2, grad_rows, PIECE), bfloat),
                jax.ShapeDtypeStruct((16, width), single),
            ],
            in_specs=[
                vmem, smem, hbm, vmem, vmem, hbm, vmem, vmem, vmem, hbm, vmem, hbm, vmem, vmem,
                vmem, hbm,
            ],
            out_specs=[vmem, vmem, hbm, vmem],
            scratch_shapes=[
                pltpu.VMEM(we.shape, bfloat),
                pltpu.VMEM(wo.shape, bfloat),
                pltpu.VMEM(w1.shape, bfloat),
                pltpu.VMEM(w2.shape, bfloat),
                pltpu.VMEM(cot.shape, bfloat),
                dma((5,)),
                pltpu.VMEM((seqs, HEADS, 3 * HEAD + 16, tokens), bfloat),
                pltpu.VMEM((seqs, 3 * HEAD + 16, length), bfloat),
                pltpu.VMEM((seqs, length, HEAD), bfloat),
                pltpu.VMEM((seqs, length, HEAD), bfloat),
                pltpu.VMEM((seqs, length, length), bfloat),
                pltpu.VMEM((seqs, 1, length), single),
                pltpu.VMEM((seqs, HEAD, length), single),
                pltpu.VMEM((seqs, HEAD, length), bfloat),
                pltpu.VMEM((width, rows), bfloat),
                pltpu.VMEM((rows, width), single),
                pltpu.VMEM((rows, 1), single),
                pltpu.VMEM((rows, width), bfloat),
                pltpu.VMEM((rows, ff), bfloat),
                pltpu.VMEM((tokens, ff), single),
                pltpu.VMEM((rows, ff), bfloat),
                pltpu.VMEM((rows, width), bfloat),
                pltpu.VMEM((rows, width), single),
                pltpu.VMEM((rows, width), bfloat),
                pltpu.VMEM((width, rows), bfloat),
                pltpu.VMEM((seqs, HEAD, length), bfloat),
                pltpu.VMEM((seqs, 3 * HEAD, length), bfloat),
                pltpu.VMEM((HEAD, length), single),
                pltpu.VMEM((HEAD, length), single),
                pltpu.VMEM((3, width, rows), bfloat),
                pltpu.VMEM((width, rows), bfloat),
                pltpu.VMEM((2, grad_rows, PIECE), bfloat),
                pltpu.VMEM((2, grad_rows // 2, PIECE), bfloat),
                pltpu.VMEM((2, grad_rows // 4, PIECE), bfloat),
                pltpu.VMEM((2, grad_rows // 8, PIECE), bfloat),
                pltpu.VMEM((max(groups - 1, 1), 2, grad_rows // (8 * groups), PIECE), bfloat),
                pltpu.VMEM((2, grad_rows, PIECE), bfloat),
                pltpu.VMEM((3 + groups, 16, width), single),
                dma((seqs, 8)),
                dma((seqs, 8)),
                dma((seqs, 8)),
                dma((seqs, 8)),
                dma((seqs, 8)),
                dma((seqs, 8)),
                dma((seqs, 8, 3)),
                dma((seqs, 8, 3)),
                dma((4, 6, 2)),
                dma((4, 6, 2)),
                dma((4, 2, max(groups - 1, 1), 2)),
                dma((4, 2, max(groups - 1, 1), 2)),
                dma((3 + groups,)),
                dma((3 + groups,)),
                dma((4,)),
            ],
            compiler_params=pltpu.CompilerParams(
                collective_id=0, has_side_effects=True, vmem_limit_bytes=60 * 2**20
            ),
            name="layer",
        )(inputs, blocks, we, qb, vb, wo, bo, g1, s1, w1, b1, w2, b2, g2, s2, cot)

        def flat(size):
            return pl.BlockSpec((size,), lambda i: (0,))

        def shape(*dims):
            return jax.ShapeDtypeStruct(dims, single)

        tile = (WIDE, WIDE)
        grads = pl.pallas_call(
            widen_kernel,
            grid=(grad_rows // WIDE,),
            in_specs=[
                pl.BlockSpec((2, WIDE, PIECE), lambda i: (0, i, 0)),
                pl.BlockSpec((16, width), lambda i: (0, 0)),
            ],
            out_specs=[
                pl.BlockSpec(tile, lambda i: (0, jnp.clip(i - 9, 0, 2))),
                flat(width),
                flat(width),
                pl.BlockSpec(tile, lambda i: (0, 0)),
                flat(width),
                flat(width),
                flat(width),
                pl.BlockSpec(tile, lambda i: (0, jnp.clip(i - 4, 0, 3))),
                flat(ff),
                pl.BlockSpec(tile, lambda i: (jnp.clip(i, 0, 3), 0)),
                flat(width),
                flat(width),
                flat(width),
            ],
            out_shape=[
                shape(width, 3 * width),
                shape(width),
                shape(width),
                shape(width, width),
                shape(width),
                shape(width),
                shape(width),
                shape(width, ff),
                shape(ff),
                shape(ff, width),
                shape(width),
                shape(width),
                shape(width),
            ],
            name="widen",
        )(sums, small)
        return (out, dx, *grads)

    return run


def solution(mesh):
    in_specs = (
        P("dp", "seq", None),
        P("dp", None, "seq", None),
        P(),
        P(),
        P(),
        P(),
        P(),
        P(),
        P(),
        P(),
        P(),
        P(),
        P(),
        P(),
        P(),
        P("dp", "seq", None),
    )
    out_specs = (
        P("dp", "seq", None),
        P("dp", "seq", None),
        P(),
        P(),
        P(),
        P(),
        P(),
        P(),
        P(),
        P(),
        P(),
        P(),
        P(),
        P(),
        P(),
    )
    heads_fit = mesh.shape["seq"] == HEADS
    plan = by_heads(mesh.shape["dp"]) if heads_fit else on_device
    return jax.shard_map(
        plan, mesh=mesh, in_specs=in_specs, out_specs=out_specs, check_vma=False
    )
```

```python
from functools import partial

import jax
import jax.numpy as jnp
from jax import lax
from jax.experimental import pallas as pl
from jax.experimental.pallas import tpu as pltpu
from jax.sharding import PartitionSpec as P

HEADS = 8
HEAD = 64
BLOCK = 64


HIGHEST = lax.Precision.HIGHEST
EPSILON = 1e-05
NEGATIVE = -1e30


def spread_2(value, axis, root):
    mine = lax.axis_index(axis) == root
    return lax.psum(jnp.where(mine, value, jnp.zeros_like(value)), axis)


def for_sending(value):

    def short(part):
        return part.astype(jnp.bfloat16) if part.dtype == jnp.float32 else part

    return jax.tree.map(short, value)


def extended(block, sides, width):
    for axis, dim in sides:
        count = lax.axis_size(axis)
        forward = [(i, i + 1) for i in range(count - 1)]
        backward = [(target, source) for source, target in forward]
        low = lax.ppermute(
            lax.slice_in_dim(block, block.shape[dim] - width, None, axis=dim), axis, forward
        )
        high = lax.ppermute(lax.slice_in_dim(block, 0, width, axis=dim), axis, backward)
        block = jnp.concatenate([low, block, high], axis=dim)
    return block


def combined_all(part, axis, combine):
    gathered = jax.tree.map(lambda a: lax.all_gather(a, axis), part)

    def take(source):
        return jax.tree.map(lambda a: lax.dynamic_index_in_dim(a, source, 0, False), gathered)

    return lax.fori_loop(
        1, lax.axis_size(axis), lambda source, state: combine(state, take(source)), take(0)
    )


def norm_apply(values, gain_vec, shift_vec):
    center = values - jnp.mean(values, axis=-1, keepdims=True)
    spread = jnp.mean(center * center, axis=-1, keepdims=True)
    return center * lax.rsqrt(spread + EPSILON) * gain_vec + shift_vec


def pair_blocks(row_data, head_count, block_rows):
    seq_count, length_here, full_width = row_data.shape
    head_width = full_width // (2 * head_count)
    shaped = row_data.reshape(
        seq_count, length_here // block_rows, block_rows, 2, head_count, head_width
    )
    return shaped.transpose(0, 4, 1, 2, 3, 5).reshape(
        seq_count, head_count, length_here // block_rows, block_rows, 2 * head_width
    )


def pair_tokens(blocked):
    seq_count, head_count, block_count, block_rows, double_width = blocked.shape
    head_width = double_width // 2
    shaped = blocked.reshape(seq_count, head_count, block_count, block_rows, 2, head_width)
    return shaped.transpose(0, 2, 3, 4, 1, 5).reshape(
        seq_count, block_count * block_rows, 2 * head_count * head_width
    )


def head_rows(row_data, head_count):
    seq_count, length_here, full_width = row_data.shape
    return row_data.reshape(seq_count, length_here, head_count, full_width // head_count).transpose(
        0, 2, 1, 3
    )


def row_heads(split_rows):
    seq_count, head_count, length_here, head_width = split_rows.shape
    return split_rows.transpose(0, 2, 1, 3).reshape(seq_count, length_here, head_count * head_width)


def merge_parts(earlier, later):
    peak_one, total_one, out_one = earlier
    peak_two, total_two, out_two = later
    row_peak = jnp.maximum(peak_one, peak_two)
    factor_one = jnp.exp(peak_one - row_peak)
    factor_two = jnp.exp(peak_two - row_peak)
    return (
        row_peak,
        total_one * factor_one + total_two * factor_two,
        out_one * factor_one[..., None] + out_two * factor_two[..., None],
    )


def share_rows(row_data, root_device):
    return spread_2(row_data, "seq", root_device)


def share_grads(grad_rows, grad_delta, root_device):
    return (
        spread_2(grad_rows.astype(jnp.bfloat16), "seq", root_device).astype(grad_rows.dtype),
        spread_2(for_sending(grad_delta), "seq", root_device).astype(grad_delta.dtype),
    )


def on_device(
    inputs,
    random_blocks,
    entry_weight,
    query_bias,
    value_bias,
    out_weight,
    out_bias,
    norm_gain,
    norm_shift,
    inner_weight,
    inner_bias,
    outer_weight,
    outer_bias,
    final_gain,
    final_shift,
    cotangent,
):
    seq_count, token_count, model_width = inputs.shape
    head_count = HEADS
    head_width = HEAD
    block_rows = BLOCK
    per_dev = token_count // block_rows
    devices = lax.axis_size("seq")
    device = lax.axis_index("seq")
    block_total = devices * per_dev
    request_total = seq_count * head_count * per_dev * 3
    capacity = (request_total + devices - 2) // (devices - 1)
    table_rows = seq_count * head_count * per_dev
    query_scale = head_width ** (-0.5)
    is_first = device == 0
    is_last = device == devices - 1
    bfloat = jnp.bfloat16
    single = jnp.float32
    flat_in = inputs.reshape(-1, model_width)
    entry_out = jnp.dot(flat_in, entry_weight, preferred_element_type=single)
    packed = jnp.concatenate(
        [
            (entry_out[:, :model_width] + query_bias) * query_scale,
            entry_out[:, model_width : 2 * model_width],
            entry_out[:, 2 * model_width :] + value_bias,
        ],
        axis=1,
    )
    packed = packed.astype(bfloat).reshape(seq_count, token_count, 3 * model_width)
    key_value = packed[:, :, model_width:]
    padded = extended(key_value, (("seq", 1),), block_rows)
    global_rows = jnp.concatenate(
        [
            share_rows(packed[:, :block_rows], 0),
            share_rows(packed[:, token_count - block_rows :], devices - 1),
        ],
        axis=1,
    )
    owners = (random_blocks // per_dev).reshape(-1)
    within = random_blocks % per_dev
    seq_index = lax.broadcasted_iota(jnp.int32, random_blocks.shape, 0)
    head_index = lax.broadcasted_iota(jnp.int32, random_blocks.shape, 1)
    request_codes = ((seq_index * head_count + head_index) * per_dev + within).reshape(-1)
    onehot = (owners[:, None] == jnp.arange(devices, dtype=jnp.int32)[None, :]).astype(jnp.int32)
    slot_index = jnp.sum((jnp.cumsum(onehot, axis=0) - onehot) * onehot, axis=1)
    slot_place = owners * capacity + slot_index
    requests = (
        jnp.full((devices * capacity,), -1, jnp.int32)
        .at[slot_place]
        .set(request_codes)
        .reshape(devices, capacity)
    )
    incoming = lax.all_to_all(requests, "seq", split_axis=0, concat_axis=0, tiled=True)
    head_table = pair_blocks(key_value, head_count, block_rows).reshape(
        table_rows, block_rows, 2 * head_width
    )
    served = head_table[jnp.maximum(incoming, 0)]
    served = jnp.where((incoming >= 0)[:, :, None, None], served, jnp.zeros((), bfloat))
    fetched = lax.all_to_all(served, "seq", split_axis=0, concat_axis=0, tiled=True)
    random_kv = fetched.reshape(devices * capacity, block_rows, 2 * head_width)[slot_place]
    random_kv = random_kv.reshape(seq_count, head_count, per_dev, 3, block_rows, 2 * head_width)
    window_view = pair_blocks(padded, head_count, block_rows)
    window_kv = jnp.stack(
        [window_view[:, :, :per_dev], window_view[:, :, 1 : per_dev + 1], window_view[:, :, 2:]],
        axis=3,
    )
    global_kv = pair_blocks(global_rows[:, :, model_width:], head_count, block_rows)
    global_kv = jnp.broadcast_to(
        global_kv[:, :, None], (seq_count, head_count, per_dev, 2, block_rows, 2 * head_width)
    )
    all_kv = jnp.concatenate([window_kv, global_kv, random_kv], axis=3).reshape(
        seq_count, head_count, per_dev, 8 * block_rows, 2 * head_width
    )
    key_part = all_kv[..., :head_width]
    value_part = all_kv[..., head_width:]
    query_view = head_rows(packed[:, :, :model_width], head_count).reshape(
        seq_count, head_count, per_dev, block_rows, head_width
    )
    block_ids = device * per_dev + jnp.arange(per_dev)[:, None]
    column = jnp.arange(8 * block_rows)[None, :]
    neighbor = block_ids + column // block_rows - 1
    key_keep = (column >= 3 * block_rows) | (neighbor >= 1) & (neighbor <= block_total - 2)
    key_keep = key_keep[None, None, :, None, :]

    def block_scores():
        raw_scores = jnp.einsum(
            "shiqd,shikd->shiqk", query_view, key_part, preferred_element_type=single
        )
        return jnp.where(key_keep, raw_scores, NEGATIVE)

    scores = block_scores()
    row_peak = jnp.max(scores, axis=-1, keepdims=True)
    exponent = jnp.exp(scores - row_peak)
    row_total = jnp.sum(exponent, axis=-1, keepdims=True)
    probability = exponent / row_total
    log_total = row_peak + jnp.log(row_total)
    prob_low = probability.astype(bfloat)
    window_out = jnp.einsum(
        "shiqk,shikd->shiqd", prob_low, value_part, preferred_element_type=single
    )
    global_query = head_rows(global_rows[:, :, :model_width], head_count)
    local_keys = head_rows(packed[:, :, model_width : 2 * model_width], head_count)
    local_values = head_rows(packed[:, :, 2 * model_width :], head_count)
    global_scores = jnp.einsum(
        "shqd,shkd->shqk", global_query, local_keys, preferred_element_type=single
    )
    global_peak = jnp.max(global_scores, axis=-1)
    global_exp = jnp.exp(global_scores - global_peak[..., None])
    global_total = jnp.sum(global_exp, axis=-1)
    global_sum = jnp.einsum(
        "shqk,shkd->shqd", global_exp, local_values.astype(single), precision=HIGHEST
    )
    global_peak, global_total, global_sum = combined_all(
        (global_peak, global_total, global_sum), "seq", merge_parts
    )
    global_out = global_sum / global_total[..., None]
    global_log = global_peak + jnp.log(global_total)
    block_pos = jnp.arange(per_dev)
    take_first = ((block_pos == 0) & is_first)[None, None, :, None, None]
    take_last = ((block_pos == per_dev - 1) & is_last)[None, None, :, None, None]
    combined = jnp.where(take_first, global_out[:, :, None, :block_rows], window_out)
    combined = jnp.where(take_last, global_out[:, :, None, block_rows:], combined)
    attended = (
        row_heads(combined.reshape(seq_count, head_count, token_count, head_width))
        .reshape(-1, model_width)
        .astype(bfloat)
    )
    branch = jnp.dot(attended, out_weight, preferred_element_type=single) + out_bias
    residual_in = flat_in.astype(single) + branch
    first_norm, first_pull = jax.vjp(
        norm_apply, residual_in, norm_gain.astype(single), norm_shift.astype(single)
    )
    first_low = first_norm.astype(bfloat)
    inner_pre = jnp.dot(first_low, inner_weight, preferred_element_type=single) + inner_bias
    activated, gelu_pull = jax.vjp(partial(jax.nn.gelu, approximate=False), inner_pre)
    hidden = activated.astype(bfloat)
    second = first_norm + (
        jnp.dot(hidden, outer_weight, preferred_element_type=single) + outer_bias
    )
    final_norm, final_pull = jax.vjp(
        norm_apply, second, final_gain.astype(single), final_shift.astype(single)
    )
    layer_out = final_norm.astype(bfloat).reshape(inputs.shape)
    grad_second, final_gain_grad, final_shift_grad = final_pull(
        cotangent.reshape(-1, model_width).astype(single)
    )
    grad_outer = grad_second.astype(bfloat)
    outer_weight_grad = jnp.dot(hidden.T, grad_outer, preferred_element_type=single)
    outer_bias_grad = jnp.sum(grad_outer.astype(single), axis=0)
    (grad_active,) = gelu_pull(jnp.dot(grad_outer, outer_weight.T, preferred_element_type=single))
    grad_inner = grad_active.astype(bfloat)
    inner_weight_grad = jnp.dot(first_low.T, grad_inner, preferred_element_type=single)
    inner_bias_grad = jnp.sum(grad_inner.astype(single), axis=0)
    grad_first = grad_second + jnp.dot(grad_inner, inner_weight.T, preferred_element_type=single)
    grad_resid, norm_gain_grad, norm_shift_grad = first_pull(grad_first)
    grad_branch = grad_resid.astype(bfloat)
    out_weight_grad = jnp.dot(attended.T, grad_branch, preferred_element_type=single)
    out_bias_grad = jnp.sum(grad_branch.astype(single), axis=0)
    grad_attended = jnp.dot(grad_branch, out_weight.T, preferred_element_type=single).astype(bfloat)
    grad_heads = head_rows(
        grad_attended.reshape(seq_count, token_count, model_width), head_count
    ).reshape(seq_count, head_count, per_dev, block_rows, head_width)
    grad_window = jnp.where(take_first | take_last, jnp.zeros((), bfloat), grad_heads)
    probability = jnp.exp(block_scores() - log_total)
    prob_low = probability.astype(bfloat)
    grad_prob = jnp.einsum(
        "shiqd,shikd->shiqk", grad_window, value_part, preferred_element_type=single
    )
    row_delta = jnp.sum(probability * grad_prob, axis=-1, keepdims=True)
    grad_scores = (probability * (grad_prob - row_delta)).astype(bfloat)
    grad_query_block = jnp.einsum(
        "shiqk,shikd->shiqd", grad_scores, key_part, preferred_element_type=single
    )
    grad_key_block = jnp.einsum(
        "shiqk,shiqd->shikd", grad_scores, query_view, preferred_element_type=single
    )
    grad_value_block = jnp.einsum(
        "shiqk,shiqd->shikd", prob_low, grad_window, preferred_element_type=single
    )
    grad_kv = jnp.concatenate([grad_key_block, grad_value_block], axis=-1).reshape(
        seq_count, head_count, per_dev, 8, block_rows, 2 * head_width
    )
    pad_none = ((0, 0), (0, 0))
    grad_pad = (
        jnp.pad(grad_kv[:, :, :, 0], pad_none + ((0, 2), (0, 0), (0, 0)))
        + jnp.pad(grad_kv[:, :, :, 1], pad_none + ((1, 1), (0, 0), (0, 0)))
        + jnp.pad(grad_kv[:, :, :, 2], pad_none + ((2, 0), (0, 0), (0, 0)))
    )
    grad_tokens = pair_tokens(grad_pad)
    edge_grads = jnp.concatenate(
        [grad_tokens[:, :block_rows], grad_tokens[:, token_count + block_rows :]], axis=1
    )
    returned = extended(edge_grads.astype(jnp.bfloat16), (("seq", 1),), block_rows).astype(
        edge_grads.dtype
    )
    gap = token_count - block_rows
    grad_kv_local = (
        grad_tokens[:, block_rows : block_rows + token_count]
        + jnp.pad(returned[:, :block_rows], ((0, 0), (0, gap), (0, 0)))
        + jnp.pad(returned[:, 3 * block_rows :], ((0, 0), (gap, 0), (0, 0)))
    )
    grad_global_kv = pair_tokens(jnp.sum(grad_kv[:, :, :, 3:5], axis=2))
    grad_random = grad_kv[:, :, :, 5:8].reshape(request_total, block_rows, 2 * head_width)
    outgoing = (
        jnp.zeros((devices * capacity, block_rows, 2 * head_width), single)
        .at[slot_place]
        .set(grad_random)
    )
    outgoing = outgoing.reshape(devices, capacity, block_rows, 2 * head_width)
    returned_random = lax.all_to_all(
        outgoing.astype(jnp.bfloat16), "seq", split_axis=0, concat_axis=0, tiled=True
    ).astype(outgoing.dtype)
    segment_ids = jnp.where(incoming >= 0, incoming, table_rows).reshape(-1)
    grad_table = jax.ops.segment_sum(
        returned_random.reshape(devices * capacity, block_rows, 2 * head_width),
        segment_ids,
        num_segments=table_rows + 1,
    )[:table_rows]
    grad_owned = pair_tokens(
        grad_table.reshape(seq_count, head_count, per_dev, block_rows, 2 * head_width)
    )
    first_cot = grad_heads[:, :, 0].astype(single)
    last_cot = grad_heads[:, :, per_dev - 1].astype(single)
    first_cot, first_delta = share_grads(
        first_cot, jnp.sum(first_cot * global_out[:, :, :block_rows], axis=-1), 0
    )
    last_cot, last_delta = share_grads(
        last_cot, jnp.sum(last_cot * global_out[:, :, block_rows:], axis=-1), devices - 1
    )
    global_cot = jnp.concatenate([first_cot, last_cot], axis=2)
    global_delta = jnp.concatenate([first_delta, last_delta], axis=2)
    global_prob = jnp.exp(
        jnp.einsum("shqd,shkd->shqk", global_query, local_keys, preferred_element_type=single)
        - global_log[..., None]
    )
    global_dprob = jnp.einsum(
        "shqd,shkd->shqk", global_cot.astype(bfloat), local_values, preferred_element_type=single
    )
    global_grads = (global_prob * (global_dprob - global_delta[..., None])).astype(bfloat)
    grad_global_query = jnp.einsum(
        "shqk,shkd->shqd", global_grads, local_keys, preferred_element_type=single
    )
    grad_local_key = jnp.einsum(
        "shqk,shqd->shkd", global_grads, global_query, preferred_element_type=single
    )
    grad_local_value = jnp.einsum("shqk,shqd->shkd", global_prob, global_cot, precision=HIGHEST)
    partials = jnp.concatenate([row_heads(grad_global_query), grad_global_kv], axis=-1)
    partials = lax.psum(partials.astype(jnp.bfloat16), "seq").astype(jnp.float32)
    owner_part = jnp.where(
        is_first, jnp.pad(partials[:, :block_rows], ((0, 0), (0, gap), (0, 0))), 0.0
    ) + jnp.where(is_last, jnp.pad(partials[:, block_rows:], ((0, 0), (gap, 0), (0, 0))), 0.0)
    grad_query_tokens = row_heads(
        grad_query_block.reshape(seq_count, head_count, token_count, head_width)
    )
    grad_kv_tokens = (
        grad_kv_local
        + grad_owned
        + jnp.concatenate([row_heads(grad_local_key), row_heads(grad_local_value)], axis=-1)
    )
    grad_packed = (
        jnp.concatenate([grad_query_tokens, grad_kv_tokens], axis=-1) + owner_part
    ).astype(bfloat)
    column_scale = jnp.concatenate(
        [jnp.full((model_width,), query_scale, single), jnp.ones((2 * model_width,), single)]
    )
    grad_entry = (
        (grad_packed.astype(single) * column_scale).astype(bfloat).reshape(-1, 3 * model_width)
    )
    entry_weight_grad = jnp.dot(flat_in.T, grad_entry, preferred_element_type=single)
    query_bias_grad = jnp.sum(grad_entry[:, :model_width].astype(single), axis=0)
    value_bias_grad = jnp.sum(grad_entry[:, 2 * model_width :].astype(single), axis=0)
    input_grad = (
        (grad_resid + jnp.dot(grad_entry, entry_weight.T, preferred_element_type=single))
        .astype(bfloat)
        .reshape(inputs.shape)
    )
    (
        total_entry,
        total_query,
        total_value,
        total_out,
        total_out_bias,
        total_norm_gain,
        total_norm_shift,
        total_inner,
        total_inner_bias,
        total_outer,
        total_outer_bias,
        total_final_gain,
        total_final_shift,
    ) = lax.psum(
        (
            entry_weight_grad,
            query_bias_grad,
            value_bias_grad,
            out_weight_grad,
            out_bias_grad,
            norm_gain_grad,
            norm_shift_grad,
            inner_weight_grad,
            inner_bias_grad,
            outer_weight_grad,
            outer_bias_grad,
            final_gain_grad,
            final_shift_grad,
        ),
        ("dp", "seq"),
    )
    return (
        layer_out,
        input_grad,
        total_entry,
        total_query,
        total_value,
        total_out,
        total_out_bias,
        total_norm_gain,
        total_norm_shift,
        total_inner,
        total_inner_bias,
        total_outer,
        total_outer_bias,
        total_final_gain,
        total_final_shift,
    )


MESH = pl.DeviceIdType.MESH
bfloat = jnp.bfloat16
single = jnp.float32
WIDE = 512
QUERIES = 256
INV_SQRT2 = 0.7071067811865476
INV_SQRT_2PI = 0.3989422804014327


def dot(a, b, a_dim, b_dim):
    return lax.dot_general(
        a, b, (((a_dim,), (b_dim,)), ((), ())), preferred_element_type=single
    )


def aligned(index, step):
    return pl.multiple_of(index, step)


class Place:
    def __init__(self, groups):
        self.groups = groups
        self.z = lax.axis_index("dp")
        self.me = lax.axis_index("seq")
        self.y = self.me // 4
        self.x = (self.me // 2) % 2
        self.core = self.me % 2

    def peer(self, offset):
        off_y, off_x, off_core = offset // 4, (offset // 2) % 2, offset % 2
        return (
            ((self.y + off_y) % 2) * 4
            + ((self.x + off_x) % 2) * 2
            + (self.core + off_core) % 2
        )

    def in_plane(self, offset):
        return (self.z, self.peer(offset))

    def in_column(self, offset):
        return ((self.z + offset) % self.groups, self.me)


def remote(src, dst, send, recv, device):
    return pltpu.make_async_remote_copy(
        src_ref=src,
        dst_ref=dst,
        send_sem=send,
        recv_sem=recv,
        device_id=device,
        device_id_type=MESH,
    )


def layer_kernel(
    groups,
    units,
    plan,
    x_hbm,
    blocks_ref,
    we_hbm,
    qb_hbm,
    vb_hbm,
    wo_hbm,
    bo_hbm,
    g1_hbm,
    s1_hbm,
    w1_hbm,
    b1_hbm,
    w2_hbm,
    b2_hbm,
    g2_hbm,
    s2_hbm,
    cot_hbm,
    out_hbm,
    dx_hbm,
    sums_hbm,
    entry_hbm,
    small_hbm,
    x_ref,
    qb_ref,
    vb_ref,
    bo_ref,
    g1_ref,
    s1_ref,
    b1_ref,
    b2_ref,
    g2_ref,
    s2_ref,
    out_ref,
    dx_ref,
    small_ref,
    we,
    wo,
    w1,
    w2,
    cot,
    load_sem,
    wh_t,
    xall,
    ids_send,
    ids_all,
    ids,
    qkv,
    krow,
    vrow,
    probs,
    inv_total,
    out_wide,
    out_low,
    att_t,
    hat1,
    rstd1,
    low1,
    hidden,
    slope,
    grad_inner,
    grad_outer,
    grad_resid,
    grad_branch,
    gatt_t,
    dout_t,
    dqkv,
    dk_acc,
    dv_acc,
    gpacked_t,
    entry_acc,
    entry_part,
    entry_in,
    part,
    landed,
    total,
    small_in,
    x_send,
    x_recv,
    i_send,
    i_recv,
    o_send,
    o_recv,
    d_send,
    d_recv,
    p_send,
    p_recv,
    rs_send,
    rs_recv,
    e_send,
    e_recv,
    v_send,
    v_recv,
    done_sem,
    store_sem,
):
    seqs, tokens, width = x_ref.shape
    place = Place(groups)
    me = place.me
    barrier = pltpu.get_barrier_semaphore()
    for k in range(1, 8):
        pl.semaphore_signal(
            barrier, inc=1, device_id=place.in_plane(k), device_id_type=MESH
        )
    for k in range(1, groups):
        pl.semaphore_signal(
            barrier, inc=1, device_id=place.in_column(k), device_id_type=MESH
        )
    def load(*pairs):
        copies = []
        for src, dst in pairs:
            copies.append(pltpu.make_async_copy(src, dst, load_sem.at[len(loads)]))
            copies[-1].start()
            loads.append(copies[-1])
        return copies

    loads = []
    load_x = load((x_hbm, x_ref))
    load_entry = load((we_hbm, we), (qb_hbm, qb_ref), (vb_hbm, vb_ref))
    load_rest = load(
        (wo_hbm, wo),
        (bo_hbm, bo_ref),
        (g1_hbm, g1_ref),
        (s1_hbm, s1_ref),
        (w1_hbm, w1),
        (b1_hbm, b1_ref),
        (w2_hbm, w2),
        (b2_hbm, b2_ref),
        (g2_hbm, g2_ref),
        (s2_hbm, s2_ref),
        (cot_hbm, cot),
    )

    def lanes_of(device):
        return pl.ds(aligned(device * tokens, 128), tokens)

    def head_rows_of(device):
        return pl.ds(aligned(device * HEAD, HEAD), HEAD)

    def seq_lanes(s):
        return pl.ds(aligned(s * tokens, 128), tokens)

    def vec(ref):
        return ref[...].astype(single).reshape(1, ref.shape[0])

    lane = lax.broadcasted_iota(jnp.int32, (16, tokens), 1)
    row = lax.broadcasted_iota(jnp.int32, (16, tokens), 0)
    for h in range(HEADS):
        numbers = jnp.zeros((16, tokens), jnp.int32)
        for s in range(seqs):
            for j in range(3):
                picked = jnp.where(
                    lane < BLOCK, blocks_ref[s, j, 0, h], blocks_ref[s, j, 1, h]
                )
                numbers = jnp.where(row == s * 3 + j, picked, numbers)
        ids_send[h] = numbers.astype(single).astype(bfloat)
    small_ref[...] = jnp.zeros(small_ref.shape, single)
    entry_acc[...] = jnp.zeros(entry_acc.shape, single)

    load_x[0].wait()
    pl.semaphore_wait(barrier, 7 + groups - 1)

    def x_copy(s, k):
        return remote(
            x_ref.at[s],
            xall.at[s, lanes_of(me), :],
            x_send.at[s, k],
            x_recv.at[s, k],
            place.in_plane(k),
        )

    def x_forward(s, k):
        slab = xall.at[s, lanes_of(place.peer(k)), :]
        return remote(
            slab, slab, x_send.at[s, k + 1], x_recv.at[s, k + 1], place.in_plane(1)
        )

    def x_arrived(s, k):
        slab = xall.at[s, lanes_of(place.peer(k)), :]
        remote(slab, slab, x_send.at[s, k], x_recv.at[s, k], place.in_plane(k)).wait_recv()

    def ids_copy(k):
        other = place.peer(k)
        return remote(
            ids_send.at[other],
            ids_all.at[:, lanes_of(me)],
            i_send.at[k],
            i_recv.at[k],
            place.in_plane(k),
        )

    for s in range(seqs):
        for k in (6, 2, 4, 1):
            x_copy(s, k).start()
        if s == 0:
            for k in range(1, 8):
                ids_copy(k).start()
    ids_all[:, lanes_of(me)] = ids_send[me]
    for s in range(seqs):
        xall[s, lanes_of(me), :] = x_ref[s]

    for copy in load_entry:
        copy.wait()
    pair = me // 2
    odd = me % 2
    for j in range(3):
        columns = we[:, pl.ds(aligned(j * width + pair * 2 * HEAD, 128), 2 * HEAD)].T
        wh_t[j * HEAD : (j + 1) * HEAD, :] = jnp.where(
            odd == 1, columns[HEAD:], columns[:HEAD]
        )
    spread = lax.broadcasted_iota(jnp.int32, (HEAD, width), 1) == me * HEAD + (
        lax.broadcasted_iota(jnp.int32, (HEAD, width), 0)
    )

    def column(ref):
        return jnp.sum(jnp.where(spread, vec(ref), 0.0), axis=1, keepdims=True)

    query_column = column(qb_ref)
    value_column = column(vb_ref)

    def arrived_at(ref_of, send, recv, s):
        for k in range(1, 8):
            slot = ref_of(place.peer(k))
            remote(slot, slot, send.at[s, k], recv.at[s, k], place.in_plane(k)).wait_recv()

    def sent(ref_of, send, recv, s):
        for k in range(1, 8):
            slot = ref_of(place.peer(k))
            remote(slot, slot, send.at[s, k], recv.at[s, k], place.in_plane(k)).wait_send()

    for k in range(1, 8):
        slot = ids_all.at[:, lanes_of(place.peer(k))]
        remote(slot, slot, i_send.at[k], i_recv.at[k], place.in_plane(k)).wait_recv()
    for s in range(seqs):
        ids[s, 0:3, :] = ids_all[...].astype(single)[3 * s : 3 * s + 3]

    length = qkv.shape[2]
    chunks = length // QUERIES
    blocks = length // BLOCK
    key_block = lax.broadcasted_iota(jnp.int32, (blocks, QUERIES), 0)
    query_lane = lax.broadcasted_iota(jnp.int32, (blocks, QUERIES), 1)

    def out_copy(s, k):
        return remote(
            out_low.at[s, :, lanes_of(place.peer(k))],
            att_t.at[head_rows_of(me), seq_lanes(s)],
            o_send.at[s, k],
            o_recv.at[s, k],
            place.in_plane(k),
        )

    def project(s, k):
        owner = place.peer(k)
        packed = dot(wh_t[...], xall[s, lanes_of(owner), :], 1, 1)
        qkv[s, 0:HEAD, lanes_of(owner)] = (
            (packed[0:HEAD] + query_column) * HEAD**-0.5
        ).astype(bfloat)
        qkv[s, HEAD : 2 * HEAD, lanes_of(owner)] = packed[HEAD : 2 * HEAD].astype(bfloat)
        qkv[s, 2 * HEAD :, lanes_of(owner)] = (packed[2 * HEAD :] + value_column).astype(bfloat)

    def attend(s, _):
        for k in (2, 4, 6):
            x_arrived(s, k)
            x_forward(s, k).start()
        for k in (0, 2, 4, 6):
            project(s, k)
        for k in (1, 3, 5, 7):
            x_arrived(s, k)
            project(s, k)
        krow[s] = qkv[s, HEAD : 2 * HEAD, :].T
        vrow[s] = qkv[s, 2 * HEAD : 3 * HEAD, :].T

        def chunk(i, _):
            at = pl.ds(aligned(i * QUERIES, QUERIES), QUERIES)
            query_block = (i * QUERIES + query_lane) // BLOCK
            inside = (key_block >= 1) & (key_block <= blocks - 2)
            near = (key_block >= query_block - 1) & (key_block <= query_block + 1) & inside
            times = jnp.where(near, 1.0, 0.0) + jnp.where(inside, 0.0, 1.0)
            for j in range(3):
                times = times + jnp.where(
                    ids[s, j : j + 1, at] == key_block.astype(single), 1.0, 0.0
                )
            bias = jnp.where(times > 1.5, 0.6931471805599453, 0.0)
            bias = jnp.where(times > 0.5, bias, NEGATIVE)
            bias = jnp.where((query_block == 0) | (query_block == blocks - 1), 0.0, bias)
            score = jnp.dot(krow[s], qkv[s, 0:HEAD, at], preferred_element_type=single)
            score = score.reshape(blocks, BLOCK, QUERIES) + bias[:, None, :]
            score = score.reshape(length, QUERIES)
            peak = jnp.max(score, axis=0, keepdims=True)
            grown = jnp.exp(score - peak)
            inverse = 1.0 / jnp.sum(grown, axis=0, keepdims=True)
            grown = grown.astype(bfloat)
            probs[s, :, at] = grown
            inv_total[s, :, at] = inverse
            result = inverse * jnp.dot(
                qkv[s, 2 * HEAD :, :], grown, preferred_element_type=single
            )
            out_wide[s, :, at] = result
            out_low[s, :, at] = result.astype(bfloat)
            return 0

        lax.fori_loop(0, chunks, chunk, 0)
        for k in (6, 7, 2, 3, 4, 5, 1):
            out_copy(s, k).start()
        att_t[head_rows_of(me), seq_lanes(s)] = out_low[s, :, lanes_of(me)]
        return 0

    lax.fori_loop(0, seqs, attend, 0)
    for copy in load_rest:
        copy.wait()

    def dout_copy(s, k):
        return remote(
            gatt_t.at[head_rows_of(place.peer(k)), seq_lanes(s)],
            dout_t.at[s, :, lanes_of(me)],
            d_send.at[s, k],
            d_recv.at[s, k],
            place.in_plane(k),
        )

    def mean_of(value):
        return jnp.mean(value, axis=-1, keepdims=True)

    def add_small(row, value):
        small_ref[row : row + 1, :] += jnp.sum(value, axis=0, keepdims=True)

    ff = hidden.shape[1]

    def store(which, s):
        src, dst = ((out_ref, out_hbm), (dx_ref, dx_hbm))[which]
        return pltpu.make_async_copy(src.at[s], dst.at[s], store_sem.at[which, s])

    def forward(s, _):
        arrived_at(lambda other: att_t.at[head_rows_of(other), seq_lanes(s)], o_send, o_recv, s)
        here = seq_lanes(s)
        branch = dot(att_t[:, here], wo[...], 0, 0) + vec(bo_ref)
        resid = x_ref[s].astype(single) + branch
        center = resid - mean_of(resid)
        scale1 = lax.rsqrt(mean_of(center * center) + EPSILON)
        normed1 = center * scale1
        hat1[here, :] = normed1
        rstd1[here, :] = scale1
        first = normed1 * vec(g1_ref) + vec(s1_ref)
        first_low = first.astype(bfloat)
        low1[here, :] = first_low
        second = first + vec(b2_ref)
        bias1 = vec(b1_ref)
        for j in range(ff // WIDE):
            span = slice(j * WIDE, (j + 1) * WIDE)
            pre = jnp.dot(first_low, w1[:, span], preferred_element_type=single) + bias1[:, span]
            share = 0.5 * (1.0 + lax.erf(pre * INV_SQRT2))
            active = (pre * share).astype(bfloat)
            hidden[here, span] = active
            slope[here, span] = share + pre * jnp.exp(-0.5 * pre * pre) * INV_SQRT_2PI
            second = second + jnp.dot(active, w2[span, :], preferred_element_type=single)
        center = second - mean_of(second)
        scale2 = lax.rsqrt(mean_of(center * center) + EPSILON)
        normed2 = center * scale2
        out_ref[s] = (normed2 * vec(g2_ref) + vec(s2_ref)).astype(bfloat)
        store(0, s).start()
        incoming = cot[s].astype(single)
        add_small(10, incoming * normed2)
        add_small(11, incoming)
        scaled = incoming * vec(g2_ref)
        grad_second = scale2 * (
            scaled - mean_of(scaled) - normed2 * mean_of(scaled * normed2)
        )
        grad_resid[here, :] = grad_second
        grad_low = grad_second.astype(bfloat)
        grad_outer[here, :] = grad_low
        add_small(9, grad_low.astype(single))
        return 0

    lax.fori_loop(0, seqs, forward, 0)

    def stages_of(unit):
        base, count, order = units[unit]
        size = count // 2
        start = base + place.core * size
        stages = [("c", start, base + (1 - place.core) * size, size)]
        for axis in order:
            if axis == "z":
                size = size // groups
                stages.append((axis, start + place.z * size, start, size))
                start = start + place.z * size
            else:
                size = size // 2
                index = place.x if axis == "x" else place.y
                stages.append((axis, start + index * size, start + (1 - index) * size, size))
                start = start + index * size
        return stages

    hops = {"c": 1, "x": 2, "y": 4}

    def rows_at(start, count):
        return pl.ds(aligned(start, 16), count)

    def landing(unit, stage):
        before = 0
        for other in range(unit):
            before += units[other][1]
        for earlier in range(stage):
            axis, _, _, size = stages_of(unit)[earlier]
            before += size * (groups - 1 if axis == "z" else 1)
        return before

    def reduce_copies(unit, stage):
        axis, _, away, size = stages_of(unit)[stage]
        at = landing(unit, stage)
        if axis != "z":
            return [
                remote(
                    part.at[rows_at(away, size), :],
                    landed.at[at : at + size, :],
                    rs_send.at[unit, stage, 0],
                    rs_recv.at[unit, stage, 0],
                    place.in_plane(hops[axis]),
                )
            ]
        return [
            remote(
                part.at[rows_at(away + ((place.z + offset) % groups) * size, size), :],
                landed.at[at + (offset - 1) * size : at + offset * size, :],
                rs_send.at[unit, stage, offset - 1],
                rs_recv.at[unit, stage, offset - 1],
                place.in_column(offset),
            )
            for offset in range(1, groups)
        ]

    def reduce_start(unit, stage):
        for copy in reduce_copies(unit, stage):
            copy.start()

    def reduce_finish(unit, stage):
        copies = reduce_copies(unit, stage)
        for copy in copies:
            copy.wait()
        _, keep, _, size = stages_of(unit)[stage]
        at = landing(unit, stage)
        result = total if stage == 3 else part
        tile = next(rows for rows in (64, 32, 16) if size % rows == 0)

        def add(i, _):
            mine = rows_at(keep + i * tile, tile)
            value = part[mine, :].astype(single)
            for j in range(len(copies)):
                value = value + landed[rows_at(at + j * size + i * tile, tile), :].astype(single)
            result[mine, :] = value.astype(bfloat)
            return 0

        lax.fori_loop(0, size // tile, add, 0)

    def gather_copies(unit, stage, arriving):
        axis, keep, away, size = stages_of(unit)[stage]
        if axis != "z":
            slot = total.at[rows_at(away if arriving else keep, size), :]
            return [
                remote(
                    slot,
                    slot,
                    rs_send.at[unit, 4 + stage, 0],
                    rs_recv.at[unit, 4 + stage, 0],
                    place.in_plane(hops[axis]),
                )
            ]
        copies = []
        for offset in range(1, groups):
            owner = (place.z + groups - offset) % groups
            slot = total.at[rows_at(away + owner * size if arriving else keep, size), :]
            copies.append(
                remote(
                    slot,
                    slot,
                    rs_send.at[unit, 4 + stage, offset - 1],
                    rs_recv.at[unit, 4 + stage, offset - 1],
                    place.in_column(offset),
                )
            )
        return copies

    def gather_start(unit, stage):
        for copy in gather_copies(unit, stage, False):
            copy.start()

    def gather_finish(unit, stage):
        for copy in gather_copies(unit, stage, False):
            copy.wait_send()
        for copy in gather_copies(unit, stage, True):
            copy.wait_recv()

    def result_copy(unit):
        base, count, _ = units[unit]
        at = pl.ds(base, count)
        return pltpu.make_async_copy(total.at[at, :], sums_hbm.at[at, :], done_sem.at[unit])

    def step(unit, stage):
        if stage < 3:
            reduce_finish(unit, stage)
            reduce_start(unit, stage + 1)
        elif stage == 3:
            reduce_finish(unit, stage)
            gather_start(unit, 3)
        elif stage < 7:
            gather_finish(unit, 7 - stage)
            gather_start(unit, 6 - stage)
        else:
            gather_finish(unit, 0)
            result_copy(unit).start()

    def ready_units(j, tile):
        for unit, (base, count, _) in enumerate(units):
            last = (base + count) // WIDE - 1
            if last in tile:

                @pl.when(j == last - tile[0])
                def _():
                    reduce_start(unit, 0)

    def steps_at(name, index):
        for at, unit, stage in plan[name]:

            @pl.when(index == at)
            def _():
                step(unit, stage)

    def keep_part(base, value):
        part[pl.ds(aligned(base, 128), value.shape[0]), :] = value.astype(bfloat)

    outer_tiles = range(0, ff // WIDE)
    inner_tiles = range(ff // WIDE, 2 * ff // WIDE)

    def outer_tile(j, _):
        at = pl.ds(aligned(j * WIDE, WIDE), WIDE)
        keep_part(j * WIDE, dot(hidden[:, at], grad_outer[...], 0, 0))
        ready_units(j, outer_tiles)
        return 0

    def inner_tile(j, _):
        at = pl.ds(aligned(j * WIDE, WIDE), WIDE)
        keep_part(ff + j * WIDE, dot(low1[...], grad_inner[:, at], 0, 0))
        ready_units(j, inner_tiles)
        steps_at("inner", j)
        return 0

    lax.fori_loop(0, ff // WIDE, outer_tile, 0)

    def backward(s, _):
        here = seq_lanes(s)
        back = grad_resid[here, :]
        grad_low = grad_outer[here, :]
        for j in range(ff // WIDE):
            span = slice(j * WIDE, (j + 1) * WIDE)
            grad_hidden = dot(grad_low, w2[span, :], 1, 1)
            inner = (grad_hidden * slope[here, span]).astype(bfloat)
            grad_inner[here, span] = inner
            add_small(5 + j, inner.astype(single))
            back = back + dot(inner, w1[:, span], 1, 1)
        normed1 = hat1[here, :]
        add_small(3, back * normed1)
        add_small(4, back)
        scaled = back * vec(g1_ref)
        grad = rstd1[here, :] * (scaled - mean_of(scaled) - normed1 * mean_of(scaled * normed1))
        grad_resid[here, :] = grad
        grad = grad.astype(bfloat)
        grad_branch[here, :] = grad
        add_small(2, grad.astype(single))
        gatt_t[:, here] = dot(wo[...], grad, 1, 1).astype(bfloat)
        for k in (6, 7, 2, 3, 4, 5, 1):
            dout_copy(s, k).start()
        dout_t[s, :, lanes_of(me)] = gatt_t[head_rows_of(me), seq_lanes(s)]
        steps_at("backward", s)
        return 0

    lax.fori_loop(0, seqs, backward, 0)
    lax.fori_loop(0, ff // WIDE, inner_tile, 0)
    keep_part(2 * ff, jnp.dot(att_t[...], grad_branch[...], preferred_element_type=single))
    ready_units(0, (2 * ff // WIDE,))
    steps_at("inner", ff // WIDE)

    def pack_copies(s, k):
        other = place.peer(k)
        return [
            remote(
                dqkv.at[s, j * HEAD : (j + 1) * HEAD, lanes_of(other)],
                gpacked_t.at[j, head_rows_of(me), seq_lanes(s)],
                p_send.at[s, k, j],
                p_recv.at[s, k, j],
                place.in_plane(k),
            )
            for j in range(3)
        ]

    def back_chunk(turn, _):
        s = turn // chunks
        i = turn % chunks

        @pl.when(i == 0)
        def _():
            arrived_at(lambda other: dout_t.at[s, :, lanes_of(other)], d_send, d_recv, s)
            dk_acc[...] = jnp.zeros(dk_acc.shape, single)
            dv_acc[...] = jnp.zeros(dv_acc.shape, single)

        at = pl.ds(aligned(i * QUERIES, QUERIES), QUERIES)
        cot_t = dout_t[s, :, at].astype(single)
        inverse = inv_total[s, :, at]
        delta = inverse * jnp.sum(cot_t * out_wide[s, :, at], axis=0, keepdims=True)
        cot_low = (cot_t * inverse).astype(bfloat)
        grown = probs[s, :, at]
        grad = jnp.dot(vrow[s], cot_low, preferred_element_type=single) - delta
        grad = (grown.astype(single) * grad).astype(bfloat)
        query_grad = jnp.dot(qkv[s, HEAD : 2 * HEAD, :], grad, preferred_element_type=single)
        dqkv[s, 0:HEAD, at] = (query_grad.astype(bfloat) * HEAD**-0.5).astype(bfloat)
        dv_acc[...] += dot(cot_low, grown, 1, 1)
        dk_acc[...] += dot(qkv[s, 0:HEAD, at], grad, 1, 1)

        @pl.when(i == chunks - 1)
        def _():
            dqkv[s, HEAD : 2 * HEAD, :] = dk_acc[...].astype(bfloat)
            dqkv[s, 2 * HEAD :, :] = dv_acc[...].astype(bfloat)
            for k in (6, 7, 2, 3, 4, 5, 1):
                for copy in pack_copies(s, k):
                    copy.start()
            for j in range(3):
                gpacked_t[j, head_rows_of(me), seq_lanes(s)] = dqkv[
                    s, j * HEAD : (j + 1) * HEAD, lanes_of(me)
                ]
            entry_acc[...] += jnp.dot(dqkv[s], xall[s], preferred_element_type=single)

        steps_at("attention", turn)
        return 0

    lax.fori_loop(0, seqs * chunks, back_chunk, 0)

    entry_base = 2 * ff + width
    head_share = 3 * HEAD
    fourth = head_share // groups

    def entry_rows(device, z=None):
        start = entry_base + device * head_share
        if z is None:
            return rows_at(start, head_share)
        return rows_at(start + z * fourth, fourth)

    def entry_copy(offset):
        target = (place.z + offset) % groups
        return remote(
            entry_part.at[rows_at(target * fourth, fourth), :],
            entry_in.at[offset - 1],
            e_send.at[0, offset],
            e_recv.at[0, offset],
            place.in_column(offset),
        )

    def entry_back(offset, arriving):
        owner = (place.z + groups - offset) % groups if arriving else place.z
        slot = total.at[entry_rows(me, owner), :]
        return remote(slot, slot, e_send.at[1, offset], e_recv.at[1, offset], place.in_column(offset))

    def entry_plane(k, owner, to):
        slot = total.at[entry_rows(owner), :]
        return remote(slot, slot, e_send.at[2, k], e_recv.at[2, k], place.in_plane(to))

    def entry_result():
        rows = pl.ds(entry_base, HEADS * head_share)
        return pltpu.make_async_copy(total.at[rows, :], entry_hbm, done_sem.at[len(units)])

    def entry_step(stage):
        if stage == 0:
            entry_part[...] = entry_acc[...].astype(bfloat)
            for offset in range(1, groups):
                entry_copy(offset).start()
        elif stage == 1:
            value = entry_part[rows_at(place.z * fourth, fourth), :].astype(single)
            for offset in range(1, groups):
                entry_copy(offset).wait()
                value = value + entry_in[offset - 1].astype(single)
            total[entry_rows(me, place.z), :] = value.astype(bfloat)
            for offset in range(1, groups):
                entry_back(offset, False).start()
        elif stage == 2:
            for offset in range(1, groups):
                entry_back(offset, False).wait_send()
                entry_back(offset, True).wait_recv()
            for k in (6, 2, 4, 1):
                entry_plane(k, me, k).start()
        elif stage == 3:
            for k in (2, 4, 6):
                entry_plane(k, place.peer(k), k).wait_recv()
                entry_plane(k + 1, place.peer(k), 1).start()
        else:
            for k in (1, 3, 5, 7):
                entry_plane(k, place.peer(k), 1).wait_recv()
            for k in (1, 2, 4, 6):
                entry_plane(k, me, k).wait_send()
            for k in (3, 5, 7):
                entry_plane(k, place.peer(k - 1), 1).wait_send()
            entry_result().start()

    def small_copy(turn, device):
        return remote(
            small_ref, small_in.at[turn], v_send.at[turn], v_recv.at[turn], device
        )

    def small_column(offset):
        return small_copy(2 + offset, place.in_column(offset))

    def small_step(stage):
        if stage == 0:
            ones = jnp.ones((8, length), bfloat)
            sums = jnp.zeros((8, head_share), single)
            for s in range(seqs):
                sums = sums + dot(ones, dqkv[s], 1, 1)
            here = lax.broadcasted_iota(jnp.int32, (1, width), 1) // HEAD == me
            for at, start in ((0, 0), (1, 2 * HEAD)):
                wide = jnp.concatenate([sums[0:1, start : start + HEAD]] * HEADS, axis=1)
                small_ref[at : at + 1, :] = jnp.where(here, wide, 0.0)
            small_copy(0, place.in_plane(1)).start()
        elif stage < 3:
            small_copy(stage - 1, place.in_plane(2 ** (stage - 1))).wait()
            small_ref[...] += small_in[stage - 1]
            small_copy(stage, place.in_plane(2**stage)).start()
        elif stage == 3:
            small_copy(2, place.in_plane(4)).wait()
            small_ref[...] += small_in[2]
            for offset in range(1, groups):
                small_column(offset).start()
        else:
            for offset in range(1, groups):
                small_column(offset).wait()
            mine = small_ref[...]
            sum_small = jnp.zeros(small_ref.shape, single)
            for source in range(groups):
                for offset in range(groups):
                    term = mine if offset == 0 else small_in[2 + offset]
                    sum_small = sum_small + jnp.where(
                        (place.z + groups - offset) % groups == source, term, 0.0
                    )
            small_ref[...] = sum_small
            small_store.start()

    small_store = pltpu.make_async_copy(small_ref, small_hbm, store_sem.at[2, 0])

    def input_step():
        for s in range(seqs):
            for k in range(1, 8):
                other = place.peer(k)
                for j in range(3):
                    slot = gpacked_t.at[j, head_rows_of(other), seq_lanes(s)]
                    remote(
                        slot, slot, p_send.at[s, k, j], p_recv.at[s, k, j], place.in_plane(k)
                    ).wait_recv()
        grad_in = grad_resid[...]
        for j in range(3):
            grad_in = grad_in + dot(gpacked_t[j], we[:, j * width : (j + 1) * width], 0, 1)
        for s in range(seqs):
            dx_ref[s] = grad_in[s * tokens : (s + 1) * tokens].astype(bfloat)
            store(1, s).start()

    for kind, *what in plan["tail"]:
        if kind == "unit":
            step(*what)
        elif kind == "entry":
            entry_step(*what)
        elif kind == "small":
            small_step(*what)
        else:
            input_step()
    for unit in range(len(units)):
        result_copy(unit).wait()
    entry_result().wait()
    small_store.wait()
    for s in range(seqs):
        store(0, s).wait()
        store(1, s).wait()
        for k in (1, 2, 4, 6):
            x_copy(s, k).wait_send()
        for k in (2, 4, 6):
            x_forward(s, k).wait_send()
        sent(lambda other: out_low.at[s, :, lanes_of(other)], o_send, o_recv, s)
        sent(lambda other: gatt_t.at[head_rows_of(other), seq_lanes(s)], d_send, d_recv, s)
        for k in range(1, 8):
            for copy in pack_copies(s, k):
                copy.wait_send()
    for k in range(1, 8):
        ids_copy(k).wait_send()


def widen_kernel(sums_hbm, entry_hbm, small_hbm, out_in, dx_in, *refs):
    outs, vectors, scratch = refs[:15], refs[15:23], refs[23:]
    sums, entry_low, small, passed, inner_bias, outer_v, inner_v, out_v, entry_v = scratch[:9]
    in_sem, out_sem = scratch[9:]
    out_ref, dx_ref, entry, query_b, value_b, out_w, out_b = outs[:7]
    gain1, shift1, inner_w, inner_b, outer_w, outer_b, gain2, shift2 = outs[7:]
    width = WIDE
    ff = outer_w.shape[0]
    pieces = sums.shape[0] // WIDE
    reads = []
    writes = []

    def read(src, dst):
        reads.append(pltpu.make_async_copy(src, dst, in_sem.at[len(reads)]))
        reads[-1].start()

    def write(src, dst):
        writes.append(pltpu.make_async_copy(src, dst, out_sem.at[len(writes)]))
        writes[-1].start()

    for i in range(pieces):
        rows = slice(i * WIDE, (i + 1) * WIDE)
        read(sums_hbm.at[rows, :], sums.at[rows, :])
    read(entry_hbm, entry_low)
    read(small_hbm, small)
    read(out_in, passed.at[0])
    read(dx_in, passed.at[1])
    for i in range(pieces):
        reads[i].wait()
        rows = slice(i * WIDE, (i + 1) * WIDE)
        value = sums[rows, :].astype(single)
        j = i - ff // WIDE
        if j < 0:
            outer_v[rows, :] = value
            write(outer_v.at[rows], outer_w.at[rows])
        elif j < ff // WIDE:
            columns = slice(j * WIDE, (j + 1) * WIDE)
            inner_v[:, columns] = value
            write(inner_v.at[:, columns], inner_w.at[:, columns])
        else:
            out_v[...] = value
            write(out_v, out_w)
    reads[pieces].wait()
    for j in range(3):
        columns = slice(j * width, (j + 1) * width)
        value = entry_low[:, j * HEAD : (j + 1) * HEAD, :].reshape(width, width)
        entry_v[:, columns] = value.astype(single).T
        write(entry_v.at[:, columns], entry.at[:, columns])
    for read_done in reads[pieces + 1 :]:
        read_done.wait()
    write(passed.at[0], out_ref)
    write(passed.at[1], dx_ref)

    def small_row(at):
        return small[at : at + 1, :].reshape(width)

    for j, (ref, at) in enumerate(
        (
            (query_b, 0),
            (value_b, 1),
            (out_b, 2),
            (gain1, 3),
            (shift1, 4),
            (outer_b, 9),
            (gain2, 10),
            (shift2, 11),
        )
    ):
        vectors[j][...] = small_row(at)
        write(vectors[j], ref)
    for j in range(ff // WIDE):
        inner_bias[j * WIDE : (j + 1) * WIDE] = small_row(5 + j)
    write(inner_bias, inner_b)
    for copy in writes:
        copy.wait()


UNITS = (
    (0, 1024, "xyz"),
    (1024, 1024, "yxz"),
    (2048, 1024, "xyz"),
    (3072, 1024, "zyx"),
    (4096, 512, "xyz"),
)
PLAN = {
    "backward": (
        (0, 0, 0),
        (0, 1, 0),
    ),
    "inner": (
    ),
    "attention": (
        (0, 2, 0),
        (0, 3, 0),
        (0, 0, 1),
        (0, 1, 1),
        (0, 4, 0),
        (3, 0, 2),
        (5, 2, 1),
        (6, 1, 2),
        (8, 3, 1),
        (8, 2, 2),
        (8, 4, 1),
        (9, 0, 3),
        (11, 1, 3),
        (11, 3, 2),
    ),
    "tail": (
        ("entry", 0),
        ("small", 0),
        ("unit", 2, 3),
        ("unit", 4, 2),
        ("small", 1),
        ("unit", 0, 4),
        ("input",),
        ("small", 2),
        ("unit", 1, 4),
        ("unit", 3, 3),
        ("unit", 0, 5),
        ("entry", 1),
        ("small", 3),
        ("unit", 1, 5),
        ("unit", 2, 4),
        ("unit", 3, 4),
        ("unit", 4, 3),
        ("entry", 2),
        ("unit", 0, 6),
        ("unit", 0, 7),
        ("unit", 1, 6),
        ("small", 4),
        ("unit", 4, 4),
        ("unit", 1, 7),
        ("unit", 2, 5),
        ("unit", 3, 5),
        ("entry", 3),
        ("unit", 4, 5),
        ("unit", 2, 6),
        ("entry", 4),
        ("unit", 2, 7),
        ("unit", 3, 6),
        ("unit", 4, 6),
        ("unit", 3, 7),
        ("unit", 4, 7),
    ),
}


def by_heads(groups):
    def run(inputs, blocks, we, qb, vb, wo, bo, g1, s1, w1, b1, w2, b2, g2, s2, cot):
        seqs, tokens, width = inputs.shape
        ff = w1.shape[1]
        rows = seqs * tokens
        length = tokens * HEADS
        grad_rows = 2 * ff + width
        units = UNITS
        others = max(groups - 1, 1)
        head_share = 3 * HEAD
        smem = pl.BlockSpec(memory_space=pltpu.SMEM)
        hbm = pl.BlockSpec(memory_space=pl.ANY)
        dma = pltpu.SemaphoreType.DMA

        def shape(*dims):
            return jax.ShapeDtypeStruct(dims, single)

        entry_shape = (HEADS, head_share, width)
        out, dx, sums, entry, small = pl.pallas_call(
            partial(layer_kernel, groups, units, PLAN),
            out_shape=[
                jax.ShapeDtypeStruct(inputs.shape, bfloat),
                jax.ShapeDtypeStruct(inputs.shape, bfloat),
                jax.ShapeDtypeStruct((grad_rows, width), bfloat),
                jax.ShapeDtypeStruct((HEADS * head_share, width), bfloat),
                shape(16, width),
            ],
            in_specs=[hbm, smem] + [hbm] * 14,
            out_specs=[hbm] * 5,
            scratch_shapes=[
                pltpu.VMEM(inputs.shape, bfloat),
                pltpu.VMEM(qb.shape, bfloat),
                pltpu.VMEM(vb.shape, bfloat),
                pltpu.VMEM(bo.shape, bfloat),
                pltpu.VMEM(g1.shape, bfloat),
                pltpu.VMEM(s1.shape, bfloat),
                pltpu.VMEM(b1.shape, bfloat),
                pltpu.VMEM(b2.shape, bfloat),
                pltpu.VMEM(g2.shape, bfloat),
                pltpu.VMEM(s2.shape, bfloat),
                pltpu.VMEM(inputs.shape, bfloat),
                pltpu.VMEM(inputs.shape, bfloat),
                pltpu.VMEM((16, width), single),
                pltpu.VMEM(we.shape, bfloat),
                pltpu.VMEM(wo.shape, bfloat),
                pltpu.VMEM(w1.shape, bfloat),
                pltpu.VMEM(w2.shape, bfloat),
                pltpu.VMEM(cot.shape, bfloat),
                dma((15,)),
                pltpu.VMEM((head_share, width), bfloat),
                pltpu.VMEM((seqs, length, width), bfloat),
                pltpu.VMEM((HEADS, 16, tokens), bfloat),
                pltpu.VMEM((16, length), bfloat),
                pltpu.VMEM((seqs, 8, length), single),
                pltpu.VMEM((seqs, head_share, length), bfloat),
                pltpu.VMEM((seqs, length, HEAD), bfloat),
                pltpu.VMEM((seqs, length, HEAD), bfloat),
                pltpu.VMEM((seqs, length, length), bfloat),
                pltpu.VMEM((seqs, 1, length), single),
                pltpu.VMEM((seqs, HEAD, length), single),
                pltpu.VMEM((seqs, HEAD, length), bfloat),
                pltpu.VMEM((width, rows), bfloat),
                pltpu.VMEM((rows, width), single),
                pltpu.VMEM((rows, 1), single),
                pltpu.VMEM((rows, width), bfloat),
                pltpu.VMEM((rows, ff), bfloat),
                pltpu.VMEM((rows, ff), single),
                pltpu.VMEM((rows, ff), bfloat),
                pltpu.VMEM((rows, width), bfloat),
                pltpu.VMEM((rows, width), single),
                pltpu.VMEM((rows, width), bfloat),
                pltpu.VMEM((width, rows), bfloat),
                pltpu.VMEM((seqs, HEAD, length), bfloat),
                pltpu.VMEM((seqs, head_share, length), bfloat),
                pltpu.VMEM((HEAD, length), single),
                pltpu.VMEM((HEAD, length), single),
                pltpu.VMEM((3, width, rows), bfloat),
                pltpu.VMEM((head_share, width), single),
                pltpu.VMEM((head_share, width), bfloat),
                pltpu.VMEM((others, head_share // groups, width), bfloat),
                pltpu.VMEM((grad_rows, width), bfloat),
                pltpu.VMEM((grad_rows, width), bfloat),
                pltpu.VMEM((grad_rows + HEADS * head_share, width), bfloat),
                pltpu.VMEM((3 + groups, 16, width), single),
                dma((seqs, 8)),
                dma((seqs, 8)),
                dma((8,)),
                dma((8,)),
                dma((seqs, 8)),
                dma((seqs, 8)),
                dma((seqs, 8)),
                dma((seqs, 8)),
                dma((seqs, 8, 3)),
                dma((seqs, 8, 3)),
                dma((len(units), 8, others)),
                dma((len(units), 8, others)),
                dma((3, 8)),
                dma((3, 8)),
                dma((3 + groups,)),
                dma((3 + groups,)),
                dma((len(units) + 1,)),
                dma((3, seqs)),
            ],
            compiler_params=pltpu.CompilerParams(
                collective_id=0, has_side_effects=True, vmem_limit_bytes=60 * 2**20
            ),
            name="layer",
        )(
            inputs, blocks.transpose(0, 3, 2, 1), we, qb, vb, wo, bo, g1, s1, w1, b1, w2, b2,
            g2, s2, cot,
        )
        pieces = grad_rows // WIDE
        return pl.pallas_call(
            widen_kernel,
            in_specs=[hbm] * 5,
            out_specs=[hbm] * 15,
            out_shape=[
                jax.ShapeDtypeStruct(inputs.shape, bfloat),
                jax.ShapeDtypeStruct(inputs.shape, bfloat),
                shape(width, 3 * width),
                shape(width),
                shape(width),
                shape(width, width),
                shape(width),
                shape(width),
                shape(width),
                shape(width, ff),
                shape(ff),
                shape(ff, width),
                shape(width),
                shape(width),
                shape(width),
            ],
            scratch_shapes=[
                *[pltpu.VMEM((width,), single)] * 8,
                pltpu.VMEM((grad_rows, width), bfloat),
                pltpu.VMEM(entry_shape, bfloat),
                pltpu.VMEM((16, width), single),
                pltpu.VMEM((2, *inputs.shape), bfloat),
                pltpu.VMEM((ff,), single),
                pltpu.VMEM((ff, width), single),
                pltpu.VMEM((width, ff), single),
                pltpu.VMEM((width, width), single),
                pltpu.VMEM((width, 3 * width), single),
                dma((pieces + 4,)),
                dma((pieces + 14,)),
            ],
            compiler_params=pltpu.CompilerParams(vmem_limit_bytes=60 * 2**20),
            name="widen",
        )(sums, entry.reshape(entry_shape), small, out, dx)

    return run


def solution(mesh):
    in_specs = (
        P("dp", "seq", None),
        P("dp", None, "seq", None),
        P(),
        P(),
        P(),
        P(),
        P(),
        P(),
        P(),
        P(),
        P(),
        P(),
        P(),
        P(),
        P(),
        P("dp", "seq", None),
    )
    out_specs = (
        P("dp", "seq", None),
        P("dp", "seq", None),
        P(),
        P(),
        P(),
        P(),
        P(),
        P(),
        P(),
        P(),
        P(),
        P(),
        P(),
        P(),
        P(),
    )
    heads_fit = mesh.shape["seq"] == HEADS
    plan = by_heads(mesh.shape["dp"]) if heads_fit else on_device
    return jax.shard_map(
        plan, mesh=mesh, in_specs=in_specs, out_specs=out_specs, check_vma=False
    )
```

```python
from functools import partial

import jax
import jax.numpy as jnp
from jax import lax
from jax.experimental import pallas as pl
from jax.experimental.pallas import tpu as pltpu
from jax.sharding import PartitionSpec as P

HEADS = 8
HEAD = 64
BLOCK = 64


HIGHEST = lax.Precision.HIGHEST
EPSILON = 1e-05
NEGATIVE = -1e30


def spread_2(value, axis, root):
    mine = lax.axis_index(axis) == root
    return lax.psum(jnp.where(mine, value, jnp.zeros_like(value)), axis)


def for_sending(value):

    def short(part):
        return part.astype(jnp.bfloat16) if part.dtype == jnp.float32 else part

    return jax.tree.map(short, value)


def extended(block, sides, width):
    for axis, dim in sides:
        count = lax.axis_size(axis)
        forward = [(i, i + 1) for i in range(count - 1)]
        backward = [(target, source) for source, target in forward]
        low = lax.ppermute(
            lax.slice_in_dim(block, block.shape[dim] - width, None, axis=dim), axis, forward
        )
        high = lax.ppermute(lax.slice_in_dim(block, 0, width, axis=dim), axis, backward)
        block = jnp.concatenate([low, block, high], axis=dim)
    return block


def combined_all(part, axis, combine):
    gathered = jax.tree.map(lambda a: lax.all_gather(a, axis), part)

    def take(source):
        return jax.tree.map(lambda a: lax.dynamic_index_in_dim(a, source, 0, False), gathered)

    return lax.fori_loop(
        1, lax.axis_size(axis), lambda source, state: combine(state, take(source)), take(0)
    )


def norm_apply(values, gain_vec, shift_vec):
    center = values - jnp.mean(values, axis=-1, keepdims=True)
    spread = jnp.mean(center * center, axis=-1, keepdims=True)
    return center * lax.rsqrt(spread + EPSILON) * gain_vec + shift_vec


def pair_blocks(row_data, head_count, block_rows):
    seq_count, length_here, full_width = row_data.shape
    head_width = full_width // (2 * head_count)
    shaped = row_data.reshape(
        seq_count, length_here // block_rows, block_rows, 2, head_count, head_width
    )
    return shaped.transpose(0, 4, 1, 2, 3, 5).reshape(
        seq_count, head_count, length_here // block_rows, block_rows, 2 * head_width
    )


def pair_tokens(blocked):
    seq_count, head_count, block_count, block_rows, double_width = blocked.shape
    head_width = double_width // 2
    shaped = blocked.reshape(seq_count, head_count, block_count, block_rows, 2, head_width)
    return shaped.transpose(0, 2, 3, 4, 1, 5).reshape(
        seq_count, block_count * block_rows, 2 * head_count * head_width
    )


def head_rows(row_data, head_count):
    seq_count, length_here, full_width = row_data.shape
    return row_data.reshape(seq_count, length_here, head_count, full_width // head_count).transpose(
        0, 2, 1, 3
    )


def row_heads(split_rows):
    seq_count, head_count, length_here, head_width = split_rows.shape
    return split_rows.transpose(0, 2, 1, 3).reshape(seq_count, length_here, head_count * head_width)


def merge_parts(earlier, later):
    peak_one, total_one, out_one = earlier
    peak_two, total_two, out_two = later
    row_peak = jnp.maximum(peak_one, peak_two)
    factor_one = jnp.exp(peak_one - row_peak)
    factor_two = jnp.exp(peak_two - row_peak)
    return (
        row_peak,
        total_one * factor_one + total_two * factor_two,
        out_one * factor_one[..., None] + out_two * factor_two[..., None],
    )


def share_rows(row_data, root_device):
    return spread_2(row_data, "seq", root_device)


def share_grads(grad_rows, grad_delta, root_device):
    return (
        spread_2(grad_rows.astype(jnp.bfloat16), "seq", root_device).astype(grad_rows.dtype),
        spread_2(for_sending(grad_delta), "seq", root_device).astype(grad_delta.dtype),
    )


def on_device(
    inputs,
    random_blocks,
    entry_weight,
    query_bias,
    value_bias,
    out_weight,
    out_bias,
    norm_gain,
    norm_shift,
    inner_weight,
    inner_bias,
    outer_weight,
    outer_bias,
    final_gain,
    final_shift,
    cotangent,
):
    seq_count, token_count, model_width = inputs.shape
    head_count = HEADS
    head_width = HEAD
    block_rows = BLOCK
    per_dev = token_count // block_rows
    devices = lax.axis_size("seq")
    device = lax.axis_index("seq")
    block_total = devices * per_dev
    request_total = seq_count * head_count * per_dev * 3
    capacity = (request_total + devices - 2) // (devices - 1)
    table_rows = seq_count * head_count * per_dev
    query_scale = head_width ** (-0.5)
    is_first = device == 0
    is_last = device == devices - 1
    bfloat = jnp.bfloat16
    single = jnp.float32
    flat_in = inputs.reshape(-1, model_width)
    entry_out = jnp.dot(flat_in, entry_weight, preferred_element_type=single)
    packed = jnp.concatenate(
        [
            (entry_out[:, :model_width] + query_bias) * query_scale,
            entry_out[:, model_width : 2 * model_width],
            entry_out[:, 2 * model_width :] + value_bias,
        ],
        axis=1,
    )
    packed = packed.astype(bfloat).reshape(seq_count, token_count, 3 * model_width)
    key_value = packed[:, :, model_width:]
    padded = extended(key_value, (("seq", 1),), block_rows)
    global_rows = jnp.concatenate(
        [
            share_rows(packed[:, :block_rows], 0),
            share_rows(packed[:, token_count - block_rows :], devices - 1),
        ],
        axis=1,
    )
    owners = (random_blocks // per_dev).reshape(-1)
    within = random_blocks % per_dev
    seq_index = lax.broadcasted_iota(jnp.int32, random_blocks.shape, 0)
    head_index = lax.broadcasted_iota(jnp.int32, random_blocks.shape, 1)
    request_codes = ((seq_index * head_count + head_index) * per_dev + within).reshape(-1)
    onehot = (owners[:, None] == jnp.arange(devices, dtype=jnp.int32)[None, :]).astype(jnp.int32)
    slot_index = jnp.sum((jnp.cumsum(onehot, axis=0) - onehot) * onehot, axis=1)
    slot_place = owners * capacity + slot_index
    requests = (
        jnp.full((devices * capacity,), -1, jnp.int32)
        .at[slot_place]
        .set(request_codes)
        .reshape(devices, capacity)
    )
    incoming = lax.all_to_all(requests, "seq", split_axis=0, concat_axis=0, tiled=True)
    head_table = pair_blocks(key_value, head_count, block_rows).reshape(
        table_rows, block_rows, 2 * head_width
    )
    served = head_table[jnp.maximum(incoming, 0)]
    served = jnp.where((incoming >= 0)[:, :, None, None], served, jnp.zeros((), bfloat))
    fetched = lax.all_to_all(served, "seq", split_axis=0, concat_axis=0, tiled=True)
    random_kv = fetched.reshape(devices * capacity, block_rows, 2 * head_width)[slot_place]
    random_kv = random_kv.reshape(seq_count, head_count, per_dev, 3, block_rows, 2 * head_width)
    window_view = pair_blocks(padded, head_count, block_rows)
    window_kv = jnp.stack(
        [window_view[:, :, :per_dev], window_view[:, :, 1 : per_dev + 1], window_view[:, :, 2:]],
        axis=3,
    )
    global_kv = pair_blocks(global_rows[:, :, model_width:], head_count, block_rows)
    global_kv = jnp.broadcast_to(
        global_kv[:, :, None], (seq_count, head_count, per_dev, 2, block_rows, 2 * head_width)
    )
    all_kv = jnp.concatenate([window_kv, global_kv, random_kv], axis=3).reshape(
        seq_count, head_count, per_dev, 8 * block_rows, 2 * head_width
    )
    key_part = all_kv[..., :head_width]
    value_part = all_kv[..., head_width:]
    query_view = head_rows(packed[:, :, :model_width], head_count).reshape(
        seq_count, head_count, per_dev, block_rows, head_width
    )
    block_ids = device * per_dev + jnp.arange(per_dev)[:, None]
    column = jnp.arange(8 * block_rows)[None, :]
    neighbor = block_ids + column // block_rows - 1
    key_keep = (column >= 3 * block_rows) | (neighbor >= 1) & (neighbor <= block_total - 2)
    key_keep = key_keep[None, None, :, None, :]

    def block_scores():
        raw_scores = jnp.einsum(
            "shiqd,shikd->shiqk", query_view, key_part, preferred_element_type=single
        )
        return jnp.where(key_keep, raw_scores, NEGATIVE)

    scores = block_scores()
    row_peak = jnp.max(scores, axis=-1, keepdims=True)
    exponent = jnp.exp(scores - row_peak)
    row_total = jnp.sum(exponent, axis=-1, keepdims=True)
    probability = exponent / row_total
    log_total = row_peak + jnp.log(row_total)
    prob_low = probability.astype(bfloat)
    window_out = jnp.einsum(
        "shiqk,shikd->shiqd", prob_low, value_part, preferred_element_type=single
    )
    global_query = head_rows(global_rows[:, :, :model_width], head_count)
    local_keys = head_rows(packed[:, :, model_width : 2 * model_width], head_count)
    local_values = head_rows(packed[:, :, 2 * model_width :], head_count)
    global_scores = jnp.einsum(
        "shqd,shkd->shqk", global_query, local_keys, preferred_element_type=single
    )
    global_peak = jnp.max(global_scores, axis=-1)
    global_exp = jnp.exp(global_scores - global_peak[..., None])
    global_total = jnp.sum(global_exp, axis=-1)
    global_sum = jnp.einsum(
        "shqk,shkd->shqd", global_exp, local_values.astype(single), precision=HIGHEST
    )
    global_peak, global_total, global_sum = combined_all(
        (global_peak, global_total, global_sum), "seq", merge_parts
    )
    global_out = global_sum / global_total[..., None]
    global_log = global_peak + jnp.log(global_total)
    block_pos = jnp.arange(per_dev)
    take_first = ((block_pos == 0) & is_first)[None, None, :, None, None]
    take_last = ((block_pos == per_dev - 1) & is_last)[None, None, :, None, None]
    combined = jnp.where(take_first, global_out[:, :, None, :block_rows], window_out)
    combined = jnp.where(take_last, global_out[:, :, None, block_rows:], combined)
    attended = (
        row_heads(combined.reshape(seq_count, head_count, token_count, head_width))
        .reshape(-1, model_width)
        .astype(bfloat)
    )
    branch = jnp.dot(attended, out_weight, preferred_element_type=single) + out_bias
    residual_in = flat_in.astype(single) + branch
    first_norm, first_pull = jax.vjp(
        norm_apply, residual_in, norm_gain.astype(single), norm_shift.astype(single)
    )
    first_low = first_norm.astype(bfloat)
    inner_pre = jnp.dot(first_low, inner_weight, preferred_element_type=single) + inner_bias
    activated, gelu_pull = jax.vjp(partial(jax.nn.gelu, approximate=False), inner_pre)
    hidden = activated.astype(bfloat)
    second = first_norm + (
        jnp.dot(hidden, outer_weight, preferred_element_type=single) + outer_bias
    )
    final_norm, final_pull = jax.vjp(
        norm_apply, second, final_gain.astype(single), final_shift.astype(single)
    )
    layer_out = final_norm.astype(bfloat).reshape(inputs.shape)
    grad_second, final_gain_grad, final_shift_grad = final_pull(
        cotangent.reshape(-1, model_width).astype(single)
    )
    grad_outer = grad_second.astype(bfloat)
    outer_weight_grad = jnp.dot(hidden.T, grad_outer, preferred_element_type=single)
    outer_bias_grad = jnp.sum(grad_outer.astype(single), axis=0)
    (grad_active,) = gelu_pull(jnp.dot(grad_outer, outer_weight.T, preferred_element_type=single))
    grad_inner = grad_active.astype(bfloat)
    inner_weight_grad = jnp.dot(first_low.T, grad_inner, preferred_element_type=single)
    inner_bias_grad = jnp.sum(grad_inner.astype(single), axis=0)
    grad_first = grad_second + jnp.dot(grad_inner, inner_weight.T, preferred_element_type=single)
    grad_resid, norm_gain_grad, norm_shift_grad = first_pull(grad_first)
    grad_branch = grad_resid.astype(bfloat)
    out_weight_grad = jnp.dot(attended.T, grad_branch, preferred_element_type=single)
    out_bias_grad = jnp.sum(grad_branch.astype(single), axis=0)
    grad_attended = jnp.dot(grad_branch, out_weight.T, preferred_element_type=single).astype(bfloat)
    grad_heads = head_rows(
        grad_attended.reshape(seq_count, token_count, model_width), head_count
    ).reshape(seq_count, head_count, per_dev, block_rows, head_width)
    grad_window = jnp.where(take_first | take_last, jnp.zeros((), bfloat), grad_heads)
    probability = jnp.exp(block_scores() - log_total)
    prob_low = probability.astype(bfloat)
    grad_prob = jnp.einsum(
        "shiqd,shikd->shiqk", grad_window, value_part, preferred_element_type=single
    )
    row_delta = jnp.sum(probability * grad_prob, axis=-1, keepdims=True)
    grad_scores = (probability * (grad_prob - row_delta)).astype(bfloat)
    grad_query_block = jnp.einsum(
        "shiqk,shikd->shiqd", grad_scores, key_part, preferred_element_type=single
    )
    grad_key_block = jnp.einsum(
        "shiqk,shiqd->shikd", grad_scores, query_view, preferred_element_type=single
    )
    grad_value_block = jnp.einsum(
        "shiqk,shiqd->shikd", prob_low, grad_window, preferred_element_type=single
    )
    grad_kv = jnp.concatenate([grad_key_block, grad_value_block], axis=-1).reshape(
        seq_count, head_count, per_dev, 8, block_rows, 2 * head_width
    )
    pad_none = ((0, 0), (0, 0))
    grad_pad = (
        jnp.pad(grad_kv[:, :, :, 0], pad_none + ((0, 2), (0, 0), (0, 0)))
        + jnp.pad(grad_kv[:, :, :, 1], pad_none + ((1, 1), (0, 0), (0, 0)))
        + jnp.pad(grad_kv[:, :, :, 2], pad_none + ((2, 0), (0, 0), (0, 0)))
    )
    grad_tokens = pair_tokens(grad_pad)
    edge_grads = jnp.concatenate(
        [grad_tokens[:, :block_rows], grad_tokens[:, token_count + block_rows :]], axis=1
    )
    returned = extended(edge_grads.astype(jnp.bfloat16), (("seq", 1),), block_rows).astype(
        edge_grads.dtype
    )
    gap = token_count - block_rows
    grad_kv_local = (
        grad_tokens[:, block_rows : block_rows + token_count]
        + jnp.pad(returned[:, :block_rows], ((0, 0), (0, gap), (0, 0)))
        + jnp.pad(returned[:, 3 * block_rows :], ((0, 0), (gap, 0), (0, 0)))
    )
    grad_global_kv = pair_tokens(jnp.sum(grad_kv[:, :, :, 3:5], axis=2))
    grad_random = grad_kv[:, :, :, 5:8].reshape(request_total, block_rows, 2 * head_width)
    outgoing = (
        jnp.zeros((devices * capacity, block_rows, 2 * head_width), single)
        .at[slot_place]
        .set(grad_random)
    )
    outgoing = outgoing.reshape(devices, capacity, block_rows, 2 * head_width)
    returned_random = lax.all_to_all(
        outgoing.astype(jnp.bfloat16), "seq", split_axis=0, concat_axis=0, tiled=True
    ).astype(outgoing.dtype)
    segment_ids = jnp.where(incoming >= 0, incoming, table_rows).reshape(-1)
    grad_table = jax.ops.segment_sum(
        returned_random.reshape(devices * capacity, block_rows, 2 * head_width),
        segment_ids,
        num_segments=table_rows + 1,
    )[:table_rows]
    grad_owned = pair_tokens(
        grad_table.reshape(seq_count, head_count, per_dev, block_rows, 2 * head_width)
    )
    first_cot = grad_heads[:, :, 0].astype(single)
    last_cot = grad_heads[:, :, per_dev - 1].astype(single)
    first_cot, first_delta = share_grads(
        first_cot, jnp.sum(first_cot * global_out[:, :, :block_rows], axis=-1), 0
    )
    last_cot, last_delta = share_grads(
        last_cot, jnp.sum(last_cot * global_out[:, :, block_rows:], axis=-1), devices - 1
    )
    global_cot = jnp.concatenate([first_cot, last_cot], axis=2)
    global_delta = jnp.concatenate([first_delta, last_delta], axis=2)
    global_prob = jnp.exp(
        jnp.einsum("shqd,shkd->shqk", global_query, local_keys, preferred_element_type=single)
        - global_log[..., None]
    )
    global_dprob = jnp.einsum(
        "shqd,shkd->shqk", global_cot.astype(bfloat), local_values, preferred_element_type=single
    )
    global_grads = (global_prob * (global_dprob - global_delta[..., None])).astype(bfloat)
    grad_global_query = jnp.einsum(
        "shqk,shkd->shqd", global_grads, local_keys, preferred_element_type=single
    )
    grad_local_key = jnp.einsum(
        "shqk,shqd->shkd", global_grads, global_query, preferred_element_type=single
    )
    grad_local_value = jnp.einsum("shqk,shqd->shkd", global_prob, global_cot, precision=HIGHEST)
    partials = jnp.concatenate([row_heads(grad_global_query), grad_global_kv], axis=-1)
    partials = lax.psum(partials.astype(jnp.bfloat16), "seq").astype(jnp.float32)
    owner_part = jnp.where(
        is_first, jnp.pad(partials[:, :block_rows], ((0, 0), (0, gap), (0, 0))), 0.0
    ) + jnp.where(is_last, jnp.pad(partials[:, block_rows:], ((0, 0), (gap, 0), (0, 0))), 0.0)
    grad_query_tokens = row_heads(
        grad_query_block.reshape(seq_count, head_count, token_count, head_width)
    )
    grad_kv_tokens = (
        grad_kv_local
        + grad_owned
        + jnp.concatenate([row_heads(grad_local_key), row_heads(grad_local_value)], axis=-1)
    )
    grad_packed = (
        jnp.concatenate([grad_query_tokens, grad_kv_tokens], axis=-1) + owner_part
    ).astype(bfloat)
    column_scale = jnp.concatenate(
        [jnp.full((model_width,), query_scale, single), jnp.ones((2 * model_width,), single)]
    )
    grad_entry = (
        (grad_packed.astype(single) * column_scale).astype(bfloat).reshape(-1, 3 * model_width)
    )
    entry_weight_grad = jnp.dot(flat_in.T, grad_entry, preferred_element_type=single)
    query_bias_grad = jnp.sum(grad_entry[:, :model_width].astype(single), axis=0)
    value_bias_grad = jnp.sum(grad_entry[:, 2 * model_width :].astype(single), axis=0)
    input_grad = (
        (grad_resid + jnp.dot(grad_entry, entry_weight.T, preferred_element_type=single))
        .astype(bfloat)
        .reshape(inputs.shape)
    )
    (
        total_entry,
        total_query,
        total_value,
        total_out,
        total_out_bias,
        total_norm_gain,
        total_norm_shift,
        total_inner,
        total_inner_bias,
        total_outer,
        total_outer_bias,
        total_final_gain,
        total_final_shift,
    ) = lax.psum(
        (
            entry_weight_grad,
            query_bias_grad,
            value_bias_grad,
            out_weight_grad,
            out_bias_grad,
            norm_gain_grad,
            norm_shift_grad,
            inner_weight_grad,
            inner_bias_grad,
            outer_weight_grad,
            outer_bias_grad,
            final_gain_grad,
            final_shift_grad,
        ),
        ("dp", "seq"),
    )
    return (
        layer_out,
        input_grad,
        total_entry,
        total_query,
        total_value,
        total_out,
        total_out_bias,
        total_norm_gain,
        total_norm_shift,
        total_inner,
        total_inner_bias,
        total_outer,
        total_outer_bias,
        total_final_gain,
        total_final_shift,
    )


MESH = pl.DeviceIdType.MESH
bfloat = jnp.bfloat16
single = jnp.float32
WIDE = 512
QUERIES = 1024
BACK_QUERIES = 512
FORWARD = ((0, 2), (2, 3))
BACKWARD = ((0, 1), (1, 3))
TILES = 1024
INV_SQRT2 = 0.7071067811865476
INV_SQRT_2PI = 0.3989422804014327


def dot(a, b, a_dim, b_dim):
    return lax.dot_general(
        a, b, (((a_dim,), (b_dim,)), ((), ())), preferred_element_type=single
    )


def aligned(index, step):
    return pl.multiple_of(index, step)


class Place:
    def __init__(self, groups):
        self.groups = groups
        self.z = lax.axis_index("dp")
        self.me = lax.axis_index("seq")
        self.y = self.me // 4
        self.x = (self.me // 2) % 2
        self.core = self.me % 2

    def peer(self, offset):
        off_y, off_x, off_core = offset // 4, (offset // 2) % 2, offset % 2
        return (
            ((self.y + off_y) % 2) * 4
            + ((self.x + off_x) % 2) * 2
            + (self.core + off_core) % 2
        )

    def in_plane(self, offset):
        return (self.z, self.peer(offset))

    def in_column(self, offset):
        return ((self.z + offset) % self.groups, self.me)


def remote(src, dst, send, recv, device):
    return pltpu.make_async_remote_copy(
        src_ref=src,
        dst_ref=dst,
        send_sem=send,
        recv_sem=recv,
        device_id=device,
        device_id_type=MESH,
    )


def layer_kernel(
    groups,
    units,
    plan,
    x_hbm,
    blocks_ref,
    we_hbm,
    qb_hbm,
    vb_hbm,
    wo_hbm,
    bo_hbm,
    g1_hbm,
    s1_hbm,
    w1_hbm,
    b1_hbm,
    w2_hbm,
    b2_hbm,
    g2_hbm,
    s2_hbm,
    cot_hbm,
    out_hbm,
    dx_hbm,
    sums_hbm,
    entry_hbm,
    small_hbm,
    bias_hbm,
    x_ref,
    qb_ref,
    vb_ref,
    bo_ref,
    g1_ref,
    s1_ref,
    b1_ref,
    b2_ref,
    g2_ref,
    s2_ref,
    out_ref,
    dx_ref,
    small_ref,
    we,
    wo,
    w1,
    w2,
    cot,
    load_sem,
    wh_t,
    xall,
    ids_send,
    ids_all,
    ids,
    qkv,
    krow,
    vrow,
    probs,
    inv_total,
    out_wide,
    out_low,
    att_t,
    hat1,
    rstd1,
    low1,
    hidden,
    slope,
    grad_inner,
    grad_outer,
    grad_resid,
    grad_branch,
    gatt_t,
    dout_t,
    dqkv,
    dk_acc,
    dv_acc,
    gpacked_t,
    entry_acc,
    entry_part,
    entry_in,
    part,
    landed,
    total,
    small_in,
    bias_own,
    bias_in,
    bias_all,
    bias_rows,
    x_send,
    x_recv,
    i_send,
    i_recv,
    o_send,
    o_recv,
    d_send,
    d_recv,
    p_send,
    p_recv,
    rs_send,
    rs_recv,
    e_send,
    e_recv,
    v_send,
    v_recv,
    b_send,
    b_recv,
    done_sem,
    store_sem,
):
    seqs, tokens, width = x_ref.shape
    place = Place(groups)
    me = place.me
    barrier = pltpu.get_barrier_semaphore()
    for k in range(1, 8):
        pl.semaphore_signal(
            barrier, inc=1, device_id=place.in_plane(k), device_id_type=MESH
        )
    for k in range(1, groups):
        pl.semaphore_signal(
            barrier, inc=1, device_id=place.in_column(k), device_id_type=MESH
        )
    def load(*pairs):
        copies = []
        for src, dst in pairs:
            copies.append(pltpu.make_async_copy(src, dst, load_sem.at[len(loads)]))
            copies[-1].start()
            loads.append(copies[-1])
        return copies

    loads = []
    load_x = load((x_hbm, x_ref))
    load_entry = load((we_hbm, we), (qb_hbm, qb_ref), (vb_hbm, vb_ref))
    load_rest = load(
        (wo_hbm, wo),
        (bo_hbm, bo_ref),
        (g1_hbm, g1_ref),
        (s1_hbm, s1_ref),
        (w1_hbm, w1),
        (b1_hbm, b1_ref),
        (w2_hbm, w2),
        (b2_hbm, b2_ref),
        (g2_hbm, g2_ref),
        (s2_hbm, s2_ref),
        (cot_hbm, cot),
    )

    def lanes_of(device):
        return pl.ds(aligned(device * tokens, 128), tokens)

    def head_rows_of(device):
        return pl.ds(aligned(device * HEAD, HEAD), HEAD)

    def seq_lanes(s):
        return pl.ds(aligned(s * tokens, 128), tokens)

    def vec(ref):
        return ref[...].astype(single).reshape(1, ref.shape[0])

    others = HEADS - 1

    def take(ref, sem):
        remote(ref, ref, sem, sem, place.in_plane(1)).wait_recv()

    def gone(ref, sem):
        remote(ref, ref, sem, sem, place.in_plane(1)).wait_send()

    lane = lax.broadcasted_iota(jnp.int32, (16, tokens), 1)
    row = lax.broadcasted_iota(jnp.int32, (16, tokens), 0)
    for h in range(HEADS):
        numbers = jnp.zeros((16, tokens), jnp.int32)
        for s in range(seqs):
            for j in range(3):
                picked = jnp.where(
                    lane < BLOCK, blocks_ref[s, j, 0, h], blocks_ref[s, j, 1, h]
                )
                numbers = jnp.where(row == s * 3 + j, picked, numbers)
        ids_send[h] = numbers.astype(single).astype(bfloat)
    small_ref[...] = jnp.zeros(small_ref.shape, single)
    bias_rows[...] = jnp.zeros(bias_rows.shape, single)
    bias_own[...] = jnp.zeros(bias_own.shape, single)
    entry_acc[...] = jnp.zeros(entry_acc.shape, single)

    load_x[0].wait()
    pl.semaphore_wait(barrier, 7 + groups - 1)

    half_width = width // 2

    def x_copy(s, k):
        return remote(
            x_ref.at[s],
            xall.at[s, lanes_of(me), :],
            x_send,
            x_recv.at[s, 2 if k == 1 else 0],
            place.in_plane(k),
        )

    def x_across(s, k):
        columns = slice(0, half_width) if k == 2 else slice(half_width, width)
        slab = xall.at[s, lanes_of(place.peer(6 - k)), columns]
        return remote(slab, slab, x_send, x_recv.at[s, 1], place.in_plane(k))

    def x_forward(s, k):
        slab = xall.at[s, lanes_of(place.peer(k)), :]
        return remote(slab, slab, x_send, x_recv.at[s, 2], place.in_plane(1))

    def x_arrived(s, which):
        slabs = (2, 1, 4)[which]
        take(xall.at[s, 0 : slabs * tokens, :], x_recv.at[s, which])

    def x_begin(s):
        for k in (2, 4, 1):
            x_copy(s, k).start()

    def x_pass(s):
        x_arrived(s, 0)
        for k in (2, 4):
            x_across(s, k).start()
            x_forward(s, k).start()

    def ids_copy(k):
        other = place.peer(k)
        return remote(
            ids_send.at[other],
            ids_all.at[:, lanes_of(me)],
            i_send,
            i_recv,
            place.in_plane(k),
        )

    x_begin(0)
    for k in range(1, 8):
        ids_copy(k).start()
    x_begin(1)
    ids_all[:, lanes_of(me)] = ids_send[me]
    for s in range(seqs):
        xall[s, lanes_of(me), :] = x_ref[s]

    for copy in load_entry:
        copy.wait()
    pair = me // 2
    odd = me % 2
    for j in range(3):
        columns = we[:, pl.ds(aligned(j * width + pair * 2 * HEAD, 128), 2 * HEAD)].T
        wh_t[j * HEAD : (j + 1) * HEAD, :] = jnp.where(
            odd == 1, columns[HEAD:], columns[:HEAD]
        )
    spread = lax.broadcasted_iota(jnp.int32, (HEAD, width), 1) == me * HEAD + (
        lax.broadcasted_iota(jnp.int32, (HEAD, width), 0)
    )

    def column(ref):
        return jnp.sum(jnp.where(spread, vec(ref), 0.0), axis=1, keepdims=True)

    query_column = column(qb_ref)
    value_column = column(vb_ref)

    take(ids_all.at[:, 0 : others * tokens], i_recv)
    for s in range(seqs):
        ids[s, 0:3, :] = ids_all[...].astype(single)[3 * s : 3 * s + 3]

    length = qkv.shape[2]
    chunks = length // QUERIES
    blocks = length // BLOCK
    key_block = lax.broadcasted_iota(jnp.int32, (blocks, QUERIES), 0)
    query_lane = lax.broadcasted_iota(jnp.int32, (blocks, QUERIES), 1)

    def out_copy(s, k):
        return remote(
            out_low.at[s, :, lanes_of(place.peer(k))],
            att_t.at[head_rows_of(me), seq_lanes(s)],
            o_send,
            o_recv.at[s],
            place.in_plane(k),
        )

    def take_x(s):
        x_arrived(s, 1)
        x_forward(s, 6).start()

        @pl.when(s < seqs - 2)
        def _():
            x_pass(s + 2)

        x_arrived(s, 2)
        packed = dot(wh_t[...], xall[s], 1, 1)
        qkv[s, 0:HEAD, :] = ((packed[0:HEAD] + query_column) * HEAD**-0.5).astype(bfloat)
        qkv[s, HEAD : 2 * HEAD, :] = packed[HEAD : 2 * HEAD].astype(bfloat)
        qkv[s, 2 * HEAD :, :] = (packed[2 * HEAD :] + value_column).astype(bfloat)

    def attend(s, _):
        take_x(s)
        krow[s] = qkv[s, HEAD : 2 * HEAD, :].T
        vrow[s] = qkv[s, 2 * HEAD : 3 * HEAD, :].T

        def chunk(i, _):
            at = pl.ds(aligned(i * QUERIES, QUERIES), QUERIES)
            query_block = (i * QUERIES + query_lane) // BLOCK
            inside = (key_block >= 1) & (key_block <= blocks - 2)
            near = (key_block >= query_block - 1) & (key_block <= query_block + 1) & inside
            times = jnp.where(near, 1.0, 0.0) + jnp.where(inside, 0.0, 1.0)
            for j in range(3):
                times = times + jnp.where(
                    ids[s, j : j + 1, at] == key_block.astype(single), 1.0, 0.0
                )
            bias = jnp.where(times > 1.5, 0.6931471805599453, 0.0)
            bias = jnp.where(times > 0.5, bias, NEGATIVE)
            bias = jnp.where((query_block == 0) | (query_block == blocks - 1), 0.0, bias)
            score = jnp.dot(krow[s], qkv[s, 0:HEAD, at], preferred_element_type=single)
            score = score.reshape(blocks, BLOCK, QUERIES) + bias[:, None, :]
            score = score.reshape(length, QUERIES)
            peak = jnp.max(score, axis=0, keepdims=True)
            grown = jnp.exp(score - peak)
            inverse = 1.0 / jnp.sum(grown, axis=0, keepdims=True)
            grown = grown.astype(bfloat)
            probs[s, :, at] = grown
            inv_total[s, :, at] = inverse
            result = inverse * jnp.dot(
                qkv[s, 2 * HEAD :, :], grown, preferred_element_type=single
            )
            out_wide[s, :, at] = result
            out_low[s, :, at] = result.astype(bfloat)
            return 0

        lax.fori_loop(0, chunks, chunk, 0)
        for k in (6, 7, 2, 3, 4, 5, 1):
            out_copy(s, k).start()
        att_t[head_rows_of(me), seq_lanes(s)] = out_low[s, :, lanes_of(me)]
        return 0

    x_pass(0)
    for s in range(2, seqs):
        x_begin(s)
    x_pass(1)
    lax.fori_loop(0, seqs, attend, 0)
    for copy in load_rest:
        copy.wait()

    def dout_copy(s, k):
        return remote(
            gatt_t.at[head_rows_of(place.peer(k)), seq_lanes(s)],
            dout_t.at[s, :, lanes_of(me)],
            d_send,
            d_recv.at[s],
            place.in_plane(k),
        )

    def mean_of(value):
        return jnp.mean(value, axis=-1, keepdims=True)

    def add_small(row, value):
        small_ref[row : row + 1, :] += jnp.sum(value, axis=0, keepdims=True)

    ff = hidden.shape[1]

    def store(which, s):
        src, dst = ((out_ref, out_hbm), (dx_ref, dx_hbm))[which]
        return pltpu.make_async_copy(src.at[s], dst.at[s], store_sem.at[which])

    def forward(first_seq, last_seq):
        for s in range(first_seq, last_seq):
            take(att_t.at[0 : others * HEAD, seq_lanes(s)], o_recv.at[s])
        here = slice(first_seq * tokens, last_seq * tokens)
        count = (last_seq - first_seq) * tokens
        branch = dot(att_t[:, here], wo[...], 0, 0) + vec(bo_ref)
        resid = x_ref[first_seq:last_seq].reshape(count, width).astype(single) + branch
        center = resid - mean_of(resid)
        scale1 = lax.rsqrt(mean_of(center * center) + EPSILON)
        normed1 = center * scale1
        hat1[here, :] = normed1
        rstd1[here, :] = scale1
        first = normed1 * vec(g1_ref) + vec(s1_ref)
        first_low = first.astype(bfloat)
        low1[here, :] = first_low
        second = first + vec(b2_ref)
        bias1 = vec(b1_ref)
        for j in range(ff // WIDE):
            span = slice(j * WIDE, (j + 1) * WIDE)
            pre = jnp.dot(first_low, w1[:, span], preferred_element_type=single) + bias1[:, span]
            share = 0.5 * (1.0 + lax.erf(pre * INV_SQRT2))
            active = (pre * share).astype(bfloat)
            hidden[here, span] = active
            slope[here, span] = share + pre * jnp.exp(-0.5 * pre * pre) * INV_SQRT_2PI
            second = second + jnp.dot(active, w2[span, :], preferred_element_type=single)
        center = second - mean_of(second)
        scale2 = lax.rsqrt(mean_of(center * center) + EPSILON)
        normed2 = center * scale2
        result = (normed2 * vec(g2_ref) + vec(s2_ref)).astype(bfloat)
        out_ref[first_seq:last_seq] = result.reshape(last_seq - first_seq, tokens, width)
        for s in range(first_seq, last_seq):
            store(0, s).start()
        incoming = cot[first_seq:last_seq].reshape(count, width).astype(single)
        add_small(10, incoming * normed2)
        add_small(11, incoming)
        scaled = incoming * vec(g2_ref)
        grad_second = scale2 * (
            scaled - mean_of(scaled) - normed2 * mean_of(scaled * normed2)
        )
        grad_resid[here, :] = grad_second
        grad_low = grad_second.astype(bfloat)
        grad_outer[here, :] = grad_low
        add_small(9, grad_low.astype(single))

    for group in FORWARD:
        forward(*group)

    def stages_of(unit):
        base, count, order = units[unit]
        size = count // 2
        start = base + place.core * size
        stages = [("c", start, base + (1 - place.core) * size, size)]
        for axis in order:
            if axis == "z":
                size = size // groups
                stages.append((axis, start + place.z * size, start, size))
                start = start + place.z * size
            else:
                size = size // 2
                index = {"x": place.x, "y": place.y, "u": place.z % 2, "v": place.z // 2}[axis]
                stages.append((axis, start + index * size, start + (1 - index) * size, size))
                start = start + index * size
        return stages

    def partner(axis):
        if axis in "uv":
            step = 1 if axis == "u" else 2
            bit = (place.z // step) % 2
            return (place.z + step * (1 - 2 * bit), me)
        return place.in_plane({"c": 1, "x": 2, "y": 4}[axis])

    def rows_at(start, count):
        return pl.ds(aligned(start, 16), count)

    def landing(unit, stage):
        before = 0
        for other in range(unit):
            before += units[other][1]
        for earlier in range(stage):
            axis, _, _, size = stages_of(unit)[earlier]
            before += size * (groups - 1 if axis == "z" else 1)
        return before

    def reduce_copies(unit, stage):
        axis, _, away, size = stages_of(unit)[stage]
        at = landing(unit, stage)
        send, recv = rs_send.at[unit], rs_recv.at[unit, stage]
        if axis != "z":
            return [
                remote(
                    part.at[rows_at(away, size), :],
                    landed.at[at : at + size, :],
                    send,
                    recv,
                    partner(axis),
                )
            ]
        return [
            remote(
                part.at[rows_at(away + ((place.z + offset) % groups) * size, size), :],
                landed.at[at + (offset - 1) * size : at + offset * size, :],
                send,
                recv,
                place.in_column(offset),
            )
            for offset in range(1, groups)
        ]

    def reduce_start(unit, stage):
        for copy in reduce_copies(unit, stage):
            copy.start()

    def reduce_finish(unit, stage):
        axis, keep, _, size = stages_of(unit)[stage]
        at = landing(unit, stage)
        count = groups - 1 if axis == "z" else 1
        arrived = landed.at[at : at + count * size, :]
        gone(arrived, rs_send.at[unit])
        take(arrived, rs_recv.at[unit, stage])
        result = total if stage == len(units[unit][2]) else part
        tile = next(rows for rows in (128, 64, 32, 16) if size % rows == 0)

        def add(i, _):
            mine = rows_at(keep + i * tile, tile)
            if count == 1:
                value = part[mine, :] + landed[rows_at(at + i * tile, tile), :]
            else:
                value = part[mine, :].astype(single)
                for j in range(count):
                    other = landed[rows_at(at + j * size + i * tile, tile), :]
                    value = value + other.astype(single)
            result[mine, :] = value.astype(bfloat)
            return 0

        if size == tile:
            add(0, 0)
        else:
            lax.fori_loop(0, size // tile, add, 0)

    def gather_start(unit, stage):
        axis, keep, _, size = stages_of(unit)[stage]
        slot = total.at[rows_at(keep, size), :]
        send, recv = rs_send.at[unit], rs_recv.at[unit, 5 + stage]
        if axis != "z":
            remote(slot, slot, send, recv, partner(axis)).start()
        else:
            for offset in range(1, groups):
                remote(slot, slot, send, recv, place.in_column(offset)).start()

    def gather_finish(unit, stage):
        axis, _, away, size = stages_of(unit)[stage]
        count = groups - 1 if axis == "z" else 1
        slot = total.at[rows_at(away, count * size), :]
        gone(slot, rs_send.at[unit])
        take(slot, rs_recv.at[unit, 5 + stage])

    def result_copy(unit):
        base, count, _ = units[unit]
        at = pl.ds(base, count)
        return pltpu.make_async_copy(total.at[at, :], sums_hbm.at[at, :], done_sem.at[0])

    def step(unit, stage):
        last = len(units[unit][2])
        if stage < last:
            reduce_finish(unit, stage)
            reduce_start(unit, stage + 1)
        elif stage == last:
            reduce_finish(unit, stage)
            gather_start(unit, last)
        elif stage <= 2 * last:
            gather_finish(unit, 2 * last + 1 - stage)
            gather_start(unit, 2 * last - stage)
        else:
            gather_finish(unit, 0)
            result_copy(unit).start()

    def ready_units(begin, end):
        for unit, (base, count, _) in enumerate(units):
            if begin < base + count <= end:
                reduce_start(unit, 0)

    def steps_at(name, index):
        for at, kind, *what in plan[name]:

            def do():
                small_step(*what) if kind == "small" else step(*what)

            if not isinstance(index, int):
                pl.when(index == at)(do)
            elif index == at:
                do()

    def keep_part(base, value):
        part[base : base + value.shape[0], :] = value.astype(bfloat)

    def small_copy(turn, device):
        return remote(small_ref, small_in.at[turn], v_send, v_recv.at[min(turn, 3)], device)

    def small_arrived(turn, count):
        slot = small_in.at[turn : turn + count]
        gone(slot, v_send)
        take(slot, v_recv.at[turn])

    def in_place_order(mine, others):
        result = jnp.zeros(mine.shape, single)
        for source in range(groups):
            for offset in range(groups):
                term = mine if offset == 0 else others[offset - 1]
                result = result + jnp.where(
                    (place.z + groups - offset) % groups == source, term, 0.0
                )
        return result

    small_store = pltpu.make_async_copy(small_ref, small_hbm, store_sem.at[2])

    def small_step(stage):
        if stage > 0 and stage < 4:
            small_arrived(stage - 1, 1)
            small_ref[...] += small_in[stage - 1]
        if stage < 3:
            small_copy(stage, place.in_plane(2**stage)).start()
        elif stage == 3:
            for offset in range(1, groups):
                small_copy(2 + offset, place.in_column(offset)).start()
        else:
            if groups > 1:
                small_arrived(3, groups - 1)
            terms = [small_in[2 + offset] for offset in range(1, groups)]
            small_ref[...] = in_place_order(small_ref[...], terms)
            small_store.start()

    def outer_tile(start):
        at = slice(start, start + TILES)
        keep_part(start, dot(hidden[:, at], grad_outer[...], 0, 0))
        ready_units(start, start + TILES)

    def inner_tile(start):
        for j in range(start, start + TILES, WIDE):
            keep_part(ff + j, dot(low1[...], grad_inner[:, j : j + WIDE], 0, 0))
        ready_units(ff + start, ff + start + TILES)

    for start in range(0, ff, TILES):
        outer_tile(start)

    def backward(first_seq, last_seq):
        here = slice(first_seq * tokens, last_seq * tokens)
        back = grad_resid[here, :]
        grad_low = grad_outer[here, :]
        for j in range(ff // WIDE):
            span = slice(j * WIDE, (j + 1) * WIDE)
            grad_hidden = dot(grad_low, w2[span, :], 1, 1)
            inner = (grad_hidden * slope[here, span]).astype(bfloat)
            grad_inner[here, span] = inner
            add_small(5 + j, inner.astype(single))
            back = back + dot(inner, w1[:, span], 1, 1)
        normed1 = hat1[here, :]
        add_small(3, back * normed1)
        add_small(4, back)
        scaled = back * vec(g1_ref)
        grad = rstd1[here, :] * (scaled - mean_of(scaled) - normed1 * mean_of(scaled * normed1))
        grad_resid[here, :] = grad
        grad = grad.astype(bfloat)
        grad_branch[here, :] = grad
        add_small(2, grad.astype(single))
        gatt_t[:, here] = dot(wo[...], grad, 1, 1).astype(bfloat)
        for s in range(first_seq, last_seq):
            for k in (6, 7, 2, 3, 4, 5, 1):
                dout_copy(s, k).start()
        for s in range(first_seq, last_seq):
            dout_t[s, :, lanes_of(me)] = gatt_t[head_rows_of(me), seq_lanes(s)]

    for index, group in enumerate(BACKWARD):
        backward(*group)
        steps_at("backward", index)
    for index, start in enumerate(range(0, ff, TILES)):
        inner_tile(start)
        steps_at("inner", index)
    keep_part(2 * ff, jnp.dot(att_t[...], grad_branch[...], preferred_element_type=single))
    ready_units(2 * ff, 2 * ff + width)
    steps_at("inner", ff // TILES)

    def pack_copies(s, k):
        other = place.peer(k)
        return [
            remote(
                dqkv.at[s, j * HEAD : (j + 1) * HEAD, lanes_of(other)],
                gpacked_t.at[j, head_rows_of(me), seq_lanes(s)],
                p_send,
                p_recv,
                place.in_plane(k),
            )
            for j in range(3)
        ]

    turns = length // BACK_QUERIES

    def back_math(s, i):
        at = pl.ds(aligned(i * BACK_QUERIES, BACK_QUERIES), BACK_QUERIES)
        cot_t = dout_t[s, :, at].astype(single)
        inverse = inv_total[s, :, at]
        delta = inverse * jnp.sum(cot_t * out_wide[s, :, at], axis=0, keepdims=True)
        cot_low = (cot_t * inverse).astype(bfloat)
        grown = probs[s, :, at]
        grad = jnp.dot(vrow[s], cot_low, preferred_element_type=single) - delta
        grad = (grown.astype(single) * grad).astype(bfloat)
        query_grad = jnp.dot(qkv[s, HEAD : 2 * HEAD, :], grad, preferred_element_type=single)
        dqkv[s, 0:HEAD, at] = (query_grad.astype(bfloat) * HEAD**-0.5).astype(bfloat)
        return dot(qkv[s, 0:HEAD, at], grad, 1, 1), dot(cot_low, grown, 1, 1)

    def back_chunk(turn, _):
        s = turn // turns
        i = turn % turns

        @pl.when(i == 0)
        def _():
            take(dout_t.at[s, :, 0 : others * tokens], d_recv.at[s])
            dk_acc[...] = jnp.zeros(dk_acc.shape, single)
            dv_acc[...] = jnp.zeros(dv_acc.shape, single)

        key_grad, value_grad = back_math(s, i)
        dk_acc[...] += key_grad
        dv_acc[...] += value_grad

        @pl.when(i == turns - 1)
        def _():
            dqkv[s, HEAD : 2 * HEAD, :] = dk_acc[...].astype(bfloat)
            dqkv[s, 2 * HEAD :, :] = dv_acc[...].astype(bfloat)
            for k in (6, 7, 2, 3, 4, 5, 1):
                for copy in pack_copies(s, k):
                    copy.start()
            for j in range(3):
                gpacked_t[j, head_rows_of(me), seq_lanes(s)] = dqkv[
                    s, j * HEAD : (j + 1) * HEAD, lanes_of(me)
                ]
            entry_acc[...] += jnp.dot(dqkv[s], xall[s], preferred_element_type=single)

        steps_at("attention", turn)
        return 0

    lax.fori_loop(0, seqs * turns, back_chunk, 0)

    entry_base = 2 * ff + width
    head_share = 3 * HEAD
    fourth = head_share // groups

    def entry_rows(device, z=None):
        start = entry_base + device * head_share
        if z is None:
            return rows_at(start, head_share)
        return rows_at(start + z * fourth, fourth)

    def entry_copy(offset):
        target = (place.z + offset) % groups
        return remote(
            entry_part.at[rows_at(target * fourth, fourth), :],
            entry_in.at[offset - 1],
            e_send.at[0],
            e_recv.at[0],
            place.in_column(offset),
        )

    def entry_back(offset):
        slot = total.at[entry_rows(me, place.z), :]
        return remote(slot, slot, e_send.at[1], e_recv.at[1], place.in_column(offset))

    def entry_plane(owner, to):
        slot = total.at[entry_rows(owner), :]
        recv = e_recv.at[3 if to == 1 else 2]
        return remote(slot, slot, e_send.at[2], recv, place.in_plane(to))

    def entry_shares(count):
        return total.at[pl.ds(entry_base, count * head_share), :]

    def entry_result():
        rows = pl.ds(entry_base, HEADS * head_share)
        return pltpu.make_async_copy(total.at[rows, :], entry_hbm, done_sem.at[1])

    def entry_step(stage):
        if stage == 0:
            entry_part[...] = entry_acc[...].astype(bfloat)
            for offset in range(1, groups):
                entry_copy(offset).start()
        elif stage == 1:
            if groups > 1:
                gone(entry_in, e_send.at[0])
                take(entry_in, e_recv.at[0])
            value = entry_part[rows_at(place.z * fourth, fourth), :].astype(single)
            for offset in range(1, groups):
                value = value + entry_in[offset - 1].astype(single)
            total[entry_rows(me, place.z), :] = value.astype(bfloat)
            for offset in range(1, groups):
                entry_back(offset).start()
        elif stage == 2:
            if groups > 1:
                slot = total.at[pl.ds(entry_base, (groups - 1) * fourth), :]
                gone(slot, e_send.at[1])
                take(slot, e_recv.at[1])
            for k in (6, 2, 4, 1):
                entry_plane(me, k).start()
        elif stage == 3:
            take(entry_shares(3), e_recv.at[2])
            for k in (2, 4, 6):
                entry_plane(place.peer(k), 1).start()
        else:
            take(entry_shares(4), e_recv.at[3])
            gone(entry_shares(7), e_send.at[2])
            entry_result().start()

    bias_store = pltpu.make_async_copy(bias_rows, bias_hbm, store_sem.at[3])

    def bias_column(offset):
        return remote(
            bias_own,
            bias_in.at[offset - 1],
            b_send.at[0],
            b_recv.at[0],
            place.in_column(offset),
        )

    def bias_plane(k, owner):
        slot = bias_all.at[owner]
        return remote(slot, slot, b_send.at[1], b_recv.at[1], place.in_plane(k))

    def bias_step(stage):
        if stage == 0:
            ones = jnp.ones((8, length), bfloat)
            sums = jnp.zeros((8, head_share), single)
            for s in range(seqs):
                sums = sums + dot(ones, dqkv[s], 1, 1)
            bias_own[:, 0:head_share] = sums
            for offset in range(1, groups):
                bias_column(offset).start()
        elif stage == 1:
            if groups > 1:
                gone(bias_in, b_send.at[0])
                take(bias_in, b_recv.at[0])
            terms = [bias_in[offset - 1] for offset in range(1, groups)]
            bias_all[me] = in_place_order(bias_own[...], terms)
            for k in range(1, 8):
                bias_plane(k, me).start()
        else:
            gone(bias_all.at[0:others], b_send.at[1])
            take(bias_all.at[0:others], b_recv.at[1])
            for at, start in ((0, 0), (1, 2 * HEAD)):
                bias_rows[at : at + 1, :] = jnp.concatenate(
                    [bias_all[p, 0:1, start : start + HEAD] for p in range(HEADS)], axis=1
                )
            bias_store.start()


    def input_step():
        take(gpacked_t.at[:, 0 : others * HEAD, :], p_recv)
        grad_in = grad_resid[...]
        for j in range(3):
            grad_in = grad_in + dot(gpacked_t[j], we[:, j * width : (j + 1) * width], 0, 1)
        for s in range(seqs):
            dx_ref[s] = grad_in[s * tokens : (s + 1) * tokens].astype(bfloat)
            store(1, s).start()

    for kind, *what in plan["tail"]:
        if kind == "unit":
            step(*what)
        elif kind == "entry":
            entry_step(*what)
        elif kind == "bias":
            bias_step(*what)
        elif kind == "small":
            small_step(*what)
        else:
            input_step()
    pltpu.make_async_copy(total.at[0 : sums_hbm.shape[0], :], sums_hbm, done_sem.at[0]).wait()
    entry_result().wait()
    small_store.wait()
    bias_store.wait()
    pltpu.make_async_copy(out_ref, out_hbm, store_sem.at[0]).wait()
    pltpu.make_async_copy(dx_ref, dx_hbm, store_sem.at[1]).wait()
    gone(xall.at[:, 0 : others * tokens, :], x_send)
    gone(ids_all.at[:, 0 : others * tokens], i_send)
    gone(out_low.at[:, :, 0 : others * tokens], o_send)
    gone(gatt_t.at[0 : others * HEAD, :], d_send)
    gone(dqkv.at[:, :, 0 : others * tokens], p_send)


def widen_kernel(sums_hbm, entry_hbm, small_hbm, bias_hbm, out_in, dx_in, *refs):
    outs, vectors, scratch = refs[:15], refs[15:23], refs[23:]
    sums, entry_low, small, bias, passed, inner_bias, outer_v, inner_v, out_v, entry_v = scratch[:10]
    in_sem, out_sem = scratch[10:]
    out_ref, dx_ref, entry, query_b, value_b, out_w, out_b = outs[:7]
    gain1, shift1, inner_w, inner_b, outer_w, outer_b, gain2, shift2 = outs[7:]
    width = WIDE
    ff = outer_w.shape[0]
    pieces = sums.shape[0] // WIDE
    reads = []
    writes = []

    def read(src, dst):
        reads.append(pltpu.make_async_copy(src, dst, in_sem.at[len(reads)]))
        reads[-1].start()

    def write(src, dst):
        writes.append(pltpu.make_async_copy(src, dst, out_sem.at[len(writes)]))
        writes[-1].start()

    for i in range(pieces):
        rows = slice(i * WIDE, (i + 1) * WIDE)
        read(sums_hbm.at[rows, :], sums.at[rows, :])
    read(entry_hbm, entry_low)
    read(small_hbm, small)
    read(bias_hbm, bias)
    read(out_in, passed.at[0])
    read(dx_in, passed.at[1])
    for i in range(pieces):
        reads[i].wait()
        rows = slice(i * WIDE, (i + 1) * WIDE)
        value = sums[rows, :].astype(single)
        j = i - ff // WIDE
        if j < 0:
            outer_v[rows, :] = value
            write(outer_v.at[rows], outer_w.at[rows])
        elif j < ff // WIDE:
            columns = slice(j * WIDE, (j + 1) * WIDE)
            inner_v[:, columns] = value
            write(inner_v.at[:, columns], inner_w.at[:, columns])
        else:
            out_v[...] = value
            write(out_v, out_w)
    reads[pieces].wait()
    for j in range(3):
        columns = slice(j * width, (j + 1) * width)
        value = entry_low[:, j * HEAD : (j + 1) * HEAD, :].reshape(width, width)
        entry_v[:, columns] = value.astype(single).T
        write(entry_v.at[:, columns], entry.at[:, columns])
    for read_done in reads[pieces + 1 :]:
        read_done.wait()
    write(passed.at[0], out_ref)
    write(passed.at[1], dx_ref)

    def small_row(at):
        return (bias if at < 2 else small)[at : at + 1, :].reshape(width)

    for j, (ref, at) in enumerate(
        (
            (query_b, 0),
            (value_b, 1),
            (out_b, 2),
            (gain1, 3),
            (shift1, 4),
            (outer_b, 9),
            (gain2, 10),
            (shift2, 11),
        )
    ):
        vectors[j][...] = small_row(at)
        write(vectors[j], ref)
    for j in range(ff // WIDE):
        inner_bias[j * WIDE : (j + 1) * WIDE] = small_row(5 + j)
    write(inner_bias, inner_b)
    for copy in writes:
        copy.wait()


UNITS = (
    (0, 512, "yxuv"),
    (512, 512, "zyx"),
    (1024, 512, "xuvy"),
    (1536, 512, "uxvy"),
    (2048, 512, "yzx"),
    (2560, 512, "xuyv"),
    (3072, 512, "yxuv"),
    (3584, 512, "xyuv"),
    (4096, 512, "uxyv"),
)
PLAN = {
    "backward": (
        (0, "unit", 1, 0),
        (0, "unit", 2, 0),
        (0, "unit", 0, 0),
        (0, "unit", 3, 0),
    ),
    "inner": (
        (0, "small", 0),
        (2, "unit", 4, 0),
    ),
    "attention": (
        (0, "unit", 5, 0),
        (0, "unit", 6, 0),
        (0, "unit", 7, 0),
        (0, "unit", 0, 1),
        (0, "small", 1),
        (0, "unit", 2, 1),
        (0, "unit", 8, 0),
        (1, "unit", 3, 1),
        (1, "unit", 1, 1),
        (3, "unit", 4, 1),
        (3, "unit", 2, 2),
        (3, "unit", 5, 1),
        (4, "unit", 6, 1),
        (4, "unit", 8, 1),
        (4, "unit", 7, 1),
        (5, "unit", 0, 2),
        (5, "small", 2),
    ),
    "tail": (
        ("entry", 0),
        ("bias", 0),
        ("unit", 4, 2),
        ("unit", 1, 2),
        ("unit", 5, 2),
        ("unit", 2, 3),
        ("unit", 0, 3),
        ("unit", 3, 2),
        ("entry", 1),
        ("unit", 7, 2),
        ("bias", 1),
        ("unit", 0, 4),
        ("unit", 3, 3),
        ("unit", 6, 2),
        ("unit", 8, 2),
        ("small", 3),
        ("unit", 5, 3),
        ("unit", 2, 4),
        ("unit", 7, 3),
        ("unit", 3, 4),
        ("unit", 6, 3),
        ("entry", 2),
        ("unit", 8, 3),
        ("unit", 0, 5),
        ("unit", 2, 5),
        ("unit", 4, 3),
        ("input",),
        ("bias", 2),
        ("unit", 1, 3),
        ("small", 4),
        ("unit", 3, 5),
        ("unit", 5, 4),
        ("unit", 0, 6),
        ("unit", 7, 4),
        ("unit", 6, 4),
        ("unit", 8, 4),
        ("unit", 2, 6),
        ("unit", 3, 6),
        ("unit", 5, 5),
        ("unit", 7, 5),
        ("unit", 6, 5),
        ("unit", 2, 7),
        ("unit", 4, 4),
        ("entry", 3),
        ("unit", 8, 5),
        ("unit", 1, 4),
        ("unit", 5, 6),
        ("unit", 0, 7),
        ("unit", 7, 6),
        ("entry", 4),
        ("unit", 6, 6),
        ("unit", 3, 7),
        ("unit", 8, 6),
        ("unit", 1, 5),
        ("unit", 2, 8),
        ("unit", 5, 7),
        ("unit", 4, 5),
        ("unit", 2, 9),
        ("unit", 0, 8),
        ("unit", 6, 7),
        ("unit", 0, 9),
        ("unit", 7, 7),
        ("unit", 8, 7),
        ("unit", 3, 8),
        ("unit", 3, 9),
        ("unit", 5, 8),
        ("unit", 4, 6),
        ("unit", 5, 9),
        ("unit", 4, 7),
        ("unit", 1, 6),
        ("unit", 7, 8),
        ("unit", 6, 8),
        ("unit", 1, 7),
        ("unit", 7, 9),
        ("unit", 8, 8),
        ("unit", 6, 9),
        ("unit", 8, 9),
    ),
}


def by_heads(groups):
    def run(inputs, blocks, we, qb, vb, wo, bo, g1, s1, w1, b1, w2, b2, g2, s2, cot):
        seqs, tokens, width = inputs.shape
        ff = w1.shape[1]
        rows = seqs * tokens
        length = tokens * HEADS
        grad_rows = 2 * ff + width
        units = UNITS
        others = max(groups - 1, 1)
        head_share = 3 * HEAD
        smem = pl.BlockSpec(memory_space=pltpu.SMEM)
        hbm = pl.BlockSpec(memory_space=pl.ANY)
        dma = pltpu.SemaphoreType.DMA

        def shape(*dims):
            return jax.ShapeDtypeStruct(dims, single)

        entry_shape = (HEADS, head_share, width)
        out, dx, sums, entry, small, bias = pl.pallas_call(
            partial(layer_kernel, groups, units, PLAN),
            out_shape=[
                jax.ShapeDtypeStruct(inputs.shape, bfloat),
                jax.ShapeDtypeStruct(inputs.shape, bfloat),
                jax.ShapeDtypeStruct((grad_rows, width), bfloat),
                jax.ShapeDtypeStruct((HEADS * head_share, width), bfloat),
                shape(16, width),
                shape(8, width),
            ],
            in_specs=[hbm, smem] + [hbm] * 14,
            out_specs=[hbm] * 6,
            scratch_shapes=[
                pltpu.VMEM(inputs.shape, bfloat),
                pltpu.VMEM(qb.shape, bfloat),
                pltpu.VMEM(vb.shape, bfloat),
                pltpu.VMEM(bo.shape, bfloat),
                pltpu.VMEM(g1.shape, bfloat),
                pltpu.VMEM(s1.shape, bfloat),
                pltpu.VMEM(b1.shape, bfloat),
                pltpu.VMEM(b2.shape, bfloat),
                pltpu.VMEM(g2.shape, bfloat),
                pltpu.VMEM(s2.shape, bfloat),
                pltpu.VMEM(inputs.shape, bfloat),
                pltpu.VMEM(inputs.shape, bfloat),
                pltpu.VMEM((16, width), single),
                pltpu.VMEM(we.shape, bfloat),
                pltpu.VMEM(wo.shape, bfloat),
                pltpu.VMEM(w1.shape, bfloat),
                pltpu.VMEM(w2.shape, bfloat),
                pltpu.VMEM(cot.shape, bfloat),
                dma((15,)),
                pltpu.VMEM((head_share, width), bfloat),
                pltpu.VMEM((seqs, length, width), bfloat),
                pltpu.VMEM((HEADS, 16, tokens), bfloat),
                pltpu.VMEM((16, length), bfloat),
                pltpu.VMEM((seqs, 8, length), single),
                pltpu.VMEM((seqs, head_share, length), bfloat),
                pltpu.VMEM((seqs, length, HEAD), bfloat),
                pltpu.VMEM((seqs, length, HEAD), bfloat),
                pltpu.VMEM((seqs, length, length), bfloat),
                pltpu.VMEM((seqs, 1, length), single),
                pltpu.VMEM((seqs, HEAD, length), single),
                pltpu.VMEM((seqs, HEAD, length), bfloat),
                pltpu.VMEM((width, rows), bfloat),
                pltpu.VMEM((rows, width), single),
                pltpu.VMEM((rows, 1), single),
                pltpu.VMEM((rows, width), bfloat),
                pltpu.VMEM((rows, ff), bfloat),
                pltpu.VMEM((rows, ff), single),
                pltpu.VMEM((rows, ff), bfloat),
                pltpu.VMEM((rows, width), bfloat),
                pltpu.VMEM((rows, width), single),
                pltpu.VMEM((rows, width), bfloat),
                pltpu.VMEM((width, rows), bfloat),
                pltpu.VMEM((seqs, HEAD, length), bfloat),
                pltpu.VMEM((seqs, head_share, length), bfloat),
                pltpu.VMEM((HEAD, length), single),
                pltpu.VMEM((HEAD, length), single),
                pltpu.VMEM((3, width, rows), bfloat),
                pltpu.VMEM((head_share, width), single),
                pltpu.VMEM((head_share, width), bfloat),
                pltpu.VMEM((others, head_share // groups, width), bfloat),
                pltpu.VMEM((grad_rows, width), bfloat),
                pltpu.VMEM((grad_rows, width), bfloat),
                pltpu.VMEM((grad_rows + HEADS * head_share, width), bfloat),
                pltpu.VMEM((3 + groups, 16, width), single),
                pltpu.VMEM((8, 256), single),
                pltpu.VMEM((others, 8, 256), single),
                pltpu.VMEM((HEADS, 8, 256), single),
                pltpu.VMEM((8, width), single),
                dma(()),
                dma((seqs, 3)),
                dma(()),
                dma(()),
                dma(()),
                dma((seqs,)),
                dma(()),
                dma((seqs,)),
                dma(()),
                dma(()),
                dma((len(units),)),
                dma((len(units), 10)),
                dma((3,)),
                dma((4,)),
                dma(()),
                dma((4,)),
                dma((2,)),
                dma((2,)),
                dma((2,)),
                dma((4,)),
            ],
            compiler_params=pltpu.CompilerParams(
                collective_id=0, has_side_effects=True, vmem_limit_bytes=60 * 2**20
            ),
            name="layer",
        )(
            inputs, blocks.transpose(0, 3, 2, 1), we, qb, vb, wo, bo, g1, s1, w1, b1, w2, b2,
            g2, s2, cot,
        )
        pieces = grad_rows // WIDE
        return pl.pallas_call(
            widen_kernel,
            in_specs=[hbm] * 6,
            out_specs=[hbm] * 15,
            out_shape=[
                jax.ShapeDtypeStruct(inputs.shape, bfloat),
                jax.ShapeDtypeStruct(inputs.shape, bfloat),
                shape(width, 3 * width),
                shape(width),
                shape(width),
                shape(width, width),
                shape(width),
                shape(width),
                shape(width),
                shape(width, ff),
                shape(ff),
                shape(ff, width),
                shape(width),
                shape(width),
                shape(width),
            ],
            scratch_shapes=[
                *[pltpu.VMEM((width,), single)] * 8,
                pltpu.VMEM((grad_rows, width), bfloat),
                pltpu.VMEM(entry_shape, bfloat),
                pltpu.VMEM((16, width), single),
                pltpu.VMEM((8, width), single),
                pltpu.VMEM((2, *inputs.shape), bfloat),
                pltpu.VMEM((ff,), single),
                pltpu.VMEM((ff, width), single),
                pltpu.VMEM((width, ff), single),
                pltpu.VMEM((width, width), single),
                pltpu.VMEM((width, 3 * width), single),
                dma((pieces + 5,)),
                dma((pieces + 14,)),
            ],
            compiler_params=pltpu.CompilerParams(vmem_limit_bytes=60 * 2**20),
            name="widen",
        )(sums, entry.reshape(entry_shape), small, bias, out, dx)

    return run


def solution(mesh):
    in_specs = (
        P("dp", "seq", None),
        P("dp", None, "seq", None),
        P(),
        P(),
        P(),
        P(),
        P(),
        P(),
        P(),
        P(),
        P(),
        P(),
        P(),
        P(),
        P(),
        P("dp", "seq", None),
    )
    out_specs = (
        P("dp", "seq", None),
        P("dp", "seq", None),
        P(),
        P(),
        P(),
        P(),
        P(),
        P(),
        P(),
        P(),
        P(),
        P(),
        P(),
        P(),
        P(),
    )
    heads_fit = mesh.shape["seq"] == HEADS
    plan = by_heads(mesh.shape["dp"]) if heads_fit else on_device
    return jax.shard_map(
        plan, mesh=mesh, in_specs=in_specs, out_specs=out_specs, check_vma=False
    )
```

```python
from functools import partial

import jax
import jax.numpy as jnp
from jax import lax
from jax.experimental import pallas as pl
from jax.experimental.pallas import tpu as pltpu
from jax.sharding import PartitionSpec as P

HEADS = 8
HEAD = 64
BLOCK = 64


HIGHEST = lax.Precision.HIGHEST
EPSILON = 1e-05
NEGATIVE = -1e30


def spread_2(value, axis, root):
    mine = lax.axis_index(axis) == root
    return lax.psum(jnp.where(mine, value, jnp.zeros_like(value)), axis)


def for_sending(value):

    def short(part):
        return part.astype(jnp.bfloat16) if part.dtype == jnp.float32 else part

    return jax.tree.map(short, value)


def extended(block, sides, width):
    for axis, dim in sides:
        count = lax.axis_size(axis)
        forward = [(i, i + 1) for i in range(count - 1)]
        backward = [(target, source) for source, target in forward]
        low = lax.ppermute(
            lax.slice_in_dim(block, block.shape[dim] - width, None, axis=dim), axis, forward
        )
        high = lax.ppermute(lax.slice_in_dim(block, 0, width, axis=dim), axis, backward)
        block = jnp.concatenate([low, block, high], axis=dim)
    return block


def combined_all(part, axis, combine):
    gathered = jax.tree.map(lambda a: lax.all_gather(a, axis), part)

    def take(source):
        return jax.tree.map(lambda a: lax.dynamic_index_in_dim(a, source, 0, False), gathered)

    return lax.fori_loop(
        1, lax.axis_size(axis), lambda source, state: combine(state, take(source)), take(0)
    )


def norm_apply(values, gain_vec, shift_vec):
    center = values - jnp.mean(values, axis=-1, keepdims=True)
    spread = jnp.mean(center * center, axis=-1, keepdims=True)
    return center * lax.rsqrt(spread + EPSILON) * gain_vec + shift_vec


def pair_blocks(row_data, head_count, block_rows):
    seq_count, length_here, full_width = row_data.shape
    head_width = full_width // (2 * head_count)
    shaped = row_data.reshape(
        seq_count, length_here // block_rows, block_rows, 2, head_count, head_width
    )
    return shaped.transpose(0, 4, 1, 2, 3, 5).reshape(
        seq_count, head_count, length_here // block_rows, block_rows, 2 * head_width
    )


def pair_tokens(blocked):
    seq_count, head_count, block_count, block_rows, double_width = blocked.shape
    head_width = double_width // 2
    shaped = blocked.reshape(seq_count, head_count, block_count, block_rows, 2, head_width)
    return shaped.transpose(0, 2, 3, 4, 1, 5).reshape(
        seq_count, block_count * block_rows, 2 * head_count * head_width
    )


def head_rows(row_data, head_count):
    seq_count, length_here, full_width = row_data.shape
    return row_data.reshape(seq_count, length_here, head_count, full_width // head_count).transpose(
        0, 2, 1, 3
    )


def row_heads(split_rows):
    seq_count, head_count, length_here, head_width = split_rows.shape
    return split_rows.transpose(0, 2, 1, 3).reshape(seq_count, length_here, head_count * head_width)


def merge_parts(earlier, later):
    peak_one, total_one, out_one = earlier
    peak_two, total_two, out_two = later
    row_peak = jnp.maximum(peak_one, peak_two)
    factor_one = jnp.exp(peak_one - row_peak)
    factor_two = jnp.exp(peak_two - row_peak)
    return (
        row_peak,
        total_one * factor_one + total_two * factor_two,
        out_one * factor_one[..., None] + out_two * factor_two[..., None],
    )


def share_rows(row_data, root_device):
    return spread_2(row_data, "seq", root_device)


def share_grads(grad_rows, grad_delta, root_device):
    return (
        spread_2(grad_rows.astype(jnp.bfloat16), "seq", root_device).astype(grad_rows.dtype),
        spread_2(for_sending(grad_delta), "seq", root_device).astype(grad_delta.dtype),
    )


def on_device(
    inputs,
    random_blocks,
    entry_weight,
    query_bias,
    value_bias,
    out_weight,
    out_bias,
    norm_gain,
    norm_shift,
    inner_weight,
    inner_bias,
    outer_weight,
    outer_bias,
    final_gain,
    final_shift,
    cotangent,
):
    seq_count, token_count, model_width = inputs.shape
    head_count = HEADS
    head_width = HEAD
    block_rows = BLOCK
    per_dev = token_count // block_rows
    devices = lax.axis_size("seq")
    device = lax.axis_index("seq")
    block_total = devices * per_dev
    request_total = seq_count * head_count * per_dev * 3
    capacity = (request_total + devices - 2) // (devices - 1)
    table_rows = seq_count * head_count * per_dev
    query_scale = head_width ** (-0.5)
    is_first = device == 0
    is_last = device == devices - 1
    bfloat = jnp.bfloat16
    single = jnp.float32
    flat_in = inputs.reshape(-1, model_width)
    entry_out = jnp.dot(flat_in, entry_weight, preferred_element_type=single)
    packed = jnp.concatenate(
        [
            (entry_out[:, :model_width] + query_bias) * query_scale,
            entry_out[:, model_width : 2 * model_width],
            entry_out[:, 2 * model_width :] + value_bias,
        ],
        axis=1,
    )
    packed = packed.astype(bfloat).reshape(seq_count, token_count, 3 * model_width)
    key_value = packed[:, :, model_width:]
    padded = extended(key_value, (("seq", 1),), block_rows)
    global_rows = jnp.concatenate(
        [
            share_rows(packed[:, :block_rows], 0),
            share_rows(packed[:, token_count - block_rows :], devices - 1),
        ],
        axis=1,
    )
    owners = (random_blocks // per_dev).reshape(-1)
    within = random_blocks % per_dev
    seq_index = lax.broadcasted_iota(jnp.int32, random_blocks.shape, 0)
    head_index = lax.broadcasted_iota(jnp.int32, random_blocks.shape, 1)
    request_codes = ((seq_index * head_count + head_index) * per_dev + within).reshape(-1)
    onehot = (owners[:, None] == jnp.arange(devices, dtype=jnp.int32)[None, :]).astype(jnp.int32)
    slot_index = jnp.sum((jnp.cumsum(onehot, axis=0) - onehot) * onehot, axis=1)
    slot_place = owners * capacity + slot_index
    requests = (
        jnp.full((devices * capacity,), -1, jnp.int32)
        .at[slot_place]
        .set(request_codes)
        .reshape(devices, capacity)
    )
    incoming = lax.all_to_all(requests, "seq", split_axis=0, concat_axis=0, tiled=True)
    head_table = pair_blocks(key_value, head_count, block_rows).reshape(
        table_rows, block_rows, 2 * head_width
    )
    served = head_table[jnp.maximum(incoming, 0)]
    served = jnp.where((incoming >= 0)[:, :, None, None], served, jnp.zeros((), bfloat))
    fetched = lax.all_to_all(served, "seq", split_axis=0, concat_axis=0, tiled=True)
    random_kv = fetched.reshape(devices * capacity, block_rows, 2 * head_width)[slot_place]
    random_kv = random_kv.reshape(seq_count, head_count, per_dev, 3, block_rows, 2 * head_width)
    window_view = pair_blocks(padded, head_count, block_rows)
    window_kv = jnp.stack(
        [window_view[:, :, :per_dev], window_view[:, :, 1 : per_dev + 1], window_view[:, :, 2:]],
        axis=3,
    )
    global_kv = pair_blocks(global_rows[:, :, model_width:], head_count, block_rows)
    global_kv = jnp.broadcast_to(
        global_kv[:, :, None], (seq_count, head_count, per_dev, 2, block_rows, 2 * head_width)
    )
    all_kv = jnp.concatenate([window_kv, global_kv, random_kv], axis=3).reshape(
        seq_count, head_count, per_dev, 8 * block_rows, 2 * head_width
    )
    key_part = all_kv[..., :head_width]
    value_part = all_kv[..., head_width:]
    query_view = head_rows(packed[:, :, :model_width], head_count).reshape(
        seq_count, head_count, per_dev, block_rows, head_width
    )
    block_ids = device * per_dev + jnp.arange(per_dev)[:, None]
    column = jnp.arange(8 * block_rows)[None, :]
    neighbor = block_ids + column // block_rows - 1
    key_keep = (column >= 3 * block_rows) | (neighbor >= 1) & (neighbor <= block_total - 2)
    key_keep = key_keep[None, None, :, None, :]

    def block_scores():
        raw_scores = jnp.einsum(
            "shiqd,shikd->shiqk", query_view, key_part, preferred_element_type=single
        )
        return jnp.where(key_keep, raw_scores, NEGATIVE)

    scores = block_scores()
    row_peak = jnp.max(scores, axis=-1, keepdims=True)
    exponent = jnp.exp(scores - row_peak)
    row_total = jnp.sum(exponent, axis=-1, keepdims=True)
    probability = exponent / row_total
    log_total = row_peak + jnp.log(row_total)
    prob_low = probability.astype(bfloat)
    window_out = jnp.einsum(
        "shiqk,shikd->shiqd", prob_low, value_part, preferred_element_type=single
    )
    global_query = head_rows(global_rows[:, :, :model_width], head_count)
    local_keys = head_rows(packed[:, :, model_width : 2 * model_width], head_count)
    local_values = head_rows(packed[:, :, 2 * model_width :], head_count)
    global_scores = jnp.einsum(
        "shqd,shkd->shqk", global_query, local_keys, preferred_element_type=single
    )
    global_peak = jnp.max(global_scores, axis=-1)
    global_exp = jnp.exp(global_scores - global_peak[..., None])
    global_total = jnp.sum(global_exp, axis=-1)
    global_sum = jnp.einsum(
        "shqk,shkd->shqd", global_exp, local_values.astype(single), precision=HIGHEST
    )
    global_peak, global_total, global_sum = combined_all(
        (global_peak, global_total, global_sum), "seq", merge_parts
    )
    global_out = global_sum / global_total[..., None]
    global_log = global_peak + jnp.log(global_total)
    block_pos = jnp.arange(per_dev)
    take_first = ((block_pos == 0) & is_first)[None, None, :, None, None]
    take_last = ((block_pos == per_dev - 1) & is_last)[None, None, :, None, None]
    combined = jnp.where(take_first, global_out[:, :, None, :block_rows], window_out)
    combined = jnp.where(take_last, global_out[:, :, None, block_rows:], combined)
    attended = (
        row_heads(combined.reshape(seq_count, head_count, token_count, head_width))
        .reshape(-1, model_width)
        .astype(bfloat)
    )
    branch = jnp.dot(attended, out_weight, preferred_element_type=single) + out_bias
    residual_in = flat_in.astype(single) + branch
    first_norm, first_pull = jax.vjp(
        norm_apply, residual_in, norm_gain.astype(single), norm_shift.astype(single)
    )
    first_low = first_norm.astype(bfloat)
    inner_pre = jnp.dot(first_low, inner_weight, preferred_element_type=single) + inner_bias
    activated, gelu_pull = jax.vjp(partial(jax.nn.gelu, approximate=False), inner_pre)
    hidden = activated.astype(bfloat)
    second = first_norm + (
        jnp.dot(hidden, outer_weight, preferred_element_type=single) + outer_bias
    )
    final_norm, final_pull = jax.vjp(
        norm_apply, second, final_gain.astype(single), final_shift.astype(single)
    )
    layer_out = final_norm.astype(bfloat).reshape(inputs.shape)
    grad_second, final_gain_grad, final_shift_grad = final_pull(
        cotangent.reshape(-1, model_width).astype(single)
    )
    grad_outer = grad_second.astype(bfloat)
    outer_weight_grad = jnp.dot(hidden.T, grad_outer, preferred_element_type=single)
    outer_bias_grad = jnp.sum(grad_outer.astype(single), axis=0)
    (grad_active,) = gelu_pull(jnp.dot(grad_outer, outer_weight.T, preferred_element_type=single))
    grad_inner = grad_active.astype(bfloat)
    inner_weight_grad = jnp.dot(first_low.T, grad_inner, preferred_element_type=single)
    inner_bias_grad = jnp.sum(grad_inner.astype(single), axis=0)
    grad_first = grad_second + jnp.dot(grad_inner, inner_weight.T, preferred_element_type=single)
    grad_resid, norm_gain_grad, norm_shift_grad = first_pull(grad_first)
    grad_branch = grad_resid.astype(bfloat)
    out_weight_grad = jnp.dot(attended.T, grad_branch, preferred_element_type=single)
    out_bias_grad = jnp.sum(grad_branch.astype(single), axis=0)
    grad_attended = jnp.dot(grad_branch, out_weight.T, preferred_element_type=single).astype(bfloat)
    grad_heads = head_rows(
        grad_attended.reshape(seq_count, token_count, model_width), head_count
    ).reshape(seq_count, head_count, per_dev, block_rows, head_width)
    grad_window = jnp.where(take_first | take_last, jnp.zeros((), bfloat), grad_heads)
    probability = jnp.exp(block_scores() - log_total)
    prob_low = probability.astype(bfloat)
    grad_prob = jnp.einsum(
        "shiqd,shikd->shiqk", grad_window, value_part, preferred_element_type=single
    )
    row_delta = jnp.sum(probability * grad_prob, axis=-1, keepdims=True)
    grad_scores = (probability * (grad_prob - row_delta)).astype(bfloat)
    grad_query_block = jnp.einsum(
        "shiqk,shikd->shiqd", grad_scores, key_part, preferred_element_type=single
    )
    grad_key_block = jnp.einsum(
        "shiqk,shiqd->shikd", grad_scores, query_view, preferred_element_type=single
    )
    grad_value_block = jnp.einsum(
        "shiqk,shiqd->shikd", prob_low, grad_window, preferred_element_type=single
    )
    grad_kv = jnp.concatenate([grad_key_block, grad_value_block], axis=-1).reshape(
        seq_count, head_count, per_dev, 8, block_rows, 2 * head_width
    )
    pad_none = ((0, 0), (0, 0))
    grad_pad = (
        jnp.pad(grad_kv[:, :, :, 0], pad_none + ((0, 2), (0, 0), (0, 0)))
        + jnp.pad(grad_kv[:, :, :, 1], pad_none + ((1, 1), (0, 0), (0, 0)))
        + jnp.pad(grad_kv[:, :, :, 2], pad_none + ((2, 0), (0, 0), (0, 0)))
    )
    grad_tokens = pair_tokens(grad_pad)
    edge_grads = jnp.concatenate(
        [grad_tokens[:, :block_rows], grad_tokens[:, token_count + block_rows :]], axis=1
    )
    returned = extended(edge_grads.astype(jnp.bfloat16), (("seq", 1),), block_rows).astype(
        edge_grads.dtype
    )
    gap = token_count - block_rows
    grad_kv_local = (
        grad_tokens[:, block_rows : block_rows + token_count]
        + jnp.pad(returned[:, :block_rows], ((0, 0), (0, gap), (0, 0)))
        + jnp.pad(returned[:, 3 * block_rows :], ((0, 0), (gap, 0), (0, 0)))
    )
    grad_global_kv = pair_tokens(jnp.sum(grad_kv[:, :, :, 3:5], axis=2))
    grad_random = grad_kv[:, :, :, 5:8].reshape(request_total, block_rows, 2 * head_width)
    outgoing = (
        jnp.zeros((devices * capacity, block_rows, 2 * head_width), single)
        .at[slot_place]
        .set(grad_random)
    )
    outgoing = outgoing.reshape(devices, capacity, block_rows, 2 * head_width)
    returned_random = lax.all_to_all(
        outgoing.astype(jnp.bfloat16), "seq", split_axis=0, concat_axis=0, tiled=True
    ).astype(outgoing.dtype)
    segment_ids = jnp.where(incoming >= 0, incoming, table_rows).reshape(-1)
    grad_table = jax.ops.segment_sum(
        returned_random.reshape(devices * capacity, block_rows, 2 * head_width),
        segment_ids,
        num_segments=table_rows + 1,
    )[:table_rows]
    grad_owned = pair_tokens(
        grad_table.reshape(seq_count, head_count, per_dev, block_rows, 2 * head_width)
    )
    first_cot = grad_heads[:, :, 0].astype(single)
    last_cot = grad_heads[:, :, per_dev - 1].astype(single)
    first_cot, first_delta = share_grads(
        first_cot, jnp.sum(first_cot * global_out[:, :, :block_rows], axis=-1), 0
    )
    last_cot, last_delta = share_grads(
        last_cot, jnp.sum(last_cot * global_out[:, :, block_rows:], axis=-1), devices - 1
    )
    global_cot = jnp.concatenate([first_cot, last_cot], axis=2)
    global_delta = jnp.concatenate([first_delta, last_delta], axis=2)
    global_prob = jnp.exp(
        jnp.einsum("shqd,shkd->shqk", global_query, local_keys, preferred_element_type=single)
        - global_log[..., None]
    )
    global_dprob = jnp.einsum(
        "shqd,shkd->shqk", global_cot.astype(bfloat), local_values, preferred_element_type=single
    )
    global_grads = (global_prob * (global_dprob - global_delta[..., None])).astype(bfloat)
    grad_global_query = jnp.einsum(
        "shqk,shkd->shqd", global_grads, local_keys, preferred_element_type=single
    )
    grad_local_key = jnp.einsum(
        "shqk,shqd->shkd", global_grads, global_query, preferred_element_type=single
    )
    grad_local_value = jnp.einsum("shqk,shqd->shkd", global_prob, global_cot, precision=HIGHEST)
    partials = jnp.concatenate([row_heads(grad_global_query), grad_global_kv], axis=-1)
    partials = lax.psum(partials.astype(jnp.bfloat16), "seq").astype(jnp.float32)
    owner_part = jnp.where(
        is_first, jnp.pad(partials[:, :block_rows], ((0, 0), (0, gap), (0, 0))), 0.0
    ) + jnp.where(is_last, jnp.pad(partials[:, block_rows:], ((0, 0), (gap, 0), (0, 0))), 0.0)
    grad_query_tokens = row_heads(
        grad_query_block.reshape(seq_count, head_count, token_count, head_width)
    )
    grad_kv_tokens = (
        grad_kv_local
        + grad_owned
        + jnp.concatenate([row_heads(grad_local_key), row_heads(grad_local_value)], axis=-1)
    )
    grad_packed = (
        jnp.concatenate([grad_query_tokens, grad_kv_tokens], axis=-1) + owner_part
    ).astype(bfloat)
    column_scale = jnp.concatenate(
        [jnp.full((model_width,), query_scale, single), jnp.ones((2 * model_width,), single)]
    )
    grad_entry = (
        (grad_packed.astype(single) * column_scale).astype(bfloat).reshape(-1, 3 * model_width)
    )
    entry_weight_grad = jnp.dot(flat_in.T, grad_entry, preferred_element_type=single)
    query_bias_grad = jnp.sum(grad_entry[:, :model_width].astype(single), axis=0)
    value_bias_grad = jnp.sum(grad_entry[:, 2 * model_width :].astype(single), axis=0)
    input_grad = (
        (grad_resid + jnp.dot(grad_entry, entry_weight.T, preferred_element_type=single))
        .astype(bfloat)
        .reshape(inputs.shape)
    )
    (
        total_entry,
        total_query,
        total_value,
        total_out,
        total_out_bias,
        total_norm_gain,
        total_norm_shift,
        total_inner,
        total_inner_bias,
        total_outer,
        total_outer_bias,
        total_final_gain,
        total_final_shift,
    ) = lax.psum(
        (
            entry_weight_grad,
            query_bias_grad,
            value_bias_grad,
            out_weight_grad,
            out_bias_grad,
            norm_gain_grad,
            norm_shift_grad,
            inner_weight_grad,
            inner_bias_grad,
            outer_weight_grad,
            outer_bias_grad,
            final_gain_grad,
            final_shift_grad,
        ),
        ("dp", "seq"),
    )
    return (
        layer_out,
        input_grad,
        total_entry,
        total_query,
        total_value,
        total_out,
        total_out_bias,
        total_norm_gain,
        total_norm_shift,
        total_inner,
        total_inner_bias,
        total_outer,
        total_outer_bias,
        total_final_gain,
        total_final_shift,
    )


MESH = pl.DeviceIdType.MESH
bfloat = jnp.bfloat16
single = jnp.float32
WIDE = 512
QUERIES = 1024
BACK_QUERIES = 512
FORWARD = ((0, 2), (2, 3))
EARLY = (
    ("outer", 0),
    ("back", 0, 1),
    ("outer", 1024),
    ("back", 1, 3),
    ("inner", 0),
    ("inner", 1024),
    ("out",),
)
TILES = 1024
LAYER_VMEM = 56 * 2**20
WIDEN_VMEM = 56 * 2**20
INV_SQRT2 = 0.7071067811865476
INV_SQRT_2PI = 0.3989422804014327


def dot(a, b, a_dim, b_dim):
    return lax.dot_general(
        a, b, (((a_dim,), (b_dim,)), ((), ())), preferred_element_type=single
    )


def aligned(index, step):
    return pl.multiple_of(index, step)


class Place:
    def __init__(self, groups):
        self.groups = groups
        self.z = lax.axis_index("dp")
        self.me = lax.axis_index("seq")
        self.y = self.me // 4
        self.x = (self.me // 2) % 2
        self.core = self.me % 2

    def peer(self, offset):
        off_y, off_x, off_core = offset // 4, (offset // 2) % 2, offset % 2
        return (
            ((self.y + off_y) % 2) * 4
            + ((self.x + off_x) % 2) * 2
            + (self.core + off_core) % 2
        )

    def in_plane(self, offset):
        return (self.z, self.peer(offset))

    def in_column(self, offset):
        return ((self.z + offset) % self.groups, self.me)


def remote(src, dst, send, recv, device):
    return pltpu.make_async_remote_copy(
        src_ref=src,
        dst_ref=dst,
        send_sem=send,
        recv_sem=recv,
        device_id=device,
        device_id_type=MESH,
    )


def layer_kernel(
    groups,
    units,
    plan,
    x_hbm,
    blocks_ref,
    we_hbm,
    qb_hbm,
    vb_hbm,
    wo_hbm,
    bo_hbm,
    g1_hbm,
    s1_hbm,
    w1_hbm,
    b1_hbm,
    w2_hbm,
    b2_hbm,
    g2_hbm,
    s2_hbm,
    cot_hbm,
    out_hbm,
    dx_hbm,
    total,
    small_hbm,
    bias_hbm,
    x_ref,
    qb_ref,
    vb_ref,
    bo_ref,
    g1_ref,
    s1_ref,
    b1_ref,
    b2_ref,
    g2_ref,
    s2_ref,
    out_ref,
    dx_ref,
    small_ref,
    we,
    wo,
    w1,
    w2,
    cot,
    load_sem,
    wh_t,
    xall,
    ids_send,
    ids_all,
    ids,
    qkv,
    krow,
    vrow,
    probs,
    inv_total,
    out_wide,
    out_low,
    att_t,
    hat1,
    rstd1,
    low1,
    hidden,
    slope,
    grad_inner,
    grad_outer,
    grad_resid,
    grad_branch,
    gatt_t,
    dout_t,
    dqkv,
    dk_acc,
    dv_acc,
    gpacked_t,
    entry_acc,
    entry_part,
    entry_in,
    part,
    landed,
    small_in,
    bias_own,
    bias_in,
    bias_all,
    bias_rows,
    x_send,
    x_recv,
    i_send,
    i_recv,
    o_send,
    o_recv,
    d_send,
    d_recv,
    p_send,
    p_recv,
    rs_send,
    rs_recv,
    e_send,
    e_recv,
    v_send,
    v_recv,
    b_send,
    b_recv,
    store_sem,
):
    seqs, tokens, width = x_ref.shape
    place = Place(groups)
    me = place.me
    barrier = pltpu.get_barrier_semaphore()
    for k in range(1, 8):
        pl.semaphore_signal(
            barrier, inc=1, device_id=place.in_plane(k), device_id_type=MESH
        )
    for k in range(1, groups):
        pl.semaphore_signal(
            barrier, inc=1, device_id=place.in_column(k), device_id_type=MESH
        )
    def load(*pairs):
        copies = []
        for src, dst in pairs:
            copies.append(pltpu.make_async_copy(src, dst, load_sem.at[len(loads)]))
            copies[-1].start()
            loads.append(copies[-1])
        return copies

    loads = []
    load_x = load((x_hbm, x_ref))
    load_entry = load((we_hbm, we), (qb_hbm, qb_ref), (vb_hbm, vb_ref))
    load_rest = load(
        (wo_hbm, wo),
        (bo_hbm, bo_ref),
        (g1_hbm, g1_ref),
        (s1_hbm, s1_ref),
        (w1_hbm, w1),
        (b1_hbm, b1_ref),
        (w2_hbm, w2),
        (b2_hbm, b2_ref),
        (g2_hbm, g2_ref),
        (s2_hbm, s2_ref),
        (cot_hbm, cot),
    )

    def lanes_of(device):
        return pl.ds(aligned(device * tokens, 128), tokens)

    def head_rows_of(device):
        return pl.ds(aligned(device * HEAD, HEAD), HEAD)

    def seq_lanes(s):
        return pl.ds(aligned(s * tokens, 128), tokens)

    def vec(ref):
        return ref[...].astype(single).reshape(1, ref.shape[0])

    others = HEADS - 1

    def take(ref, sem):
        remote(ref, ref, sem, sem, place.in_plane(1)).wait_recv()

    def gone(ref, sem):
        remote(ref, ref, sem, sem, place.in_plane(1)).wait_send()

    lane = lax.broadcasted_iota(jnp.int32, (16, tokens), 1)
    row = lax.broadcasted_iota(jnp.int32, (16, tokens), 0)
    for h in range(HEADS):
        numbers = jnp.zeros((16, tokens), jnp.int32)
        for s in range(seqs):
            for j in range(3):
                picked = jnp.where(
                    lane < BLOCK, blocks_ref[s, j, 0, h], blocks_ref[s, j, 1, h]
                )
                numbers = jnp.where(row == s * 3 + j, picked, numbers)
        ids_send[h] = numbers.astype(single).astype(bfloat)
    small_ref[...] = jnp.zeros(small_ref.shape, single)
    bias_rows[...] = jnp.zeros(bias_rows.shape, single)
    bias_own[...] = jnp.zeros(bias_own.shape, single)
    entry_acc[...] = jnp.zeros(entry_acc.shape, single)

    load_x[0].wait()
    pl.semaphore_wait(barrier, 7 + groups - 1)

    half_width = width // 2

    def x_copy(s, k):
        return remote(
            x_ref.at[s],
            xall.at[s, lanes_of(me), :],
            x_send,
            x_recv.at[s, 2 if k == 1 else 0],
            place.in_plane(k),
        )

    def x_across(s, k):
        columns = slice(0, half_width) if k == 2 else slice(half_width, width)
        slab = xall.at[s, lanes_of(place.peer(6 - k)), columns]
        return remote(slab, slab, x_send, x_recv.at[s, 1], place.in_plane(k))

    def x_forward(s, k):
        slab = xall.at[s, lanes_of(place.peer(k)), :]
        return remote(slab, slab, x_send, x_recv.at[s, 2], place.in_plane(1))

    def x_arrived(s, which):
        slabs = (2, 1, 4)[which]
        take(xall.at[s, 0 : slabs * tokens, :], x_recv.at[s, which])

    def x_begin(s):
        for k in (2, 4, 1):
            x_copy(s, k).start()

    def x_pass(s):
        x_arrived(s, 0)
        for k in (2, 4):
            x_across(s, k).start()
            x_forward(s, k).start()

    def ids_copy(k):
        other = place.peer(k)
        return remote(
            ids_send.at[other],
            ids_all.at[:, lanes_of(me)],
            i_send,
            i_recv,
            place.in_plane(k),
        )

    x_begin(0)
    for k in range(1, 8):
        ids_copy(k).start()
    x_begin(1)
    ids_all[:, lanes_of(me)] = ids_send[me]
    for s in range(seqs):
        xall[s, lanes_of(me), :] = x_ref[s]

    for copy in load_entry:
        copy.wait()
    pair = me // 2
    odd = me % 2
    for j in range(3):
        columns = we[:, pl.ds(aligned(j * width + pair * 2 * HEAD, 128), 2 * HEAD)].T
        wh_t[j * HEAD : (j + 1) * HEAD, :] = jnp.where(
            odd == 1, columns[HEAD:], columns[:HEAD]
        )
    spread = lax.broadcasted_iota(jnp.int32, (HEAD, width), 1) == me * HEAD + (
        lax.broadcasted_iota(jnp.int32, (HEAD, width), 0)
    )

    def column(ref):
        return jnp.sum(jnp.where(spread, vec(ref), 0.0), axis=1, keepdims=True)

    query_column = column(qb_ref)
    value_column = column(vb_ref)

    take(ids_all.at[:, 0 : others * tokens], i_recv)
    for s in range(seqs):
        ids[s, 0:3, :] = ids_all[...].astype(single)[3 * s : 3 * s + 3]

    length = qkv.shape[2]
    chunks = length // QUERIES
    blocks = length // BLOCK
    key_block = lax.broadcasted_iota(jnp.int32, (blocks, QUERIES), 0)
    query_lane = lax.broadcasted_iota(jnp.int32, (blocks, QUERIES), 1)

    def out_copy(s, k):
        return remote(
            out_low.at[s, :, lanes_of(place.peer(k))],
            att_t.at[head_rows_of(me), seq_lanes(s)],
            o_send,
            o_recv.at[s],
            place.in_plane(k),
        )

    def take_x(s):
        x_arrived(s, 1)
        x_forward(s, 6).start()

        @pl.when(s < seqs - 2)
        def _():
            x_pass(s + 2)

        x_arrived(s, 2)
        packed = dot(wh_t[...], xall[s], 1, 1)
        qkv[s, 0:HEAD, :] = ((packed[0:HEAD] + query_column) * HEAD**-0.5).astype(bfloat)
        qkv[s, HEAD : 2 * HEAD, :] = packed[HEAD : 2 * HEAD].astype(bfloat)
        qkv[s, 2 * HEAD :, :] = (packed[2 * HEAD :] + value_column).astype(bfloat)

    def attend(s, _):
        take_x(s)
        krow[s] = qkv[s, HEAD : 2 * HEAD, :].T
        vrow[s] = qkv[s, 2 * HEAD : 3 * HEAD, :].T

        def chunk(i, _):
            at = pl.ds(aligned(i * QUERIES, QUERIES), QUERIES)
            query_block = (i * QUERIES + query_lane) // BLOCK
            inside = (key_block >= 1) & (key_block <= blocks - 2)
            near = (key_block >= query_block - 1) & (key_block <= query_block + 1) & inside
            times = jnp.where(near, 1.0, 0.0) + jnp.where(inside, 0.0, 1.0)
            for j in range(3):
                times = times + jnp.where(
                    ids[s, j : j + 1, at] == key_block.astype(single), 1.0, 0.0
                )
            bias = jnp.where(times > 1.5, 0.6931471805599453, 0.0)
            bias = jnp.where(times > 0.5, bias, NEGATIVE)
            bias = jnp.where((query_block == 0) | (query_block == blocks - 1), 0.0, bias)
            score = jnp.dot(krow[s], qkv[s, 0:HEAD, at], preferred_element_type=single)
            score = score.reshape(blocks, BLOCK, QUERIES) + bias[:, None, :]
            score = score.reshape(length, QUERIES)
            peak = jnp.max(score, axis=0, keepdims=True)
            grown = jnp.exp(score - peak)
            inverse = 1.0 / jnp.sum(grown, axis=0, keepdims=True)
            grown = grown.astype(bfloat)
            probs[s, :, at] = grown
            inv_total[s, :, at] = inverse
            result = inverse * jnp.dot(
                qkv[s, 2 * HEAD :, :], grown, preferred_element_type=single
            )
            out_wide[s, :, at] = result
            out_low[s, :, at] = result.astype(bfloat)
            return 0

        lax.fori_loop(0, chunks, chunk, 0)
        for k in (6, 7, 2, 3, 4, 5, 1):
            out_copy(s, k).start()
        att_t[head_rows_of(me), seq_lanes(s)] = out_low[s, :, lanes_of(me)]
        return 0

    x_pass(0)
    for s in range(2, seqs):
        x_begin(s)
    x_pass(1)
    lax.fori_loop(0, seqs, attend, 0)
    for copy in load_rest:
        copy.wait()

    def dout_copy(s, k):
        return remote(
            gatt_t.at[head_rows_of(place.peer(k)), seq_lanes(s)],
            dout_t.at[s, :, lanes_of(me)],
            d_send,
            d_recv.at[s],
            place.in_plane(k),
        )

    def mean_of(value):
        return jnp.mean(value, axis=-1, keepdims=True)

    def add_small(row, value):
        small_ref[row : row + 1, :] += jnp.sum(value, axis=0, keepdims=True)

    ff = hidden.shape[1]

    def store(which, s):
        src, dst = ((out_ref, out_hbm), (dx_ref, dx_hbm))[which]
        return pltpu.make_async_copy(src.at[s], dst.at[s], store_sem.at[which])

    def forward(first_seq, last_seq):
        for s in range(first_seq, last_seq):
            take(att_t.at[0 : others * HEAD, seq_lanes(s)], o_recv.at[s])
        here = slice(first_seq * tokens, last_seq * tokens)
        count = (last_seq - first_seq) * tokens
        branch = dot(att_t[:, here], wo[...], 0, 0) + vec(bo_ref)
        resid = x_ref[first_seq:last_seq].reshape(count, width).astype(single) + branch
        center = resid - mean_of(resid)
        scale1 = lax.rsqrt(mean_of(center * center) + EPSILON)
        normed1 = center * scale1
        hat1[here, :] = normed1
        rstd1[here, :] = scale1
        first = normed1 * vec(g1_ref) + vec(s1_ref)
        first_low = first.astype(bfloat)
        low1[here, :] = first_low
        second = first + vec(b2_ref)
        bias1 = vec(b1_ref)
        for j in range(ff // WIDE):
            span = slice(j * WIDE, (j + 1) * WIDE)
            pre = jnp.dot(first_low, w1[:, span], preferred_element_type=single) + bias1[:, span]
            share = 0.5 * (1.0 + lax.erf(pre * INV_SQRT2))
            active = (pre * share).astype(bfloat)
            hidden[here, span] = active
            slope[here, span] = share + pre * jnp.exp(-0.5 * pre * pre) * INV_SQRT_2PI
            second = second + jnp.dot(active, w2[span, :], preferred_element_type=single)
        center = second - mean_of(second)
        scale2 = lax.rsqrt(mean_of(center * center) + EPSILON)
        normed2 = center * scale2
        result = (normed2 * vec(g2_ref) + vec(s2_ref)).astype(bfloat)
        out_ref[first_seq:last_seq] = result.reshape(last_seq - first_seq, tokens, width)
        for s in range(first_seq, last_seq):
            store(0, s).start()
        incoming = cot[first_seq:last_seq].reshape(count, width).astype(single)
        add_small(10, incoming * normed2)
        add_small(11, incoming)
        scaled = incoming * vec(g2_ref)
        grad_second = scale2 * (
            scaled - mean_of(scaled) - normed2 * mean_of(scaled * normed2)
        )
        grad_resid[here, :] = grad_second
        grad_low = grad_second.astype(bfloat)
        grad_outer[here, :] = grad_low
        add_small(9, grad_low.astype(single))

    for group in FORWARD:
        forward(*group)

    def stages_of(unit):
        base, count, order = units[unit]
        size = count // 2
        start = base + place.core * size
        stages = [("c", start, base + (1 - place.core) * size, size)]
        for axis in order:
            if axis == "z":
                size = size // groups
                stages.append((axis, start + place.z * size, start, size))
                start = start + place.z * size
            else:
                size = size // 2
                index = {"x": place.x, "y": place.y, "u": place.z % 2, "v": place.z // 2}[axis]
                stages.append((axis, start + index * size, start + (1 - index) * size, size))
                start = start + index * size
        return stages

    def partner(axis):
        if axis in "uv":
            step = 1 if axis == "u" else 2
            bit = (place.z // step) % 2
            return (place.z + step * (1 - 2 * bit), me)
        return place.in_plane({"c": 1, "x": 2, "y": 4}[axis])

    def rows_at(start, count):
        return pl.ds(aligned(start, 16), count)

    def landing(unit, stage):
        before = 0
        for other in range(unit):
            before += units[other][1]
        for earlier in range(stage):
            axis, _, _, size = stages_of(unit)[earlier]
            before += size * (groups - 1 if axis == "z" else 1)
        return before

    def reduce_copies(unit, stage):
        axis, _, away, size = stages_of(unit)[stage]
        at = landing(unit, stage)
        send, recv = rs_send.at[unit], rs_recv.at[unit, stage]
        if axis != "z":
            return [
                remote(
                    part.at[rows_at(away, size), :],
                    landed.at[at : at + size, :],
                    send,
                    recv,
                    partner(axis),
                )
            ]
        return [
            remote(
                part.at[rows_at(away + ((place.z + offset) % groups) * size, size), :],
                landed.at[at + (offset - 1) * size : at + offset * size, :],
                send,
                recv,
                place.in_column(offset),
            )
            for offset in range(1, groups)
        ]

    def reduce_start(unit, stage):
        for copy in reduce_copies(unit, stage):
            copy.start()

    def reduce_finish(unit, stage):
        axis, keep, _, size = stages_of(unit)[stage]
        at = landing(unit, stage)
        count = groups - 1 if axis == "z" else 1
        arrived = landed.at[at : at + count * size, :]
        gone(arrived, rs_send.at[unit])
        take(arrived, rs_recv.at[unit, stage])
        result = total if stage == len(units[unit][2]) else part
        tile = next(rows for rows in (128, 64, 32, 16) if size % rows == 0)

        def add(i, _):
            mine = rows_at(keep + i * tile, tile)
            if count == 1:
                value = part[mine, :] + landed[rows_at(at + i * tile, tile), :]
            else:
                value = part[mine, :].astype(single)
                for j in range(count):
                    other = landed[rows_at(at + j * size + i * tile, tile), :]
                    value = value + other.astype(single)
            result[mine, :] = value.astype(bfloat)
            return 0

        if size == tile:
            add(0, 0)
        else:
            lax.fori_loop(0, size // tile, add, 0)

    def gather_start(unit, stage):
        axis, keep, _, size = stages_of(unit)[stage]
        slot = total.at[rows_at(keep, size), :]
        send, recv = rs_send.at[unit], rs_recv.at[unit, 5 + stage]
        if axis != "z":
            remote(slot, slot, send, recv, partner(axis)).start()
        else:
            for offset in range(1, groups):
                remote(slot, slot, send, recv, place.in_column(offset)).start()

    def gather_finish(unit, stage):
        axis, _, away, size = stages_of(unit)[stage]
        count = groups - 1 if axis == "z" else 1
        slot = total.at[rows_at(away, count * size), :]
        gone(slot, rs_send.at[unit])
        take(slot, rs_recv.at[unit, 5 + stage])

    def step(unit, stage):
        last = len(units[unit][2])
        if stage < last:
            reduce_finish(unit, stage)
            reduce_start(unit, stage + 1)
        elif stage == last:
            reduce_finish(unit, stage)
            gather_start(unit, last)
        elif stage <= 2 * last:
            gather_finish(unit, 2 * last + 1 - stage)
            gather_start(unit, 2 * last - stage)
        else:
            gather_finish(unit, 0)

    def ready_units(begin, end):
        for unit, (base, count, _) in enumerate(units):
            if begin < base + count <= end:
                reduce_start(unit, 0)

    def steps_at(name, index):
        for at, kind, *what in plan[name]:

            def do():
                small_step(*what) if kind == "small" else step(*what)

            if not isinstance(index, int):
                pl.when(index == at)(do)
            elif index == at:
                do()

    def keep_part(base, value):
        part[base : base + value.shape[0], :] = value.astype(bfloat)

    def small_copy(turn, device):
        return remote(small_ref, small_in.at[turn], v_send, v_recv.at[min(turn, 3)], device)

    def small_arrived(turn, count):
        slot = small_in.at[turn : turn + count]
        gone(slot, v_send)
        take(slot, v_recv.at[turn])

    def in_place_order(mine, others):
        result = jnp.zeros(mine.shape, single)
        for source in range(groups):
            for offset in range(groups):
                term = mine if offset == 0 else others[offset - 1]
                result = result + jnp.where(
                    (place.z + groups - offset) % groups == source, term, 0.0
                )
        return result

    small_store = pltpu.make_async_copy(small_ref, small_hbm, store_sem.at[2])

    def small_step(stage):
        if stage > 0 and stage < 4:
            small_arrived(stage - 1, 1)
            small_ref[...] += small_in[stage - 1]
        if stage < 3:
            small_copy(stage, place.in_plane(2**stage)).start()
        elif stage == 3:
            for offset in range(1, groups):
                small_copy(2 + offset, place.in_column(offset)).start()
        else:
            if groups > 1:
                small_arrived(3, groups - 1)
            terms = [small_in[2 + offset] for offset in range(1, groups)]
            small_ref[...] = in_place_order(small_ref[...], terms)
            small_store.start()

    def outer_tile(start):
        at = slice(start, start + TILES)
        keep_part(start, dot(hidden[:, at], grad_outer[...], 0, 0))
        ready_units(start, start + TILES)

    def inner_tile(start):
        for j in range(start, start + TILES, WIDE):
            keep_part(ff + j, dot(low1[...], grad_inner[:, j : j + WIDE], 0, 0))
        ready_units(ff + start, ff + start + TILES)

    def backward(first_seq, last_seq):
        here = slice(first_seq * tokens, last_seq * tokens)
        back = grad_resid[here, :]
        grad_low = grad_outer[here, :]
        for j in range(ff // WIDE):
            span = slice(j * WIDE, (j + 1) * WIDE)
            grad_hidden = dot(grad_low, w2[span, :], 1, 1)
            inner = (grad_hidden * slope[here, span]).astype(bfloat)
            grad_inner[here, span] = inner
            add_small(5 + j, inner.astype(single))
            back = back + dot(inner, w1[:, span], 1, 1)
        normed1 = hat1[here, :]
        add_small(3, back * normed1)
        add_small(4, back)
        scaled = back * vec(g1_ref)
        grad = rstd1[here, :] * (scaled - mean_of(scaled) - normed1 * mean_of(scaled * normed1))
        grad_resid[here, :] = grad
        grad = grad.astype(bfloat)
        grad_branch[here, :] = grad
        add_small(2, grad.astype(single))
        gatt_t[:, here] = dot(wo[...], grad, 1, 1).astype(bfloat)
        for s in range(first_seq, last_seq):
            for k in (6, 7, 2, 3, 4, 5, 1):
                dout_copy(s, k).start()
        for s in range(first_seq, last_seq):
            dout_t[s, :, lanes_of(me)] = gatt_t[head_rows_of(me), seq_lanes(s)]

    def out_tile():
        keep_part(2 * ff, jnp.dot(att_t[...], grad_branch[...], preferred_element_type=single))
        ready_units(2 * ff, 2 * ff + width)

    for index, (kind, *what) in enumerate(EARLY):
        {"outer": outer_tile, "back": backward, "inner": inner_tile, "out": out_tile}[kind](*what)
        steps_at("early", index)

    def pack_copies(s, k):
        other = place.peer(k)
        return [
            remote(
                dqkv.at[s, j * HEAD : (j + 1) * HEAD, lanes_of(other)],
                gpacked_t.at[j, head_rows_of(me), seq_lanes(s)],
                p_send,
                p_recv,
                place.in_plane(k),
            )
            for j in range(3)
        ]

    turns = length // BACK_QUERIES

    def back_math(s, i):
        at = pl.ds(aligned(i * BACK_QUERIES, BACK_QUERIES), BACK_QUERIES)
        cot_t = dout_t[s, :, at].astype(single)
        inverse = inv_total[s, :, at]
        delta = inverse * jnp.sum(cot_t * out_wide[s, :, at], axis=0, keepdims=True)
        cot_low = (cot_t * inverse).astype(bfloat)
        grown = probs[s, :, at]
        grad = jnp.dot(vrow[s], cot_low, preferred_element_type=single) - delta
        grad = (grown.astype(single) * grad).astype(bfloat)
        query_grad = jnp.dot(qkv[s, HEAD : 2 * HEAD, :], grad, preferred_element_type=single)
        dqkv[s, 0:HEAD, at] = (query_grad.astype(bfloat) * HEAD**-0.5).astype(bfloat)
        return dot(qkv[s, 0:HEAD, at], grad, 1, 1), dot(cot_low, grown, 1, 1)

    def back_chunk(turn, _):
        s = turn // turns
        i = turn % turns

        @pl.when(i == 0)
        def _():
            take(dout_t.at[s, :, 0 : others * tokens], d_recv.at[s])
            dk_acc[...] = jnp.zeros(dk_acc.shape, single)
            dv_acc[...] = jnp.zeros(dv_acc.shape, single)

        key_grad, value_grad = back_math(s, i)
        dk_acc[...] += key_grad
        dv_acc[...] += value_grad

        @pl.when(i == turns - 1)
        def _():
            dqkv[s, HEAD : 2 * HEAD, :] = dk_acc[...].astype(bfloat)
            dqkv[s, 2 * HEAD :, :] = dv_acc[...].astype(bfloat)
            for k in (6, 7, 2, 3, 4, 5, 1):
                for copy in pack_copies(s, k):
                    copy.start()
            for j in range(3):
                gpacked_t[j, head_rows_of(me), seq_lanes(s)] = dqkv[
                    s, j * HEAD : (j + 1) * HEAD, lanes_of(me)
                ]
            entry_acc[...] += jnp.dot(dqkv[s], xall[s], preferred_element_type=single)

        steps_at("attention", turn)
        return 0

    lax.fori_loop(0, seqs * turns, back_chunk, 0)

    entry_base = 2 * ff + width
    head_share = 3 * HEAD
    fourth = head_share // groups

    def entry_rows(device, z=None):
        start = entry_base + device * head_share
        if z is None:
            return rows_at(start, head_share)
        return rows_at(start + z * fourth, fourth)

    def entry_copy(offset):
        target = (place.z + offset) % groups
        return remote(
            entry_part.at[rows_at(target * fourth, fourth), :],
            entry_in.at[offset - 1],
            e_send.at[0],
            e_recv.at[0],
            place.in_column(offset),
        )

    def entry_back(offset):
        slot = total.at[entry_rows(me, place.z), :]
        return remote(slot, slot, e_send.at[1], e_recv.at[1], place.in_column(offset))

    def entry_plane(owner, to, half, turn=2):
        columns = (slice(0, half_width), slice(half_width, width), slice(0, width))[half]
        slot = total.at[entry_rows(owner), columns]
        return remote(slot, slot, e_send.at[2], e_recv.at[turn], place.in_plane(to))

    def entry_shares(count):
        return total.at[pl.ds(entry_base, count * head_share), :]

    def entry_step(stage):
        if stage == 0:
            entry_part[...] = entry_acc[...].astype(bfloat)
            for offset in range(1, groups):
                entry_copy(offset).start()
        elif stage == 1:
            if groups > 1:
                gone(entry_in, e_send.at[0])
                take(entry_in, e_recv.at[0])
            value = entry_part[rows_at(place.z * fourth, fourth), :].astype(single)
            for offset in range(1, groups):
                value = value + entry_in[offset - 1].astype(single)
            total[entry_rows(me, place.z), :] = value.astype(bfloat)
            for offset in range(1, groups):
                entry_back(offset).start()
        elif stage == 2:
            if groups > 1:
                slot = total.at[pl.ds(entry_base, (groups - 1) * fourth), :]
                gone(slot, e_send.at[1])
                take(slot, e_recv.at[1])
            entry_plane(me, 2, 0).start()
            entry_plane(me, 4, 1).start()
            entry_plane(me, 1, 2, 4).start()
        elif stage == 3:
            take(entry_shares(1), e_recv.at[2])
            for owner in (me, place.peer(2)):
                entry_plane(owner, 4, 0, 3).start()
            for owner in (me, place.peer(4)):
                entry_plane(owner, 2, 1, 3).start()
        elif stage == 4:
            take(entry_shares(2), e_recv.at[3])
            for k in (2, 4, 6):
                entry_plane(place.peer(k), 1, 2, 4).start()
        else:
            take(entry_shares(4), e_recv.at[4])
            gone(entry_shares(7), e_send.at[2])

    bias_store = pltpu.make_async_copy(bias_rows, bias_hbm, store_sem.at[3])

    def bias_column(offset):
        return remote(
            bias_own,
            bias_in.at[offset - 1],
            b_send.at[0],
            b_recv.at[0],
            place.in_column(offset),
        )

    def bias_plane(k, owner):
        slot = bias_all.at[owner]
        return remote(slot, slot, b_send.at[1], b_recv.at[1], place.in_plane(k))

    def bias_step(stage):
        if stage == 0:
            ones = jnp.ones((8, length), bfloat)
            sums = jnp.zeros((8, head_share), single)
            for s in range(seqs):
                sums = sums + dot(ones, dqkv[s], 1, 1)
            bias_own[...] = jnp.concatenate([sums[:, 0:HEAD], sums[:, 2 * HEAD :]], axis=1)
            for offset in range(1, groups):
                bias_column(offset).start()
        elif stage == 1:
            if groups > 1:
                gone(bias_in, b_send.at[0])
                take(bias_in, b_recv.at[0])
            terms = [bias_in[offset - 1] for offset in range(1, groups)]
            bias_all[me] = in_place_order(bias_own[...], terms)
            for k in range(1, 8):
                bias_plane(k, me).start()
        else:
            gone(bias_all.at[0:others], b_send.at[1])
            take(bias_all.at[0:others], b_recv.at[1])
            for at, start in ((0, 0), (1, HEAD)):
                bias_rows[at : at + 1, :] = jnp.concatenate(
                    [bias_all[p, 0:1, start : start + HEAD] for p in range(HEADS)], axis=1
                )
            bias_store.start()


    def input_step():
        take(gpacked_t.at[:, 0 : others * HEAD, :], p_recv)
        grad_in = grad_resid[...]
        for j in range(3):
            grad_in = grad_in + dot(gpacked_t[j], we[:, j * width : (j + 1) * width], 0, 1)
        for s in range(seqs):
            dx_ref[s] = grad_in[s * tokens : (s + 1) * tokens].astype(bfloat)
            store(1, s).start()

    for kind, *what in plan["tail"]:
        if kind == "unit":
            step(*what)
        elif kind == "entry":
            entry_step(*what)
        elif kind == "bias":
            bias_step(*what)
        elif kind == "small":
            small_step(*what)
        else:
            input_step()
    small_store.wait()
    bias_store.wait()
    pltpu.make_async_copy(out_ref, out_hbm, store_sem.at[0]).wait()
    pltpu.make_async_copy(dx_ref, dx_hbm, store_sem.at[1]).wait()
    gone(xall.at[:, 0 : others * tokens, :], x_send)
    gone(ids_all.at[:, 0 : others * tokens], i_send)
    gone(out_low.at[:, :, 0 : others * tokens], o_send)
    gone(gatt_t.at[0 : others * HEAD, :], d_send)
    gone(dqkv.at[:, :, 0 : others * tokens], p_send)


def widen_kernel(sums, small_hbm, bias_hbm, out_in, dx_in, *refs):
    outs, vectors, scratch = refs[:15], refs[15:23], refs[23:]
    small, bias, passed, inner_bias, outer_v, inner_v, out_v, entry_v = scratch[:8]
    in_sem, out_sem = scratch[8:]
    out_ref, dx_ref, entry, query_b, value_b, out_w, out_b = outs[:7]
    gain1, shift1, inner_w, inner_b, outer_w, outer_b, gain2, shift2 = outs[7:]
    width = WIDE
    ff = outer_w.shape[0]
    pieces = (2 * ff + width) // WIDE
    head_share = 3 * HEAD
    reads = []
    writes = []

    def read(src, dst):
        reads.append(pltpu.make_async_copy(src, dst, in_sem.at[len(reads)]))
        reads[-1].start()

    def write(src, dst):
        writes.append(pltpu.make_async_copy(src, dst, out_sem.at[len(writes)]))
        writes[-1].start()

    read(small_hbm, small)
    read(bias_hbm, bias)
    read(out_in, passed.at[0])
    read(dx_in, passed.at[1])
    for i in range(pieces):
        rows = slice(i * WIDE, (i + 1) * WIDE)
        value = sums[rows, :].astype(single)
        j = i - ff // WIDE
        if j < 0:
            outer_v[rows, :] = value
            write(outer_v.at[rows], outer_w.at[rows])
        elif j < ff // WIDE:
            columns = slice(j * WIDE, (j + 1) * WIDE)
            inner_v[:, columns] = value
            write(inner_v.at[:, columns], inner_w.at[:, columns])
        else:
            out_v[...] = value
            write(out_v, out_w)
    for j in range(3):
        columns = slice(j * width, (j + 1) * width)
        starts = [2 * ff + width + h * head_share + j * HEAD for h in range(HEADS)]
        value = jnp.concatenate([sums[at : at + HEAD, :] for at in starts], axis=0)
        entry_v[:, columns] = value.astype(single).T
        write(entry_v.at[:, columns], entry.at[:, columns])
    for read_done in reads:
        read_done.wait()
    write(passed.at[0], out_ref)
    write(passed.at[1], dx_ref)

    def small_row(at):
        return (bias if at < 2 else small)[at : at + 1, :].reshape(width)

    for j, (ref, at) in enumerate(
        (
            (query_b, 0),
            (value_b, 1),
            (out_b, 2),
            (gain1, 3),
            (shift1, 4),
            (outer_b, 9),
            (gain2, 10),
            (shift2, 11),
        )
    ):
        vectors[j][...] = small_row(at)
        write(vectors[j], ref)
    for j in range(ff // WIDE):
        inner_bias[j * WIDE : (j + 1) * WIDE] = small_row(5 + j)
    write(inner_bias, inner_b)
    for copy in writes:
        copy.wait()


UNITS = (
    (0, 512, "xyz"),
    (512, 512, "yuvx"),
    (1024, 512, "zyx"),
    (1536, 512, "uyxv"),
    (2048, 512, "xyuv"),
    (2560, 512, "yuxv"),
    (3072, 512, "xyz"),
    (3584, 512, "xyz"),
    (4096, 512, "zyx"),
)
PLAN = {
    "early": (
        (1, "unit", 1, 0),
        (1, "unit", 0, 0),
        (3, "small", 0),
        (3, "unit", 3, 0),
        (3, "unit", 2, 0),
        (4, "small", 1),
        (6, "unit", 0, 1),
        (6, "unit", 4, 0),
        (6, "unit", 5, 0),
        (6, "unit", 1, 1),
    ),
    "attention": (
        (0, "unit", 7, 0),
        (0, "unit", 8, 0),
        (0, "unit", 6, 0),
        (1, "unit", 0, 2),
        (1, "unit", 3, 1),
        (1, "small", 2),
        (3, "unit", 4, 1),
        (3, "unit", 5, 1),
        (3, "unit", 2, 1),
        (4, "unit", 7, 1),
        (4, "unit", 1, 2),
    ),
    "tail": (
        ("entry", 0),
        ("bias", 0),
        ("unit", 6, 1),
        ("unit", 3, 2),
        ("small", 3),
        ("unit", 8, 1),
        ("unit", 0, 3),
        ("unit", 5, 2),
        ("unit", 1, 3),
        ("unit", 4, 2),
        ("unit", 2, 2),
        ("entry", 1),
        ("bias", 1),
        ("unit", 7, 2),
        ("small", 4),
        ("unit", 4, 3),
        ("unit", 0, 4),
        ("unit", 3, 3),
        ("input",),
        ("unit", 1, 4),
        ("unit", 5, 3),
        ("unit", 8, 2),
        ("unit", 2, 3),
        ("unit", 6, 2),
        ("entry", 2),
        ("bias", 2),
        ("unit", 0, 5),
        ("unit", 7, 3),
        ("unit", 4, 4),
        ("unit", 1, 5),
        ("unit", 3, 4),
        ("unit", 8, 3),
        ("unit", 2, 4),
        ("unit", 5, 4),
        ("unit", 6, 3),
        ("entry", 3),
        ("unit", 2, 5),
        ("unit", 7, 4),
        ("unit", 4, 5),
        ("unit", 0, 6),
        ("unit", 1, 6),
        ("unit", 8, 4),
        ("unit", 3, 5),
        ("unit", 0, 7),
        ("unit", 5, 5),
        ("unit", 6, 4),
        ("entry", 4),
        ("unit", 3, 6),
        ("unit", 7, 5),
        ("unit", 5, 6),
        ("unit", 4, 6),
        ("unit", 8, 5),
        ("entry", 5),
        ("unit", 1, 7),
        ("unit", 6, 5),
        ("unit", 2, 6),
        ("unit", 3, 7),
        ("unit", 5, 7),
        ("unit", 2, 7),
        ("unit", 4, 7),
        ("unit", 7, 6),
        ("unit", 7, 7),
        ("unit", 1, 8),
        ("unit", 6, 6),
        ("unit", 1, 9),
        ("unit", 6, 7),
        ("unit", 8, 6),
        ("unit", 5, 8),
        ("unit", 4, 8),
        ("unit", 8, 7),
        ("unit", 3, 8),
        ("unit", 5, 9),
        ("unit", 4, 9),
        ("unit", 3, 9),
    ),
}


def by_heads(groups):
    def run(inputs, blocks, we, qb, vb, wo, bo, g1, s1, w1, b1, w2, b2, g2, s2, cot):
        seqs, tokens, width = inputs.shape
        ff = w1.shape[1]
        rows = seqs * tokens
        length = tokens * HEADS
        grad_rows = 2 * ff + width
        units = UNITS
        others = max(groups - 1, 1)
        head_share = 3 * HEAD
        smem = pl.BlockSpec(memory_space=pltpu.SMEM)
        vmem = pl.BlockSpec(memory_space=pltpu.VMEM)
        hbm = pl.BlockSpec(memory_space=pl.ANY)
        dma = pltpu.SemaphoreType.DMA

        def shape(*dims):
            return jax.ShapeDtypeStruct(dims, single)

        out, dx, total, small, bias = pl.pallas_call(
            partial(layer_kernel, groups, units, PLAN),
            out_shape=[
                jax.ShapeDtypeStruct(inputs.shape, bfloat),
                jax.ShapeDtypeStruct(inputs.shape, bfloat),
                pltpu.VMEM((grad_rows + HEADS * head_share, width), bfloat),
                shape(16, width),
                shape(8, width),
            ],
            in_specs=[hbm, smem] + [hbm] * 14,
            out_specs=[hbm, hbm, vmem, hbm, hbm],
            scratch_shapes=[
                pltpu.VMEM(inputs.shape, bfloat),
                pltpu.VMEM(qb.shape, bfloat),
                pltpu.VMEM(vb.shape, bfloat),
                pltpu.VMEM(bo.shape, bfloat),
                pltpu.VMEM(g1.shape, bfloat),
                pltpu.VMEM(s1.shape, bfloat),
                pltpu.VMEM(b1.shape, bfloat),
                pltpu.VMEM(b2.shape, bfloat),
                pltpu.VMEM(g2.shape, bfloat),
                pltpu.VMEM(s2.shape, bfloat),
                pltpu.VMEM(inputs.shape, bfloat),
                pltpu.VMEM(inputs.shape, bfloat),
                pltpu.VMEM((16, width), single),
                pltpu.VMEM(we.shape, bfloat),
                pltpu.VMEM(wo.shape, bfloat),
                pltpu.VMEM(w1.shape, bfloat),
                pltpu.VMEM(w2.shape, bfloat),
                pltpu.VMEM(cot.shape, bfloat),
                dma((15,)),
                pltpu.VMEM((head_share, width), bfloat),
                pltpu.VMEM((seqs, length, width), bfloat),
                pltpu.VMEM((HEADS, 16, tokens), bfloat),
                pltpu.VMEM((16, length), bfloat),
                pltpu.VMEM((seqs, 8, length), single),
                pltpu.VMEM((seqs, head_share, length), bfloat),
                pltpu.VMEM((seqs, length, HEAD), bfloat),
                pltpu.VMEM((seqs, length, HEAD), bfloat),
                pltpu.VMEM((seqs, length, length), bfloat),
                pltpu.VMEM((seqs, 1, length), single),
                pltpu.VMEM((seqs, HEAD, length), single),
                pltpu.VMEM((seqs, HEAD, length), bfloat),
                pltpu.VMEM((width, rows), bfloat),
                pltpu.VMEM((rows, width), single),
                pltpu.VMEM((rows, 1), single),
                pltpu.VMEM((rows, width), bfloat),
                pltpu.VMEM((rows, ff), bfloat),
                pltpu.VMEM((rows, ff), single),
                pltpu.VMEM((rows, ff), bfloat),
                pltpu.VMEM((rows, width), bfloat),
                pltpu.VMEM((rows, width), single),
                pltpu.VMEM((rows, width), bfloat),
                pltpu.VMEM((width, rows), bfloat),
                pltpu.VMEM((seqs, HEAD, length), bfloat),
                pltpu.VMEM((seqs, head_share, length), bfloat),
                pltpu.VMEM((HEAD, length), single),
                pltpu.VMEM((HEAD, length), single),
                pltpu.VMEM((3, width, rows), bfloat),
                pltpu.VMEM((head_share, width), single),
                pltpu.VMEM((head_share, width), bfloat),
                pltpu.VMEM((others, head_share // groups, width), bfloat),
                pltpu.VMEM((grad_rows, width), bfloat),
                pltpu.VMEM((grad_rows, width), bfloat),
                pltpu.VMEM((3 + groups, 16, width), single),
                pltpu.VMEM((8, 2 * HEAD), single),
                pltpu.VMEM((others, 8, 2 * HEAD), single),
                pltpu.VMEM((HEADS, 8, 2 * HEAD), single),
                pltpu.VMEM((8, width), single),
                dma(()),
                dma((seqs, 3)),
                dma(()),
                dma(()),
                dma(()),
                dma((seqs,)),
                dma(()),
                dma((seqs,)),
                dma(()),
                dma(()),
                dma((len(units),)),
                dma((len(units), 10)),
                dma((3,)),
                dma((5,)),
                dma(()),
                dma((4,)),
                dma((2,)),
                dma((2,)),
                dma((4,)),
            ],
            compiler_params=pltpu.CompilerParams(
                collective_id=0, has_side_effects=True, vmem_limit_bytes=LAYER_VMEM
            ),
            name="layer",
        )(
            inputs, blocks.transpose(0, 3, 2, 1), we, qb, vb, wo, bo, g1, s1, w1, b1, w2, b2,
            g2, s2, cot,
        )
        pieces = grad_rows // WIDE
        return pl.pallas_call(
            widen_kernel,
            in_specs=[vmem] + [hbm] * 4,
            out_specs=[hbm] * 15,
            out_shape=[
                jax.ShapeDtypeStruct(inputs.shape, bfloat),
                jax.ShapeDtypeStruct(inputs.shape, bfloat),
                shape(width, 3 * width),
                shape(width),
                shape(width),
                shape(width, width),
                shape(width),
                shape(width),
                shape(width),
                shape(width, ff),
                shape(ff),
                shape(ff, width),
                shape(width),
                shape(width),
                shape(width),
            ],
            scratch_shapes=[
                *[pltpu.VMEM((width,), single)] * 8,
                pltpu.VMEM((16, width), single),
                pltpu.VMEM((8, width), single),
                pltpu.VMEM((2, *inputs.shape), bfloat),
                pltpu.VMEM((ff,), single),
                pltpu.VMEM((ff, width), single),
                pltpu.VMEM((width, ff), single),
                pltpu.VMEM((width, width), single),
                pltpu.VMEM((width, 3 * width), single),
                dma((4,)),
                dma((pieces + 14,)),
            ],
            compiler_params=pltpu.CompilerParams(vmem_limit_bytes=WIDEN_VMEM),
            name="widen",
        )(pltpu.with_memory_space_constraint(total, pltpu.VMEM), small, bias, out, dx)

    return run


def solution(mesh):
    in_specs = (
        P("dp", "seq", None),
        P("dp", None, "seq", None),
        P(),
        P(),
        P(),
        P(),
        P(),
        P(),
        P(),
        P(),
        P(),
        P(),
        P(),
        P(),
        P(),
        P("dp", "seq", None),
    )
    out_specs = (
        P("dp", "seq", None),
        P("dp", "seq", None),
        P(),
        P(),
        P(),
        P(),
        P(),
        P(),
        P(),
        P(),
        P(),
        P(),
        P(),
        P(),
        P(),
    )
    heads_fit = mesh.shape["seq"] == HEADS
    plan = by_heads(mesh.shape["dp"]) if heads_fit else on_device
    return jax.shard_map(
        plan, mesh=mesh, in_specs=in_specs, out_specs=out_specs, check_vma=False
    )
```

```python
from functools import partial

import jax
import jax.numpy as jnp
from jax import lax
from jax.experimental import pallas as pl
from jax.experimental.pallas import tpu as pltpu
from jax.sharding import PartitionSpec as P

HEADS = 8
HEAD = 64
BLOCK = 64


HIGHEST = lax.Precision.HIGHEST
EPSILON = 1e-05
NEGATIVE = -1e30


def spread_2(value, axis, root):
    mine = lax.axis_index(axis) == root
    return lax.psum(jnp.where(mine, value, jnp.zeros_like(value)), axis)


def for_sending(value):

    def short(part):
        return part.astype(jnp.bfloat16) if part.dtype == jnp.float32 else part

    return jax.tree.map(short, value)


def extended(block, sides, width):
    for axis, dim in sides:
        count = lax.axis_size(axis)
        forward = [(i, i + 1) for i in range(count - 1)]
        backward = [(target, source) for source, target in forward]
        low = lax.ppermute(
            lax.slice_in_dim(block, block.shape[dim] - width, None, axis=dim), axis, forward
        )
        high = lax.ppermute(lax.slice_in_dim(block, 0, width, axis=dim), axis, backward)
        block = jnp.concatenate([low, block, high], axis=dim)
    return block


def combined_all(part, axis, combine):
    gathered = jax.tree.map(lambda a: lax.all_gather(a, axis), part)

    def take(source):
        return jax.tree.map(lambda a: lax.dynamic_index_in_dim(a, source, 0, False), gathered)

    return lax.fori_loop(
        1, lax.axis_size(axis), lambda source, state: combine(state, take(source)), take(0)
    )


def norm_apply(values, gain_vec, shift_vec):
    center = values - jnp.mean(values, axis=-1, keepdims=True)
    spread = jnp.mean(center * center, axis=-1, keepdims=True)
    return center * lax.rsqrt(spread + EPSILON) * gain_vec + shift_vec


def pair_blocks(row_data, head_count, block_rows):
    seq_count, length_here, full_width = row_data.shape
    head_width = full_width // (2 * head_count)
    shaped = row_data.reshape(
        seq_count, length_here // block_rows, block_rows, 2, head_count, head_width
    )
    return shaped.transpose(0, 4, 1, 2, 3, 5).reshape(
        seq_count, head_count, length_here // block_rows, block_rows, 2 * head_width
    )


def pair_tokens(blocked):
    seq_count, head_count, block_count, block_rows, double_width = blocked.shape
    head_width = double_width // 2
    shaped = blocked.reshape(seq_count, head_count, block_count, block_rows, 2, head_width)
    return shaped.transpose(0, 2, 3, 4, 1, 5).reshape(
        seq_count, block_count * block_rows, 2 * head_count * head_width
    )


def head_rows(row_data, head_count):
    seq_count, length_here, full_width = row_data.shape
    return row_data.reshape(seq_count, length_here, head_count, full_width // head_count).transpose(
        0, 2, 1, 3
    )


def row_heads(split_rows):
    seq_count, head_count, length_here, head_width = split_rows.shape
    return split_rows.transpose(0, 2, 1, 3).reshape(seq_count, length_here, head_count * head_width)


def merge_parts(earlier, later):
    peak_one, total_one, out_one = earlier
    peak_two, total_two, out_two = later
    row_peak = jnp.maximum(peak_one, peak_two)
    factor_one = jnp.exp(peak_one - row_peak)
    factor_two = jnp.exp(peak_two - row_peak)
    return (
        row_peak,
        total_one * factor_one + total_two * factor_two,
        out_one * factor_one[..., None] + out_two * factor_two[..., None],
    )


def share_rows(row_data, root_device):
    return spread_2(row_data, "seq", root_device)


def share_grads(grad_rows, grad_delta, root_device):
    return (
        spread_2(grad_rows.astype(jnp.bfloat16), "seq", root_device).astype(grad_rows.dtype),
        spread_2(for_sending(grad_delta), "seq", root_device).astype(grad_delta.dtype),
    )


def on_device(
    inputs,
    random_blocks,
    entry_weight,
    query_bias,
    value_bias,
    out_weight,
    out_bias,
    norm_gain,
    norm_shift,
    inner_weight,
    inner_bias,
    outer_weight,
    outer_bias,
    final_gain,
    final_shift,
    cotangent,
):
    seq_count, token_count, model_width = inputs.shape
    head_count = HEADS
    head_width = HEAD
    block_rows = BLOCK
    per_dev = token_count // block_rows
    devices = lax.axis_size("seq")
    device = lax.axis_index("seq")
    block_total = devices * per_dev
    request_total = seq_count * head_count * per_dev * 3
    capacity = (request_total + devices - 2) // (devices - 1)
    table_rows = seq_count * head_count * per_dev
    query_scale = head_width ** (-0.5)
    is_first = device == 0
    is_last = device == devices - 1
    bfloat = jnp.bfloat16
    single = jnp.float32
    flat_in = inputs.reshape(-1, model_width)
    entry_out = jnp.dot(flat_in, entry_weight, preferred_element_type=single)
    packed = jnp.concatenate(
        [
            (entry_out[:, :model_width] + query_bias) * query_scale,
            entry_out[:, model_width : 2 * model_width],
            entry_out[:, 2 * model_width :] + value_bias,
        ],
        axis=1,
    )
    packed = packed.astype(bfloat).reshape(seq_count, token_count, 3 * model_width)
    key_value = packed[:, :, model_width:]
    padded = extended(key_value, (("seq", 1),), block_rows)
    global_rows = jnp.concatenate(
        [
            share_rows(packed[:, :block_rows], 0),
            share_rows(packed[:, token_count - block_rows :], devices - 1),
        ],
        axis=1,
    )
    owners = (random_blocks // per_dev).reshape(-1)
    within = random_blocks % per_dev
    seq_index = lax.broadcasted_iota(jnp.int32, random_blocks.shape, 0)
    head_index = lax.broadcasted_iota(jnp.int32, random_blocks.shape, 1)
    request_codes = ((seq_index * head_count + head_index) * per_dev + within).reshape(-1)
    onehot = (owners[:, None] == jnp.arange(devices, dtype=jnp.int32)[None, :]).astype(jnp.int32)
    slot_index = jnp.sum((jnp.cumsum(onehot, axis=0) - onehot) * onehot, axis=1)
    slot_place = owners * capacity + slot_index
    requests = (
        jnp.full((devices * capacity,), -1, jnp.int32)
        .at[slot_place]
        .set(request_codes)
        .reshape(devices, capacity)
    )
    incoming = lax.all_to_all(requests, "seq", split_axis=0, concat_axis=0, tiled=True)
    head_table = pair_blocks(key_value, head_count, block_rows).reshape(
        table_rows, block_rows, 2 * head_width
    )
    served = head_table[jnp.maximum(incoming, 0)]
    served = jnp.where((incoming >= 0)[:, :, None, None], served, jnp.zeros((), bfloat))
    fetched = lax.all_to_all(served, "seq", split_axis=0, concat_axis=0, tiled=True)
    random_kv = fetched.reshape(devices * capacity, block_rows, 2 * head_width)[slot_place]
    random_kv = random_kv.reshape(seq_count, head_count, per_dev, 3, block_rows, 2 * head_width)
    window_view = pair_blocks(padded, head_count, block_rows)
    window_kv = jnp.stack(
        [window_view[:, :, :per_dev], window_view[:, :, 1 : per_dev + 1], window_view[:, :, 2:]],
        axis=3,
    )
    global_kv = pair_blocks(global_rows[:, :, model_width:], head_count, block_rows)
    global_kv = jnp.broadcast_to(
        global_kv[:, :, None], (seq_count, head_count, per_dev, 2, block_rows, 2 * head_width)
    )
    all_kv = jnp.concatenate([window_kv, global_kv, random_kv], axis=3).reshape(
        seq_count, head_count, per_dev, 8 * block_rows, 2 * head_width
    )
    key_part = all_kv[..., :head_width]
    value_part = all_kv[..., head_width:]
    query_view = head_rows(packed[:, :, :model_width], head_count).reshape(
        seq_count, head_count, per_dev, block_rows, head_width
    )
    block_ids = device * per_dev + jnp.arange(per_dev)[:, None]
    column = jnp.arange(8 * block_rows)[None, :]
    neighbor = block_ids + column // block_rows - 1
    key_keep = (column >= 3 * block_rows) | (neighbor >= 1) & (neighbor <= block_total - 2)
    key_keep = key_keep[None, None, :, None, :]

    def block_scores():
        raw_scores = jnp.einsum(
            "shiqd,shikd->shiqk", query_view, key_part, preferred_element_type=single
        )
        return jnp.where(key_keep, raw_scores, NEGATIVE)

    scores = block_scores()
    row_peak = jnp.max(scores, axis=-1, keepdims=True)
    exponent = jnp.exp(scores - row_peak)
    row_total = jnp.sum(exponent, axis=-1, keepdims=True)
    probability = exponent / row_total
    log_total = row_peak + jnp.log(row_total)
    prob_low = probability.astype(bfloat)
    window_out = jnp.einsum(
        "shiqk,shikd->shiqd", prob_low, value_part, preferred_element_type=single
    )
    global_query = head_rows(global_rows[:, :, :model_width], head_count)
    local_keys = head_rows(packed[:, :, model_width : 2 * model_width], head_count)
    local_values = head_rows(packed[:, :, 2 * model_width :], head_count)
    global_scores = jnp.einsum(
        "shqd,shkd->shqk", global_query, local_keys, preferred_element_type=single
    )
    global_peak = jnp.max(global_scores, axis=-1)
    global_exp = jnp.exp(global_scores - global_peak[..., None])
    global_total = jnp.sum(global_exp, axis=-1)
    global_sum = jnp.einsum(
        "shqk,shkd->shqd", global_exp, local_values.astype(single), precision=HIGHEST
    )
    global_peak, global_total, global_sum = combined_all(
        (global_peak, global_total, global_sum), "seq", merge_parts
    )
    global_out = global_sum / global_total[..., None]
    global_log = global_peak + jnp.log(global_total)
    block_pos = jnp.arange(per_dev)
    take_first = ((block_pos == 0) & is_first)[None, None, :, None, None]
    take_last = ((block_pos == per_dev - 1) & is_last)[None, None, :, None, None]
    combined = jnp.where(take_first, global_out[:, :, None, :block_rows], window_out)
    combined = jnp.where(take_last, global_out[:, :, None, block_rows:], combined)
    attended = (
        row_heads(combined.reshape(seq_count, head_count, token_count, head_width))
        .reshape(-1, model_width)
        .astype(bfloat)
    )
    branch = jnp.dot(attended, out_weight, preferred_element_type=single) + out_bias
    residual_in = flat_in.astype(single) + branch
    first_norm, first_pull = jax.vjp(
        norm_apply, residual_in, norm_gain.astype(single), norm_shift.astype(single)
    )
    first_low = first_norm.astype(bfloat)
    inner_pre = jnp.dot(first_low, inner_weight, preferred_element_type=single) + inner_bias
    activated, gelu_pull = jax.vjp(partial(jax.nn.gelu, approximate=False), inner_pre)
    hidden = activated.astype(bfloat)
    second = first_norm + (
        jnp.dot(hidden, outer_weight, preferred_element_type=single) + outer_bias
    )
    final_norm, final_pull = jax.vjp(
        norm_apply, second, final_gain.astype(single), final_shift.astype(single)
    )
    layer_out = final_norm.astype(bfloat).reshape(inputs.shape)
    grad_second, final_gain_grad, final_shift_grad = final_pull(
        cotangent.reshape(-1, model_width).astype(single)
    )
    grad_outer = grad_second.astype(bfloat)
    outer_weight_grad = jnp.dot(hidden.T, grad_outer, preferred_element_type=single)
    outer_bias_grad = jnp.sum(grad_outer.astype(single), axis=0)
    (grad_active,) = gelu_pull(jnp.dot(grad_outer, outer_weight.T, preferred_element_type=single))
    grad_inner = grad_active.astype(bfloat)
    inner_weight_grad = jnp.dot(first_low.T, grad_inner, preferred_element_type=single)
    inner_bias_grad = jnp.sum(grad_inner.astype(single), axis=0)
    grad_first = grad_second + jnp.dot(grad_inner, inner_weight.T, preferred_element_type=single)
    grad_resid, norm_gain_grad, norm_shift_grad = first_pull(grad_first)
    grad_branch = grad_resid.astype(bfloat)
    out_weight_grad = jnp.dot(attended.T, grad_branch, preferred_element_type=single)
    out_bias_grad = jnp.sum(grad_branch.astype(single), axis=0)
    grad_attended = jnp.dot(grad_branch, out_weight.T, preferred_element_type=single).astype(bfloat)
    grad_heads = head_rows(
        grad_attended.reshape(seq_count, token_count, model_width), head_count
    ).reshape(seq_count, head_count, per_dev, block_rows, head_width)
    grad_window = jnp.where(take_first | take_last, jnp.zeros((), bfloat), grad_heads)
    probability = jnp.exp(block_scores() - log_total)
    prob_low = probability.astype(bfloat)
    grad_prob = jnp.einsum(
        "shiqd,shikd->shiqk", grad_window, value_part, preferred_element_type=single
    )
    row_delta = jnp.sum(probability * grad_prob, axis=-1, keepdims=True)
    grad_scores = (probability * (grad_prob - row_delta)).astype(bfloat)
    grad_query_block = jnp.einsum(
        "shiqk,shikd->shiqd", grad_scores, key_part, preferred_element_type=single
    )
    grad_key_block = jnp.einsum(
        "shiqk,shiqd->shikd", grad_scores, query_view, preferred_element_type=single
    )
    grad_value_block = jnp.einsum(
        "shiqk,shiqd->shikd", prob_low, grad_window, preferred_element_type=single
    )
    grad_kv = jnp.concatenate([grad_key_block, grad_value_block], axis=-1).reshape(
        seq_count, head_count, per_dev, 8, block_rows, 2 * head_width
    )
    pad_none = ((0, 0), (0, 0))
    grad_pad = (
        jnp.pad(grad_kv[:, :, :, 0], pad_none + ((0, 2), (0, 0), (0, 0)))
        + jnp.pad(grad_kv[:, :, :, 1], pad_none + ((1, 1), (0, 0), (0, 0)))
        + jnp.pad(grad_kv[:, :, :, 2], pad_none + ((2, 0), (0, 0), (0, 0)))
    )
    grad_tokens = pair_tokens(grad_pad)
    edge_grads = jnp.concatenate(
        [grad_tokens[:, :block_rows], grad_tokens[:, token_count + block_rows :]], axis=1
    )
    returned = extended(edge_grads.astype(jnp.bfloat16), (("seq", 1),), block_rows).astype(
        edge_grads.dtype
    )
    gap = token_count - block_rows
    grad_kv_local = (
        grad_tokens[:, block_rows : block_rows + token_count]
        + jnp.pad(returned[:, :block_rows], ((0, 0), (0, gap), (0, 0)))
        + jnp.pad(returned[:, 3 * block_rows :], ((0, 0), (gap, 0), (0, 0)))
    )
    grad_global_kv = pair_tokens(jnp.sum(grad_kv[:, :, :, 3:5], axis=2))
    grad_random = grad_kv[:, :, :, 5:8].reshape(request_total, block_rows, 2 * head_width)
    outgoing = (
        jnp.zeros((devices * capacity, block_rows, 2 * head_width), single)
        .at[slot_place]
        .set(grad_random)
    )
    outgoing = outgoing.reshape(devices, capacity, block_rows, 2 * head_width)
    returned_random = lax.all_to_all(
        outgoing.astype(jnp.bfloat16), "seq", split_axis=0, concat_axis=0, tiled=True
    ).astype(outgoing.dtype)
    segment_ids = jnp.where(incoming >= 0, incoming, table_rows).reshape(-1)
    grad_table = jax.ops.segment_sum(
        returned_random.reshape(devices * capacity, block_rows, 2 * head_width),
        segment_ids,
        num_segments=table_rows + 1,
    )[:table_rows]
    grad_owned = pair_tokens(
        grad_table.reshape(seq_count, head_count, per_dev, block_rows, 2 * head_width)
    )
    first_cot = grad_heads[:, :, 0].astype(single)
    last_cot = grad_heads[:, :, per_dev - 1].astype(single)
    first_cot, first_delta = share_grads(
        first_cot, jnp.sum(first_cot * global_out[:, :, :block_rows], axis=-1), 0
    )
    last_cot, last_delta = share_grads(
        last_cot, jnp.sum(last_cot * global_out[:, :, block_rows:], axis=-1), devices - 1
    )
    global_cot = jnp.concatenate([first_cot, last_cot], axis=2)
    global_delta = jnp.concatenate([first_delta, last_delta], axis=2)
    global_prob = jnp.exp(
        jnp.einsum("shqd,shkd->shqk", global_query, local_keys, preferred_element_type=single)
        - global_log[..., None]
    )
    global_dprob = jnp.einsum(
        "shqd,shkd->shqk", global_cot.astype(bfloat), local_values, preferred_element_type=single
    )
    global_grads = (global_prob * (global_dprob - global_delta[..., None])).astype(bfloat)
    grad_global_query = jnp.einsum(
        "shqk,shkd->shqd", global_grads, local_keys, preferred_element_type=single
    )
    grad_local_key = jnp.einsum(
        "shqk,shqd->shkd", global_grads, global_query, preferred_element_type=single
    )
    grad_local_value = jnp.einsum("shqk,shqd->shkd", global_prob, global_cot, precision=HIGHEST)
    partials = jnp.concatenate([row_heads(grad_global_query), grad_global_kv], axis=-1)
    partials = lax.psum(partials.astype(jnp.bfloat16), "seq").astype(jnp.float32)
    owner_part = jnp.where(
        is_first, jnp.pad(partials[:, :block_rows], ((0, 0), (0, gap), (0, 0))), 0.0
    ) + jnp.where(is_last, jnp.pad(partials[:, block_rows:], ((0, 0), (gap, 0), (0, 0))), 0.0)
    grad_query_tokens = row_heads(
        grad_query_block.reshape(seq_count, head_count, token_count, head_width)
    )
    grad_kv_tokens = (
        grad_kv_local
        + grad_owned
        + jnp.concatenate([row_heads(grad_local_key), row_heads(grad_local_value)], axis=-1)
    )
    grad_packed = (
        jnp.concatenate([grad_query_tokens, grad_kv_tokens], axis=-1) + owner_part
    ).astype(bfloat)
    column_scale = jnp.concatenate(
        [jnp.full((model_width,), query_scale, single), jnp.ones((2 * model_width,), single)]
    )
    grad_entry = (
        (grad_packed.astype(single) * column_scale).astype(bfloat).reshape(-1, 3 * model_width)
    )
    entry_weight_grad = jnp.dot(flat_in.T, grad_entry, preferred_element_type=single)
    query_bias_grad = jnp.sum(grad_entry[:, :model_width].astype(single), axis=0)
    value_bias_grad = jnp.sum(grad_entry[:, 2 * model_width :].astype(single), axis=0)
    input_grad = (
        (grad_resid + jnp.dot(grad_entry, entry_weight.T, preferred_element_type=single))
        .astype(bfloat)
        .reshape(inputs.shape)
    )
    (
        total_entry,
        total_query,
        total_value,
        total_out,
        total_out_bias,
        total_norm_gain,
        total_norm_shift,
        total_inner,
        total_inner_bias,
        total_outer,
        total_outer_bias,
        total_final_gain,
        total_final_shift,
    ) = lax.psum(
        (
            entry_weight_grad,
            query_bias_grad,
            value_bias_grad,
            out_weight_grad,
            out_bias_grad,
            norm_gain_grad,
            norm_shift_grad,
            inner_weight_grad,
            inner_bias_grad,
            outer_weight_grad,
            outer_bias_grad,
            final_gain_grad,
            final_shift_grad,
        ),
        ("dp", "seq"),
    )
    return (
        layer_out,
        input_grad,
        total_entry,
        total_query,
        total_value,
        total_out,
        total_out_bias,
        total_norm_gain,
        total_norm_shift,
        total_inner,
        total_inner_bias,
        total_outer,
        total_outer_bias,
        total_final_gain,
        total_final_shift,
    )


MESH = pl.DeviceIdType.MESH
bfloat = jnp.bfloat16
single = jnp.float32
WIDE = 512
QUERIES = 1024
BACK_QUERIES = 512
FORWARD = ((0, 2), (2, 3))
EARLY = (
    ("outer", 0),
    ("back", 0, 1),
    ("outer", 1024),
    ("back", 1, 3),
    ("inner", 0),
    ("inner", 1024),
    ("out",),
)
TILES = 1024
LAYER_VMEM = 56 * 2**20
WIDEN_VMEM = 56 * 2**20
INV_SQRT2 = 0.7071067811865476
INV_SQRT_2PI = 0.3989422804014327


def dot(a, b, a_dim, b_dim):
    return lax.dot_general(
        a, b, (((a_dim,), (b_dim,)), ((), ())), preferred_element_type=single
    )


def aligned(index, step):
    return pl.multiple_of(index, step)


class Place:
    def __init__(self, groups):
        self.groups = groups
        self.z = lax.axis_index("dp")
        self.me = lax.axis_index("seq")
        self.y = self.me // 4
        self.x = (self.me // 2) % 2
        self.core = self.me % 2

    def peer(self, offset):
        off_y, off_x, off_core = offset // 4, (offset // 2) % 2, offset % 2
        return (
            ((self.y + off_y) % 2) * 4
            + ((self.x + off_x) % 2) * 2
            + (self.core + off_core) % 2
        )

    def in_plane(self, offset):
        return (self.z, self.peer(offset))

    def in_column(self, offset):
        return ((self.z + offset) % self.groups, self.me)


def remote(src, dst, send, recv, device):
    return pltpu.make_async_remote_copy(
        src_ref=src,
        dst_ref=dst,
        send_sem=send,
        recv_sem=recv,
        device_id=device,
        device_id_type=MESH,
    )


def layer_kernel(
    groups,
    units,
    plan,
    x_hbm,
    blocks_hbm,
    we_hbm,
    qb_hbm,
    vb_hbm,
    wo_hbm,
    bo_hbm,
    g1_hbm,
    s1_hbm,
    w1_hbm,
    b1_hbm,
    w2_hbm,
    b2_hbm,
    g2_hbm,
    s2_hbm,
    cot_hbm,
    out_hbm,
    dx_hbm,
    total,
    small_hbm,
    bias_hbm,
    blocks_ref,
    x_ref,
    qb_ref,
    vb_ref,
    bo_ref,
    g1_ref,
    s1_ref,
    b1_ref,
    b2_ref,
    g2_ref,
    s2_ref,
    out_ref,
    dx_ref,
    small_ref,
    we,
    wo,
    w1,
    w2,
    cot,
    load_sem,
    wh_t,
    xall,
    ids_send,
    ids_all,
    ids,
    qkv,
    krow,
    vrow,
    probs,
    inv_total,
    out_wide,
    out_low,
    att_t,
    hat1,
    rstd1,
    low1,
    hidden,
    slope,
    grad_inner,
    grad_outer,
    grad_resid,
    grad_branch,
    gatt_t,
    dout_t,
    dqkv,
    dk_acc,
    dv_acc,
    gpacked_t,
    entry_acc,
    entry_part,
    entry_in,
    part,
    landed,
    small_in,
    bias_own,
    bias_in,
    bias_all,
    bias_rows,
    x_send,
    x_recv,
    i_send,
    i_recv,
    o_send,
    o_recv,
    d_send,
    d_recv,
    p_send,
    p_recv,
    rs_send,
    rs_recv,
    e_send,
    e_recv,
    v_send,
    v_recv,
    b_send,
    b_recv,
    store_sem,
    second_round,
    third_round,
):
    seqs, tokens, width = x_ref.shape
    place = Place(groups)
    me = place.me
    barrier = pltpu.get_barrier_semaphore()
    neighbours = 3 + (place.z > 0).astype(jnp.int32) + (place.z < groups - 1).astype(jnp.int32)

    def greet(sem):
        for k in (1, 2, 4):
            pl.semaphore_signal(sem, inc=1, device_id=place.in_plane(k), device_id_type=MESH)

        @pl.when(place.z > 0)
        def _():
            pl.semaphore_signal(sem, inc=1, device_id=(place.z - 1, me), device_id_type=MESH)

        @pl.when(place.z < groups - 1)
        def _():
            pl.semaphore_signal(sem, inc=1, device_id=(place.z + 1, me), device_id_type=MESH)

    greet(barrier)

    def load(*pairs):
        copies = []
        for src, dst in pairs:
            copies.append(pltpu.make_async_copy(src, dst, load_sem.at[len(loads)]))
            copies[-1].start()
            loads.append(copies[-1])
        return copies

    loads = []
    load_x = load((x_hbm, x_ref))
    load_blocks = load((blocks_hbm, blocks_ref))
    def lanes_of(device):
        return pl.ds(aligned(device * tokens, 128), tokens)

    def head_rows_of(device):
        return pl.ds(aligned(device * HEAD, HEAD), HEAD)

    def seq_lanes(s):
        return pl.ds(aligned(s * tokens, 128), tokens)

    def vec(ref):
        return ref[...].astype(single).reshape(1, ref.shape[0])

    others = HEADS - 1

    def take(ref, sem):
        remote(ref, ref, sem, sem, place.in_plane(1)).wait_recv()

    def gone(ref, sem):
        remote(ref, ref, sem, sem, place.in_plane(1)).wait_send()

    small_ref[...] = jnp.zeros(small_ref.shape, single)
    bias_rows[...] = jnp.zeros(bias_rows.shape, single)
    bias_own[...] = jnp.zeros(bias_own.shape, single)
    entry_acc[...] = jnp.zeros(entry_acc.shape, single)

    load_x[0].wait()
    pl.semaphore_wait(barrier, neighbours)
    greet(second_round)

    half_width = width // 2

    def x_copy(s, k):
        return remote(
            x_ref.at[s],
            xall.at[s, lanes_of(me), :],
            x_send,
            x_recv.at[s, 2 if k == 1 else 0],
            place.in_plane(k),
        )

    def x_across(s, k):
        columns = slice(0, half_width) if k == 2 else slice(half_width, width)
        slab = xall.at[s, lanes_of(place.peer(6 - k)), columns]
        return remote(slab, slab, x_send, x_recv.at[s, 1], place.in_plane(k))

    def x_forward(s, k):
        slab = xall.at[s, lanes_of(place.peer(k)), :]
        return remote(slab, slab, x_send, x_recv.at[s, 2], place.in_plane(1))

    def x_arrived(s, which):
        slabs = (2, 1, 4)[which]
        take(xall.at[s, 0 : slabs * tokens, :], x_recv.at[s, which])

    def x_begin(s):
        for k in (2, 4, 1):
            x_copy(s, k).start()

    def x_pass(s):
        x_arrived(s, 0)
        for k in (2, 4):
            x_across(s, k).start()
            x_forward(s, k).start()

    def ids_copy(k):
        other = place.peer(k)
        return remote(
            ids_send.at[other],
            ids_all.at[:, lanes_of(me)],
            i_send,
            i_recv,
            place.in_plane(k),
        )

    x_begin(0)
    load_entry = load((we_hbm, we), (qb_hbm, qb_ref), (vb_hbm, vb_ref))
    x_begin(1)
    load_rest = load(
        (wo_hbm, wo),
        (bo_hbm, bo_ref),
        (g1_hbm, g1_ref),
        (s1_hbm, s1_ref),
        (w1_hbm, w1),
        (b1_hbm, b1_ref),
        (w2_hbm, w2),
        (b2_hbm, b2_ref),
        (g2_hbm, g2_ref),
        (s2_hbm, s2_ref),
        (cot_hbm, cot),
    )
    for s in range(seqs):
        xall[s, lanes_of(me), :] = x_ref[s]

    load_blocks[0].wait()

    lane = lax.broadcasted_iota(jnp.int32, (16, tokens), 1)
    row = lax.broadcasted_iota(jnp.int32, (16, tokens), 0)
    for h in range(HEADS):
        numbers = jnp.zeros((16, tokens), jnp.int32)
        for s in range(seqs):
            for j in range(3):
                picked = jnp.where(
                    lane < BLOCK, blocks_ref[s, j, 0, h], blocks_ref[s, j, 1, h]
                )
                numbers = jnp.where(row == s * 3 + j, picked, numbers)
        ids_send[h] = numbers.astype(single).astype(bfloat)
    pl.semaphore_wait(second_round, neighbours)
    greet(third_round)

    for copy in load_entry:
        copy.wait()
    pair = me // 2
    odd = me % 2
    for j in range(3):
        columns = we[:, pl.ds(aligned(j * width + pair * 2 * HEAD, 128), 2 * HEAD)].T
        wh_t[j * HEAD : (j + 1) * HEAD, :] = jnp.where(
            odd == 1, columns[HEAD:], columns[:HEAD]
        )
    spread = lax.broadcasted_iota(jnp.int32, (HEAD, width), 1) == me * HEAD + (
        lax.broadcasted_iota(jnp.int32, (HEAD, width), 0)
    )

    def column(ref):
        return jnp.sum(jnp.where(spread, vec(ref), 0.0), axis=1, keepdims=True)

    query_column = column(qb_ref)
    value_column = column(vb_ref)

    ids_all[:, lanes_of(me)] = ids_send[me]
    pl.semaphore_wait(third_round, neighbours)
    for k in range(1, 8):
        ids_copy(k).start()
    x_pass(0)
    for s in range(2, seqs):
        x_begin(s)
    x_pass(1)
    take(ids_all.at[:, 0 : others * tokens], i_recv)
    for s in range(seqs):
        ids[s, 0:3, :] = ids_all[...].astype(single)[3 * s : 3 * s + 3]

    length = qkv.shape[2]
    chunks = length // QUERIES
    blocks = length // BLOCK
    key_block = lax.broadcasted_iota(jnp.int32, (blocks, QUERIES), 0)
    query_lane = lax.broadcasted_iota(jnp.int32, (blocks, QUERIES), 1)

    def out_copy(s, k):
        return remote(
            out_low.at[s, :, lanes_of(place.peer(k))],
            att_t.at[head_rows_of(me), seq_lanes(s)],
            o_send,
            o_recv.at[s],
            place.in_plane(k),
        )

    def take_x(s):
        x_arrived(s, 1)
        x_forward(s, 6).start()

        @pl.when(s < seqs - 2)
        def _():
            x_pass(s + 2)

        x_arrived(s, 2)
        packed = dot(wh_t[...], xall[s], 1, 1)
        qkv[s, 0:HEAD, :] = ((packed[0:HEAD] + query_column) * HEAD**-0.5).astype(bfloat)
        qkv[s, HEAD : 2 * HEAD, :] = packed[HEAD : 2 * HEAD].astype(bfloat)
        qkv[s, 2 * HEAD : 3 * HEAD, :] = (packed[2 * HEAD :] + value_column).astype(bfloat)
        qkv[s, 3 * HEAD :, :] = jnp.ones((16, length), bfloat)

    def attend(s, _):
        take_x(s)
        krow[s] = qkv[s, HEAD : 2 * HEAD, :].T
        vrow[s] = qkv[s, 2 * HEAD : 3 * HEAD, :].T

        def chunk(i, _):
            at = pl.ds(aligned(i * QUERIES, QUERIES), QUERIES)
            query_block = (i * QUERIES + query_lane) // BLOCK
            inside = (key_block >= 1) & (key_block <= blocks - 2)
            near = (key_block >= query_block - 1) & (key_block <= query_block + 1) & inside
            times = jnp.where(near, 1.0, 0.0) + jnp.where(inside, 0.0, 1.0)
            for j in range(3):
                times = times + jnp.where(
                    ids[s, j : j + 1, at] == key_block.astype(single), 1.0, 0.0
                )
            bias = jnp.where(times > 1.5, 0.6931471805599453, 0.0)
            bias = jnp.where(times > 0.5, bias, NEGATIVE)
            bias = jnp.where((query_block == 0) | (query_block == blocks - 1), 0.0, bias)
            score = jnp.dot(krow[s], qkv[s, 0:HEAD, at], preferred_element_type=single)
            score = score.reshape(blocks, BLOCK, QUERIES) + bias[:, None, :]
            score = score.reshape(length, QUERIES)
            peak = jnp.max(score, axis=0, keepdims=True)
            grown = jnp.exp(score - peak)
            grown = grown.astype(bfloat)
            probs[s, :, at] = grown
            summed = jnp.dot(qkv[s, 2 * HEAD :, :], grown, preferred_element_type=single)
            inverse = 1.0 / summed[HEAD : HEAD + 1]
            inv_total[s, :, at] = inverse
            result = inverse * summed[0:HEAD]
            out_wide[s, :, at] = result
            out_low[s, :, at] = result.astype(bfloat)
            return 0

        lax.fori_loop(0, chunks, chunk, 0)
        for k in (6, 7, 2, 3, 4, 5, 1):
            out_copy(s, k).start()
        att_t[head_rows_of(me), seq_lanes(s)] = out_low[s, :, lanes_of(me)]
        return 0

    lax.fori_loop(0, seqs, attend, 0)
    for copy in load_rest:
        copy.wait()

    def dout_copy(s, k):
        return remote(
            gatt_t.at[head_rows_of(place.peer(k)), seq_lanes(s)],
            dout_t.at[s, :, lanes_of(me)],
            d_send,
            d_recv.at[s],
            place.in_plane(k),
        )

    def mean_of(value):
        return jnp.mean(value, axis=-1, keepdims=True)

    def add_small(row, value):
        small_ref[row : row + 1, :] += jnp.sum(value, axis=0, keepdims=True)

    ff = hidden.shape[1]

    def store(which, s):
        src, dst = ((out_ref, out_hbm), (dx_ref, dx_hbm))[which]
        return pltpu.make_async_copy(src.at[s], dst.at[s], store_sem.at[which])

    def forward(first_seq, last_seq):
        for s in range(first_seq, last_seq):
            take(att_t.at[0 : others * HEAD, seq_lanes(s)], o_recv.at[s])
        here = slice(first_seq * tokens, last_seq * tokens)
        count = (last_seq - first_seq) * tokens
        branch = dot(att_t[:, here], wo[...], 0, 0) + vec(bo_ref)
        resid = x_ref[first_seq:last_seq].reshape(count, width).astype(single) + branch
        center = resid - mean_of(resid)
        scale1 = lax.rsqrt(mean_of(center * center) + EPSILON)
        normed1 = center * scale1
        hat1[here, :] = normed1
        rstd1[here, :] = scale1
        first = normed1 * vec(g1_ref) + vec(s1_ref)
        first_low = first.astype(bfloat)
        low1[here, :] = first_low
        second = first + vec(b2_ref)
        bias1 = vec(b1_ref)
        for j in range(ff // WIDE):
            span = slice(j * WIDE, (j + 1) * WIDE)
            pre = jnp.dot(first_low, w1[:, span], preferred_element_type=single) + bias1[:, span]
            share = 0.5 * (1.0 + lax.erf(pre * INV_SQRT2))
            active = (pre * share).astype(bfloat)
            hidden[here, span] = active
            slope[here, span] = share + pre * jnp.exp(-0.5 * pre * pre) * INV_SQRT_2PI
            second = second + jnp.dot(active, w2[span, :], preferred_element_type=single)
        center = second - mean_of(second)
        scale2 = lax.rsqrt(mean_of(center * center) + EPSILON)
        normed2 = center * scale2
        result = (normed2 * vec(g2_ref) + vec(s2_ref)).astype(bfloat)
        out_ref[first_seq:last_seq] = result.reshape(last_seq - first_seq, tokens, width)
        for s in range(first_seq, last_seq):
            store(0, s).start()
        incoming = cot[first_seq:last_seq].reshape(count, width).astype(single)
        add_small(10, incoming * normed2)
        add_small(11, incoming)
        scaled = incoming * vec(g2_ref)
        grad_second = scale2 * (
            scaled - mean_of(scaled) - normed2 * mean_of(scaled * normed2)
        )
        grad_resid[here, :] = grad_second
        grad_low = grad_second.astype(bfloat)
        grad_outer[here, :] = grad_low
        add_small(9, grad_low.astype(single))

    def outer_early(start, rows):
        at = slice(start, start + TILES)
        keep_part(start, dot(hidden[0:rows, at], grad_outer[0:rows, :], 0, 0))

    def keep_part(base, value):
        part[base : base + value.shape[0], :] = value.astype(bfloat)

    forward(*FORWARD[0])
    rows_early = FORWARD[0][1] * tokens
    for start in range(0, ff, TILES):
        outer_early(start, rows_early)
    forward(*FORWARD[1])

    def stages_of(unit):
        base, count, order = units[unit]
        size = count // 2
        start = base + place.core * size
        stages = [("c", start, base + (1 - place.core) * size, size)]
        for axis in order:
            if axis == "z":
                size = size // groups
                stages.append((axis, start + place.z * size, start, size))
                start = start + place.z * size
            else:
                size = size // 2
                index = {"x": place.x, "y": place.y, "u": place.z % 2, "v": place.z // 2}[axis]
                stages.append((axis, start + index * size, start + (1 - index) * size, size))
                start = start + index * size
        return stages

    def partner(axis):
        if axis in "uv":
            step = 1 if axis == "u" else 2
            bit = (place.z // step) % 2
            return (place.z + step * (1 - 2 * bit), me)
        return place.in_plane({"c": 1, "x": 2, "y": 4}[axis])

    def rows_at(start, count):
        return pl.ds(aligned(start, 16), count)

    def landing(unit, stage):
        before = 0
        for other in range(unit):
            before += units[other][1]
        for earlier in range(stage):
            axis, _, _, size = stages_of(unit)[earlier]
            before += size * (groups - 1 if axis == "z" else 1)
        return before

    def reduce_copies(unit, stage):
        axis, _, away, size = stages_of(unit)[stage]
        at = landing(unit, stage)
        send, recv = rs_send.at[unit], rs_recv.at[unit, stage]
        if axis != "z":
            return [
                remote(
                    part.at[rows_at(away, size), :],
                    landed.at[at : at + size, :],
                    send,
                    recv,
                    partner(axis),
                )
            ]
        return [
            remote(
                part.at[rows_at(away + ((place.z + offset) % groups) * size, size), :],
                landed.at[at + (offset - 1) * size : at + offset * size, :],
                send,
                recv,
                place.in_column(offset),
            )
            for offset in range(1, groups)
        ]

    def reduce_start(unit, stage):
        for copy in reduce_copies(unit, stage):
            copy.start()

    def reduce_finish(unit, stage):
        axis, keep, _, size = stages_of(unit)[stage]
        at = landing(unit, stage)
        count = groups - 1 if axis == "z" else 1
        arrived = landed.at[at : at + count * size, :]
        gone(arrived, rs_send.at[unit])
        take(arrived, rs_recv.at[unit, stage])
        result = total if stage == len(units[unit][2]) else part
        tile = next(rows for rows in (128, 64, 32, 16) if size % rows == 0)

        def add(i, _):
            mine = rows_at(keep + i * tile, tile)
            if count == 1:
                value = part[mine, :] + landed[rows_at(at + i * tile, tile), :]
            else:
                value = part[mine, :].astype(single)
                for j in range(count):
                    other = landed[rows_at(at + j * size + i * tile, tile), :]
                    value = value + other.astype(single)
            result[mine, :] = value.astype(bfloat)
            return 0

        if size == tile:
            add(0, 0)
        else:
            lax.fori_loop(0, size // tile, add, 0)

    def gather_start(unit, stage):
        axis, keep, _, size = stages_of(unit)[stage]
        slot = total.at[rows_at(keep, size), :]
        send, recv = rs_send.at[unit], rs_recv.at[unit, 5 + stage]
        if axis != "z":
            remote(slot, slot, send, recv, partner(axis)).start()
        else:
            for offset in range(1, groups):
                remote(slot, slot, send, recv, place.in_column(offset)).start()

    def gather_finish(unit, stage):
        axis, _, away, size = stages_of(unit)[stage]
        count = groups - 1 if axis == "z" else 1
        slot = total.at[rows_at(away, count * size), :]
        gone(slot, rs_send.at[unit])
        take(slot, rs_recv.at[unit, 5 + stage])

    def step(unit, stage):
        last = len(units[unit][2])
        if stage < last:
            reduce_finish(unit, stage)
            reduce_start(unit, stage + 1)
        elif stage == last:
            reduce_finish(unit, stage)
            gather_start(unit, last)
        elif stage <= 2 * last:
            gather_finish(unit, 2 * last + 1 - stage)
            gather_start(unit, 2 * last - stage)
        else:
            gather_finish(unit, 0)

    def ready_units(begin, end):
        for unit, (base, count, _) in enumerate(units):
            if begin < base + count <= end:
                reduce_start(unit, 0)

    def steps_at(name, index):
        for at, kind, *what in plan[name]:

            def do():
                small_step(*what) if kind == "small" else step(*what)

            if not isinstance(index, int):
                pl.when(index == at)(do)
            elif index == at:
                do()

    def small_copy(turn, device):
        return remote(small_ref, small_in.at[turn], v_send, v_recv.at[min(turn, 3)], device)

    def small_arrived(turn, count):
        slot = small_in.at[turn : turn + count]
        gone(slot, v_send)
        take(slot, v_recv.at[turn])

    def in_place_order(mine, others):
        result = jnp.zeros(mine.shape, single)
        for source in range(groups):
            for offset in range(groups):
                term = mine if offset == 0 else others[offset - 1]
                result = result + jnp.where(
                    (place.z + groups - offset) % groups == source, term, 0.0
                )
        return result

    small_store = pltpu.make_async_copy(small_ref, small_hbm, store_sem.at[2])

    def small_step(stage):
        if stage > 0 and stage < 4:
            small_arrived(stage - 1, 1)
            small_ref[...] += small_in[stage - 1]
        if stage < 3:
            small_copy(stage, place.in_plane(2**stage)).start()
        elif stage == 3:
            for offset in range(1, groups):
                small_copy(2 + offset, place.in_column(offset)).start()
        else:
            if groups > 1:
                small_arrived(3, groups - 1)
            terms = [small_in[2 + offset] for offset in range(1, groups)]
            small_ref[...] = in_place_order(small_ref[...], terms)
            small_store.start()

    ticks = iter(range(100))

    def tick():
        steps_at("early", next(ticks))

    def outer_tile(start):
        at = slice(start, start + TILES)
        late = dot(hidden[rows_early:, at], grad_outer[rows_early:, :], 0, 0)
        keep_part(start, part[at, :].astype(single) + late)
        ready_units(start, start + TILES)
        tick()

    def inner_tile(start):
        for j in range(start, start + TILES, WIDE):
            keep_part(ff + j, dot(low1[...], grad_inner[:, j : j + WIDE], 0, 0))
        ready_units(ff + start, ff + start + TILES)
        tick()

    def backward(first_seq, last_seq):
        here = slice(first_seq * tokens, last_seq * tokens)
        back = grad_resid[here, :]
        grad_low = grad_outer[here, :]
        for j in range(ff // WIDE):
            span = slice(j * WIDE, (j + 1) * WIDE)
            grad_hidden = dot(grad_low, w2[span, :], 1, 1)
            inner = (grad_hidden * slope[here, span]).astype(bfloat)
            grad_inner[here, span] = inner
            add_small(5 + j, inner.astype(single))
            back = back + dot(inner, w1[:, span], 1, 1)
            if j % 2 == 1:
                tick()
        normed1 = hat1[here, :]
        add_small(3, back * normed1)
        add_small(4, back)
        scaled = back * vec(g1_ref)
        grad = rstd1[here, :] * (scaled - mean_of(scaled) - normed1 * mean_of(scaled * normed1))
        grad_resid[here, :] = grad
        grad = grad.astype(bfloat)
        grad_branch[here, :] = grad
        add_small(2, grad.astype(single))
        gatt_t[:, here] = dot(wo[...], grad, 1, 1).astype(bfloat)
        for s in range(first_seq, last_seq):
            for k in (6, 7, 2, 3, 4, 5, 1):
                dout_copy(s, k).start()
        for s in range(first_seq, last_seq):
            dout_t[s, :, lanes_of(me)] = gatt_t[head_rows_of(me), seq_lanes(s)]
        tick()

    def out_tile():
        keep_part(2 * ff, jnp.dot(att_t[...], grad_branch[...], preferred_element_type=single))
        ready_units(2 * ff, 2 * ff + width)
        tick()

    for kind, *what in EARLY:
        {"outer": outer_tile, "back": backward, "inner": inner_tile, "out": out_tile}[kind](*what)

    def pack_copies(s, k):
        other = place.peer(k)
        return [
            remote(
                dqkv.at[s, j * HEAD : (j + 1) * HEAD, lanes_of(other)],
                gpacked_t.at[j, head_rows_of(me), seq_lanes(s)],
                p_send,
                p_recv,
                place.in_plane(k),
            )
            for j in range(3)
        ]

    turns = length // BACK_QUERIES

    def back_math(s, i):
        at = pl.ds(aligned(i * BACK_QUERIES, BACK_QUERIES), BACK_QUERIES)
        cot_t = dout_t[s, :, at].astype(single)
        inverse = inv_total[s, :, at]
        cot_low = (cot_t * inverse).astype(bfloat)
        delta = jnp.sum(cot_low.astype(single) * out_wide[s, :, at], axis=0, keepdims=True)
        grown = probs[s, :, at]
        grad = jnp.dot(vrow[s], cot_low, preferred_element_type=single) - delta
        grad = (grown.astype(single) * grad).astype(bfloat)
        query_grad = jnp.dot(qkv[s, HEAD : 2 * HEAD, :], grad, preferred_element_type=single)
        dqkv[s, 0:HEAD, at] = (query_grad.astype(bfloat) * HEAD**-0.5).astype(bfloat)
        return dot(qkv[s, 0:HEAD, at], grad, 1, 1), dot(cot_low, grown, 1, 1)

    def back_chunk(turn, _):
        s = turn // turns
        i = turn % turns

        @pl.when(i == 0)
        def _():
            take(dout_t.at[s, :, 0 : others * tokens], d_recv.at[s])
            dk_acc[...] = jnp.zeros(dk_acc.shape, single)
            dv_acc[...] = jnp.zeros(dv_acc.shape, single)

        key_grad, value_grad = back_math(s, i)
        dk_acc[...] += key_grad
        dv_acc[...] += value_grad

        @pl.when(i == turns - 1)
        def _():
            dqkv[s, HEAD : 2 * HEAD, :] = dk_acc[...].astype(bfloat)
            dqkv[s, 2 * HEAD :, :] = dv_acc[...].astype(bfloat)
            for k in (6, 7, 2, 3, 4, 5, 1):
                for copy in pack_copies(s, k):
                    copy.start()
            for j in range(3):
                gpacked_t[j, head_rows_of(me), seq_lanes(s)] = dqkv[
                    s, j * HEAD : (j + 1) * HEAD, lanes_of(me)
                ]
            entry_acc[...] += jnp.dot(dqkv[s], xall[s], preferred_element_type=single)

        steps_at("attention", turn)
        return 0

    lax.fori_loop(0, seqs * turns, back_chunk, 0)

    entry_base = 2 * ff + width
    head_share = 3 * HEAD
    fourth = head_share // groups

    def entry_rows(device, z=None):
        start = entry_base + device * head_share
        if z is None:
            return rows_at(start, head_share)
        return rows_at(start + z * fourth, fourth)

    def entry_copy(offset):
        target = (place.z + offset) % groups
        return remote(
            entry_part.at[rows_at(target * fourth, fourth), :],
            entry_in.at[offset - 1],
            e_send.at[0],
            e_recv.at[0],
            place.in_column(offset),
        )

    def entry_back(offset):
        slot = total.at[entry_rows(me, place.z), :]
        return remote(slot, slot, e_send.at[1], e_recv.at[1], place.in_column(offset))

    def entry_plane(owner, to, half, turn=2):
        columns = (slice(0, half_width), slice(half_width, width), slice(0, width))[half]
        slot = total.at[entry_rows(owner), columns]
        return remote(slot, slot, e_send.at[2], e_recv.at[turn], place.in_plane(to))

    def entry_shares(count):
        return total.at[pl.ds(entry_base, count * head_share), :]

    def entry_step(stage):
        if stage == 0:
            entry_part[...] = entry_acc[...].astype(bfloat)
            for offset in range(1, groups):
                entry_copy(offset).start()
        elif stage == 1:
            if groups > 1:
                gone(entry_in, e_send.at[0])
                take(entry_in, e_recv.at[0])
            value = entry_part[rows_at(place.z * fourth, fourth), :].astype(single)
            for offset in range(1, groups):
                value = value + entry_in[offset - 1].astype(single)
            total[entry_rows(me, place.z), :] = value.astype(bfloat)
            for offset in range(1, groups):
                entry_back(offset).start()
        elif stage == 2:
            if groups > 1:
                slot = total.at[pl.ds(entry_base, (groups - 1) * fourth), :]
                gone(slot, e_send.at[1])
                take(slot, e_recv.at[1])
            entry_plane(me, 2, 0).start()
            entry_plane(me, 4, 1).start()
            entry_plane(me, 1, 2, 4).start()
        elif stage == 3:
            take(entry_shares(1), e_recv.at[2])
            for owner in (me, place.peer(2)):
                entry_plane(owner, 4, 0, 3).start()
            for owner in (me, place.peer(4)):
                entry_plane(owner, 2, 1, 3).start()
        elif stage == 4:
            take(entry_shares(2), e_recv.at[3])
            for k in (2, 4, 6):
                entry_plane(place.peer(k), 1, 2, 4).start()
        else:
            take(entry_shares(4), e_recv.at[4])
            gone(entry_shares(7), e_send.at[2])

    bias_store = pltpu.make_async_copy(bias_rows, bias_hbm, store_sem.at[3])

    def bias_column(offset):
        return remote(
            bias_own,
            bias_in.at[offset - 1],
            b_send.at[0],
            b_recv.at[0],
            place.in_column(offset),
        )

    def bias_plane(k, owner):
        slot = bias_all.at[owner]
        return remote(slot, slot, b_send.at[1], b_recv.at[1], place.in_plane(k))

    def bias_step(stage):
        if stage == 0:
            ones = jnp.ones((8, length), bfloat)
            sums = jnp.zeros((8, head_share), single)
            for s in range(seqs):
                sums = sums + dot(ones, dqkv[s], 1, 1)
            bias_own[...] = jnp.concatenate([sums[:, 0:HEAD], sums[:, 2 * HEAD :]], axis=1)
            for offset in range(1, groups):
                bias_column(offset).start()
        elif stage == 1:
            if groups > 1:
                gone(bias_in, b_send.at[0])
                take(bias_in, b_recv.at[0])
            terms = [bias_in[offset - 1] for offset in range(1, groups)]
            bias_all[me] = in_place_order(bias_own[...], terms)
            for k in range(1, 8):
                bias_plane(k, me).start()
        else:
            gone(bias_all.at[0:others], b_send.at[1])
            take(bias_all.at[0:others], b_recv.at[1])
            for at, start in ((0, 0), (1, HEAD)):
                bias_rows[at : at + 1, :] = jnp.concatenate(
                    [bias_all[p, 0:1, start : start + HEAD] for p in range(HEADS)], axis=1
                )
            bias_store.start()


    def input_step():
        take(gpacked_t.at[:, 0 : others * HEAD, :], p_recv)
        grad_in = grad_resid[...]
        for j in range(3):
            grad_in = grad_in + dot(gpacked_t[j], we[:, j * width : (j + 1) * width], 0, 1)
        for s in range(seqs):
            dx_ref[s] = grad_in[s * tokens : (s + 1) * tokens].astype(bfloat)
            store(1, s).start()

    for kind, *what in plan["tail"]:
        if kind == "unit":
            step(*what)
        elif kind == "entry":
            entry_step(*what)
        elif kind == "bias":
            bias_step(*what)
        elif kind == "small":
            small_step(*what)
        else:
            input_step()
    small_store.wait()
    bias_store.wait()
    pltpu.make_async_copy(out_ref, out_hbm, store_sem.at[0]).wait()
    pltpu.make_async_copy(dx_ref, dx_hbm, store_sem.at[1]).wait()
    gone(xall.at[:, 0 : others * tokens, :], x_send)
    gone(ids_all.at[:, 0 : others * tokens], i_send)
    gone(out_low.at[:, :, 0 : others * tokens], o_send)
    gone(gatt_t.at[0 : others * HEAD, :], d_send)
    gone(dqkv.at[:, :, 0 : others * tokens], p_send)


def widen_kernel(sums, small_hbm, bias_hbm, out_in, dx_in, *refs):
    outs, vectors, scratch = refs[:15], refs[15:23], refs[23:]
    small, bias, passed, inner_bias, outer_v, inner_v, out_v, entry_v = scratch[:8]
    in_sem, out_sem = scratch[8:]
    out_ref, dx_ref, entry, query_b, value_b, out_w, out_b = outs[:7]
    gain1, shift1, inner_w, inner_b, outer_w, outer_b, gain2, shift2 = outs[7:]
    width = WIDE
    ff = outer_w.shape[0]
    pieces = (2 * ff + width) // WIDE
    head_share = 3 * HEAD
    reads = []
    writes = []

    def read(src, dst):
        reads.append(pltpu.make_async_copy(src, dst, in_sem.at[len(reads)]))
        reads[-1].start()

    def write(src, dst):
        writes.append(pltpu.make_async_copy(src, dst, out_sem.at[len(writes)]))
        writes[-1].start()

    read(small_hbm, small)
    read(bias_hbm, bias)
    read(out_in, passed.at[0])
    read(dx_in, passed.at[1])
    for i in range(pieces):
        rows = slice(i * WIDE, (i + 1) * WIDE)
        value = sums[rows, :].astype(single)
        j = i - ff // WIDE
        if j < 0:
            outer_v[rows, :] = value
            write(outer_v.at[rows], outer_w.at[rows])
        elif j < ff // WIDE:
            columns = slice(j * WIDE, (j + 1) * WIDE)
            inner_v[:, columns] = value
            write(inner_v.at[:, columns], inner_w.at[:, columns])
        else:
            out_v[...] = value
            write(out_v, out_w)
    for j in range(3):
        columns = slice(j * width, (j + 1) * width)
        starts = [2 * ff + width + h * head_share + j * HEAD for h in range(HEADS)]
        value = jnp.concatenate([sums[at : at + HEAD, :] for at in starts], axis=0)
        entry_v[:, columns] = value.astype(single).T
        write(entry_v.at[:, columns], entry.at[:, columns])
    for read_done in reads:
        read_done.wait()
    write(passed.at[0], out_ref)
    write(passed.at[1], dx_ref)

    def small_row(at):
        return (bias if at < 2 else small)[at : at + 1, :].reshape(width)

    for j, (ref, at) in enumerate(
        (
            (query_b, 0),
            (value_b, 1),
            (out_b, 2),
            (gain1, 3),
            (shift1, 4),
            (outer_b, 9),
            (gain2, 10),
            (shift2, 11),
        )
    ):
        vectors[j][...] = small_row(at)
        write(vectors[j], ref)
    for j in range(ff // WIDE):
        inner_bias[j * WIDE : (j + 1) * WIDE] = small_row(5 + j)
    write(inner_bias, inner_b)
    for copy in writes:
        copy.wait()


UNITS = (
    (0, 512, "yuvx"),
    (512, 512, "uvxy"),
    (1024, 512, "yxuv"),
    (1536, 512, "xuvy"),
    (2048, 512, "uxyv"),
    (2560, 512, "xyuv"),
    (3072, 512, "yxz"),
    (3584, 512, "xyuv"),
    (4096, 512, "zyx"),
)
PLAN = {
    "early": (
        (2, "unit", 0, 0),
        (3, "unit", 1, 0),
        (6, "unit", 3, 0),
        (6, "unit", 2, 0),
        (7, "small", 0),
        (8, "small", 1),
        (8, "unit", 0, 1),
        (9, "unit", 4, 0),
        (9, "unit", 1, 1),
        (10, "unit", 5, 0),
    ),
    "attention": (
        (0, "unit", 7, 0),
        (0, "unit", 3, 1),
        (0, "unit", 8, 0),
        (0, "unit", 6, 0),
        (0, "unit", 2, 1),
        (1, "unit", 0, 2),
        (2, "unit", 4, 1),
        (2, "small", 2),
        (3, "unit", 1, 2),
        (3, "unit", 5, 1),
        (3, "unit", 6, 1),
        (3, "unit", 3, 2),
        (5, "unit", 7, 1),
    ),
    "tail": (
        ("entry", 0),
        ("bias", 0),
        ("unit", 2, 2),
        ("small", 3),
        ("unit", 8, 1),
        ("unit", 0, 3),
        ("unit", 3, 3),
        ("unit", 4, 2),
        ("unit", 2, 3),
        ("unit", 5, 2),
        ("entry", 1),
        ("bias", 1),
        ("unit", 5, 3),
        ("small", 4),
        ("unit", 1, 3),
        ("unit", 2, 4),
        ("unit", 7, 2),
        ("unit", 6, 2),
        ("unit", 8, 2),
        ("unit", 3, 4),
        ("unit", 4, 3),
        ("unit", 1, 4),
        ("entry", 2),
        ("unit", 7, 3),
        ("unit", 5, 4),
        ("unit", 3, 5),
        ("unit", 2, 5),
        ("unit", 0, 4),
        ("input",),
        ("bias", 2),
        ("unit", 8, 3),
        ("unit", 4, 4),
        ("unit", 1, 5),
        ("unit", 6, 3),
        ("unit", 7, 4),
        ("unit", 5, 5),
        ("entry", 3),
        ("unit", 2, 6),
        ("unit", 0, 5),
        ("unit", 3, 6),
        ("unit", 8, 4),
        ("unit", 1, 6),
        ("unit", 4, 5),
        ("unit", 5, 6),
        ("unit", 6, 4),
        ("unit", 7, 5),
        ("unit", 3, 7),
        ("unit", 0, 6),
        ("entry", 4),
        ("unit", 8, 5),
        ("unit", 7, 6),
        ("unit", 4, 6),
        ("unit", 2, 7),
        ("unit", 1, 7),
        ("entry", 5),
        ("unit", 5, 7),
        ("unit", 6, 5),
        ("unit", 0, 7),
        ("unit", 7, 7),
        ("unit", 3, 8),
        ("unit", 3, 9),
        ("unit", 4, 7),
        ("unit", 2, 8),
        ("unit", 2, 9),
        ("unit", 5, 8),
        ("unit", 8, 6),
        ("unit", 1, 8),
        ("unit", 6, 6),
        ("unit", 5, 9),
        ("unit", 8, 7),
        ("unit", 1, 9),
        ("unit", 7, 8),
        ("unit", 6, 7),
        ("unit", 4, 8),
        ("unit", 0, 8),
        ("unit", 7, 9),
        ("unit", 4, 9),
        ("unit", 0, 9),
    ),
}


def by_heads(groups):
    def run(inputs, blocks, we, qb, vb, wo, bo, g1, s1, w1, b1, w2, b2, g2, s2, cot):
        seqs, tokens, width = inputs.shape
        ff = w1.shape[1]
        rows = seqs * tokens
        length = tokens * HEADS
        grad_rows = 2 * ff + width
        units = UNITS
        others = max(groups - 1, 1)
        head_share = 3 * HEAD
        vmem = pl.BlockSpec(memory_space=pltpu.VMEM)
        hbm = pl.BlockSpec(memory_space=pl.ANY)
        dma = pltpu.SemaphoreType.DMA

        def shape(*dims):
            return jax.ShapeDtypeStruct(dims, single)

        out, dx, total, small, bias = pl.pallas_call(
            partial(layer_kernel, groups, units, PLAN),
            out_shape=[
                jax.ShapeDtypeStruct(inputs.shape, bfloat),
                jax.ShapeDtypeStruct(inputs.shape, bfloat),
                pltpu.VMEM((grad_rows + HEADS * head_share, width), bfloat),
                shape(16, width),
                shape(8, width),
            ],
            in_specs=[hbm] * 16,
            out_specs=[hbm, hbm, vmem, hbm, hbm],
            scratch_shapes=[
                pltpu.SMEM((seqs, 3, 2, HEADS), jnp.int32),
                pltpu.VMEM(inputs.shape, bfloat),
                pltpu.VMEM(qb.shape, bfloat),
                pltpu.VMEM(vb.shape, bfloat),
                pltpu.VMEM(bo.shape, bfloat),
                pltpu.VMEM(g1.shape, bfloat),
                pltpu.VMEM(s1.shape, bfloat),
                pltpu.VMEM(b1.shape, bfloat),
                pltpu.VMEM(b2.shape, bfloat),
                pltpu.VMEM(g2.shape, bfloat),
                pltpu.VMEM(s2.shape, bfloat),
                pltpu.VMEM(inputs.shape, bfloat),
                pltpu.VMEM(inputs.shape, bfloat),
                pltpu.VMEM((16, width), single),
                pltpu.VMEM(we.shape, bfloat),
                pltpu.VMEM(wo.shape, bfloat),
                pltpu.VMEM(w1.shape, bfloat),
                pltpu.VMEM(w2.shape, bfloat),
                pltpu.VMEM(cot.shape, bfloat),
                dma((16,)),
                pltpu.VMEM((head_share, width), bfloat),
                pltpu.VMEM((seqs, length, width), bfloat),
                pltpu.VMEM((HEADS, 16, tokens), bfloat),
                pltpu.VMEM((16, length), bfloat),
                pltpu.VMEM((seqs, 8, length), single),
                pltpu.VMEM((seqs, head_share + 16, length), bfloat),
                pltpu.VMEM((seqs, length, HEAD), bfloat),
                pltpu.VMEM((seqs, length, HEAD), bfloat),
                pltpu.VMEM((seqs, length, length), bfloat),
                pltpu.VMEM((seqs, 1, length), single),
                pltpu.VMEM((seqs, HEAD, length), single),
                pltpu.VMEM((seqs, HEAD, length), bfloat),
                pltpu.VMEM((width, rows), bfloat),
                pltpu.VMEM((rows, width), single),
                pltpu.VMEM((rows, 1), single),
                pltpu.VMEM((rows, width), bfloat),
                pltpu.VMEM((rows, ff), bfloat),
                pltpu.VMEM((rows, ff), single),
                pltpu.VMEM((rows, ff), bfloat),
                pltpu.VMEM((rows, width), bfloat),
                pltpu.VMEM((rows, width), single),
                pltpu.VMEM((rows, width), bfloat),
                pltpu.VMEM((width, rows), bfloat),
                pltpu.VMEM((seqs, HEAD, length), bfloat),
                pltpu.VMEM((seqs, head_share, length), bfloat),
                pltpu.VMEM((HEAD, length), single),
                pltpu.VMEM((HEAD, length), single),
                pltpu.VMEM((3, width, rows), bfloat),
                pltpu.VMEM((head_share, width), single),
                pltpu.VMEM((head_share, width), bfloat),
                pltpu.VMEM((others, head_share // groups, width), bfloat),
                pltpu.VMEM((grad_rows, width), bfloat),
                pltpu.VMEM((grad_rows, width), bfloat),
                pltpu.VMEM((3 + groups, 16, width), single),
                pltpu.VMEM((8, 2 * HEAD), single),
                pltpu.VMEM((others, 8, 2 * HEAD), single),
                pltpu.VMEM((HEADS, 8, 2 * HEAD), single),
                pltpu.VMEM((8, width), single),
                dma(()),
                dma((seqs, 3)),
                dma(()),
                dma(()),
                dma(()),
                dma((seqs,)),
                dma(()),
                dma((seqs,)),
                dma(()),
                dma(()),
                dma((len(units),)),
                dma((len(units), 10)),
                dma((3,)),
                dma((5,)),
                dma(()),
                dma((4,)),
                dma((2,)),
                dma((2,)),
                dma((4,)),
                pltpu.SemaphoreType.REGULAR,
                pltpu.SemaphoreType.REGULAR,
            ],
            compiler_params=pltpu.CompilerParams(
                collective_id=0, has_side_effects=True, vmem_limit_bytes=LAYER_VMEM
            ),
            name="layer",
        )(
            inputs, blocks.transpose(0, 3, 2, 1), we, qb, vb, wo, bo, g1, s1, w1, b1, w2, b2,
            g2, s2, cot,
        )
        pieces = grad_rows // WIDE
        return pl.pallas_call(
            widen_kernel,
            in_specs=[vmem] + [hbm] * 4,
            out_specs=[hbm] * 15,
            out_shape=[
                jax.ShapeDtypeStruct(inputs.shape, bfloat),
                jax.ShapeDtypeStruct(inputs.shape, bfloat),
                shape(width, 3 * width),
                shape(width),
                shape(width),
                shape(width, width),
                shape(width),
                shape(width),
                shape(width),
                shape(width, ff),
                shape(ff),
                shape(ff, width),
                shape(width),
                shape(width),
                shape(width),
            ],
            scratch_shapes=[
                *[pltpu.VMEM((width,), single)] * 8,
                pltpu.VMEM((16, width), single),
                pltpu.VMEM((8, width), single),
                pltpu.VMEM((2, *inputs.shape), bfloat),
                pltpu.VMEM((ff,), single),
                pltpu.VMEM((ff, width), single),
                pltpu.VMEM((width, ff), single),
                pltpu.VMEM((width, width), single),
                pltpu.VMEM((width, 3 * width), single),
                dma((4,)),
                dma((pieces + 14,)),
            ],
            compiler_params=pltpu.CompilerParams(vmem_limit_bytes=WIDEN_VMEM),
            name="widen",
        )(pltpu.with_memory_space_constraint(total, pltpu.VMEM), small, bias, out, dx)

    return run


def solution(mesh):
    in_specs = (
        P("dp", "seq", None),
        P("dp", None, "seq", None),
        P(),
        P(),
        P(),
        P(),
        P(),
        P(),
        P(),
        P(),
        P(),
        P(),
        P(),
        P(),
        P(),
        P("dp", "seq", None),
    )
    out_specs = (
        P("dp", "seq", None),
        P("dp", "seq", None),
        P(),
        P(),
        P(),
        P(),
        P(),
        P(),
        P(),
        P(),
        P(),
        P(),
        P(),
        P(),
        P(),
    )
    heads_fit = mesh.shape["seq"] == HEADS
    plan = by_heads(mesh.shape["dp"]) if heads_fit else on_device
    return jax.shard_map(
        plan, mesh=mesh, in_specs=in_specs, out_specs=out_specs, check_vma=False
    )
```

```python
from functools import partial

import jax
import jax.numpy as jnp
from jax import lax
from jax.experimental import pallas as pl
from jax.experimental.pallas import tpu as pltpu
from jax.sharding import PartitionSpec as P

HEADS = 8
HEAD = 64
BLOCK = 64


HIGHEST = lax.Precision.HIGHEST
EPSILON = 1e-05
NEGATIVE = -1e30


def spread_2(value, axis, root):
    mine = lax.axis_index(axis) == root
    return lax.psum(jnp.where(mine, value, jnp.zeros_like(value)), axis)


def for_sending(value):

    def short(part):
        return part.astype(jnp.bfloat16) if part.dtype == jnp.float32 else part

    return jax.tree.map(short, value)


def extended(block, sides, width):
    for axis, dim in sides:
        count = lax.axis_size(axis)
        forward = [(i, i + 1) for i in range(count - 1)]
        backward = [(target, source) for source, target in forward]
        low = lax.ppermute(
            lax.slice_in_dim(block, block.shape[dim] - width, None, axis=dim), axis, forward
        )
        high = lax.ppermute(lax.slice_in_dim(block, 0, width, axis=dim), axis, backward)
        block = jnp.concatenate([low, block, high], axis=dim)
    return block


def combined_all(part, axis, combine):
    gathered = jax.tree.map(lambda a: lax.all_gather(a, axis), part)

    def take(source):
        return jax.tree.map(lambda a: lax.dynamic_index_in_dim(a, source, 0, False), gathered)

    return lax.fori_loop(
        1, lax.axis_size(axis), lambda source, state: combine(state, take(source)), take(0)
    )


def norm_apply(values, gain_vec, shift_vec):
    center = values - jnp.mean(values, axis=-1, keepdims=True)
    spread = jnp.mean(center * center, axis=-1, keepdims=True)
    return center * lax.rsqrt(spread + EPSILON) * gain_vec + shift_vec


def pair_blocks(row_data, head_count, block_rows):
    seq_count, length_here, full_width = row_data.shape
    head_width = full_width // (2 * head_count)
    shaped = row_data.reshape(
        seq_count, length_here // block_rows, block_rows, 2, head_count, head_width
    )
    return shaped.transpose(0, 4, 1, 2, 3, 5).reshape(
        seq_count, head_count, length_here // block_rows, block_rows, 2 * head_width
    )


def pair_tokens(blocked):
    seq_count, head_count, block_count, block_rows, double_width = blocked.shape
    head_width = double_width // 2
    shaped = blocked.reshape(seq_count, head_count, block_count, block_rows, 2, head_width)
    return shaped.transpose(0, 2, 3, 4, 1, 5).reshape(
        seq_count, block_count * block_rows, 2 * head_count * head_width
    )


def head_rows(row_data, head_count):
    seq_count, length_here, full_width = row_data.shape
    return row_data.reshape(seq_count, length_here, head_count, full_width // head_count).transpose(
        0, 2, 1, 3
    )


def row_heads(split_rows):
    seq_count, head_count, length_here, head_width = split_rows.shape
    return split_rows.transpose(0, 2, 1, 3).reshape(seq_count, length_here, head_count * head_width)


def merge_parts(earlier, later):
    peak_one, total_one, out_one = earlier
    peak_two, total_two, out_two = later
    row_peak = jnp.maximum(peak_one, peak_two)
    factor_one = jnp.exp(peak_one - row_peak)
    factor_two = jnp.exp(peak_two - row_peak)
    return (
        row_peak,
        total_one * factor_one + total_two * factor_two,
        out_one * factor_one[..., None] + out_two * factor_two[..., None],
    )


def share_rows(row_data, root_device):
    return spread_2(row_data, "seq", root_device)


def share_grads(grad_rows, grad_delta, root_device):
    return (
        spread_2(grad_rows.astype(jnp.bfloat16), "seq", root_device).astype(grad_rows.dtype),
        spread_2(for_sending(grad_delta), "seq", root_device).astype(grad_delta.dtype),
    )


def on_device(
    inputs,
    random_blocks,
    entry_weight,
    query_bias,
    value_bias,
    out_weight,
    out_bias,
    norm_gain,
    norm_shift,
    inner_weight,
    inner_bias,
    outer_weight,
    outer_bias,
    final_gain,
    final_shift,
    cotangent,
):
    seq_count, token_count, model_width = inputs.shape
    head_count = HEADS
    head_width = HEAD
    block_rows = BLOCK
    per_dev = token_count // block_rows
    devices = lax.axis_size("seq")
    device = lax.axis_index("seq")
    block_total = devices * per_dev
    request_total = seq_count * head_count * per_dev * 3
    capacity = (request_total + devices - 2) // (devices - 1)
    table_rows = seq_count * head_count * per_dev
    query_scale = head_width ** (-0.5)
    is_first = device == 0
    is_last = device == devices - 1
    bfloat = jnp.bfloat16
    single = jnp.float32
    flat_in = inputs.reshape(-1, model_width)
    entry_out = jnp.dot(flat_in, entry_weight, preferred_element_type=single)
    packed = jnp.concatenate(
        [
            (entry_out[:, :model_width] + query_bias) * query_scale,
            entry_out[:, model_width : 2 * model_width],
            entry_out[:, 2 * model_width :] + value_bias,
        ],
        axis=1,
    )
    packed = packed.astype(bfloat).reshape(seq_count, token_count, 3 * model_width)
    key_value = packed[:, :, model_width:]
    padded = extended(key_value, (("seq", 1),), block_rows)
    global_rows = jnp.concatenate(
        [
            share_rows(packed[:, :block_rows], 0),
            share_rows(packed[:, token_count - block_rows :], devices - 1),
        ],
        axis=1,
    )
    owners = (random_blocks // per_dev).reshape(-1)
    within = random_blocks % per_dev
    seq_index = lax.broadcasted_iota(jnp.int32, random_blocks.shape, 0)
    head_index = lax.broadcasted_iota(jnp.int32, random_blocks.shape, 1)
    request_codes = ((seq_index * head_count + head_index) * per_dev + within).reshape(-1)
    onehot = (owners[:, None] == jnp.arange(devices, dtype=jnp.int32)[None, :]).astype(jnp.int32)
    slot_index = jnp.sum((jnp.cumsum(onehot, axis=0) - onehot) * onehot, axis=1)
    slot_place = owners * capacity + slot_index
    requests = (
        jnp.full((devices * capacity,), -1, jnp.int32)
        .at[slot_place]
        .set(request_codes)
        .reshape(devices, capacity)
    )
    incoming = lax.all_to_all(requests, "seq", split_axis=0, concat_axis=0, tiled=True)
    head_table = pair_blocks(key_value, head_count, block_rows).reshape(
        table_rows, block_rows, 2 * head_width
    )
    served = head_table[jnp.maximum(incoming, 0)]
    served = jnp.where((incoming >= 0)[:, :, None, None], served, jnp.zeros((), bfloat))
    fetched = lax.all_to_all(served, "seq", split_axis=0, concat_axis=0, tiled=True)
    random_kv = fetched.reshape(devices * capacity, block_rows, 2 * head_width)[slot_place]
    random_kv = random_kv.reshape(seq_count, head_count, per_dev, 3, block_rows, 2 * head_width)
    window_view = pair_blocks(padded, head_count, block_rows)
    window_kv = jnp.stack(
        [window_view[:, :, :per_dev], window_view[:, :, 1 : per_dev + 1], window_view[:, :, 2:]],
        axis=3,
    )
    global_kv = pair_blocks(global_rows[:, :, model_width:], head_count, block_rows)
    global_kv = jnp.broadcast_to(
        global_kv[:, :, None], (seq_count, head_count, per_dev, 2, block_rows, 2 * head_width)
    )
    all_kv = jnp.concatenate([window_kv, global_kv, random_kv], axis=3).reshape(
        seq_count, head_count, per_dev, 8 * block_rows, 2 * head_width
    )
    key_part = all_kv[..., :head_width]
    value_part = all_kv[..., head_width:]
    query_view = head_rows(packed[:, :, :model_width], head_count).reshape(
        seq_count, head_count, per_dev, block_rows, head_width
    )
    block_ids = device * per_dev + jnp.arange(per_dev)[:, None]
    column = jnp.arange(8 * block_rows)[None, :]
    neighbor = block_ids + column // block_rows - 1
    key_keep = (column >= 3 * block_rows) | (neighbor >= 1) & (neighbor <= block_total - 2)
    key_keep = key_keep[None, None, :, None, :]

    def block_scores():
        raw_scores = jnp.einsum(
            "shiqd,shikd->shiqk", query_view, key_part, preferred_element_type=single
        )
        return jnp.where(key_keep, raw_scores, NEGATIVE)

    scores = block_scores()
    row_peak = jnp.max(scores, axis=-1, keepdims=True)
    exponent = jnp.exp(scores - row_peak)
    row_total = jnp.sum(exponent, axis=-1, keepdims=True)
    probability = exponent / row_total
    log_total = row_peak + jnp.log(row_total)
    prob_low = probability.astype(bfloat)
    window_out = jnp.einsum(
        "shiqk,shikd->shiqd", prob_low, value_part, preferred_element_type=single
    )
    global_query = head_rows(global_rows[:, :, :model_width], head_count)
    local_keys = head_rows(packed[:, :, model_width : 2 * model_width], head_count)
    local_values = head_rows(packed[:, :, 2 * model_width :], head_count)
    global_scores = jnp.einsum(
        "shqd,shkd->shqk", global_query, local_keys, preferred_element_type=single
    )
    global_peak = jnp.max(global_scores, axis=-1)
    global_exp = jnp.exp(global_scores - global_peak[..., None])
    global_total = jnp.sum(global_exp, axis=-1)
    global_sum = jnp.einsum(
        "shqk,shkd->shqd", global_exp, local_values.astype(single), precision=HIGHEST
    )
    global_peak, global_total, global_sum = combined_all(
        (global_peak, global_total, global_sum), "seq", merge_parts
    )
    global_out = global_sum / global_total[..., None]
    global_log = global_peak + jnp.log(global_total)
    block_pos = jnp.arange(per_dev)
    take_first = ((block_pos == 0) & is_first)[None, None, :, None, None]
    take_last = ((block_pos == per_dev - 1) & is_last)[None, None, :, None, None]
    combined = jnp.where(take_first, global_out[:, :, None, :block_rows], window_out)
    combined = jnp.where(take_last, global_out[:, :, None, block_rows:], combined)
    attended = (
        row_heads(combined.reshape(seq_count, head_count, token_count, head_width))
        .reshape(-1, model_width)
        .astype(bfloat)
    )
    branch = jnp.dot(attended, out_weight, preferred_element_type=single) + out_bias
    residual_in = flat_in.astype(single) + branch
    first_norm, first_pull = jax.vjp(
        norm_apply, residual_in, norm_gain.astype(single), norm_shift.astype(single)
    )
    first_low = first_norm.astype(bfloat)
    inner_pre = jnp.dot(first_low, inner_weight, preferred_element_type=single) + inner_bias
    activated, gelu_pull = jax.vjp(partial(jax.nn.gelu, approximate=False), inner_pre)
    hidden = activated.astype(bfloat)
    second = first_norm + (
        jnp.dot(hidden, outer_weight, preferred_element_type=single) + outer_bias
    )
    final_norm, final_pull = jax.vjp(
        norm_apply, second, final_gain.astype(single), final_shift.astype(single)
    )
    layer_out = final_norm.astype(bfloat).reshape(inputs.shape)
    grad_second, final_gain_grad, final_shift_grad = final_pull(
        cotangent.reshape(-1, model_width).astype(single)
    )
    grad_outer = grad_second.astype(bfloat)
    outer_weight_grad = jnp.dot(hidden.T, grad_outer, preferred_element_type=single)
    outer_bias_grad = jnp.sum(grad_outer.astype(single), axis=0)
    (grad_active,) = gelu_pull(jnp.dot(grad_outer, outer_weight.T, preferred_element_type=single))
    grad_inner = grad_active.astype(bfloat)
    inner_weight_grad = jnp.dot(first_low.T, grad_inner, preferred_element_type=single)
    inner_bias_grad = jnp.sum(grad_inner.astype(single), axis=0)
    grad_first = grad_second + jnp.dot(grad_inner, inner_weight.T, preferred_element_type=single)
    grad_resid, norm_gain_grad, norm_shift_grad = first_pull(grad_first)
    grad_branch = grad_resid.astype(bfloat)
    out_weight_grad = jnp.dot(attended.T, grad_branch, preferred_element_type=single)
    out_bias_grad = jnp.sum(grad_branch.astype(single), axis=0)
    grad_attended = jnp.dot(grad_branch, out_weight.T, preferred_element_type=single).astype(bfloat)
    grad_heads = head_rows(
        grad_attended.reshape(seq_count, token_count, model_width), head_count
    ).reshape(seq_count, head_count, per_dev, block_rows, head_width)
    grad_window = jnp.where(take_first | take_last, jnp.zeros((), bfloat), grad_heads)
    probability = jnp.exp(block_scores() - log_total)
    prob_low = probability.astype(bfloat)
    grad_prob = jnp.einsum(
        "shiqd,shikd->shiqk", grad_window, value_part, preferred_element_type=single
    )
    row_delta = jnp.sum(probability * grad_prob, axis=-1, keepdims=True)
    grad_scores = (probability * (grad_prob - row_delta)).astype(bfloat)
    grad_query_block = jnp.einsum(
        "shiqk,shikd->shiqd", grad_scores, key_part, preferred_element_type=single
    )
    grad_key_block = jnp.einsum(
        "shiqk,shiqd->shikd", grad_scores, query_view, preferred_element_type=single
    )
    grad_value_block = jnp.einsum(
        "shiqk,shiqd->shikd", prob_low, grad_window, preferred_element_type=single
    )
    grad_kv = jnp.concatenate([grad_key_block, grad_value_block], axis=-1).reshape(
        seq_count, head_count, per_dev, 8, block_rows, 2 * head_width
    )
    pad_none = ((0, 0), (0, 0))
    grad_pad = (
        jnp.pad(grad_kv[:, :, :, 0], pad_none + ((0, 2), (0, 0), (0, 0)))
        + jnp.pad(grad_kv[:, :, :, 1], pad_none + ((1, 1), (0, 0), (0, 0)))
        + jnp.pad(grad_kv[:, :, :, 2], pad_none + ((2, 0), (0, 0), (0, 0)))
    )
    grad_tokens = pair_tokens(grad_pad)
    edge_grads = jnp.concatenate(
        [grad_tokens[:, :block_rows], grad_tokens[:, token_count + block_rows :]], axis=1
    )
    returned = extended(edge_grads.astype(jnp.bfloat16), (("seq", 1),), block_rows).astype(
        edge_grads.dtype
    )
    gap = token_count - block_rows
    grad_kv_local = (
        grad_tokens[:, block_rows : block_rows + token_count]
        + jnp.pad(returned[:, :block_rows], ((0, 0), (0, gap), (0, 0)))
        + jnp.pad(returned[:, 3 * block_rows :], ((0, 0), (gap, 0), (0, 0)))
    )
    grad_global_kv = pair_tokens(jnp.sum(grad_kv[:, :, :, 3:5], axis=2))
    grad_random = grad_kv[:, :, :, 5:8].reshape(request_total, block_rows, 2 * head_width)
    outgoing = (
        jnp.zeros((devices * capacity, block_rows, 2 * head_width), single)
        .at[slot_place]
        .set(grad_random)
    )
    outgoing = outgoing.reshape(devices, capacity, block_rows, 2 * head_width)
    returned_random = lax.all_to_all(
        outgoing.astype(jnp.bfloat16), "seq", split_axis=0, concat_axis=0, tiled=True
    ).astype(outgoing.dtype)
    segment_ids = jnp.where(incoming >= 0, incoming, table_rows).reshape(-1)
    grad_table = jax.ops.segment_sum(
        returned_random.reshape(devices * capacity, block_rows, 2 * head_width),
        segment_ids,
        num_segments=table_rows + 1,
    )[:table_rows]
    grad_owned = pair_tokens(
        grad_table.reshape(seq_count, head_count, per_dev, block_rows, 2 * head_width)
    )
    first_cot = grad_heads[:, :, 0].astype(single)
    last_cot = grad_heads[:, :, per_dev - 1].astype(single)
    first_cot, first_delta = share_grads(
        first_cot, jnp.sum(first_cot * global_out[:, :, :block_rows], axis=-1), 0
    )
    last_cot, last_delta = share_grads(
        last_cot, jnp.sum(last_cot * global_out[:, :, block_rows:], axis=-1), devices - 1
    )
    global_cot = jnp.concatenate([first_cot, last_cot], axis=2)
    global_delta = jnp.concatenate([first_delta, last_delta], axis=2)
    global_prob = jnp.exp(
        jnp.einsum("shqd,shkd->shqk", global_query, local_keys, preferred_element_type=single)
        - global_log[..., None]
    )
    global_dprob = jnp.einsum(
        "shqd,shkd->shqk", global_cot.astype(bfloat), local_values, preferred_element_type=single
    )
    global_grads = (global_prob * (global_dprob - global_delta[..., None])).astype(bfloat)
    grad_global_query = jnp.einsum(
        "shqk,shkd->shqd", global_grads, local_keys, preferred_element_type=single
    )
    grad_local_key = jnp.einsum(
        "shqk,shqd->shkd", global_grads, global_query, preferred_element_type=single
    )
    grad_local_value = jnp.einsum("shqk,shqd->shkd", global_prob, global_cot, precision=HIGHEST)
    partials = jnp.concatenate([row_heads(grad_global_query), grad_global_kv], axis=-1)
    partials = lax.psum(partials.astype(jnp.bfloat16), "seq").astype(jnp.float32)
    owner_part = jnp.where(
        is_first, jnp.pad(partials[:, :block_rows], ((0, 0), (0, gap), (0, 0))), 0.0
    ) + jnp.where(is_last, jnp.pad(partials[:, block_rows:], ((0, 0), (gap, 0), (0, 0))), 0.0)
    grad_query_tokens = row_heads(
        grad_query_block.reshape(seq_count, head_count, token_count, head_width)
    )
    grad_kv_tokens = (
        grad_kv_local
        + grad_owned
        + jnp.concatenate([row_heads(grad_local_key), row_heads(grad_local_value)], axis=-1)
    )
    grad_packed = (
        jnp.concatenate([grad_query_tokens, grad_kv_tokens], axis=-1) + owner_part
    ).astype(bfloat)
    column_scale = jnp.concatenate(
        [jnp.full((model_width,), query_scale, single), jnp.ones((2 * model_width,), single)]
    )
    grad_entry = (
        (grad_packed.astype(single) * column_scale).astype(bfloat).reshape(-1, 3 * model_width)
    )
    entry_weight_grad = jnp.dot(flat_in.T, grad_entry, preferred_element_type=single)
    query_bias_grad = jnp.sum(grad_entry[:, :model_width].astype(single), axis=0)
    value_bias_grad = jnp.sum(grad_entry[:, 2 * model_width :].astype(single), axis=0)
    input_grad = (
        (grad_resid + jnp.dot(grad_entry, entry_weight.T, preferred_element_type=single))
        .astype(bfloat)
        .reshape(inputs.shape)
    )
    (
        total_entry,
        total_query,
        total_value,
        total_out,
        total_out_bias,
        total_norm_gain,
        total_norm_shift,
        total_inner,
        total_inner_bias,
        total_outer,
        total_outer_bias,
        total_final_gain,
        total_final_shift,
    ) = lax.psum(
        (
            entry_weight_grad,
            query_bias_grad,
            value_bias_grad,
            out_weight_grad,
            out_bias_grad,
            norm_gain_grad,
            norm_shift_grad,
            inner_weight_grad,
            inner_bias_grad,
            outer_weight_grad,
            outer_bias_grad,
            final_gain_grad,
            final_shift_grad,
        ),
        ("dp", "seq"),
    )
    return (
        layer_out,
        input_grad,
        total_entry,
        total_query,
        total_value,
        total_out,
        total_out_bias,
        total_norm_gain,
        total_norm_shift,
        total_inner,
        total_inner_bias,
        total_outer,
        total_outer_bias,
        total_final_gain,
        total_final_shift,
    )


MESH = pl.DeviceIdType.MESH
bfloat = jnp.bfloat16
single = jnp.float32
WIDE = 512
QUERIES = 1024
BACK_QUERIES = 512
FORWARD = ((0, 2), (2, 3))
EARLY = (
    ("outer", 0),
    ("outer", 1024),
    ("back", 0, 1),
    ("back", 1, 3),
    ("inner", 0),
    ("inner", 1024),
    ("out",),
)
TILES = 1024
LAYER_VMEM = 56 * 2**20
WIDEN_VMEM = 56 * 2**20
INV_SQRT2 = 0.7071067811865476
INV_SQRT_2PI = 0.3989422804014327


def dot(a, b, a_dim, b_dim):
    return lax.dot_general(
        a, b, (((a_dim,), (b_dim,)), ((), ())), preferred_element_type=single
    )


def aligned(index, step):
    return pl.multiple_of(index, step)


class Place:
    def __init__(self, groups):
        self.groups = groups
        self.z = lax.axis_index("dp")
        self.me = lax.axis_index("seq")
        self.y = self.me // 4
        self.x = (self.me // 2) % 2
        self.core = self.me % 2

    def peer(self, offset):
        off_y, off_x, off_core = offset // 4, (offset // 2) % 2, offset % 2
        return (
            ((self.y + off_y) % 2) * 4
            + ((self.x + off_x) % 2) * 2
            + (self.core + off_core) % 2
        )

    def in_plane(self, offset):
        return (self.z, self.peer(offset))

    def in_column(self, offset):
        return ((self.z + offset) % self.groups, self.me)


def remote(src, dst, send, recv, device):
    return pltpu.make_async_remote_copy(
        src_ref=src,
        dst_ref=dst,
        send_sem=send,
        recv_sem=recv,
        device_id=device,
        device_id_type=MESH,
    )


def layer_kernel(
    groups,
    units,
    plan,
    x_hbm,
    blocks_hbm,
    we_hbm,
    qb_hbm,
    vb_hbm,
    wo_hbm,
    bo_hbm,
    g1_hbm,
    s1_hbm,
    w1_hbm,
    b1_hbm,
    w2_hbm,
    b2_hbm,
    g2_hbm,
    s2_hbm,
    cot_hbm,
    out_hbm,
    dx_hbm,
    total,
    small_hbm,
    bias_hbm,
    blocks_ref,
    x_ref,
    qb_ref,
    vb_ref,
    bo_ref,
    g1_ref,
    s1_ref,
    b1_ref,
    b2_ref,
    g2_ref,
    s2_ref,
    out_ref,
    dx_ref,
    small_ref,
    we,
    wo,
    w1,
    w2,
    cot,
    load_sem,
    wh_t,
    xall,
    ids_send,
    ids_all,
    ids,
    send_last,
    qkv,
    krow,
    vrow,
    probs,
    inv_total,
    out_wide,
    out_low,
    att_t,
    hat1,
    rstd1,
    low1,
    hidden,
    slope,
    grad_inner,
    grad_outer,
    grad_resid,
    grad_branch,
    gatt_t,
    dout_t,
    dqkv,
    dk_acc,
    dv_acc,
    gpacked_t,
    entry_acc,
    entry_part,
    entry_in,
    part,
    landed,
    small_in,
    bias_own,
    bias_in,
    bias_all,
    bias_rows,
    x_send,
    x_recv,
    i_send,
    i_recv,
    l_send,
    l_recv,
    o_send,
    o_recv,
    d_send,
    d_recv,
    p_send,
    p_recv,
    rs_send,
    rs_recv,
    e_send,
    e_recv,
    v_send,
    v_recv,
    b_send,
    b_recv,
    store_sem,
    second_round,
    third_round,
):
    seqs, tokens, width = x_ref.shape
    place = Place(groups)
    me = place.me
    barrier = pltpu.get_barrier_semaphore()
    neighbours = 3 + (place.z > 0).astype(jnp.int32) + (place.z < groups - 1).astype(jnp.int32)

    def greet(sem):
        for k in (1, 2, 4):
            pl.semaphore_signal(sem, inc=1, device_id=place.in_plane(k), device_id_type=MESH)

        @pl.when(place.z > 0)
        def _():
            pl.semaphore_signal(sem, inc=1, device_id=(place.z - 1, me), device_id_type=MESH)

        @pl.when(place.z < groups - 1)
        def _():
            pl.semaphore_signal(sem, inc=1, device_id=(place.z + 1, me), device_id_type=MESH)

    greet(barrier)

    def load(*pairs):
        copies = []
        for src, dst in pairs:
            copies.append(pltpu.make_async_copy(src, dst, load_sem.at[len(loads)]))
            copies[-1].start()
            loads.append(copies[-1])
        return copies

    loads = []
    load_x = load((x_hbm, x_ref))
    load_blocks = load((blocks_hbm, blocks_ref))
    def lanes_of(device):
        return pl.ds(aligned(device * tokens, 128), tokens)

    def head_rows_of(device):
        return pl.ds(aligned(device * HEAD, HEAD), HEAD)

    def seq_lanes(s):
        return pl.ds(aligned(s * tokens, 128), tokens)

    def vec(ref):
        return ref[...].astype(single).reshape(1, ref.shape[0])

    others = HEADS - 1

    def take(ref, sem):
        remote(ref, ref, sem, sem, place.in_plane(1)).wait_recv()

    def gone(ref, sem):
        remote(ref, ref, sem, sem, place.in_plane(1)).wait_send()

    small_ref[...] = jnp.zeros(small_ref.shape, single)
    bias_rows[...] = jnp.zeros(bias_rows.shape, single)
    bias_own[...] = jnp.zeros(bias_own.shape, single)
    entry_acc[...] = jnp.zeros(entry_acc.shape, single)

    load_x[0].wait()
    pl.semaphore_wait(barrier, neighbours)
    greet(second_round)

    half_width = width // 2

    def x_copy(s, k):
        return remote(
            x_ref.at[s],
            xall.at[s, lanes_of(me), :],
            x_send,
            x_recv.at[s, 2 if k == 1 else 0],
            place.in_plane(k),
        )

    def x_across(s, k):
        columns = slice(0, half_width) if k == 2 else slice(half_width, width)
        slab = xall.at[s, lanes_of(place.peer(6 - k)), columns]
        return remote(slab, slab, x_send, x_recv.at[s, 1], place.in_plane(k))

    def x_forward(s, k):
        slab = xall.at[s, lanes_of(place.peer(k)), :]
        return remote(slab, slab, x_send, x_recv.at[s, 2], place.in_plane(1))

    def x_arrived(s, which):
        slabs = (2, 1, 4)[which]
        take(xall.at[s, 0 : slabs * tokens, :], x_recv.at[s, which])

    def x_begin(s):
        for k in (2, 4, 1):
            x_copy(s, k).start()

    def x_pass(s):
        x_arrived(s, 0)
        for k in (2, 4):
            x_across(s, k).start()
            x_forward(s, k).start()

    def ids_copy(k):
        other = place.peer(k)
        return remote(
            ids_send.at[other],
            ids_all.at[:, lanes_of(me)],
            i_send,
            i_recv,
            place.in_plane(k),
        )

    x_begin(0)
    load_entry = load((we_hbm, we), (qb_hbm, qb_ref), (vb_hbm, vb_ref))
    x_begin(1)
    load_rest = load(
        (wo_hbm, wo),
        (bo_hbm, bo_ref),
        (g1_hbm, g1_ref),
        (s1_hbm, s1_ref),
        (w1_hbm, w1),
        (b1_hbm, b1_ref),
        (w2_hbm, w2),
        (b2_hbm, b2_ref),
        (g2_hbm, g2_ref),
        (s2_hbm, s2_ref),
        (cot_hbm, cot),
    )
    for s in range(seqs):
        xall[s, lanes_of(me), :] = x_ref[s]

    load_blocks[0].wait()

    lane = lax.broadcasted_iota(jnp.int32, (16, tokens), 1)
    row = lax.broadcasted_iota(jnp.int32, (16, tokens), 0)
    for h in range(HEADS):
        numbers = jnp.zeros((16, tokens), jnp.int32)
        for s in range(seqs):
            for j in range(3):
                picked = jnp.where(
                    lane < BLOCK, blocks_ref[s, j, 0, h], blocks_ref[s, j, 1, h]
                )
                numbers = jnp.where(row == s * 3 + j, picked, numbers)
        ids_send[h] = numbers.astype(single).astype(bfloat)
    last = seqs - 1
    head_share = 3 * HEAD

    def last_copy(k):
        return remote(
            send_last.at[place.peer(k)],
            qkv.at[last, 0:head_share, lanes_of(me)],
            l_send,
            l_recv,
            place.in_plane(k),
        )

    def pack_last():
        packed = jnp.dot(x_ref[last], we[...], preferred_element_type=single)
        for j, bias in enumerate((qb_ref, None, vb_ref)):
            piece = packed[:, j * width : (j + 1) * width]
            if bias is not None:
                piece = piece + vec(bias)
            if j == 0:
                piece = piece * HEAD**-0.5
            piece = piece.astype(bfloat).T
            for h in range(HEADS):
                send_last[h, j * HEAD : (j + 1) * HEAD, :] = piece[h * HEAD : (h + 1) * HEAD]
        qkv[last, 0:head_share, lanes_of(me)] = send_last[me]
        qkv[last, head_share:, :] = jnp.ones((16, qkv.shape[2]), bfloat)

    for copy in load_entry:
        copy.wait()
    pack_last()
    pair = me // 2
    odd = me % 2
    for j in range(3):
        columns = we[:, pl.ds(aligned(j * width + pair * 2 * HEAD, 128), 2 * HEAD)].T
        wh_t[j * HEAD : (j + 1) * HEAD, :] = jnp.where(
            odd == 1, columns[HEAD:], columns[:HEAD]
        )
    spread = lax.broadcasted_iota(jnp.int32, (HEAD, width), 1) == me * HEAD + (
        lax.broadcasted_iota(jnp.int32, (HEAD, width), 0)
    )

    pl.semaphore_wait(second_round, neighbours)
    greet(third_round)

    def column(ref):
        return jnp.sum(jnp.where(spread, vec(ref), 0.0), axis=1, keepdims=True)

    query_column = column(qb_ref)
    value_column = column(vb_ref)

    ids_all[:, lanes_of(me)] = ids_send[me]
    pl.semaphore_wait(third_round, neighbours)
    for k in range(1, 8):
        ids_copy(k).start()
    x_pass(0)
    last_copy(6).start()
    x_pass(1)
    for k in (7, 2, 3, 4, 5, 1):
        last_copy(k).start()
    take(ids_all.at[:, 0 : others * tokens], i_recv)
    for s in range(seqs):
        ids[s, 0:3, :] = ids_all[...].astype(single)[3 * s : 3 * s + 3]

    length = qkv.shape[2]
    chunks = length // QUERIES
    blocks = length // BLOCK
    key_block = lax.broadcasted_iota(jnp.int32, (blocks, QUERIES), 0)
    query_lane = lax.broadcasted_iota(jnp.int32, (blocks, QUERIES), 1)

    def out_copy(s, k):
        return remote(
            out_low.at[s, :, lanes_of(place.peer(k))],
            att_t.at[head_rows_of(me), seq_lanes(s)],
            o_send,
            o_recv.at[s],
            place.in_plane(k),
        )

    def take_x(s):
        @pl.when(s < last)
        def _():
            x_arrived(s, 1)
            x_forward(s, 6).start()
            x_arrived(s, 2)
            packed = dot(wh_t[...], xall[s], 1, 1)
            qkv[s, 0:HEAD, :] = ((packed[0:HEAD] + query_column) * HEAD**-0.5).astype(bfloat)
            qkv[s, HEAD : 2 * HEAD, :] = packed[HEAD : 2 * HEAD].astype(bfloat)
            qkv[s, 2 * HEAD : head_share, :] = (packed[2 * HEAD :] + value_column).astype(bfloat)
            qkv[s, head_share:, :] = jnp.ones((16, length), bfloat)

        @pl.when(s == last)
        def _():
            take(qkv.at[last, 0:head_share, 0 : others * tokens], l_recv)

    def attend(s, _):
        take_x(s)
        krow[s] = qkv[s, HEAD : 2 * HEAD, :].T
        vrow[s] = qkv[s, 2 * HEAD : 3 * HEAD, :].T

        def chunk(i, _):
            at = pl.ds(aligned(i * QUERIES, QUERIES), QUERIES)
            query_block = (i * QUERIES + query_lane) // BLOCK
            inside = (key_block >= 1) & (key_block <= blocks - 2)
            near = (key_block >= query_block - 1) & (key_block <= query_block + 1) & inside
            times = jnp.where(near, 1.0, 0.0) + jnp.where(inside, 0.0, 1.0)
            for j in range(3):
                times = times + jnp.where(
                    ids[s, j : j + 1, at] == key_block.astype(single), 1.0, 0.0
                )
            bias = jnp.where(times > 1.5, 0.6931471805599453, 0.0)
            bias = jnp.where(times > 0.5, bias, NEGATIVE)
            bias = jnp.where((query_block == 0) | (query_block == blocks - 1), 0.0, bias)
            score = jnp.dot(krow[s], qkv[s, 0:HEAD, at], preferred_element_type=single)
            score = score.reshape(blocks, BLOCK, QUERIES) + bias[:, None, :]
            score = score.reshape(length, QUERIES)
            peak = jnp.max(score, axis=0, keepdims=True)
            grown = jnp.exp(score - peak)
            grown = grown.astype(bfloat)
            probs[s, :, at] = grown
            summed = jnp.dot(qkv[s, 2 * HEAD :, :], grown, preferred_element_type=single)
            inverse = 1.0 / summed[HEAD : HEAD + 1]
            inv_total[s, :, at] = inverse
            result = inverse * summed[0:HEAD]
            out_wide[s, :, at] = result
            out_low[s, :, at] = result.astype(bfloat)
            return 0

        lax.fori_loop(0, chunks, chunk, 0)
        for k in (6, 7, 2, 3, 4, 5, 1):
            out_copy(s, k).start()
        att_t[head_rows_of(me), seq_lanes(s)] = out_low[s, :, lanes_of(me)]
        return 0

    lax.fori_loop(0, seqs, attend, 0)
    x_begin(last)
    for copy in load_rest:
        copy.wait()

    def dout_copy(s, k):
        return remote(
            gatt_t.at[head_rows_of(place.peer(k)), seq_lanes(s)],
            dout_t.at[s, :, lanes_of(me)],
            d_send,
            d_recv.at[s],
            place.in_plane(k),
        )

    def mean_of(value):
        return jnp.mean(value, axis=-1, keepdims=True)

    def add_small(row, value):
        small_ref[row : row + 1, :] += jnp.sum(value, axis=0, keepdims=True)

    ff = hidden.shape[1]

    def store(which, s):
        src, dst = ((out_ref, out_hbm), (dx_ref, dx_hbm))[which]
        return pltpu.make_async_copy(src.at[s], dst.at[s], store_sem.at[which])

    def forward(first_seq, last_seq):
        for s in range(first_seq, last_seq):
            take(att_t.at[0 : others * HEAD, seq_lanes(s)], o_recv.at[s])
        here = slice(first_seq * tokens, last_seq * tokens)
        count = (last_seq - first_seq) * tokens
        branch = dot(att_t[:, here], wo[...], 0, 0) + vec(bo_ref)
        resid = x_ref[first_seq:last_seq].reshape(count, width).astype(single) + branch
        center = resid - mean_of(resid)
        scale1 = lax.rsqrt(mean_of(center * center) + EPSILON)
        normed1 = center * scale1
        hat1[here, :] = normed1
        rstd1[here, :] = scale1
        first = normed1 * vec(g1_ref) + vec(s1_ref)
        first_low = first.astype(bfloat)
        low1[here, :] = first_low
        second = first + vec(b2_ref)
        bias1 = vec(b1_ref)
        for j in range(ff // WIDE):
            span = slice(j * WIDE, (j + 1) * WIDE)
            pre = jnp.dot(first_low, w1[:, span], preferred_element_type=single) + bias1[:, span]
            share = 0.5 * (1.0 + lax.erf(pre * INV_SQRT2))
            active = (pre * share).astype(bfloat)
            hidden[here, span] = active
            slope[here, span] = share + pre * jnp.exp(-0.5 * pre * pre) * INV_SQRT_2PI
            second = second + jnp.dot(active, w2[span, :], preferred_element_type=single)
        center = second - mean_of(second)
        scale2 = lax.rsqrt(mean_of(center * center) + EPSILON)
        normed2 = center * scale2
        result = (normed2 * vec(g2_ref) + vec(s2_ref)).astype(bfloat)
        out_ref[first_seq:last_seq] = result.reshape(last_seq - first_seq, tokens, width)
        for s in range(first_seq, last_seq):
            store(0, s).start()
        incoming = cot[first_seq:last_seq].reshape(count, width).astype(single)
        add_small(10, incoming * normed2)
        add_small(11, incoming)
        scaled = incoming * vec(g2_ref)
        grad_second = scale2 * (
            scaled - mean_of(scaled) - normed2 * mean_of(scaled * normed2)
        )
        grad_resid[here, :] = grad_second
        grad_low = grad_second.astype(bfloat)
        grad_outer[here, :] = grad_low
        add_small(9, grad_low.astype(single))

    for group in FORWARD:
        forward(*group)
    x_pass(last)

    def stages_of(unit):
        base, count, order = units[unit]
        size = count // 2
        start = base + place.core * size
        stages = [("c", start, base + (1 - place.core) * size, size)]
        for axis in order:
            if axis == "z":
                size = size // groups
                stages.append((axis, start + place.z * size, start, size))
                start = start + place.z * size
            else:
                size = size // 2
                index = {"x": place.x, "y": place.y, "u": place.z % 2, "v": place.z // 2}[axis]
                stages.append((axis, start + index * size, start + (1 - index) * size, size))
                start = start + index * size
        return stages

    def partner(axis):
        if axis in "uv":
            step = 1 if axis == "u" else 2
            bit = (place.z // step) % 2
            return (place.z + step * (1 - 2 * bit), me)
        return place.in_plane({"c": 1, "x": 2, "y": 4}[axis])

    def rows_at(start, count):
        return pl.ds(aligned(start, 16), count)

    def landing(unit, stage):
        before = 0
        for other in range(unit):
            before += units[other][1]
        for earlier in range(stage):
            axis, _, _, size = stages_of(unit)[earlier]
            before += size * (groups - 1 if axis == "z" else 1)
        return before

    def reduce_copies(unit, stage):
        axis, _, away, size = stages_of(unit)[stage]
        at = landing(unit, stage)
        send, recv = rs_send.at[unit], rs_recv.at[unit, stage]
        if axis != "z":
            return [
                remote(
                    part.at[rows_at(away, size), :],
                    landed.at[at : at + size, :],
                    send,
                    recv,
                    partner(axis),
                )
            ]
        return [
            remote(
                part.at[rows_at(away + ((place.z + offset) % groups) * size, size), :],
                landed.at[at + (offset - 1) * size : at + offset * size, :],
                send,
                recv,
                place.in_column(offset),
            )
            for offset in range(1, groups)
        ]

    def reduce_start(unit, stage):
        for copy in reduce_copies(unit, stage):
            copy.start()

    def reduce_finish(unit, stage):
        axis, keep, _, size = stages_of(unit)[stage]
        at = landing(unit, stage)
        count = groups - 1 if axis == "z" else 1
        arrived = landed.at[at : at + count * size, :]
        gone(arrived, rs_send.at[unit])
        take(arrived, rs_recv.at[unit, stage])
        result = total if stage == len(units[unit][2]) else part
        tile = next(rows for rows in (128, 64, 32, 16) if size % rows == 0)

        def add(i, _):
            mine = rows_at(keep + i * tile, tile)
            if count == 1:
                value = part[mine, :] + landed[rows_at(at + i * tile, tile), :]
            else:
                value = part[mine, :].astype(single)
                for j in range(count):
                    other = landed[rows_at(at + j * size + i * tile, tile), :]
                    value = value + other.astype(single)
            result[mine, :] = value.astype(bfloat)
            return 0

        if size == tile:
            add(0, 0)
        else:
            lax.fori_loop(0, size // tile, add, 0)

    def gather_start(unit, stage):
        axis, keep, _, size = stages_of(unit)[stage]
        slot = total.at[rows_at(keep, size), :]
        send, recv = rs_send.at[unit], rs_recv.at[unit, 5 + stage]
        if axis != "z":
            remote(slot, slot, send, recv, partner(axis)).start()
        else:
            for offset in range(1, groups):
                remote(slot, slot, send, recv, place.in_column(offset)).start()

    def gather_finish(unit, stage):
        axis, _, away, size = stages_of(unit)[stage]
        count = groups - 1 if axis == "z" else 1
        slot = total.at[rows_at(away, count * size), :]
        gone(slot, rs_send.at[unit])
        take(slot, rs_recv.at[unit, 5 + stage])

    def step(unit, stage):
        last = len(units[unit][2])
        if stage < last:
            reduce_finish(unit, stage)
            reduce_start(unit, stage + 1)
        elif stage == last:
            reduce_finish(unit, stage)
            gather_start(unit, last)
        elif stage <= 2 * last:
            gather_finish(unit, 2 * last + 1 - stage)
            gather_start(unit, 2 * last - stage)
        else:
            gather_finish(unit, 0)

    def ready_units(begin, end):
        for unit, (base, count, _) in enumerate(units):
            if begin < base + count <= end:
                reduce_start(unit, 0)

    def steps_at(name, index):
        for at, kind, *what in plan[name]:

            def do():
                small_step(*what) if kind == "small" else step(*what)

            if not isinstance(index, int):
                pl.when(index == at)(do)
            elif index == at:
                do()

    def keep_part(base, value):
        part[base : base + value.shape[0], :] = value.astype(bfloat)

    def small_copy(turn, device):
        return remote(small_ref, small_in.at[turn], v_send, v_recv.at[min(turn, 3)], device)

    def small_arrived(turn, count):
        slot = small_in.at[turn : turn + count]
        gone(slot, v_send)
        take(slot, v_recv.at[turn])

    def in_place_order(mine, others):
        result = jnp.zeros(mine.shape, single)
        for source in range(groups):
            for offset in range(groups):
                term = mine if offset == 0 else others[offset - 1]
                result = result + jnp.where(
                    (place.z + groups - offset) % groups == source, term, 0.0
                )
        return result

    small_store = pltpu.make_async_copy(small_ref, small_hbm, store_sem.at[2])

    def small_step(stage):
        if stage > 0 and stage < 4:
            small_arrived(stage - 1, 1)
            small_ref[...] += small_in[stage - 1]
        if stage < 3:
            small_copy(stage, place.in_plane(2**stage)).start()
        elif stage == 3:
            for offset in range(1, groups):
                small_copy(2 + offset, place.in_column(offset)).start()
        else:
            if groups > 1:
                small_arrived(3, groups - 1)
            terms = [small_in[2 + offset] for offset in range(1, groups)]
            small_ref[...] = in_place_order(small_ref[...], terms)
            small_store.start()

    ticks = iter(range(100))

    def tick():
        steps_at("early", next(ticks))

    def outer_tile(start):
        at = slice(start, start + TILES)
        keep_part(start, dot(hidden[:, at], grad_outer[...], 0, 0))
        ready_units(start, start + TILES)
        tick()

    def inner_tile(start):
        for j in range(start, start + TILES, WIDE):
            keep_part(ff + j, dot(low1[...], grad_inner[:, j : j + WIDE], 0, 0))
        ready_units(ff + start, ff + start + TILES)
        tick()

    def backward(first_seq, last_seq):
        here = slice(first_seq * tokens, last_seq * tokens)
        back = grad_resid[here, :]
        grad_low = grad_outer[here, :]
        for j in range(ff // WIDE):
            span = slice(j * WIDE, (j + 1) * WIDE)
            grad_hidden = dot(grad_low, w2[span, :], 1, 1)
            inner = (grad_hidden * slope[here, span]).astype(bfloat)
            grad_inner[here, span] = inner
            add_small(5 + j, inner.astype(single))
            back = back + dot(inner, w1[:, span], 1, 1)
            if j % 2 == 1:
                tick()
        normed1 = hat1[here, :]
        add_small(3, back * normed1)
        add_small(4, back)
        scaled = back * vec(g1_ref)
        grad = rstd1[here, :] * (scaled - mean_of(scaled) - normed1 * mean_of(scaled * normed1))
        grad_resid[here, :] = grad
        grad = grad.astype(bfloat)
        grad_branch[here, :] = grad
        add_small(2, grad.astype(single))
        gatt_t[:, here] = dot(wo[...], grad, 1, 1).astype(bfloat)
        for s in range(first_seq, last_seq):
            for k in (6, 7, 2, 3, 4, 5, 1):
                dout_copy(s, k).start()
        for s in range(first_seq, last_seq):
            dout_t[s, :, lanes_of(me)] = gatt_t[head_rows_of(me), seq_lanes(s)]
        tick()

    def out_tile():
        keep_part(2 * ff, jnp.dot(att_t[...], grad_branch[...], preferred_element_type=single))
        ready_units(2 * ff, 2 * ff + width)
        tick()

    for kind, *what in EARLY:
        if kind == "out":
            x_arrived(last, 1)
            x_forward(last, 6).start()
        {"outer": outer_tile, "back": backward, "inner": inner_tile, "out": out_tile}[kind](*what)

    def pack_copies(s, k):
        other = place.peer(k)
        return [
            remote(
                dqkv.at[s, j * HEAD : (j + 1) * HEAD, lanes_of(other)],
                gpacked_t.at[j, head_rows_of(me), seq_lanes(s)],
                p_send,
                p_recv,
                place.in_plane(k),
            )
            for j in range(3)
        ]

    turns = length // BACK_QUERIES

    def back_math(s, i):
        at = pl.ds(aligned(i * BACK_QUERIES, BACK_QUERIES), BACK_QUERIES)
        cot_t = dout_t[s, :, at].astype(single)
        inverse = inv_total[s, :, at]
        cot_low = (cot_t * inverse).astype(bfloat)
        delta = jnp.sum(cot_low.astype(single) * out_wide[s, :, at], axis=0, keepdims=True)
        grown = probs[s, :, at]
        grad = jnp.dot(vrow[s], cot_low, preferred_element_type=single) - delta
        grad = (grown.astype(single) * grad).astype(bfloat)
        query_grad = jnp.dot(qkv[s, HEAD : 2 * HEAD, :], grad, preferred_element_type=single)
        dqkv[s, 0:HEAD, at] = (query_grad.astype(bfloat) * HEAD**-0.5).astype(bfloat)
        return dot(qkv[s, 0:HEAD, at], grad, 1, 1), dot(cot_low, grown, 1, 1)

    def back_chunk(turn, _):
        s = turn // turns
        i = turn % turns

        @pl.when(i == 0)
        def _():
            take(dout_t.at[s, :, 0 : others * tokens], d_recv.at[s])
            dk_acc[...] = jnp.zeros(dk_acc.shape, single)
            dv_acc[...] = jnp.zeros(dv_acc.shape, single)

        key_grad, value_grad = back_math(s, i)
        dk_acc[...] += key_grad
        dv_acc[...] += value_grad

        @pl.when(i == turns - 1)
        def _():
            dqkv[s, HEAD : 2 * HEAD, :] = dk_acc[...].astype(bfloat)
            dqkv[s, 2 * HEAD :, :] = dv_acc[...].astype(bfloat)
            for k in (6, 7, 2, 3, 4, 5, 1):
                for copy in pack_copies(s, k):
                    copy.start()
            for j in range(3):
                gpacked_t[j, head_rows_of(me), seq_lanes(s)] = dqkv[
                    s, j * HEAD : (j + 1) * HEAD, lanes_of(me)
                ]

            @pl.when(s == last)
            def _():
                x_arrived(last, 2)

            entry_acc[...] += jnp.dot(dqkv[s], xall[s], preferred_element_type=single)

        steps_at("attention", turn)
        return 0

    lax.fori_loop(0, seqs * turns, back_chunk, 0)

    entry_base = 2 * ff + width
    fourth = head_share // groups

    def entry_rows(device, z=None):
        start = entry_base + device * head_share
        if z is None:
            return rows_at(start, head_share)
        return rows_at(start + z * fourth, fourth)

    def entry_copy(offset):
        target = (place.z + offset) % groups
        return remote(
            entry_part.at[rows_at(target * fourth, fourth), :],
            entry_in.at[offset - 1],
            e_send.at[0],
            e_recv.at[0],
            place.in_column(offset),
        )

    def entry_back(offset):
        slot = total.at[entry_rows(me, place.z), :]
        return remote(slot, slot, e_send.at[1], e_recv.at[1], place.in_column(offset))

    def entry_plane(owner, to, half, turn=2):
        columns = (slice(0, half_width), slice(half_width, width), slice(0, width))[half]
        slot = total.at[entry_rows(owner), columns]
        return remote(slot, slot, e_send.at[2], e_recv.at[turn], place.in_plane(to))

    def entry_shares(count):
        return total.at[pl.ds(entry_base, count * head_share), :]

    def entry_step(stage):
        if stage == 0:
            entry_part[...] = entry_acc[...].astype(bfloat)
            for offset in range(1, groups):
                entry_copy(offset).start()
        elif stage == 1:
            if groups > 1:
                gone(entry_in, e_send.at[0])
                take(entry_in, e_recv.at[0])
            value = entry_part[rows_at(place.z * fourth, fourth), :].astype(single)
            for offset in range(1, groups):
                value = value + entry_in[offset - 1].astype(single)
            total[entry_rows(me, place.z), :] = value.astype(bfloat)
            for offset in range(1, groups):
                entry_back(offset).start()
        elif stage == 2:
            if groups > 1:
                slot = total.at[pl.ds(entry_base, (groups - 1) * fourth), :]
                gone(slot, e_send.at[1])
                take(slot, e_recv.at[1])
            entry_plane(me, 2, 0).start()
            entry_plane(me, 4, 1).start()
            entry_plane(me, 1, 2, 4).start()
        elif stage == 3:
            take(entry_shares(1), e_recv.at[2])
            for owner in (me, place.peer(2)):
                entry_plane(owner, 4, 0, 3).start()
            for owner in (me, place.peer(4)):
                entry_plane(owner, 2, 1, 3).start()
        elif stage == 4:
            take(entry_shares(2), e_recv.at[3])
            for k in (2, 4, 6):
                entry_plane(place.peer(k), 1, 2, 4).start()
        else:
            take(entry_shares(4), e_recv.at[4])
            gone(entry_shares(7), e_send.at[2])

    bias_store = pltpu.make_async_copy(bias_rows, bias_hbm, store_sem.at[3])

    def bias_column(offset):
        return remote(
            bias_own,
            bias_in.at[offset - 1],
            b_send.at[0],
            b_recv.at[0],
            place.in_column(offset),
        )

    def bias_plane(k, owner):
        slot = bias_all.at[owner]
        return remote(slot, slot, b_send.at[1], b_recv.at[1], place.in_plane(k))

    def bias_step(stage):
        if stage == 0:
            ones = jnp.ones((8, length), bfloat)
            sums = jnp.zeros((8, head_share), single)
            for s in range(seqs):
                sums = sums + dot(ones, dqkv[s], 1, 1)
            bias_own[...] = jnp.concatenate([sums[:, 0:HEAD], sums[:, 2 * HEAD :]], axis=1)
            for offset in range(1, groups):
                bias_column(offset).start()
        elif stage == 1:
            if groups > 1:
                gone(bias_in, b_send.at[0])
                take(bias_in, b_recv.at[0])
            terms = [bias_in[offset - 1] for offset in range(1, groups)]
            bias_all[me] = in_place_order(bias_own[...], terms)
            for k in range(1, 8):
                bias_plane(k, me).start()
        else:
            gone(bias_all.at[0:others], b_send.at[1])
            take(bias_all.at[0:others], b_recv.at[1])
            for at, start in ((0, 0), (1, HEAD)):
                bias_rows[at : at + 1, :] = jnp.concatenate(
                    [bias_all[p, 0:1, start : start + HEAD] for p in range(HEADS)], axis=1
                )
            bias_store.start()


    def input_step():
        take(gpacked_t.at[:, 0 : others * HEAD, :], p_recv)
        grad_in = grad_resid[...]
        for j in range(3):
            grad_in = grad_in + dot(gpacked_t[j], we[:, j * width : (j + 1) * width], 0, 1)
        for s in range(seqs):
            dx_ref[s] = grad_in[s * tokens : (s + 1) * tokens].astype(bfloat)
            store(1, s).start()

    for kind, *what in plan["tail"]:
        if kind == "unit":
            step(*what)
        elif kind == "entry":
            entry_step(*what)
        elif kind == "bias":
            bias_step(*what)
        elif kind == "small":
            small_step(*what)
        else:
            input_step()
    small_store.wait()
    bias_store.wait()
    pltpu.make_async_copy(out_ref, out_hbm, store_sem.at[0]).wait()
    pltpu.make_async_copy(dx_ref, dx_hbm, store_sem.at[1]).wait()
    gone(xall.at[:, 0 : others * tokens, :], x_send)
    gone(ids_all.at[:, 0 : others * tokens], i_send)
    gone(qkv.at[last, 0:head_share, 0 : others * tokens], l_send)
    gone(out_low.at[:, :, 0 : others * tokens], o_send)
    gone(gatt_t.at[0 : others * HEAD, :], d_send)
    gone(dqkv.at[:, :, 0 : others * tokens], p_send)


def widen_kernel(sums, small_hbm, bias_hbm, out_in, dx_in, *refs):
    outs, vectors, scratch = refs[:15], refs[15:23], refs[23:]
    small, bias, passed, inner_bias, outer_v, inner_v, out_v, entry_v = scratch[:8]
    in_sem, out_sem = scratch[8:]
    out_ref, dx_ref, entry, query_b, value_b, out_w, out_b = outs[:7]
    gain1, shift1, inner_w, inner_b, outer_w, outer_b, gain2, shift2 = outs[7:]
    width = WIDE
    ff = outer_w.shape[0]
    pieces = (2 * ff + width) // WIDE
    head_share = 3 * HEAD
    reads = []
    writes = []

    def read(src, dst):
        reads.append(pltpu.make_async_copy(src, dst, in_sem.at[len(reads)]))
        reads[-1].start()

    def write(src, dst):
        writes.append(pltpu.make_async_copy(src, dst, out_sem.at[len(writes)]))
        writes[-1].start()

    read(small_hbm, small)
    read(bias_hbm, bias)
    read(out_in, passed.at[0])
    read(dx_in, passed.at[1])
    for i in range(pieces):
        rows = slice(i * WIDE, (i + 1) * WIDE)
        value = sums[rows, :].astype(single)
        j = i - ff // WIDE
        if j < 0:
            outer_v[rows, :] = value
            write(outer_v.at[rows], outer_w.at[rows])
        elif j < ff // WIDE:
            columns = slice(j * WIDE, (j + 1) * WIDE)
            inner_v[:, columns] = value
            write(inner_v.at[:, columns], inner_w.at[:, columns])
        else:
            out_v[...] = value
            write(out_v, out_w)
    for j in range(3):
        columns = slice(j * width, (j + 1) * width)
        starts = [2 * ff + width + h * head_share + j * HEAD for h in range(HEADS)]
        value = jnp.concatenate([sums[at : at + HEAD, :] for at in starts], axis=0)
        entry_v[:, columns] = value.astype(single).T
        write(entry_v.at[:, columns], entry.at[:, columns])
    for read_done in reads:
        read_done.wait()
    write(passed.at[0], out_ref)
    write(passed.at[1], dx_ref)

    def small_row(at):
        return (bias if at < 2 else small)[at : at + 1, :].reshape(width)

    for j, (ref, at) in enumerate(
        (
            (query_b, 0),
            (value_b, 1),
            (out_b, 2),
            (gain1, 3),
            (shift1, 4),
            (outer_b, 9),
            (gain2, 10),
            (shift2, 11),
        )
    ):
        vectors[j][...] = small_row(at)
        write(vectors[j], ref)
    for j in range(ff // WIDE):
        inner_bias[j * WIDE : (j + 1) * WIDE] = small_row(5 + j)
    write(inner_bias, inner_b)
    for copy in writes:
        copy.wait()


UNITS = (
    (0, 512, "yuxv"),
    (512, 512, "uyxv"),
    (1024, 512, "zxy"),
    (1536, 512, "xyz"),
    (2048, 512, "yxz"),
    (2560, 512, "xyuv"),
    (3072, 512, "zyx"),
    (3584, 512, "xyz"),
    (4096, 512, "xyz"),
)
PLAN = {
    "early": (
        (2, "unit", 0, 0),
        (3, "unit", 1, 0),
        (3, "unit", 2, 0),
        (4, "unit", 3, 0),
        (7, "small", 0),
        (8, "unit", 0, 1),
        (8, "small", 1),
        (9, "unit", 1, 1),
        (10, "unit", 4, 0),
        (10, "unit", 5, 0),
    ),
    "attention": (
        (0, "unit", 3, 1),
        (0, "unit", 6, 0),
        (0, "unit", 7, 0),
        (0, "unit", 8, 0),
        (1, "unit", 2, 1),
        (2, "unit", 0, 2),
        (2, "unit", 1, 2),
        (2, "small", 2),
        (3, "unit", 4, 1),
        (3, "unit", 5, 1),
        (4, "unit", 3, 2),
        (5, "unit", 7, 1),
    ),
    "tail": (
        ("entry", 0),
        ("bias", 0),
        ("unit", 6, 1),
        ("unit", 8, 1),
        ("small", 3),
        ("unit", 3, 3),
        ("unit", 2, 2),
        ("unit", 0, 3),
        ("unit", 5, 2),
        ("entry", 1),
        ("unit", 1, 3),
        ("bias", 1),
        ("small", 4),
        ("unit", 3, 4),
        ("unit", 0, 4),
        ("unit", 5, 3),
        ("unit", 7, 2),
        ("unit", 4, 2),
        ("unit", 6, 2),
        ("unit", 8, 2),
        ("unit", 2, 3),
        ("entry", 2),
        ("unit", 3, 5),
        ("unit", 1, 4),
        ("input",),
        ("bias", 2),
        ("unit", 2, 4),
        ("unit", 0, 5),
        ("unit", 5, 4),
        ("unit", 6, 3),
        ("unit", 7, 3),
        ("entry", 3),
        ("unit", 4, 3),
        ("unit", 8, 3),
        ("unit", 1, 5),
        ("unit", 5, 5),
        ("unit", 3, 6),
        ("unit", 2, 5),
        ("unit", 7, 4),
        ("unit", 0, 6),
        ("unit", 3, 7),
        ("unit", 6, 4),
        ("unit", 4, 4),
        ("unit", 5, 6),
        ("unit", 8, 4),
        ("unit", 7, 5),
        ("entry", 4),
        ("unit", 6, 5),
        ("unit", 1, 6),
        ("unit", 4, 5),
        ("unit", 5, 7),
        ("entry", 5),
        ("unit", 8, 5),
        ("unit", 2, 6),
        ("unit", 0, 7),
        ("unit", 1, 7),
        ("unit", 7, 6),
        ("unit", 2, 7),
        ("unit", 7, 7),
        ("unit", 4, 6),
        ("unit", 5, 8),
        ("unit", 4, 7),
        ("unit", 6, 6),
        ("unit", 5, 9),
        ("unit", 0, 8),
        ("unit", 8, 6),
        ("unit", 6, 7),
        ("unit", 1, 8),
        ("unit", 0, 9),
        ("unit", 8, 7),
        ("unit", 1, 9),
    ),
}


def by_heads(groups):
    def run(inputs, blocks, we, qb, vb, wo, bo, g1, s1, w1, b1, w2, b2, g2, s2, cot):
        seqs, tokens, width = inputs.shape
        ff = w1.shape[1]
        rows = seqs * tokens
        length = tokens * HEADS
        grad_rows = 2 * ff + width
        units = UNITS
        others = max(groups - 1, 1)
        head_share = 3 * HEAD
        vmem = pl.BlockSpec(memory_space=pltpu.VMEM)
        hbm = pl.BlockSpec(memory_space=pl.ANY)
        dma = pltpu.SemaphoreType.DMA

        def shape(*dims):
            return jax.ShapeDtypeStruct(dims, single)

        out, dx, total, small, bias = pl.pallas_call(
            partial(layer_kernel, groups, units, PLAN),
            out_shape=[
                jax.ShapeDtypeStruct(inputs.shape, bfloat),
                jax.ShapeDtypeStruct(inputs.shape, bfloat),
                pltpu.VMEM((grad_rows + HEADS * head_share, width), bfloat),
                shape(16, width),
                shape(8, width),
            ],
            in_specs=[hbm] * 16,
            out_specs=[hbm, hbm, vmem, hbm, hbm],
            scratch_shapes=[
                pltpu.SMEM((seqs, 3, 2, HEADS), jnp.int32),
                pltpu.VMEM(inputs.shape, bfloat),
                pltpu.VMEM(qb.shape, bfloat),
                pltpu.VMEM(vb.shape, bfloat),
                pltpu.VMEM(bo.shape, bfloat),
                pltpu.VMEM(g1.shape, bfloat),
                pltpu.VMEM(s1.shape, bfloat),
                pltpu.VMEM(b1.shape, bfloat),
                pltpu.VMEM(b2.shape, bfloat),
                pltpu.VMEM(g2.shape, bfloat),
                pltpu.VMEM(s2.shape, bfloat),
                pltpu.VMEM(inputs.shape, bfloat),
                pltpu.VMEM(inputs.shape, bfloat),
                pltpu.VMEM((16, width), single),
                pltpu.VMEM(we.shape, bfloat),
                pltpu.VMEM(wo.shape, bfloat),
                pltpu.VMEM(w1.shape, bfloat),
                pltpu.VMEM(w2.shape, bfloat),
                pltpu.VMEM(cot.shape, bfloat),
                dma((16,)),
                pltpu.VMEM((head_share, width), bfloat),
                pltpu.VMEM((seqs, length, width), bfloat),
                pltpu.VMEM((HEADS, 16, tokens), bfloat),
                pltpu.VMEM((16, length), bfloat),
                pltpu.VMEM((seqs, 8, length), single),
                pltpu.VMEM((HEADS, head_share, tokens), bfloat),
                pltpu.VMEM((seqs, head_share + 16, length), bfloat),
                pltpu.VMEM((seqs, length, HEAD), bfloat),
                pltpu.VMEM((seqs, length, HEAD), bfloat),
                pltpu.VMEM((seqs, length, length), bfloat),
                pltpu.VMEM((seqs, 1, length), single),
                pltpu.VMEM((seqs, HEAD, length), single),
                pltpu.VMEM((seqs, HEAD, length), bfloat),
                pltpu.VMEM((width, rows), bfloat),
                pltpu.VMEM((rows, width), single),
                pltpu.VMEM((rows, 1), single),
                pltpu.VMEM((rows, width), bfloat),
                pltpu.VMEM((rows, ff), bfloat),
                pltpu.VMEM((rows, ff), single),
                pltpu.VMEM((rows, ff), bfloat),
                pltpu.VMEM((rows, width), bfloat),
                pltpu.VMEM((rows, width), single),
                pltpu.VMEM((rows, width), bfloat),
                pltpu.VMEM((width, rows), bfloat),
                pltpu.VMEM((seqs, HEAD, length), bfloat),
                pltpu.VMEM((seqs, head_share, length), bfloat),
                pltpu.VMEM((HEAD, length), single),
                pltpu.VMEM((HEAD, length), single),
                pltpu.VMEM((3, width, rows), bfloat),
                pltpu.VMEM((head_share, width), single),
                pltpu.VMEM((head_share, width), bfloat),
                pltpu.VMEM((others, head_share // groups, width), bfloat),
                pltpu.VMEM((grad_rows, width), bfloat),
                pltpu.VMEM((grad_rows, width), bfloat),
                pltpu.VMEM((3 + groups, 16, width), single),
                pltpu.VMEM((8, 2 * HEAD), single),
                pltpu.VMEM((others, 8, 2 * HEAD), single),
                pltpu.VMEM((HEADS, 8, 2 * HEAD), single),
                pltpu.VMEM((8, width), single),
                dma(()),
                dma((seqs, 3)),
                dma(()),
                dma(()),
                dma(()),
                dma(()),
                dma(()),
                dma((seqs,)),
                dma(()),
                dma((seqs,)),
                dma(()),
                dma(()),
                dma((len(units),)),
                dma((len(units), 10)),
                dma((3,)),
                dma((5,)),
                dma(()),
                dma((4,)),
                dma((2,)),
                dma((2,)),
                dma((4,)),
                pltpu.SemaphoreType.REGULAR,
                pltpu.SemaphoreType.REGULAR,
            ],
            compiler_params=pltpu.CompilerParams(
                collective_id=0, has_side_effects=True, vmem_limit_bytes=LAYER_VMEM
            ),
            name="layer",
        )(
            inputs, blocks.transpose(0, 3, 2, 1), we, qb, vb, wo, bo, g1, s1, w1, b1, w2, b2,
            g2, s2, cot,
        )
        pieces = grad_rows // WIDE
        return pl.pallas_call(
            widen_kernel,
            in_specs=[vmem] + [hbm] * 4,
            out_specs=[hbm] * 15,
            out_shape=[
                jax.ShapeDtypeStruct(inputs.shape, bfloat),
                jax.ShapeDtypeStruct(inputs.shape, bfloat),
                shape(width, 3 * width),
                shape(width),
                shape(width),
                shape(width, width),
                shape(width),
                shape(width),
                shape(width),
                shape(width, ff),
                shape(ff),
                shape(ff, width),
                shape(width),
                shape(width),
                shape(width),
            ],
            scratch_shapes=[
                *[pltpu.VMEM((width,), single)] * 8,
                pltpu.VMEM((16, width), single),
                pltpu.VMEM((8, width), single),
                pltpu.VMEM((2, *inputs.shape), bfloat),
                pltpu.VMEM((ff,), single),
                pltpu.VMEM((ff, width), single),
                pltpu.VMEM((width, ff), single),
                pltpu.VMEM((width, width), single),
                pltpu.VMEM((width, 3 * width), single),
                dma((4,)),
                dma((pieces + 14,)),
            ],
            compiler_params=pltpu.CompilerParams(vmem_limit_bytes=WIDEN_VMEM),
            name="widen",
        )(pltpu.with_memory_space_constraint(total, pltpu.VMEM), small, bias, out, dx)

    return run


def solution(mesh):
    in_specs = (
        P("dp", "seq", None),
        P("dp", None, "seq", None),
        P(),
        P(),
        P(),
        P(),
        P(),
        P(),
        P(),
        P(),
        P(),
        P(),
        P(),
        P(),
        P(),
        P("dp", "seq", None),
    )
    out_specs = (
        P("dp", "seq", None),
        P("dp", "seq", None),
        P(),
        P(),
        P(),
        P(),
        P(),
        P(),
        P(),
        P(),
        P(),
        P(),
        P(),
        P(),
        P(),
    )
    heads_fit = mesh.shape["seq"] == HEADS
    plan = by_heads(mesh.shape["dp"]) if heads_fit else on_device
    return jax.shard_map(
        plan, mesh=mesh, in_specs=in_specs, out_specs=out_specs, check_vma=False
    )
```

```python
from functools import partial

import jax
import jax.numpy as jnp
from jax import lax
from jax.experimental import pallas as pl
from jax.experimental.pallas import tpu as pltpu
from jax.sharding import PartitionSpec as P

HEADS = 8
HEAD = 64
BLOCK = 64


HIGHEST = lax.Precision.HIGHEST
EPSILON = 1e-05
NEGATIVE = -1e30


def spread_2(value, axis, root):
    mine = lax.axis_index(axis) == root
    return lax.psum(jnp.where(mine, value, jnp.zeros_like(value)), axis)


def for_sending(value):

    def short(part):
        return part.astype(jnp.bfloat16) if part.dtype == jnp.float32 else part

    return jax.tree.map(short, value)


def extended(block, sides, width):
    for axis, dim in sides:
        count = lax.axis_size(axis)
        forward = [(i, i + 1) for i in range(count - 1)]
        backward = [(target, source) for source, target in forward]
        low = lax.ppermute(
            lax.slice_in_dim(block, block.shape[dim] - width, None, axis=dim), axis, forward
        )
        high = lax.ppermute(lax.slice_in_dim(block, 0, width, axis=dim), axis, backward)
        block = jnp.concatenate([low, block, high], axis=dim)
    return block


def combined_all(part, axis, combine):
    gathered = jax.tree.map(lambda a: lax.all_gather(a, axis), part)

    def take(source):
        return jax.tree.map(lambda a: lax.dynamic_index_in_dim(a, source, 0, False), gathered)

    return lax.fori_loop(
        1, lax.axis_size(axis), lambda source, state: combine(state, take(source)), take(0)
    )


def norm_apply(values, gain_vec, shift_vec):
    center = values - jnp.mean(values, axis=-1, keepdims=True)
    spread = jnp.mean(center * center, axis=-1, keepdims=True)
    return center * lax.rsqrt(spread + EPSILON) * gain_vec + shift_vec


def pair_blocks(row_data, head_count, block_rows):
    seq_count, length_here, full_width = row_data.shape
    head_width = full_width // (2 * head_count)
    shaped = row_data.reshape(
        seq_count, length_here // block_rows, block_rows, 2, head_count, head_width
    )
    return shaped.transpose(0, 4, 1, 2, 3, 5).reshape(
        seq_count, head_count, length_here // block_rows, block_rows, 2 * head_width
    )


def pair_tokens(blocked):
    seq_count, head_count, block_count, block_rows, double_width = blocked.shape
    head_width = double_width // 2
    shaped = blocked.reshape(seq_count, head_count, block_count, block_rows, 2, head_width)
    return shaped.transpose(0, 2, 3, 4, 1, 5).reshape(
        seq_count, block_count * block_rows, 2 * head_count * head_width
    )


def head_rows(row_data, head_count):
    seq_count, length_here, full_width = row_data.shape
    return row_data.reshape(seq_count, length_here, head_count, full_width // head_count).transpose(
        0, 2, 1, 3
    )


def row_heads(split_rows):
    seq_count, head_count, length_here, head_width = split_rows.shape
    return split_rows.transpose(0, 2, 1, 3).reshape(seq_count, length_here, head_count * head_width)


def merge_parts(earlier, later):
    peak_one, total_one, out_one = earlier
    peak_two, total_two, out_two = later
    row_peak = jnp.maximum(peak_one, peak_two)
    factor_one = jnp.exp(peak_one - row_peak)
    factor_two = jnp.exp(peak_two - row_peak)
    return (
        row_peak,
        total_one * factor_one + total_two * factor_two,
        out_one * factor_one[..., None] + out_two * factor_two[..., None],
    )


def share_rows(row_data, root_device):
    return spread_2(row_data, "seq", root_device)


def share_grads(grad_rows, grad_delta, root_device):
    return (
        spread_2(grad_rows.astype(jnp.bfloat16), "seq", root_device).astype(grad_rows.dtype),
        spread_2(for_sending(grad_delta), "seq", root_device).astype(grad_delta.dtype),
    )


def on_device(
    inputs,
    random_blocks,
    entry_weight,
    query_bias,
    value_bias,
    out_weight,
    out_bias,
    norm_gain,
    norm_shift,
    inner_weight,
    inner_bias,
    outer_weight,
    outer_bias,
    final_gain,
    final_shift,
    cotangent,
):
    seq_count, token_count, model_width = inputs.shape
    head_count = HEADS
    head_width = HEAD
    block_rows = BLOCK
    per_dev = token_count // block_rows
    devices = lax.axis_size("seq")
    device = lax.axis_index("seq")
    block_total = devices * per_dev
    request_total = seq_count * head_count * per_dev * 3
    capacity = (request_total + devices - 2) // (devices - 1)
    table_rows = seq_count * head_count * per_dev
    query_scale = head_width ** (-0.5)
    is_first = device == 0
    is_last = device == devices - 1
    bfloat = jnp.bfloat16
    single = jnp.float32
    flat_in = inputs.reshape(-1, model_width)
    entry_out = jnp.dot(flat_in, entry_weight, preferred_element_type=single)
    packed = jnp.concatenate(
        [
            (entry_out[:, :model_width] + query_bias) * query_scale,
            entry_out[:, model_width : 2 * model_width],
            entry_out[:, 2 * model_width :] + value_bias,
        ],
        axis=1,
    )
    packed = packed.astype(bfloat).reshape(seq_count, token_count, 3 * model_width)
    key_value = packed[:, :, model_width:]
    padded = extended(key_value, (("seq", 1),), block_rows)
    global_rows = jnp.concatenate(
        [
            share_rows(packed[:, :block_rows], 0),
            share_rows(packed[:, token_count - block_rows :], devices - 1),
        ],
        axis=1,
    )
    owners = (random_blocks // per_dev).reshape(-1)
    within = random_blocks % per_dev
    seq_index = lax.broadcasted_iota(jnp.int32, random_blocks.shape, 0)
    head_index = lax.broadcasted_iota(jnp.int32, random_blocks.shape, 1)
    request_codes = ((seq_index * head_count + head_index) * per_dev + within).reshape(-1)
    onehot = (owners[:, None] == jnp.arange(devices, dtype=jnp.int32)[None, :]).astype(jnp.int32)
    slot_index = jnp.sum((jnp.cumsum(onehot, axis=0) - onehot) * onehot, axis=1)
    slot_place = owners * capacity + slot_index
    requests = (
        jnp.full((devices * capacity,), -1, jnp.int32)
        .at[slot_place]
        .set(request_codes)
        .reshape(devices, capacity)
    )
    incoming = lax.all_to_all(requests, "seq", split_axis=0, concat_axis=0, tiled=True)
    head_table = pair_blocks(key_value, head_count, block_rows).reshape(
        table_rows, block_rows, 2 * head_width
    )
    served = head_table[jnp.maximum(incoming, 0)]
    served = jnp.where((incoming >= 0)[:, :, None, None], served, jnp.zeros((), bfloat))
    fetched = lax.all_to_all(served, "seq", split_axis=0, concat_axis=0, tiled=True)
    random_kv = fetched.reshape(devices * capacity, block_rows, 2 * head_width)[slot_place]
    random_kv = random_kv.reshape(seq_count, head_count, per_dev, 3, block_rows, 2 * head_width)
    window_view = pair_blocks(padded, head_count, block_rows)
    window_kv = jnp.stack(
        [window_view[:, :, :per_dev], window_view[:, :, 1 : per_dev + 1], window_view[:, :, 2:]],
        axis=3,
    )
    global_kv = pair_blocks(global_rows[:, :, model_width:], head_count, block_rows)
    global_kv = jnp.broadcast_to(
        global_kv[:, :, None], (seq_count, head_count, per_dev, 2, block_rows, 2 * head_width)
    )
    all_kv = jnp.concatenate([window_kv, global_kv, random_kv], axis=3).reshape(
        seq_count, head_count, per_dev, 8 * block_rows, 2 * head_width
    )
    key_part = all_kv[..., :head_width]
    value_part = all_kv[..., head_width:]
    query_view = head_rows(packed[:, :, :model_width], head_count).reshape(
        seq_count, head_count, per_dev, block_rows, head_width
    )
    block_ids = device * per_dev + jnp.arange(per_dev)[:, None]
    column = jnp.arange(8 * block_rows)[None, :]
    neighbor = block_ids + column // block_rows - 1
    key_keep = (column >= 3 * block_rows) | (neighbor >= 1) & (neighbor <= block_total - 2)
    key_keep = key_keep[None, None, :, None, :]

    def block_scores():
        raw_scores = jnp.einsum(
            "shiqd,shikd->shiqk", query_view, key_part, preferred_element_type=single
        )
        return jnp.where(key_keep, raw_scores, NEGATIVE)

    scores = block_scores()
    row_peak = jnp.max(scores, axis=-1, keepdims=True)
    exponent = jnp.exp(scores - row_peak)
    row_total = jnp.sum(exponent, axis=-1, keepdims=True)
    probability = exponent / row_total
    log_total = row_peak + jnp.log(row_total)
    prob_low = probability.astype(bfloat)
    window_out = jnp.einsum(
        "shiqk,shikd->shiqd", prob_low, value_part, preferred_element_type=single
    )
    global_query = head_rows(global_rows[:, :, :model_width], head_count)
    local_keys = head_rows(packed[:, :, model_width : 2 * model_width], head_count)
    local_values = head_rows(packed[:, :, 2 * model_width :], head_count)
    global_scores = jnp.einsum(
        "shqd,shkd->shqk", global_query, local_keys, preferred_element_type=single
    )
    global_peak = jnp.max(global_scores, axis=-1)
    global_exp = jnp.exp(global_scores - global_peak[..., None])
    global_total = jnp.sum(global_exp, axis=-1)
    global_sum = jnp.einsum(
        "shqk,shkd->shqd", global_exp, local_values.astype(single), precision=HIGHEST
    )
    global_peak, global_total, global_sum = combined_all(
        (global_peak, global_total, global_sum), "seq", merge_parts
    )
    global_out = global_sum / global_total[..., None]
    global_log = global_peak + jnp.log(global_total)
    block_pos = jnp.arange(per_dev)
    take_first = ((block_pos == 0) & is_first)[None, None, :, None, None]
    take_last = ((block_pos == per_dev - 1) & is_last)[None, None, :, None, None]
    combined = jnp.where(take_first, global_out[:, :, None, :block_rows], window_out)
    combined = jnp.where(take_last, global_out[:, :, None, block_rows:], combined)
    attended = (
        row_heads(combined.reshape(seq_count, head_count, token_count, head_width))
        .reshape(-1, model_width)
        .astype(bfloat)
    )
    branch = jnp.dot(attended, out_weight, preferred_element_type=single) + out_bias
    residual_in = flat_in.astype(single) + branch
    first_norm, first_pull = jax.vjp(
        norm_apply, residual_in, norm_gain.astype(single), norm_shift.astype(single)
    )
    first_low = first_norm.astype(bfloat)
    inner_pre = jnp.dot(first_low, inner_weight, preferred_element_type=single) + inner_bias
    activated, gelu_pull = jax.vjp(partial(jax.nn.gelu, approximate=False), inner_pre)
    hidden = activated.astype(bfloat)
    second = first_norm + (
        jnp.dot(hidden, outer_weight, preferred_element_type=single) + outer_bias
    )
    final_norm, final_pull = jax.vjp(
        norm_apply, second, final_gain.astype(single), final_shift.astype(single)
    )
    layer_out = final_norm.astype(bfloat).reshape(inputs.shape)
    grad_second, final_gain_grad, final_shift_grad = final_pull(
        cotangent.reshape(-1, model_width).astype(single)
    )
    grad_outer = grad_second.astype(bfloat)
    outer_weight_grad = jnp.dot(hidden.T, grad_outer, preferred_element_type=single)
    outer_bias_grad = jnp.sum(grad_outer.astype(single), axis=0)
    (grad_active,) = gelu_pull(jnp.dot(grad_outer, outer_weight.T, preferred_element_type=single))
    grad_inner = grad_active.astype(bfloat)
    inner_weight_grad = jnp.dot(first_low.T, grad_inner, preferred_element_type=single)
    inner_bias_grad = jnp.sum(grad_inner.astype(single), axis=0)
    grad_first = grad_second + jnp.dot(grad_inner, inner_weight.T, preferred_element_type=single)
    grad_resid, norm_gain_grad, norm_shift_grad = first_pull(grad_first)
    grad_branch = grad_resid.astype(bfloat)
    out_weight_grad = jnp.dot(attended.T, grad_branch, preferred_element_type=single)
    out_bias_grad = jnp.sum(grad_branch.astype(single), axis=0)
    grad_attended = jnp.dot(grad_branch, out_weight.T, preferred_element_type=single).astype(bfloat)
    grad_heads = head_rows(
        grad_attended.reshape(seq_count, token_count, model_width), head_count
    ).reshape(seq_count, head_count, per_dev, block_rows, head_width)
    grad_window = jnp.where(take_first | take_last, jnp.zeros((), bfloat), grad_heads)
    probability = jnp.exp(block_scores() - log_total)
    prob_low = probability.astype(bfloat)
    grad_prob = jnp.einsum(
        "shiqd,shikd->shiqk", grad_window, value_part, preferred_element_type=single
    )
    row_delta = jnp.sum(probability * grad_prob, axis=-1, keepdims=True)
    grad_scores = (probability * (grad_prob - row_delta)).astype(bfloat)
    grad_query_block = jnp.einsum(
        "shiqk,shikd->shiqd", grad_scores, key_part, preferred_element_type=single
    )
    grad_key_block = jnp.einsum(
        "shiqk,shiqd->shikd", grad_scores, query_view, preferred_element_type=single
    )
    grad_value_block = jnp.einsum(
        "shiqk,shiqd->shikd", prob_low, grad_window, preferred_element_type=single
    )
    grad_kv = jnp.concatenate([grad_key_block, grad_value_block], axis=-1).reshape(
        seq_count, head_count, per_dev, 8, block_rows, 2 * head_width
    )
    pad_none = ((0, 0), (0, 0))
    grad_pad = (
        jnp.pad(grad_kv[:, :, :, 0], pad_none + ((0, 2), (0, 0), (0, 0)))
        + jnp.pad(grad_kv[:, :, :, 1], pad_none + ((1, 1), (0, 0), (0, 0)))
        + jnp.pad(grad_kv[:, :, :, 2], pad_none + ((2, 0), (0, 0), (0, 0)))
    )
    grad_tokens = pair_tokens(grad_pad)
    edge_grads = jnp.concatenate(
        [grad_tokens[:, :block_rows], grad_tokens[:, token_count + block_rows :]], axis=1
    )
    returned = extended(edge_grads.astype(jnp.bfloat16), (("seq", 1),), block_rows).astype(
        edge_grads.dtype
    )
    gap = token_count - block_rows
    grad_kv_local = (
        grad_tokens[:, block_rows : block_rows + token_count]
        + jnp.pad(returned[:, :block_rows], ((0, 0), (0, gap), (0, 0)))
        + jnp.pad(returned[:, 3 * block_rows :], ((0, 0), (gap, 0), (0, 0)))
    )
    grad_global_kv = pair_tokens(jnp.sum(grad_kv[:, :, :, 3:5], axis=2))
    grad_random = grad_kv[:, :, :, 5:8].reshape(request_total, block_rows, 2 * head_width)
    outgoing = (
        jnp.zeros((devices * capacity, block_rows, 2 * head_width), single)
        .at[slot_place]
        .set(grad_random)
    )
    outgoing = outgoing.reshape(devices, capacity, block_rows, 2 * head_width)
    returned_random = lax.all_to_all(
        outgoing.astype(jnp.bfloat16), "seq", split_axis=0, concat_axis=0, tiled=True
    ).astype(outgoing.dtype)
    segment_ids = jnp.where(incoming >= 0, incoming, table_rows).reshape(-1)
    grad_table = jax.ops.segment_sum(
        returned_random.reshape(devices * capacity, block_rows, 2 * head_width),
        segment_ids,
        num_segments=table_rows + 1,
    )[:table_rows]
    grad_owned = pair_tokens(
        grad_table.reshape(seq_count, head_count, per_dev, block_rows, 2 * head_width)
    )
    first_cot = grad_heads[:, :, 0].astype(single)
    last_cot = grad_heads[:, :, per_dev - 1].astype(single)
    first_cot, first_delta = share_grads(
        first_cot, jnp.sum(first_cot * global_out[:, :, :block_rows], axis=-1), 0
    )
    last_cot, last_delta = share_grads(
        last_cot, jnp.sum(last_cot * global_out[:, :, block_rows:], axis=-1), devices - 1
    )
    global_cot = jnp.concatenate([first_cot, last_cot], axis=2)
    global_delta = jnp.concatenate([first_delta, last_delta], axis=2)
    global_prob = jnp.exp(
        jnp.einsum("shqd,shkd->shqk", global_query, local_keys, preferred_element_type=single)
        - global_log[..., None]
    )
    global_dprob = jnp.einsum(
        "shqd,shkd->shqk", global_cot.astype(bfloat), local_values, preferred_element_type=single
    )
    global_grads = (global_prob * (global_dprob - global_delta[..., None])).astype(bfloat)
    grad_global_query = jnp.einsum(
        "shqk,shkd->shqd", global_grads, local_keys, preferred_element_type=single
    )
    grad_local_key = jnp.einsum(
        "shqk,shqd->shkd", global_grads, global_query, preferred_element_type=single
    )
    grad_local_value = jnp.einsum("shqk,shqd->shkd", global_prob, global_cot, precision=HIGHEST)
    partials = jnp.concatenate([row_heads(grad_global_query), grad_global_kv], axis=-1)
    partials = lax.psum(partials.astype(jnp.bfloat16), "seq").astype(jnp.float32)
    owner_part = jnp.where(
        is_first, jnp.pad(partials[:, :block_rows], ((0, 0), (0, gap), (0, 0))), 0.0
    ) + jnp.where(is_last, jnp.pad(partials[:, block_rows:], ((0, 0), (gap, 0), (0, 0))), 0.0)
    grad_query_tokens = row_heads(
        grad_query_block.reshape(seq_count, head_count, token_count, head_width)
    )
    grad_kv_tokens = (
        grad_kv_local
        + grad_owned
        + jnp.concatenate([row_heads(grad_local_key), row_heads(grad_local_value)], axis=-1)
    )
    grad_packed = (
        jnp.concatenate([grad_query_tokens, grad_kv_tokens], axis=-1) + owner_part
    ).astype(bfloat)
    column_scale = jnp.concatenate(
        [jnp.full((model_width,), query_scale, single), jnp.ones((2 * model_width,), single)]
    )
    grad_entry = (
        (grad_packed.astype(single) * column_scale).astype(bfloat).reshape(-1, 3 * model_width)
    )
    entry_weight_grad = jnp.dot(flat_in.T, grad_entry, preferred_element_type=single)
    query_bias_grad = jnp.sum(grad_entry[:, :model_width].astype(single), axis=0)
    value_bias_grad = jnp.sum(grad_entry[:, 2 * model_width :].astype(single), axis=0)
    input_grad = (
        (grad_resid + jnp.dot(grad_entry, entry_weight.T, preferred_element_type=single))
        .astype(bfloat)
        .reshape(inputs.shape)
    )
    (
        total_entry,
        total_query,
        total_value,
        total_out,
        total_out_bias,
        total_norm_gain,
        total_norm_shift,
        total_inner,
        total_inner_bias,
        total_outer,
        total_outer_bias,
        total_final_gain,
        total_final_shift,
    ) = lax.psum(
        (
            entry_weight_grad,
            query_bias_grad,
            value_bias_grad,
            out_weight_grad,
            out_bias_grad,
            norm_gain_grad,
            norm_shift_grad,
            inner_weight_grad,
            inner_bias_grad,
            outer_weight_grad,
            outer_bias_grad,
            final_gain_grad,
            final_shift_grad,
        ),
        ("dp", "seq"),
    )
    return (
        layer_out,
        input_grad,
        total_entry,
        total_query,
        total_value,
        total_out,
        total_out_bias,
        total_norm_gain,
        total_norm_shift,
        total_inner,
        total_inner_bias,
        total_outer,
        total_outer_bias,
        total_final_gain,
        total_final_shift,
    )


MESH = pl.DeviceIdType.MESH
bfloat = jnp.bfloat16
single = jnp.float32
WIDE = 512
QUERIES = 1024
BACK_QUERIES = 512
FORWARD = ((0, 2), (2, 3))
EARLY = (
    ("outer", 0),
    ("outer", 1024),
    ("back", 0, 1),
    ("back", 1, 3),
    ("inner", 0),
    ("inner", 1024),
    ("out",),
)
TILES = 1024
LAYER_VMEM = 56 * 2**20
WIDEN_VMEM = 56 * 2**20
INV_SQRT2 = 0.7071067811865476
INV_SQRT_2PI = 0.3989422804014327


def dot(a, b, a_dim, b_dim):
    return lax.dot_general(
        a, b, (((a_dim,), (b_dim,)), ((), ())), preferred_element_type=single
    )


def aligned(index, step):
    return pl.multiple_of(index, step)


class Place:
    def __init__(self, groups):
        self.groups = groups
        self.z = lax.axis_index("dp")
        self.me = lax.axis_index("seq")
        self.y = self.me // 4
        self.x = (self.me // 2) % 2
        self.core = self.me % 2

    def peer(self, offset):
        off_y, off_x, off_core = offset // 4, (offset // 2) % 2, offset % 2
        return (
            ((self.y + off_y) % 2) * 4
            + ((self.x + off_x) % 2) * 2
            + (self.core + off_core) % 2
        )

    def in_plane(self, offset):
        return (self.z, self.peer(offset))

    def in_column(self, offset):
        return ((self.z + offset) % self.groups, self.me)


def remote(src, dst, send, recv, device):
    return pltpu.make_async_remote_copy(
        src_ref=src,
        dst_ref=dst,
        send_sem=send,
        recv_sem=recv,
        device_id=device,
        device_id_type=MESH,
    )


def layer_kernel(
    groups,
    units,
    plan,
    x_hbm,
    blocks_hbm,
    we_hbm,
    qb_hbm,
    vb_hbm,
    wo_hbm,
    bo_hbm,
    g1_hbm,
    s1_hbm,
    w1_hbm,
    b1_hbm,
    w2_hbm,
    b2_hbm,
    g2_hbm,
    s2_hbm,
    cot_hbm,
    out_hbm,
    dx_hbm,
    total,
    small_hbm,
    bias_hbm,
    blocks_ref,
    x_ref,
    qb_ref,
    vb_ref,
    bo_ref,
    g1_ref,
    s1_ref,
    b1_ref,
    b2_ref,
    g2_ref,
    s2_ref,
    out_ref,
    dx_ref,
    small_ref,
    we,
    wo,
    w1,
    w2,
    cot,
    load_sem,
    wh_t,
    xall,
    ids_send,
    ids_all,
    ids,
    send_last,
    qkv,
    krow,
    vrow,
    probs,
    inv_total,
    out_wide,
    out_low,
    att_t,
    hat1,
    rstd1,
    low1,
    hidden,
    slope,
    grad_inner,
    grad_outer,
    grad_resid,
    grad_branch,
    gatt_t,
    dout_t,
    dqkv,
    dk_acc,
    dv_acc,
    gpacked_t,
    entry_acc,
    entry_part,
    entry_in,
    part,
    landed,
    small_in,
    bias_own,
    bias_in,
    bias_all,
    bias_rows,
    x_send,
    x_recv,
    i_send,
    i_recv,
    l_send,
    l_recv,
    o_send,
    o_recv,
    d_send,
    d_recv,
    p_send,
    p_recv,
    rs_send,
    rs_recv,
    e_send,
    e_recv,
    v_send,
    v_recv,
    b_send,
    b_recv,
    store_sem,
    second_round,
    third_round,
):
    seqs, tokens, width = x_ref.shape
    place = Place(groups)
    me = place.me
    barrier = pltpu.get_barrier_semaphore()
    neighbours = 3 + (place.z > 0).astype(jnp.int32) + (place.z < groups - 1).astype(jnp.int32)

    def greet(sem):
        for k in (1, 2, 4):
            pl.semaphore_signal(sem, inc=1, device_id=place.in_plane(k), device_id_type=MESH)

        @pl.when(place.z > 0)
        def _():
            pl.semaphore_signal(sem, inc=1, device_id=(place.z - 1, me), device_id_type=MESH)

        @pl.when(place.z < groups - 1)
        def _():
            pl.semaphore_signal(sem, inc=1, device_id=(place.z + 1, me), device_id_type=MESH)

    greet(barrier)

    def load(*pairs):
        copies = []
        for src, dst in pairs:
            copies.append(pltpu.make_async_copy(src, dst, load_sem.at[len(loads)]))
            copies[-1].start()
            loads.append(copies[-1])
        return copies

    loads = []
    load_x = load((x_hbm, x_ref))
    load_blocks = load((blocks_hbm, blocks_ref))
    def lanes_of(device):
        return pl.ds(aligned(device * tokens, 128), tokens)

    def head_rows_of(device):
        return pl.ds(aligned(device * HEAD, HEAD), HEAD)

    def seq_lanes(s):
        return pl.ds(aligned(s * tokens, 128), tokens)

    def vec(ref):
        return ref[...].astype(single).reshape(1, ref.shape[0])

    others = HEADS - 1

    def take(ref, sem):
        remote(ref, ref, sem, sem, place.in_plane(1)).wait_recv()

    def gone(ref, sem):
        remote(ref, ref, sem, sem, place.in_plane(1)).wait_send()

    small_ref[...] = jnp.zeros(small_ref.shape, single)
    bias_rows[...] = jnp.zeros(bias_rows.shape, single)
    bias_own[...] = jnp.zeros(bias_own.shape, single)
    entry_acc[...] = jnp.zeros(entry_acc.shape, single)

    load_x[0].wait()
    pl.semaphore_wait(barrier, neighbours)
    greet(second_round)

    half_width = width // 2

    def x_copy(s, k):
        return remote(
            x_ref.at[s],
            xall.at[s, lanes_of(me), :],
            x_send,
            x_recv.at[s, 2 if k == 1 else 0],
            place.in_plane(k),
        )

    def x_across(s, k):
        columns = slice(0, half_width) if k == 2 else slice(half_width, width)
        slab = xall.at[s, lanes_of(place.peer(6 - k)), columns]
        return remote(slab, slab, x_send, x_recv.at[s, 1], place.in_plane(k))

    def x_forward(s, k):
        slab = xall.at[s, lanes_of(place.peer(k)), :]
        return remote(slab, slab, x_send, x_recv.at[s, 2], place.in_plane(1))

    def x_arrived(s, which):
        slabs = (2, 1, 4)[which]
        take(xall.at[s, 0 : slabs * tokens, :], x_recv.at[s, which])

    def x_begin(s):
        for k in (2, 4, 1):
            x_copy(s, k).start()

    def x_pass(s):
        x_arrived(s, 0)
        for k in (2, 4):
            x_across(s, k).start()
            x_forward(s, k).start()

    def ids_copy(k):
        other = place.peer(k)
        return remote(
            ids_send.at[other],
            ids_all.at[:, lanes_of(me)],
            i_send,
            i_recv,
            place.in_plane(k),
        )

    x_begin(0)
    load_entry = load((we_hbm, we), (qb_hbm, qb_ref), (vb_hbm, vb_ref))
    x_begin(1)
    load_rest = load(
        (wo_hbm, wo),
        (bo_hbm, bo_ref),
        (g1_hbm, g1_ref),
        (s1_hbm, s1_ref),
        (w1_hbm, w1),
        (b1_hbm, b1_ref),
        (w2_hbm, w2),
        (b2_hbm, b2_ref),
        (g2_hbm, g2_ref),
        (s2_hbm, s2_ref),
        (cot_hbm, cot),
    )
    for s in range(seqs):
        xall[s, lanes_of(me), :] = x_ref[s]

    load_blocks[0].wait()

    lane = lax.broadcasted_iota(jnp.int32, (16, tokens), 1)
    row = lax.broadcasted_iota(jnp.int32, (16, tokens), 0)
    for h in range(HEADS):
        numbers = jnp.zeros((16, tokens), jnp.int32)
        for s in range(seqs):
            for j in range(3):
                picked = jnp.where(
                    lane < BLOCK, blocks_ref[s, j, 0, h], blocks_ref[s, j, 1, h]
                )
                numbers = jnp.where(row == s * 3 + j, picked, numbers)
        ids_send[h] = numbers.astype(single).astype(bfloat)
    last = seqs - 1
    head_share = 3 * HEAD

    def last_copy(k):
        return remote(
            send_last.at[place.peer(k)],
            qkv.at[last, 0:head_share, lanes_of(me)],
            l_send,
            l_recv,
            place.in_plane(k),
        )

    def pack_last():
        packed = jnp.dot(x_ref[last], we[...], preferred_element_type=single)
        for j, bias in enumerate((qb_ref, None, vb_ref)):
            piece = packed[:, j * width : (j + 1) * width]
            if bias is not None:
                piece = piece + vec(bias)
            if j == 0:
                piece = piece * HEAD**-0.5
            piece = piece.astype(bfloat).T
            for h in range(HEADS):
                send_last[h, j * HEAD : (j + 1) * HEAD, :] = piece[h * HEAD : (h + 1) * HEAD]
        qkv[last, 0:head_share, lanes_of(me)] = send_last[me]
        qkv[last, head_share:, :] = jnp.ones((16, qkv.shape[2]), bfloat)

    for copy in load_entry:
        copy.wait()
    pack_last()
    pair = me // 2
    odd = me % 2
    for j in range(3):
        columns = we[:, pl.ds(aligned(j * width + pair * 2 * HEAD, 128), 2 * HEAD)].T
        wh_t[j * HEAD : (j + 1) * HEAD, :] = jnp.where(
            odd == 1, columns[HEAD:], columns[:HEAD]
        )
    spread = lax.broadcasted_iota(jnp.int32, (HEAD, width), 1) == me * HEAD + (
        lax.broadcasted_iota(jnp.int32, (HEAD, width), 0)
    )

    pl.semaphore_wait(second_round, neighbours)
    greet(third_round)

    def column(ref):
        return jnp.sum(jnp.where(spread, vec(ref), 0.0), axis=1, keepdims=True)

    query_column = column(qb_ref)
    value_column = column(vb_ref)

    ids_all[:, lanes_of(me)] = ids_send[me]
    pl.semaphore_wait(third_round, neighbours)
    for k in range(1, 8):
        ids_copy(k).start()
    x_pass(0)
    last_copy(6).start()
    x_pass(1)
    for k in (7, 2, 3, 4, 5, 1):
        last_copy(k).start()
    take(ids_all.at[:, 0 : others * tokens], i_recv)
    for s in range(seqs):
        ids[s, 0:3, :] = ids_all[...].astype(single)[3 * s : 3 * s + 3]

    length = qkv.shape[2]
    chunks = length // QUERIES
    blocks = length // BLOCK
    key_block = lax.broadcasted_iota(jnp.int32, (blocks, QUERIES), 0)
    query_lane = lax.broadcasted_iota(jnp.int32, (blocks, QUERIES), 1)

    def out_copy(s, k):
        return remote(
            out_low.at[s, :, lanes_of(place.peer(k))],
            att_t.at[head_rows_of(me), seq_lanes(s)],
            o_send,
            o_recv.at[s],
            place.in_plane(k),
        )

    def take_x(s):
        @pl.when(s < last)
        def _():
            x_arrived(s, 1)
            x_forward(s, 6).start()
            x_arrived(s, 2)
            packed = dot(wh_t[...], xall[s], 1, 1)
            qkv[s, 0:HEAD, :] = ((packed[0:HEAD] + query_column) * HEAD**-0.5).astype(bfloat)
            qkv[s, HEAD : 2 * HEAD, :] = packed[HEAD : 2 * HEAD].astype(bfloat)
            qkv[s, 2 * HEAD : head_share, :] = (packed[2 * HEAD :] + value_column).astype(bfloat)
            qkv[s, head_share:, :] = jnp.ones((16, length), bfloat)

        @pl.when(s == last)
        def _():
            take(qkv.at[last, 0:head_share, 0 : others * tokens], l_recv)

    def attend(s, _):
        take_x(s)
        krow[s] = qkv[s, HEAD : 2 * HEAD, :].T
        vrow[s] = qkv[s, 2 * HEAD : 3 * HEAD, :].T

        def chunk(i, _):
            at = pl.ds(aligned(i * QUERIES, QUERIES), QUERIES)
            query_block = (i * QUERIES + query_lane) // BLOCK
            inside = (key_block >= 1) & (key_block <= blocks - 2)
            near = (key_block >= query_block - 1) & (key_block <= query_block + 1) & inside
            times = jnp.where(near, 1.0, 0.0) + jnp.where(inside, 0.0, 1.0)
            for j in range(3):
                times = times + jnp.where(
                    ids[s, j : j + 1, at] == key_block.astype(single), 1.0, 0.0
                )
            bias = jnp.where(times > 1.5, 0.6931471805599453, 0.0)
            bias = jnp.where(times > 0.5, bias, NEGATIVE)
            bias = jnp.where((query_block == 0) | (query_block == blocks - 1), 0.0, bias)
            score = jnp.dot(krow[s], qkv[s, 0:HEAD, at], preferred_element_type=single)
            score = score.reshape(blocks, BLOCK, QUERIES) + bias[:, None, :]
            score = score.reshape(length, QUERIES)
            peak = jnp.max(score, axis=0, keepdims=True)
            grown = jnp.exp(score - peak)
            grown = grown.astype(bfloat)
            probs[s, :, at] = grown
            summed = jnp.dot(qkv[s, 2 * HEAD :, :], grown, preferred_element_type=single)
            inverse = 1.0 / summed[HEAD : HEAD + 1]
            inv_total[s, :, at] = inverse
            result = inverse * summed[0:HEAD]
            out_wide[s, :, at] = result
            out_low[s, :, at] = result.astype(bfloat)
            return 0

        lax.fori_loop(0, chunks, chunk, 0)
        for k in (6, 7, 2, 3, 4, 5, 1):
            out_copy(s, k).start()
        att_t[head_rows_of(me), seq_lanes(s)] = out_low[s, :, lanes_of(me)]
        return 0

    lax.fori_loop(0, seqs, attend, 0)
    x_begin(last)
    for copy in load_rest:
        copy.wait()

    def dout_copy(s, k):
        return remote(
            gatt_t.at[head_rows_of(place.peer(k)), seq_lanes(s)],
            dout_t.at[s, :, lanes_of(me)],
            d_send,
            d_recv.at[s],
            place.in_plane(k),
        )

    def mean_of(value):
        return jnp.mean(value, axis=-1, keepdims=True)

    def add_small(row, value):
        small_ref[row : row + 1, :] += jnp.sum(value, axis=0, keepdims=True)

    ff = hidden.shape[1]

    def store(which, s):
        src, dst = ((out_ref, out_hbm), (dx_ref, dx_hbm))[which]
        return pltpu.make_async_copy(src.at[s], dst.at[s], store_sem.at[which])

    def forward(first_seq, last_seq):
        for s in range(first_seq, last_seq):
            take(att_t.at[0 : others * HEAD, seq_lanes(s)], o_recv.at[s])
        here = slice(first_seq * tokens, last_seq * tokens)
        count = (last_seq - first_seq) * tokens
        branch = dot(att_t[:, here], wo[...], 0, 0) + vec(bo_ref)
        resid = x_ref[first_seq:last_seq].reshape(count, width).astype(single) + branch
        center = resid - mean_of(resid)
        scale1 = lax.rsqrt(mean_of(center * center) + EPSILON)
        normed1 = center * scale1
        hat1[here, :] = normed1
        rstd1[here, :] = scale1
        first = normed1 * vec(g1_ref) + vec(s1_ref)
        first_low = first.astype(bfloat)
        low1[here, :] = first_low
        second = first + vec(b2_ref)
        bias1 = vec(b1_ref)
        for j in range(ff // WIDE):
            span = slice(j * WIDE, (j + 1) * WIDE)
            pre = jnp.dot(first_low, w1[:, span], preferred_element_type=single) + bias1[:, span]
            share = 0.5 * (1.0 + lax.erf(pre * INV_SQRT2))
            active = (pre * share).astype(bfloat)
            hidden[here, span] = active
            slope[here, span] = share + pre * jnp.exp(-0.5 * pre * pre) * INV_SQRT_2PI
            second = second + jnp.dot(active, w2[span, :], preferred_element_type=single)
        center = second - mean_of(second)
        scale2 = lax.rsqrt(mean_of(center * center) + EPSILON)
        normed2 = center * scale2
        result = (normed2 * vec(g2_ref) + vec(s2_ref)).astype(bfloat)
        out_ref[first_seq:last_seq] = result.reshape(last_seq - first_seq, tokens, width)
        for s in range(first_seq, last_seq):
            store(0, s).start()
        incoming = cot[first_seq:last_seq].reshape(count, width).astype(single)
        add_small(10, incoming * normed2)
        add_small(11, incoming)
        scaled = incoming * vec(g2_ref)
        grad_second = scale2 * (
            scaled - mean_of(scaled) - normed2 * mean_of(scaled * normed2)
        )
        grad_resid[here, :] = grad_second
        grad_low = grad_second.astype(bfloat)
        grad_outer[here, :] = grad_low
        add_small(9, grad_low.astype(single))

    for group in FORWARD:
        forward(*group)
    x_pass(last)

    def stages_of(unit):
        base, count, order = units[unit]
        size = count // 2
        start = base + place.core * size
        stages = [("c", start, base + (1 - place.core) * size, size)]
        for axis in order:
            if axis == "z":
                size = size // groups
                stages.append((axis, start + place.z * size, start, size))
                start = start + place.z * size
            else:
                size = size // 2
                index = {"x": place.x, "y": place.y, "u": place.z % 2, "v": place.z // 2}[axis]
                stages.append((axis, start + index * size, start + (1 - index) * size, size))
                start = start + index * size
        return stages

    def partner(axis):
        if axis in "uv":
            step = 1 if axis == "u" else 2
            bit = (place.z // step) % 2
            return (place.z + step * (1 - 2 * bit), me)
        return place.in_plane({"c": 1, "x": 2, "y": 4}[axis])

    def rows_at(start, count):
        return pl.ds(aligned(start, 16), count)

    def recv_slot(unit, stage):
        return sum(2 * len(order) + 2 for _, _, order in units[:unit]) + stage

    def landing(unit, stage):
        before = 0
        for other in range(unit):
            before += units[other][1]
        for earlier in range(stage):
            axis, _, _, size = stages_of(unit)[earlier]
            before += size * (groups - 1 if axis == "z" else 1)
        return before

    def reduce_copies(unit, stage):
        axis, _, away, size = stages_of(unit)[stage]
        at = landing(unit, stage)
        send, recv = rs_send.at[unit], rs_recv.at[recv_slot(unit, stage)]
        if axis != "z":
            return [
                remote(
                    part.at[rows_at(away, size), :],
                    landed.at[at : at + size, :],
                    send,
                    recv,
                    partner(axis),
                )
            ]
        return [
            remote(
                part.at[rows_at(away + ((place.z + offset) % groups) * size, size), :],
                landed.at[at + (offset - 1) * size : at + offset * size, :],
                send,
                recv,
                place.in_column(offset),
            )
            for offset in range(1, groups)
        ]

    def reduce_start(unit, stage):
        for copy in reduce_copies(unit, stage):
            copy.start()

    def reduce_finish(unit, stage):
        axis, keep, _, size = stages_of(unit)[stage]
        at = landing(unit, stage)
        count = groups - 1 if axis == "z" else 1
        arrived = landed.at[at : at + count * size, :]
        gone(arrived, rs_send.at[unit])
        take(arrived, rs_recv.at[recv_slot(unit, stage)])
        result = total if stage == len(units[unit][2]) else part
        tile = next(rows for rows in (128, 64, 32, 16) if size % rows == 0)

        def add(i, _):
            mine = rows_at(keep + i * tile, tile)
            if count == 1:
                value = part[mine, :] + landed[rows_at(at + i * tile, tile), :]
            else:
                value = part[mine, :].astype(single)
                for j in range(count):
                    other = landed[rows_at(at + j * size + i * tile, tile), :]
                    value = value + other.astype(single)
            result[mine, :] = value.astype(bfloat)
            return 0

        if size == tile:
            add(0, 0)
        else:
            lax.fori_loop(0, size // tile, add, 0)

    def gather_start(unit, stage):
        axis, keep, _, size = stages_of(unit)[stage]
        slot = total.at[rows_at(keep, size), :]
        send, recv = rs_send.at[unit], rs_recv.at[recv_slot(unit, len(units[unit][2]) + 1 + stage)]
        if axis != "z":
            remote(slot, slot, send, recv, partner(axis)).start()
        else:
            for offset in range(1, groups):
                remote(slot, slot, send, recv, place.in_column(offset)).start()

    def gather_finish(unit, stage):
        axis, _, away, size = stages_of(unit)[stage]
        count = groups - 1 if axis == "z" else 1
        slot = total.at[rows_at(away, count * size), :]
        gone(slot, rs_send.at[unit])
        take(slot, rs_recv.at[recv_slot(unit, len(units[unit][2]) + 1 + stage)])

    def step(unit, stage):
        last = len(units[unit][2])
        if stage < last:
            reduce_finish(unit, stage)
            reduce_start(unit, stage + 1)
        elif stage == last:
            reduce_finish(unit, stage)
            gather_start(unit, last)
        elif stage <= 2 * last:
            gather_finish(unit, 2 * last + 1 - stage)
            gather_start(unit, 2 * last - stage)
        else:
            gather_finish(unit, 0)

    def ready_units(begin, end):
        for unit, (base, count, _) in enumerate(units):
            if begin < base + count <= end:
                reduce_start(unit, 0)

    def steps_at(name, index):
        for at, kind, *what in plan[name]:

            def do():
                small_step(*what) if kind == "small" else step(*what)

            if not isinstance(index, int):
                pl.when(index == at)(do)
            elif index == at:
                do()

    def keep_part(base, value):
        part[base : base + value.shape[0], :] = value.astype(bfloat)

    def small_copy(turn, device):
        return remote(small_ref, small_in.at[turn], v_send, v_recv.at[min(turn, 3)], device)

    def small_arrived(turn, count):
        slot = small_in.at[turn : turn + count]
        gone(slot, v_send)
        take(slot, v_recv.at[turn])

    def in_place_order(mine, others):
        result = jnp.zeros(mine.shape, single)
        for source in range(groups):
            for offset in range(groups):
                term = mine if offset == 0 else others[offset - 1]
                result = result + jnp.where(
                    (place.z + groups - offset) % groups == source, term, 0.0
                )
        return result

    small_store = pltpu.make_async_copy(small_ref, small_hbm, store_sem.at[2])

    def small_step(stage):
        if stage > 0 and stage < 4:
            small_arrived(stage - 1, 1)
            small_ref[...] += small_in[stage - 1]
        if stage < 3:
            small_copy(stage, place.in_plane(2**stage)).start()
        elif stage == 3:
            for offset in range(1, groups):
                small_copy(2 + offset, place.in_column(offset)).start()
        else:
            if groups > 1:
                small_arrived(3, groups - 1)
            terms = [small_in[2 + offset] for offset in range(1, groups)]
            small_ref[...] = in_place_order(small_ref[...], terms)
            small_store.start()

    ticks = iter(range(100))

    def tick():
        steps_at("early", next(ticks))

    def outer_tile(start):
        at = slice(start, start + TILES)
        keep_part(start, dot(hidden[:, at], grad_outer[...], 0, 0))
        ready_units(start, start + TILES)
        tick()

    def inner_tile(start):
        for j in range(start, start + TILES, WIDE):
            keep_part(ff + j, dot(low1[...], grad_inner[:, j : j + WIDE], 0, 0))
        ready_units(ff + start, ff + start + TILES)
        tick()

    def backward(first_seq, last_seq):
        here = slice(first_seq * tokens, last_seq * tokens)
        back = grad_resid[here, :]
        grad_low = grad_outer[here, :]
        for j in range(ff // WIDE):
            span = slice(j * WIDE, (j + 1) * WIDE)
            grad_hidden = dot(grad_low, w2[span, :], 1, 1)
            inner = (grad_hidden * slope[here, span]).astype(bfloat)
            grad_inner[here, span] = inner
            add_small(5 + j, inner.astype(single))
            back = back + dot(inner, w1[:, span], 1, 1)
            if j % 2 == 1:
                tick()
        normed1 = hat1[here, :]
        add_small(3, back * normed1)
        add_small(4, back)
        scaled = back * vec(g1_ref)
        grad = rstd1[here, :] * (scaled - mean_of(scaled) - normed1 * mean_of(scaled * normed1))
        grad_resid[here, :] = grad
        grad = grad.astype(bfloat)
        grad_branch[here, :] = grad
        add_small(2, grad.astype(single))
        gatt_t[:, here] = dot(wo[...], grad, 1, 1).astype(bfloat)
        for s in range(first_seq, last_seq):
            for k in (6, 7, 2, 3, 4, 5, 1):
                dout_copy(s, k).start()
        for s in range(first_seq, last_seq):
            dout_t[s, :, lanes_of(me)] = gatt_t[head_rows_of(me), seq_lanes(s)]
        tick()

    def out_tile():
        keep_part(2 * ff, jnp.dot(att_t[...], grad_branch[...], preferred_element_type=single))
        ready_units(2 * ff, 2 * ff + width)
        tick()

    for kind, *what in EARLY:
        if kind == "out":
            x_arrived(last, 1)
            x_forward(last, 6).start()
        {"outer": outer_tile, "back": backward, "inner": inner_tile, "out": out_tile}[kind](*what)

    def pack_copies(s, k):
        other = place.peer(k)
        return [
            remote(
                dqkv.at[s, j * HEAD : (j + 1) * HEAD, lanes_of(other)],
                gpacked_t.at[j, head_rows_of(me), seq_lanes(s)],
                p_send,
                p_recv,
                place.in_plane(k),
            )
            for j in range(3)
        ]

    turns = length // BACK_QUERIES

    def back_math(s, i):
        at = pl.ds(aligned(i * BACK_QUERIES, BACK_QUERIES), BACK_QUERIES)
        cot_t = dout_t[s, :, at].astype(single)
        inverse = inv_total[s, :, at]
        cot_low = (cot_t * inverse).astype(bfloat)
        delta = jnp.sum(cot_low.astype(single) * out_wide[s, :, at], axis=0, keepdims=True)
        grown = probs[s, :, at]
        grad = jnp.dot(vrow[s], cot_low, preferred_element_type=single) - delta
        grad = (grown.astype(single) * grad).astype(bfloat)
        query_grad = jnp.dot(qkv[s, HEAD : 2 * HEAD, :], grad, preferred_element_type=single)
        dqkv[s, 0:HEAD, at] = (query_grad.astype(bfloat) * HEAD**-0.5).astype(bfloat)
        return dot(qkv[s, 0:HEAD, at], grad, 1, 1), dot(cot_low, grown, 1, 1)

    def back_chunk(turn, _):
        s = turn // turns
        i = turn % turns

        @pl.when(i == 0)
        def _():
            take(dout_t.at[s, :, 0 : others * tokens], d_recv.at[s])
            dk_acc[...] = jnp.zeros(dk_acc.shape, single)
            dv_acc[...] = jnp.zeros(dv_acc.shape, single)

        key_grad, value_grad = back_math(s, i)
        dk_acc[...] += key_grad
        dv_acc[...] += value_grad

        @pl.when(i == turns - 1)
        def _():
            dqkv[s, HEAD : 2 * HEAD, :] = dk_acc[...].astype(bfloat)
            dqkv[s, 2 * HEAD :, :] = dv_acc[...].astype(bfloat)
            for k in (6, 7, 2, 3, 4, 5, 1):
                for copy in pack_copies(s, k):
                    copy.start()
            for j in range(3):
                gpacked_t[j, head_rows_of(me), seq_lanes(s)] = dqkv[
                    s, j * HEAD : (j + 1) * HEAD, lanes_of(me)
                ]

            @pl.when(s == last)
            def _():
                x_arrived(last, 2)

            entry_acc[...] += jnp.dot(dqkv[s], xall[s], preferred_element_type=single)

        steps_at("attention", turn)
        return 0

    lax.fori_loop(0, seqs * turns, back_chunk, 0)

    entry_base = 2 * ff + width
    fourth = head_share // groups

    def entry_rows(device, z=None):
        start = entry_base + device * head_share
        if z is None:
            return rows_at(start, head_share)
        return rows_at(start + z * fourth, fourth)

    def entry_copy(offset):
        target = (place.z + offset) % groups
        return remote(
            entry_part.at[rows_at(target * fourth, fourth), :],
            entry_in.at[offset - 1],
            e_send.at[0],
            e_recv.at[0],
            place.in_column(offset),
        )

    def entry_back(offset):
        slot = total.at[entry_rows(me, place.z), :]
        return remote(slot, slot, e_send.at[1], e_recv.at[1], place.in_column(offset))

    def entry_plane(owner, to, half, turn=2):
        columns = (slice(0, half_width), slice(half_width, width), slice(0, width))[half]
        slot = total.at[entry_rows(owner), columns]
        return remote(slot, slot, e_send.at[2], e_recv.at[turn], place.in_plane(to))

    def entry_shares(count):
        return total.at[pl.ds(entry_base, count * head_share), :]

    def entry_step(stage):
        if stage == 0:
            entry_part[...] = entry_acc[...].astype(bfloat)
            for offset in range(1, groups):
                entry_copy(offset).start()
        elif stage == 1:
            if groups > 1:
                gone(entry_in, e_send.at[0])
                take(entry_in, e_recv.at[0])
            value = entry_part[rows_at(place.z * fourth, fourth), :].astype(single)
            for offset in range(1, groups):
                value = value + entry_in[offset - 1].astype(single)
            total[entry_rows(me, place.z), :] = value.astype(bfloat)
            for offset in range(1, groups):
                entry_back(offset).start()
        elif stage == 2:
            if groups > 1:
                slot = total.at[pl.ds(entry_base, (groups - 1) * fourth), :]
                gone(slot, e_send.at[1])
                take(slot, e_recv.at[1])
            entry_plane(me, 2, 0).start()
            entry_plane(me, 4, 1).start()
            entry_plane(me, 1, 2, 4).start()
        elif stage == 3:
            take(entry_shares(1), e_recv.at[2])
            for owner in (me, place.peer(2)):
                entry_plane(owner, 4, 0, 3).start()
            for owner in (me, place.peer(4)):
                entry_plane(owner, 2, 1, 3).start()
        elif stage == 4:
            take(entry_shares(2), e_recv.at[3])
            for k in (2, 4, 6):
                entry_plane(place.peer(k), 1, 2, 4).start()
        else:
            take(entry_shares(4), e_recv.at[4])
            gone(entry_shares(7), e_send.at[2])

    bias_store = pltpu.make_async_copy(bias_rows, bias_hbm, store_sem.at[3])

    def bias_column(offset):
        return remote(
            bias_own,
            bias_in.at[offset - 1],
            b_send.at[0],
            b_recv.at[0],
            place.in_column(offset),
        )

    def bias_plane(k, owner):
        slot = bias_all.at[owner]
        return remote(slot, slot, b_send.at[1], b_recv.at[1], place.in_plane(k))

    def bias_step(stage):
        if stage == 0:
            ones = jnp.ones((8, length), bfloat)
            sums = jnp.zeros((8, head_share), single)
            for s in range(seqs):
                sums = sums + dot(ones, dqkv[s], 1, 1)
            bias_own[...] = jnp.concatenate([sums[:, 0:HEAD], sums[:, 2 * HEAD :]], axis=1)
            for offset in range(1, groups):
                bias_column(offset).start()
        elif stage == 1:
            if groups > 1:
                gone(bias_in, b_send.at[0])
                take(bias_in, b_recv.at[0])
            terms = [bias_in[offset - 1] for offset in range(1, groups)]
            bias_all[me] = in_place_order(bias_own[...], terms)
            for k in range(1, 8):
                bias_plane(k, me).start()
        else:
            gone(bias_all.at[0:others], b_send.at[1])
            take(bias_all.at[0:others], b_recv.at[1])
            for at, start in ((0, 0), (1, HEAD)):
                bias_rows[at : at + 1, :] = jnp.concatenate(
                    [bias_all[p, 0:1, start : start + HEAD] for p in range(HEADS)], axis=1
                )
            bias_store.start()


    def input_step():
        take(gpacked_t.at[:, 0 : others * HEAD, :], p_recv)
        grad_in = grad_resid[...]
        for j in range(3):
            grad_in = grad_in + dot(gpacked_t[j], we[:, j * width : (j + 1) * width], 0, 1)
        for s in range(seqs):
            dx_ref[s] = grad_in[s * tokens : (s + 1) * tokens].astype(bfloat)
            store(1, s).start()

    for kind, *what in plan["tail"]:
        if kind == "unit":
            step(*what)
        elif kind == "entry":
            entry_step(*what)
        elif kind == "bias":
            bias_step(*what)
        elif kind == "small":
            small_step(*what)
        else:
            input_step()
    small_store.wait()
    bias_store.wait()
    pltpu.make_async_copy(out_ref, out_hbm, store_sem.at[0]).wait()
    pltpu.make_async_copy(dx_ref, dx_hbm, store_sem.at[1]).wait()
    gone(xall.at[:, 0 : others * tokens, :], x_send)
    gone(ids_all.at[:, 0 : others * tokens], i_send)
    gone(qkv.at[last, 0:head_share, 0 : others * tokens], l_send)
    gone(out_low.at[:, :, 0 : others * tokens], o_send)
    gone(gatt_t.at[0 : others * HEAD, :], d_send)
    gone(dqkv.at[:, :, 0 : others * tokens], p_send)


def widen_kernel(sums, small_hbm, bias_hbm, out_in, dx_in, *refs):
    outs, vectors, scratch = refs[:15], refs[15:23], refs[23:]
    small, bias, passed, inner_bias, outer_v, inner_v, out_v, entry_v = scratch[:8]
    in_sem, out_sem = scratch[8:]
    out_ref, dx_ref, entry, query_b, value_b, out_w, out_b = outs[:7]
    gain1, shift1, inner_w, inner_b, outer_w, outer_b, gain2, shift2 = outs[7:]
    width = WIDE
    ff = outer_w.shape[0]
    pieces = (2 * ff + width) // WIDE
    head_share = 3 * HEAD
    reads = []
    writes = []

    def read(src, dst):
        reads.append(pltpu.make_async_copy(src, dst, in_sem.at[len(reads)]))
        reads[-1].start()

    def write(src, dst):
        writes.append(pltpu.make_async_copy(src, dst, out_sem.at[len(writes)]))
        writes[-1].start()

    read(small_hbm, small)
    read(bias_hbm, bias)
    read(out_in, passed.at[0])
    read(dx_in, passed.at[1])
    for i in range(pieces):
        rows = slice(i * WIDE, (i + 1) * WIDE)
        value = sums[rows, :].astype(single)
        j = i - ff // WIDE
        if j < 0:
            outer_v[rows, :] = value
            write(outer_v.at[rows], outer_w.at[rows])
        elif j < ff // WIDE:
            columns = slice(j * WIDE, (j + 1) * WIDE)
            inner_v[:, columns] = value
            write(inner_v.at[:, columns], inner_w.at[:, columns])
        else:
            out_v[...] = value
            write(out_v, out_w)
    for j in range(3):
        columns = slice(j * width, (j + 1) * width)
        starts = [2 * ff + width + h * head_share + j * HEAD for h in range(HEADS)]
        value = jnp.concatenate([sums[at : at + HEAD, :] for at in starts], axis=0)
        entry_v[:, columns] = value.astype(single).T
        write(entry_v.at[:, columns], entry.at[:, columns])
    for read_done in reads:
        read_done.wait()
    write(passed.at[0], out_ref)
    write(passed.at[1], dx_ref)

    def small_row(at):
        return (bias if at < 2 else small)[at : at + 1, :].reshape(width)

    for j, (ref, at) in enumerate(
        (
            (query_b, 0),
            (value_b, 1),
            (out_b, 2),
            (gain1, 3),
            (shift1, 4),
            (outer_b, 9),
            (gain2, 10),
            (shift2, 11),
        )
    ):
        vectors[j][...] = small_row(at)
        write(vectors[j], ref)
    for j in range(ff // WIDE):
        inner_bias[j * WIDE : (j + 1) * WIDE] = small_row(5 + j)
    write(inner_bias, inner_b)
    for copy in writes:
        copy.wait()


UNITS = (
    (0, 512, "yuxv"),
    (512, 512, "uyxv"),
    (1024, 512, "zxy"),
    (1536, 512, "xyz"),
    (2048, 512, "yxz"),
    (2560, 512, "xyuv"),
    (3072, 512, "zyx"),
    (3584, 512, "xyz"),
    (4096, 512, "xyz"),
)
PLAN = {
    "early": (
        (2, "unit", 0, 0),
        (3, "unit", 1, 0),
        (3, "unit", 2, 0),
        (4, "unit", 3, 0),
        (7, "small", 0),
        (8, "unit", 0, 1),
        (8, "small", 1),
        (9, "unit", 1, 1),
        (10, "unit", 4, 0),
        (10, "unit", 5, 0),
    ),
    "attention": (
        (0, "unit", 3, 1),
        (0, "unit", 6, 0),
        (0, "unit", 7, 0),
        (0, "unit", 8, 0),
        (1, "unit", 2, 1),
        (2, "unit", 0, 2),
        (2, "unit", 1, 2),
        (2, "small", 2),
        (3, "unit", 4, 1),
        (3, "unit", 5, 1),
        (4, "unit", 3, 2),
        (5, "unit", 7, 1),
    ),
    "tail": (
        ("entry", 0),
        ("bias", 0),
        ("unit", 6, 1),
        ("unit", 8, 1),
        ("small", 3),
        ("unit", 3, 3),
        ("unit", 2, 2),
        ("unit", 0, 3),
        ("unit", 5, 2),
        ("entry", 1),
        ("unit", 1, 3),
        ("bias", 1),
        ("small", 4),
        ("unit", 3, 4),
        ("unit", 0, 4),
        ("unit", 5, 3),
        ("unit", 7, 2),
        ("unit", 4, 2),
        ("unit", 6, 2),
        ("unit", 8, 2),
        ("unit", 2, 3),
        ("entry", 2),
        ("unit", 3, 5),
        ("unit", 1, 4),
        ("input",),
        ("bias", 2),
        ("unit", 2, 4),
        ("unit", 0, 5),
        ("unit", 5, 4),
        ("unit", 6, 3),
        ("unit", 7, 3),
        ("entry", 3),
        ("unit", 4, 3),
        ("unit", 8, 3),
        ("unit", 1, 5),
        ("unit", 5, 5),
        ("unit", 3, 6),
        ("unit", 2, 5),
        ("unit", 7, 4),
        ("unit", 0, 6),
        ("unit", 3, 7),
        ("unit", 6, 4),
        ("unit", 4, 4),
        ("unit", 5, 6),
        ("unit", 8, 4),
        ("unit", 7, 5),
        ("entry", 4),
        ("unit", 6, 5),
        ("unit", 1, 6),
        ("unit", 4, 5),
        ("unit", 5, 7),
        ("entry", 5),
        ("unit", 8, 5),
        ("unit", 2, 6),
        ("unit", 0, 7),
        ("unit", 1, 7),
        ("unit", 7, 6),
        ("unit", 2, 7),
        ("unit", 7, 7),
        ("unit", 4, 6),
        ("unit", 5, 8),
        ("unit", 4, 7),
        ("unit", 6, 6),
        ("unit", 5, 9),
        ("unit", 0, 8),
        ("unit", 8, 6),
        ("unit", 6, 7),
        ("unit", 1, 8),
        ("unit", 0, 9),
        ("unit", 8, 7),
        ("unit", 1, 9),
    ),
}


def by_heads(groups):
    def run(inputs, blocks, we, qb, vb, wo, bo, g1, s1, w1, b1, w2, b2, g2, s2, cot):
        seqs, tokens, width = inputs.shape
        ff = w1.shape[1]
        rows = seqs * tokens
        length = tokens * HEADS
        grad_rows = 2 * ff + width
        units = UNITS
        others = max(groups - 1, 1)
        head_share = 3 * HEAD
        vmem = pl.BlockSpec(memory_space=pltpu.VMEM)
        hbm = pl.BlockSpec(memory_space=pl.ANY)
        dma = pltpu.SemaphoreType.DMA

        def shape(*dims):
            return jax.ShapeDtypeStruct(dims, single)

        out, dx, total, small, bias = pl.pallas_call(
            partial(layer_kernel, groups, units, PLAN),
            out_shape=[
                jax.ShapeDtypeStruct(inputs.shape, bfloat),
                jax.ShapeDtypeStruct(inputs.shape, bfloat),
                pltpu.VMEM((grad_rows + HEADS * head_share, width), bfloat),
                shape(16, width),
                shape(8, width),
            ],
            in_specs=[hbm] * 16,
            out_specs=[hbm, hbm, vmem, hbm, hbm],
            scratch_shapes=[
                pltpu.SMEM((seqs, 3, 2, HEADS), jnp.int32),
                pltpu.VMEM(inputs.shape, bfloat),
                pltpu.VMEM(qb.shape, bfloat),
                pltpu.VMEM(vb.shape, bfloat),
                pltpu.VMEM(bo.shape, bfloat),
                pltpu.VMEM(g1.shape, bfloat),
                pltpu.VMEM(s1.shape, bfloat),
                pltpu.VMEM(b1.shape, bfloat),
                pltpu.VMEM(b2.shape, bfloat),
                pltpu.VMEM(g2.shape, bfloat),
                pltpu.VMEM(s2.shape, bfloat),
                pltpu.VMEM(inputs.shape, bfloat),
                pltpu.VMEM(inputs.shape, bfloat),
                pltpu.VMEM((16, width), single),
                pltpu.VMEM(we.shape, bfloat),
                pltpu.VMEM(wo.shape, bfloat),
                pltpu.VMEM(w1.shape, bfloat),
                pltpu.VMEM(w2.shape, bfloat),
                pltpu.VMEM(cot.shape, bfloat),
                dma((16,)),
                pltpu.VMEM((head_share, width), bfloat),
                pltpu.VMEM((seqs, length, width), bfloat),
                pltpu.VMEM((HEADS, 16, tokens), bfloat),
                pltpu.VMEM((16, length), bfloat),
                pltpu.VMEM((seqs, 8, length), single),
                pltpu.VMEM((HEADS, head_share, tokens), bfloat),
                pltpu.VMEM((seqs, head_share + 16, length), bfloat),
                pltpu.VMEM((seqs, length, HEAD), bfloat),
                pltpu.VMEM((seqs, length, HEAD), bfloat),
                pltpu.VMEM((seqs, length, length), bfloat),
                pltpu.VMEM((seqs, 1, length), single),
                pltpu.VMEM((seqs, HEAD, length), single),
                pltpu.VMEM((seqs, HEAD, length), bfloat),
                pltpu.VMEM((width, rows), bfloat),
                pltpu.VMEM((rows, width), single),
                pltpu.VMEM((rows, 1), single),
                pltpu.VMEM((rows, width), bfloat),
                pltpu.VMEM((rows, ff), bfloat),
                pltpu.VMEM((rows, ff), single),
                pltpu.VMEM((rows, ff), bfloat),
                pltpu.VMEM((rows, width), bfloat),
                pltpu.VMEM((rows, width), single),
                pltpu.VMEM((rows, width), bfloat),
                pltpu.VMEM((width, rows), bfloat),
                pltpu.VMEM((seqs, HEAD, length), bfloat),
                pltpu.VMEM((seqs, head_share, length), bfloat),
                pltpu.VMEM((HEAD, length), single),
                pltpu.VMEM((HEAD, length), single),
                pltpu.VMEM((3, width, rows), bfloat),
                pltpu.VMEM((head_share, width), single),
                pltpu.VMEM((head_share, width), bfloat),
                pltpu.VMEM((others, head_share // groups, width), bfloat),
                pltpu.VMEM((grad_rows, width), bfloat),
                pltpu.VMEM((grad_rows, width), bfloat),
                pltpu.VMEM((3 + groups, 16, width), single),
                pltpu.VMEM((8, 2 * HEAD), single),
                pltpu.VMEM((others, 8, 2 * HEAD), single),
                pltpu.VMEM((HEADS, 8, 2 * HEAD), single),
                pltpu.VMEM((8, width), single),
                dma(()),
                dma((seqs, 3)),
                dma(()),
                dma(()),
                dma(()),
                dma(()),
                dma(()),
                dma((seqs,)),
                dma(()),
                dma((seqs,)),
                dma(()),
                dma(()),
                dma((len(units),)),
                dma((sum(2 * len(order) + 2 for _, _, order in units),)),
                dma((3,)),
                dma((5,)),
                dma(()),
                dma((4,)),
                dma((2,)),
                dma((2,)),
                dma((4,)),
                pltpu.SemaphoreType.REGULAR,
                pltpu.SemaphoreType.REGULAR,
            ],
            compiler_params=pltpu.CompilerParams(
                collective_id=0, has_side_effects=True, vmem_limit_bytes=LAYER_VMEM
            ),
            name="layer",
        )(
            inputs, blocks.transpose(0, 3, 2, 1), we, qb, vb, wo, bo, g1, s1, w1, b1, w2, b2,
            g2, s2, cot,
        )
        pieces = grad_rows // WIDE
        return pl.pallas_call(
            widen_kernel,
            in_specs=[vmem] + [hbm] * 4,
            out_specs=[hbm] * 15,
            out_shape=[
                jax.ShapeDtypeStruct(inputs.shape, bfloat),
                jax.ShapeDtypeStruct(inputs.shape, bfloat),
                shape(width, 3 * width),
                shape(width),
                shape(width),
                shape(width, width),
                shape(width),
                shape(width),
                shape(width),
                shape(width, ff),
                shape(ff),
                shape(ff, width),
                shape(width),
                shape(width),
                shape(width),
            ],
            scratch_shapes=[
                *[pltpu.VMEM((width,), single)] * 8,
                pltpu.VMEM((16, width), single),
                pltpu.VMEM((8, width), single),
                pltpu.VMEM((2, *inputs.shape), bfloat),
                pltpu.VMEM((ff,), single),
                pltpu.VMEM((ff, width), single),
                pltpu.VMEM((width, ff), single),
                pltpu.VMEM((width, width), single),
                pltpu.VMEM((width, 3 * width), single),
                dma((4,)),
                dma((pieces + 14,)),
            ],
            compiler_params=pltpu.CompilerParams(vmem_limit_bytes=WIDEN_VMEM),
            name="widen",
        )(pltpu.with_memory_space_constraint(total, pltpu.VMEM), small, bias, out, dx)

    return run


def solution(mesh):
    in_specs = (
        P("dp", "seq", None),
        P("dp", None, "seq", None),
        P(),
        P(),
        P(),
        P(),
        P(),
        P(),
        P(),
        P(),
        P(),
        P(),
        P(),
        P(),
        P(),
        P("dp", "seq", None),
    )
    out_specs = (
        P("dp", "seq", None),
        P("dp", "seq", None),
        P(),
        P(),
        P(),
        P(),
        P(),
        P(),
        P(),
        P(),
        P(),
        P(),
        P(),
        P(),
        P(),
    )
    heads_fit = mesh.shape["seq"] == HEADS
    plan = by_heads(mesh.shape["dp"]) if heads_fit else on_device
    return jax.shard_map(
        plan, mesh=mesh, in_specs=in_specs, out_specs=out_specs, check_vma=False
    )
```
